32 devices in a mesh: dp: 16 (over z, y, core), mp: 2 (over x).
Axes of the slice: x: 2, y: 2, z: 4, core: 2. Of those that a mesh axis runs over, the one named last changes fastest.
Arguments:
- tokens: bfloat16 [23040, 768], P('dp'), may hold values from -6 to 6
- cotangent: bfloat16 [23040, 768], P('dp'), may hold values from -6 to 6
- lengths: int32 [80], P('dp'), may hold values from 72 to 288, as said below
- doc_ids: int32 [80, 8], P('dp'), may hold values from 0 to 127
- doc_rows: bfloat16 [80, 8, 128], P('dp'), may hold values from -6 to 6
- w_qkv: float32 [3, 768, 768], P(None, 'dp', 'mp'), may hold values from -0.21875 to 0.21875
- m_qkv: float32 [3, 768, 768], P(None, 'dp', 'mp'), may hold values from -0.00061035156 to 0.00061035156
- v_qkv: float32 [3, 768, 768], P(None, 'dp', 'mp'), may hold values from 6.958547e-11 to 1.1133675e-09
- w_attn: float32 [768, 768], P('dp', 'mp'), may hold values from -0.875 to 0.875
- m_attn: float32 [768, 768], P('dp', 'mp'), may hold values from -0.00061035156 to 0.00061035156
- v_attn: float32 [768, 768], P('dp', 'mp'), may hold values from 6.958547e-11 to 1.1133675e-09
- w_inner: float32 [768, 3072], P('dp', 'mp'), may hold values from -0.21875 to 0.21875
- m_inner: float32 [768, 3072], P('dp', 'mp'), may hold values from -0.00061035156 to 0.00061035156
- v_inner: float32 [768, 3072], P('dp', 'mp'), may hold values from 6.958547e-11 to 1.1133675e-09
- w_outer: float32 [768, 3072], P('dp', 'mp'), may hold values from -0.109375 to 0.109375
- m_outer: float32 [768, 3072], P('dp', 'mp'), may hold values from -0.00061035156 to 0.00061035156
- v_outer: float32 [768, 3072], P('dp', 'mp'), may hold values from 6.958547e-11 to 1.1133675e-09
- w_proj: float32 [768, 128], P('dp'), may hold values from -0.21875 to 0.21875
- m_proj: float32 [768, 128], P('dp'), may hold values from -3.0517578e-05 to 3.0517578e-05
- v_proj: float32 [768, 128], P('dp'), may hold values from 1.9329297e-13 to 2.8993947e-12
- vectors: float32 [12, 768], P(None, ('dp', 'mp')), may hold values from -1.2 to 2.5, as said below
- m_vectors: float32 [12, 768], P(None, ('dp', 'mp')), may hold values from -0.005859375 to 0.005859375
- v_vectors: float32 [12, 768], P(None, ('dp', 'mp')), may hold values from 6.958547e-09 to 1.1133675e-07
Outputs:
- out_tokens: bfloat16 [23040, 768], P('dp')
- input_grad: float32 [23040, 768], P('dp')
- grad_norm: float32 [], replicated
- qkv_first: float32 [3, 768, 768], P(None, 'dp', 'mp')
- qkv_second: float32 [3, 768, 768], P(None, 'dp', 'mp')
- qkv_new: float32 [3, 768, 768], P(None, 'dp', 'mp')
- attn_first: float32 [768, 768], P('dp', 'mp')
- attn_second: float32 [768, 768], P('dp', 'mp')
- attn_new: float32 [768, 768], P('dp', 'mp')
- inner_first: float32 [768, 3072], P('dp', 'mp')
- inner_second: float32 [768, 3072], P('dp', 'mp')
- inner_new: float32 [768, 3072], P('dp', 'mp')
- outer_first: float32 [768, 3072], P('dp', 'mp')
- outer_second: float32 [768, 3072], P('dp', 'mp')
- outer_new: float32 [768, 3072], P('dp', 'mp')
- proj_first: float32 [768, 128], P('dp')
- proj_second: float32 [768, 128], P('dp')
- proj_new: float32 [768, 128], P('dp')
- vector_first: float32 [12, 768], P(None, ('dp', 'mp'))
- vector_second: float32 [12, 768], P(None, ('dp', 'mp'))
- vector_new: float32 [12, 768], P(None, ('dp', 'mp'))
- table_grad: float32 [128, 128], P('dp')
The draws below stay inside these ranges and needn't reach their ends.
Inputs may be any that keep to these rules, and one draw needn't show every extreme that they name: `lengths`: real tokens of each sequence; positions past it are padding keys; some sequence has all 288. `vectors`: norm gains positive, other rows of either sign.
All inputs are finite; a program needn't handle non-finite values.
Results may differ from the reference program's by a relative error of at most 0.012.
The reference program's roundings to bfloat16 on the way count: a program that leaves them out, or rounds other values in their place, can miss the bound.
Values may be sent and summed in bfloat16 or wider, within the bound.
A program may use at most 192 MiB of HBM per device.

```python
import math
import jax
import jax.numpy as jnp
import numpy as np
from jax import lax

D = 768
HEADS = 12
HEAD_DIM = 64
FF = 3072
PROJ = 128
CANDS = 8
SEQ = 288
STEP = 10
SEQ_DEV = 5
BATCH = 80
TOKENS = 23040
TABLE = 128
NVEC = 12
NPARAM = 7185408
N_DP = 16


def draw_lengths(key, part):
    seq_index = jnp.arange(BATCH)
    floor_len = SEQ // 4
    ceiling = floor_len + (SEQ - floor_len) * (seq_index + 1) // BATCH
    first_key, second_key = jax.random.split(key)
    raw_draw = jax.random.randint(first_key, (BATCH,), 0, 1 << 20)
    drawn = floor_len + raw_draw % (ceiling - floor_len + 1)
    chosen = jax.random.randint(second_key, (), 0, BATCH)
    return jnp.where(seq_index == chosen, SEQ, drawn).astype(jnp.int32)


def draw_vectors(key, part):
    gain_key, bias_key = jax.random.split(key)
    columns = jnp.arange(D).astype(jnp.float32) / D
    ramp = 0.5 + 1.5 * columns
    jitter = jax.random.uniform(gain_key, (NVEC, D), jnp.float32, 0.8, 1.25)
    gains = ramp[None, :] * jitter
    biases = jnp.clip(0.3 * jax.random.normal(bias_key, (NVEC, D), jnp.float32), -1.2, 1.2)
    row_index = jnp.arange(NVEC)[:, None]
    gain_rows = (row_index == 3) | (row_index == NVEC - 2)
    return jnp.where(gain_rows, gains, biases).astype(jnp.float32)


def touch_ends(result, key, least, high):
    longest = result.shape.index(max(result.shape))
    spots = []
    for shift in (0, 1):
        where = [jax.random.randint(jax.random.fold_in(key, axis), (), 0, length) for axis, length in enumerate(result.shape)]
        where[longest] = (where[longest] + shift) % result.shape[longest]
        spots.append(tuple(where))
    return result.at[spots[0]].set(least).at[spots[1]].set(high)


def raised(array, own_key, source, target, parts, factor):
    def block_of(axis_at):
        return (jnp.arange(array.shape[axis_at]) // (array.shape[axis_at] // parts)).reshape((-1,) + (1,) * (array.ndim - 1 - axis_at))

    near = jax.random.permutation(own_key, parts)[block_of(target)]
    far = (block_of(target) + parts // 2) % parts
    return jnp.where((block_of(source) == near) | (block_of(source) == far), factor * array, array)


def level_of(own_key, extent, pieces, least, largest):
    loudness = 1.0
    for axis_at, shards_of in pieces:
        steps = jax.random.uniform(jax.random.fold_in(jax.random.fold_in(own_key, 6), axis_at), (shards_of,), jnp.float32, least / len(pieces), largest / len(pieces))
        loudness = loudness * jnp.repeat(jnp.exp(steps), extent[axis_at] // shards_of).reshape((-1,) + (1,) * (len(extent) - 1 - axis_at))
    return loudness


def cumulative_ranks(count, slope):
    loads = [(1 << 20) // math.isqrt(standing ** slope) + 1 for standing in range(1, count + 1)]
    deviation = 1 + sum(loads) // (1 << 30)
    return np.cumsum(np.array([max(1, weight // deviation) for weight in loads]))


def ranked(rng, extent, number_of, skew):
    grid = cumulative_ranks(number_of, skew)
    ticket = jax.random.randint(jax.random.fold_in(rng, 1), extent, 0, int(grid[number_of - 1]))
    grade = jnp.searchsorted(jnp.asarray(grid, jnp.int32), ticket, side="right")
    return jax.random.permutation(jax.random.fold_in(rng, 2), number_of)[grade].astype(jnp.int32)


def scatter_about(stream_key, dims, deviation, reach, cuts=(), kind=jnp.bfloat16):
    gain = level_of(stream_key, dims, cuts, -0.22, 0.18) if cuts else 1.0
    values = jax.random.normal(stream_key, dims, jnp.float32) * deviation * gain
    return jnp.minimum(jnp.maximum(values, -reach), reach).astype(kind)


def noise_with(own_key, dims, width, limit, cuts, heavy, dtype=jnp.bfloat16):
    values = width * jax.random.normal(own_key, dims, jnp.float32)
    if cuts:
        values = values * level_of(own_key, dims, cuts, -0.22, 0.18)
    return jnp.clip(raised(values, jax.random.fold_in(own_key, 3), *heavy), -limit, limit).astype(dtype)


def setup_inputs(seed: int = 0) -> dict:
    seeds = jax.random.split(jax.random.key(seed), 24)
    tokens = scatter_about(seeds[0], (TOKENS, D), 1.0, 6.0, ((0, 16),))
    cotangent = noise_with(seeds[1], (TOKENS, D), 1.0, 6.0, ((0, 16),), (0, 1, 16, 2.0))
    lengths = draw_lengths(jax.random.fold_in(seeds[23], 71), 0)
    doc_ids = touch_ends(ranked(seeds[3], (BATCH, CANDS), TABLE, 2), jax.random.fold_in(seeds[3], 3), 0, TABLE - 1).astype(jnp.int32)
    doc_rows = scatter_about(seeds[4], (BATCH, CANDS, PROJ), 1.0, 6.0, ((0, 16),))
    w_qkv = scatter_about(seeds[5], (3, D, D), D ** -0.5, 0.21875, ((1, 16), (2, 2)), jnp.float32)
    m_qkv = scatter_about(seeds[6], (3, D, D), (0.11 / NPARAM ** 0.5), 0.00061035156, ((1, 16), (2, 2)), jnp.float32)
    v_qkv = jnp.clip(jnp.exp(math.log(1.1133675092978024e-09) - 2.7725887 * jax.random.uniform(seeds[7], (3, D, D), jnp.float32) ** level_of(seeds[7], (3, D, D), ((1, 16), (2, 2)), -0.2, 0.2)), 6.958546933111265e-11, 1.1133675092978024e-09)
    w_attn = scatter_about(seeds[8], (D, D), (D // 16) ** -0.5, 0.875, ((0, 16), (1, 2)), jnp.float32)
    m_attn = scatter_about(seeds[9], (D, D), (0.11 / NPARAM ** 0.5), 0.00061035156, ((0, 16), (1, 2)), jnp.float32)
    v_attn = jnp.clip(jnp.exp(math.log(1.1133675092978024e-09) - 2.7725887 * jax.random.uniform(seeds[10], (D, D), jnp.float32) ** level_of(seeds[10], (D, D), ((0, 16), (1, 2)), -0.2, 0.2)), 6.958546933111265e-11, 1.1133675092978024e-09)
    w_inner = scatter_about(seeds[11], (D, FF), D ** -0.5, 0.21875, ((0, 16), (1, 2)), jnp.float32)
    m_inner = scatter_about(seeds[12], (D, FF), (0.11 / NPARAM ** 0.5), 0.00061035156, ((0, 16), (1, 2)), jnp.float32)
    v_inner = jnp.clip(jnp.exp(math.log(1.1133675092978024e-09) - 2.7725887 * jax.random.uniform(seeds[13], (D, FF), jnp.float32) ** level_of(seeds[13], (D, FF), ((0, 16), (1, 2)), -0.2, 0.2)), 6.958546933111265e-11, 1.1133675092978024e-09)
    w_outer = scatter_about(seeds[14], (D, FF), FF ** -0.5, 0.109375, ((0, 16), (1, 2)), jnp.float32)
    m_outer = scatter_about(seeds[15], (D, FF), (0.11 / NPARAM ** 0.5), 0.00061035156, ((0, 16), (1, 2)), jnp.float32)
    v_outer = jnp.clip(jnp.exp(math.log(1.1133675092978024e-09) - 2.7725887 * jax.random.uniform(seeds[16], (D, FF), jnp.float32) ** level_of(seeds[16], (D, FF), ((0, 16), (1, 2)), -0.2, 0.2)), 6.958546933111265e-11, 1.1133675092978024e-09)
    w_proj = scatter_about(seeds[17], (D, PROJ), D ** -0.5, 0.21875, ((0, 16),), jnp.float32)
    m_proj = scatter_about(seeds[18], (D, PROJ), (0.09 / (SEQ * NPARAM) ** 0.5), 3.0517578125e-05, ((0, 16),), jnp.float32)
    v_proj = jnp.clip(jnp.exp(math.log(2.8993947000233167e-12) - 2.7080502 * jax.random.uniform(seeds[19], (D, PROJ), jnp.float32) ** level_of(seeds[19], (D, PROJ), ((0, 16),), -0.2, 0.2)), 1.9329297277353996e-13, 2.8993947000233167e-12)
    vectors = draw_vectors(jax.random.fold_in(seeds[23], 71), 0)
    m_vectors = scatter_about(seeds[21], (NVEC, D), (1.1 / NPARAM ** 0.5), 0.005859375, ((1, 32),), jnp.float32)
    v_vectors = jnp.clip(jnp.exp(math.log(1.1133675315022629e-07) - 2.7725887 * jax.random.uniform(seeds[22], (NVEC, D), jnp.float32) ** level_of(seeds[22], (NVEC, D), ((1, 32),), -0.2, 0.2)), 6.958547071889143e-09, 1.1133675315022629e-07)
    return {"tokens": tokens, "cotangent": cotangent, "lengths": lengths, "doc_ids": doc_ids, "doc_rows": doc_rows, "w_qkv": w_qkv, "m_qkv": m_qkv, "v_qkv": v_qkv, "w_attn": w_attn, "m_attn": m_attn, "v_attn": v_attn, "w_inner": w_inner, "m_inner": m_inner, "v_inner": v_inner, "w_outer": w_outer, "m_outer": m_outer, "v_outer": v_outer, "w_proj": w_proj, "m_proj": m_proj, "v_proj": v_proj, "vectors": vectors, "m_vectors": m_vectors, "v_vectors": v_vectors}


@jax.custom_vjp
def low(v):
    return lax.optimization_barrier(v.astype(jnp.bfloat16)).astype(jnp.float32)

@jax.custom_vjp
def low_back(v):
    return v

def low_keep(v):
    return (low(v), None)

def low_pass(kept, grad):
    return (grad,)

def back_keep(v):
    return (v, None)

def back_low(kept, grad):
    return (low(grad),)
low.defvjp(low_keep, low_pass)
low_back.defvjp(back_keep, back_low)
highest_mode = lax.Precision.HIGHEST
retrieval_scale = 0.17677669529663687
ln_epsilon = 1e-12
beta_first = 0.9
beta_second = 0.999
learn_rate = 0.05
vector_rate = 0.5
decay_rate = 0.01
adam_epsilon = 1e-08
clip_norm = 1.0

def layer_norm(values, gain_row, shift_row):
    centre = lax.optimization_barrier(jnp.mean(values, axis=-1, keepdims=True))
    centred = values - centre
    spread = lax.optimization_barrier(jnp.mean(centred * centred, axis=-1, keepdims=True))
    return centred * lax.rsqrt(spread + ln_epsilon) * gain_row + shift_row

def gelu_exact(values):
    return jax.nn.gelu(values, approximate=False)

def adamw_update(weight, moment, second, gradient, decay_factor, step_rate):
    moment_new = beta_first * moment + (1.0 - beta_first) * gradient
    second_new = beta_second * second + (1.0 - beta_second) * gradient * gradient
    first_hat = moment_new / (1.0 - beta_first ** STEP)
    second_hat = second_new / (1.0 - beta_second ** STEP)
    weight_new = weight - step_rate * (first_hat / (jnp.sqrt(second_hat) + adam_epsilon) + decay_factor * weight)
    return (moment_new, second_new, weight_new)

def forward(inputs, weights, doc_values, group_len):
    w_qkv, w_attn, w_inner, w_outer, w_proj, vectors = weights
    row_count = inputs.shape[0]
    ff_rows = FF // D
    projected = jnp.einsum('td,jde->jte', inputs, low(w_qkv), precision=highest_mode)
    queries = low(low_back(projected[0] + vectors[0]))
    keys_low = low(low_back(projected[1]))
    values = low(low_back(projected[2] + vectors[1]))
    head_shape = (SEQ_DEV, SEQ, HEADS, HEAD_DIM)
    raw_scores = jnp.einsum('gqhe,gkhe->ghqk', queries.reshape(head_shape), keys_low.reshape(head_shape), precision=highest_mode) * HEAD_DIM ** (-0.5)
    raw_scores = low_back(raw_scores)
    key_valid = (jnp.arange(SEQ)[None, :] < group_len[:, None])[:, None, None, :]
    raw_scores = jnp.where(key_valid, raw_scores, -1000000000.0)
    probs_low = low(jax.nn.softmax(raw_scores, axis=-1))
    mixed_out = jnp.einsum('ghqk,gkhe->gqhe', probs_low, values.reshape(head_shape), precision=highest_mode).reshape(row_count, D)
    mixed_out = low(low_back(mixed_out))
    attn_sum = low_back(jnp.einsum('te,de->td', mixed_out, low(w_attn), precision=highest_mode))
    resid_one = inputs + attn_sum + vectors[2]
    normed = layer_norm(resid_one, vectors[3], vectors[4])
    inner_pre = jnp.dot(low(normed), low(w_inner), precision=highest_mode) + vectors[5:5 + ff_rows].reshape(FF)
    inner_pre = low_back(inner_pre)
    active = low(gelu_exact(inner_pre))
    outer_out = low_back(jnp.einsum('tf,df->td', active, low(w_outer), precision=highest_mode))
    resid_two = normed + outer_out + vectors[5 + ff_rows]
    output = layer_norm(resid_two, vectors[6 + ff_rows], vectors[7 + ff_rows])
    cls_low = low(output.reshape(SEQ_DEV, SEQ, D)[:, 0])
    query_proj = low(low_back(jnp.dot(cls_low, low(w_proj), precision=highest_mode)))
    doc_scores = jnp.einsum('gp,gkp->gk', query_proj, doc_values, precision=highest_mode) * retrieval_scale
    loss_value = jnp.sum(jax.scipy.special.logsumexp(doc_scores, axis=-1) - doc_scores[:, 0])
    return (output, loss_value)

def reference(tokens, cotangent, lengths, doc_ids, doc_rows, w_qkv, m_qkv, v_qkv, w_attn, m_attn, v_attn, w_inner, m_inner, v_inner, w_outer, m_outer, v_outer, w_proj, m_proj, v_proj, vectors, m_vectors, v_vectors):
    params = (w_qkv, w_attn, w_inner, w_outer, w_proj, vectors)
    group_size = SEQ_DEV * SEQ
    group_items = (tokens.reshape(N_DP, group_size, D), cotangent.reshape(N_DP, group_size, D), lengths.reshape(N_DP, SEQ_DEV), doc_rows.reshape(N_DP, SEQ_DEV, CANDS, PROJ))

    def one_group(running, group_item):
        group_tokens, group_cot, group_len, group_docs = group_item

        def run_group(inputs, weights, doc_values):
            return forward(inputs, weights, doc_values, group_len)
        primal, pull_back = jax.vjp(run_group, group_tokens.astype(jnp.float32), params, group_docs.astype(jnp.float32))
        input_part, weight_grads, row_grads = pull_back((group_cot.astype(jnp.float32), jnp.ones((), jnp.float32)))
        running = jax.tree.map(jnp.add, running, weight_grads)
        return (running, (primal[0].astype(jnp.bfloat16), input_part, row_grads))
    zero_grads = jax.tree.map(jnp.zeros_like, params)
    totals, stacked = lax.scan(one_group, zero_grads, group_items)
    outputs, input_grads, row_grads = stacked
    grad_qkv, grad_attn, grad_inner, grad_outer, grad_proj, grad_vectors = totals
    table_grad = jax.ops.segment_sum(row_grads.reshape(-1, PROJ), doc_ids.reshape(-1).astype(jnp.int32), num_segments=TABLE)
    squares = jnp.sum(grad_qkv * grad_qkv) + jnp.sum(grad_attn * grad_attn) + jnp.sum(grad_inner * grad_inner) + jnp.sum(grad_outer * grad_outer) + jnp.sum(grad_proj * grad_proj) + jnp.sum(grad_vectors * grad_vectors)
    grad_norm = jnp.sqrt(squares)
    clip_factor = clip_norm / jnp.maximum(grad_norm, clip_norm)
    qkv_first, qkv_second, qkv_new = adamw_update(w_qkv, m_qkv, v_qkv, grad_qkv * clip_factor, decay_rate, learn_rate)
    attn_first, attn_second, attn_new = adamw_update(w_attn, m_attn, v_attn, grad_attn * clip_factor, decay_rate, learn_rate)
    inner_first, inner_second, inner_new = adamw_update(w_inner, m_inner, v_inner, grad_inner * clip_factor, decay_rate, learn_rate)
    outer_first, outer_second, outer_new = adamw_update(w_outer, m_outer, v_outer, grad_outer * clip_factor, decay_rate, learn_rate)
    proj_first, proj_second, proj_new = adamw_update(w_proj, m_proj, v_proj, grad_proj * clip_factor, decay_rate, learn_rate)
    vector_first, vector_second, vector_new = adamw_update(vectors, m_vectors, v_vectors, grad_vectors * clip_factor, 0.0, vector_rate)
    return (outputs.reshape(TOKENS, D), input_grads.reshape(TOKENS, D), grad_norm, qkv_first, qkv_second, qkv_new, attn_first, attn_second, attn_new, inner_first, inner_second, inner_new, outer_first, outer_second, outer_new, proj_first, proj_second, proj_new, vector_first, vector_second, vector_new, table_grad)
```

```python
import functools

import jax
import jax.numpy as jnp
from jax import lax
from jax.experimental import pallas as pl
from jax.experimental.pallas import tpu as pltpu
from jax.sharding import PartitionSpec as P

HEAD_DIM = 64
STEP = 10
TAB_DEV = 8
MESH = pl.DeviceIdType.MESH
ANY = pl.ANY
BF = jnp.bfloat16
F32 = jnp.float32
NZ, NY, NC, NX = 4, 2, 2, 2

highest_mode = lax.Precision.HIGHEST
retrieval_scale = 0.17677669529663687
ln_epsilon = 1e-12
beta_first = 0.9
beta_second = 0.999
learn_rate = 0.05
vector_rate = 0.5
decay_rate = 0.01
adam_epsilon = 1e-08
clip_norm = 1.0


def layer_norm(values, gain_row, shift_row):
    centre = jnp.mean(values, axis=-1, keepdims=True)
    centred = values - centre
    spread = jnp.mean(centred * centred, axis=-1, keepdims=True)
    return centred * lax.rsqrt(spread + ln_epsilon) * gain_row + shift_row


def gelu_exact(values):
    return jax.nn.gelu(values, approximate=False)


def adamw_update(weight, moment, second, gradient, decay_factor, step_rate):
    moment_new = beta_first * moment + (1.0 - beta_first) * gradient
    second_new = beta_second * second + (1.0 - beta_second) * gradient * gradient
    first_hat = moment_new / (1.0 - beta_first**STEP)
    second_hat = second_new / (1.0 - beta_second**STEP)
    weight_new = weight - step_rate * (
        first_hat / (jnp.sqrt(second_hat) + adam_epsilon) + decay_factor * weight
    )
    return (moment_new, second_new, weight_new)


def squared(values):
    return jnp.sum(values * values)


class Place:
    def __init__(self):
        dp = lax.axis_index("dp")
        self.x = lax.axis_index("mp")
        self.c = lax.rem(dp, NC)
        self.y = lax.rem(dp // NC, NY)
        self.z = dp // (NC * NY)

    def dev(self, z=None, y=None, c=None, x=None):
        z = self.z if z is None else z
        y = self.y if y is None else y
        c = self.c if c is None else c
        x = self.x if x is None else x
        return ((z * NY + y) * NC + c, x)

    def others(self):
        out = [self.dev(z=lax.rem(self.z + k, NZ)) for k in range(1, NZ)]
        out.append(self.dev(x=1 - self.x))
        out.append(self.dev(y=1 - self.y))
        out.append(self.dev(c=1 - self.c))
        return out

    def eights(self):
        out = []
        for k in range(1, 8):
            dx, dy, dc = k & 1, (k >> 1) & 1, k >> 2
            out.append(
                self.dev(
                    x=self.x + dx - 2 * dx * self.x,
                    y=self.y + dy - 2 * dy * self.y,
                    c=self.c + dc - 2 * dc * self.c,
                )
            )
        return out


def greet(devices):
    barrier = pltpu.get_barrier_semaphore()
    for d in devices:
        pl.semaphore_signal(barrier, inc=1, device_id=d, device_id_type=MESH)
    pl.semaphore_wait(barrier, len(devices))


def remote(src, dst, ssem, rsem, dev):
    return pltpu.make_async_remote_copy(
        src_ref=src, dst_ref=dst, send_sem=ssem, recv_sem=rsem, device_id=dev, device_id_type=MESH
    )


def cols(x, half):
    return pl.ds(pl.multiple_of(x * half, 128), half)


def gather_kernel(n_in, n_out, index, *refs):
    ins, outs = refs[:n_in], refs[n_in : n_in + n_out]
    lsem, zs, zr, s1, r1, s2, r2, ds, dr = refs[n_in + n_out :]
    me = Place()
    greet(me.others())
    n = len(index)
    pieces = []
    for i, li, o, lo in index:
        src = ins[i] if li is None else ins[i].at[li]
        dst = outs[o] if lo is None else outs[o].at[lo]
        pieces.append((src, dst, dst.shape[-1] // 2))

    waits = []

    def go(copy):
        copy.start()
        waits.append(copy)
        return copy

    def step1(p):
        src, dst, half = pieces[p]
        blk = dst.at[me.z, me.y, me.c, :, cols(me.x, half)]
        loc = pltpu.make_async_copy(src, blk, lsem.at[p])
        loc.start()
        for k in range(1, NZ):
            go(remote(src, blk, zs.at[p, k], zr.at[p, k], me.dev(z=lax.rem(me.z + k, NZ))))
        return loc

    def part(p, stage):
        _, dst, half = pieces[p]
        own, other = cols(me.x, half), cols(1 - me.x, half)
        if stage == "z":
            return dst.at[:, me.y, me.c, :, own]
        if p % 2 == 0:
            if stage == "in1":
                return dst.at[:, me.y, me.c, :, other]
            if stage == "out2":
                return dst.at[:, me.y, me.c]
            return dst.at[:, 1 - me.y, me.c]
        if stage == "in1":
            return dst.at[:, 1 - me.y, me.c, :, own]
        if stage == "out2":
            return dst.at[:, :, me.c, :, own]
        return dst.at[:, :, me.c, :, other]

    def cross(p, stage, ref, which):
        dev = me.dev(c=1 - me.c)
        go(remote(ref, ref, ds.at[p, which], dr.at[p, which], dev))

    def step2(p, loc):
        src, dst, half = pieces[p]
        loc.wait()
        for k in range(1, NZ):
            blk = dst.at[lax.rem(me.z + NZ - k, NZ), me.y, me.c, :, cols(me.x, half)]
            remote(blk, blk, zs.at[p, k], zr.at[p, k], me.dev()).wait_recv()
        have = part(p, "z")
        dev = me.dev(x=1 - me.x) if p % 2 == 0 else me.dev(y=1 - me.y)
        go(remote(have, have, s1.at[p], r1.at[p], dev))
        cross(p, "z", have, 0)

    def step3(p):
        got = part(p, "in1")
        remote(got, got, s1.at[p], r1.at[p], me.dev()).wait_recv()
        have = part(p, "out2")
        dev = me.dev(y=1 - me.y) if p % 2 == 0 else me.dev(x=1 - me.x)
        go(remote(have, have, s2.at[p], r2.at[p], dev))
        cross(p, "in1", got, 1)

    def step4(p):
        got = part(p, "in2")
        remote(got, got, s2.at[p], r2.at[p], me.dev()).wait_recv()
        cross(p, "in2", got, 2)

    def step5(p):
        _, dst, half = pieces[p]
        own, other = cols(me.x, half), cols(1 - me.x, half)
        oc = 1 - me.c
        got = [dst.at[:, me.y, oc, :, own]]
        if p % 2 == 0:
            got += [dst.at[:, me.y, oc, :, other], dst.at[:, 1 - me.y, oc]]
        else:
            got += [dst.at[:, 1 - me.y, oc, :, own], dst.at[:, :, oc, :, other]]
        for which, ref in enumerate(got):
            remote(ref, ref, ds.at[p, which], dr.at[p, which], me.dev()).wait_recv()

    locs = {}
    ahead = 2
    for p in range(min(ahead, n)):
        locs[p] = step1(p)
    for t in range(n + 3):
        if t < n:
            step2(t, locs[t])
            if t + ahead < n:
                locs[t + ahead] = step1(t + ahead)
        if 0 <= t - 1 < n:
            step3(t - 1)
        if 0 <= t - 2 < n:
            step4(t - 2)
        if 0 <= t - 3 < n:
            step5(t - 3)
    for copy in waits:
        copy.wait_send()


def dma(*shape):
    return pltpu.SemaphoreType.DMA(shape)


def gather_fast(shards, small, rows):
    qk, va, inner, outer = shards
    width = 2 * qk.shape[2]
    ffw = 2 * inner.shape[2]
    zyc = (NZ, NY, NC)
    index = [
        (1, 0, 1, 0),
        (2, 0, 2, 0),
        (1, 1, 1, 1),
        (2, 1, 2, 1),
        (3, 0, 3, 0),
        (3, 1, 3, 1),
        (4, 0, 4, 0),
        (4, 1, 4, 1),
        (0, None, 0, None),
    ]
    n = len(index)
    outs = pl.pallas_call(
        functools.partial(gather_kernel, 5, 5, index),
        out_shape=[
            jax.ShapeDtypeStruct(zyc + (small.shape[0], 2 * small.shape[1]), F32),
            jax.ShapeDtypeStruct((2,) + zyc + (rows, width), BF),
            jax.ShapeDtypeStruct((2,) + zyc + (rows, width), BF),
            jax.ShapeDtypeStruct((2,) + zyc + (rows, ffw), BF),
            jax.ShapeDtypeStruct((2,) + zyc + (rows, ffw), BF),
        ],
        in_specs=[pl.BlockSpec(memory_space=ANY)] * 5,
        out_specs=[pl.BlockSpec(memory_space=ANY)] * 5,
        scratch_shapes=[
            dma(n), dma(n, NZ), dma(n, NZ), dma(n), dma(n), dma(n), dma(n), dma(n, 3), dma(n, 3),
        ],
        compiler_params=pltpu.CompilerParams(collective_id=1, has_side_effects=True),
        name="gather",
    )(small, qk, va, inner, outer)
    return outs


def reduce_kernel(n_in, n_out, index, *refs):
    ins, outs = refs[:n_in], refs[n_in : n_in + n_out]
    rest = refs[n_in + n_out :]
    nb = len(index)
    bufs, rest = rest[: 5 * nb], rest[5 * nb :]
    sq4, sq8, lsem, ds, dr, s1, r1, s2, r2, zs, zr, xs, xr, qs, qr, es, er = rest
    send_out, send_dx = ins[-2:]
    peer_out, peer_dx, peer_small, norm_ref = outs[-4:]
    me = Place()
    greet(me.others() + me.eights())
    n = len(index)
    waits = []

    def go(copy):
        copy.start()
        waits.append(copy)
        return copy

    oc, oy, ox = 1 - me.c, 1 - me.y, 1 - me.x
    pieces = []
    for p, (i, li, o, lo, sx) in enumerate(index):
        src = ins[i] if li is None else ins[i].at[li]
        dst = outs[o] if lo is None else outs[o].at[lo]
        pieces.append((src, dst) + tuple(bufs[5 * p : 5 * p + 5]))

    def step1(p):
        src, _, own, got1, _, _, _ = pieces[p]
        go(remote(src.at[:, :, oc], got1, ds.at[p], dr.at[p], me.dev(c=oc)))
        loc = pltpu.make_async_copy(src.at[:, :, me.c], own, lsem.at[p])
        loc.start()
        return loc

    def half(ref):
        return ref.shape[-1] // 2

    def step2(p, loc):
        _, _, own, got1, got2, got3, got4 = pieces[p]
        loc.wait()
        remote(got1, got1, ds.at[p], dr.at[p], me.dev()).wait_recv()
        own[...] = own[...] + got1[...]
        if p % 2 == 0:
            go(remote(own.at[:, oy], got2, s1.at[p], r1.at[p], me.dev(y=oy)))
        else:
            go(remote(own.at[:, :, :, cols(ox, half(own))], got2, s1.at[p], r1.at[p], me.dev(x=ox)))

    def step3(p):
        _, _, own, _, got2, got3, _ = pieces[p]
        remote(got2, got2, s1.at[p], r1.at[p], me.dev()).wait_recv()
        h = half(own)
        if p % 2 == 0:
            own[:, me.y] = own[:, me.y] + got2[...]
            go(remote(own.at[:, me.y, :, cols(ox, h)], got3, s2.at[p], r2.at[p], me.dev(x=ox)))
        else:
            own[:, :, :, cols(me.x, h)] = own[:, :, :, cols(me.x, h)] + got2[...]
            go(remote(own.at[:, oy, :, cols(me.x, h)], got3, s2.at[p], r2.at[p], me.dev(y=oy)))

    def step4(p):
        _, _, own, _, _, got3, got4 = pieces[p]
        remote(got3, got3, s2.at[p], r2.at[p], me.dev()).wait_recv()
        h = half(own)
        mine = cols(me.x, h)
        own[:, me.y, :, mine] = own[:, me.y, :, mine] + got3[...]
        for k in range(1, NZ):
            tz = lax.rem(me.z + k, NZ)
            go(remote(own.at[tz, me.y, :, mine], got4.at[k], zs.at[p, k], zr.at[p, k], me.dev(z=tz)))

    def step5(p):
        _, dst, own, _, _, _, got4 = pieces[p]
        for k in range(1, NZ):
            remote(got4.at[k], got4.at[k], zs.at[p, k], zr.at[p, k], me.dev()).wait_recv()
        total = own[me.z, me.y, :, cols(me.x, half(own))].astype(F32)
        for k in range(1, NZ):
            total = total + got4[k].astype(F32)
        dst[...] = total
        return jnp.sum(total * total, keepdims=True)

    go(remote(send_out, peer_out, xs.at[0], xr.at[0], me.dev(x=ox)))
    locs = {}
    ahead = 2
    total = jnp.zeros((1, 1), F32)
    for p in range(min(ahead, n)):
        locs[p] = step1(p)
    for t in range(n + 3):
        if t < n:
            step2(t, locs[t])
            if t + ahead < n:
                locs[t + ahead] = step1(t + ahead)
        if 0 <= t - 1 < n:
            step3(t - 1)
        if 0 <= t - 2 < n:
            step4(t - 2)
        if 0 <= t - 3 < n:
            p = t - 3
            part = step5(p)
            if index[p][4]:
                total = total + part
    go(remote(send_dx, peer_dx, xs.at[1], xr.at[1], me.dev(x=ox)))
    small = outs[index[-1][2]]
    go(remote(small, peer_small, xs.at[2], xr.at[2], me.dev(x=ox)))
    row = lax.broadcasted_iota(jnp.int32, small.shape, 0)
    keep = jnp.where(row < 36, small[...], 0.0)
    total = total + jnp.sum(keep * keep, keepdims=True)
    sq4[0] = jnp.broadcast_to(total, (8, 128))
    copies = []
    for k in range(1, NZ):
        c = remote(sq4.at[0], sq4.at[k], qs.at[k], qr.at[k], me.dev(z=lax.rem(me.z + k, NZ)))
        copies.append(go(c))
    for k in range(1, NZ):
        copies[k - 1].wait_recv()
    def at_z(z):
        out = jnp.zeros((8, 128), F32)
        for k in range(NZ):
            src = lax.rem(me.z + NZ - k, NZ)
            out = out + jnp.where(src == z, sq4[k], 0.0)
        return out
    group = at_z(0) + at_z(1) + at_z(2) + at_z(3)
    sq8[0] = group
    copies = []
    for k, dev in enumerate(me.eights(), 1):
        copies.append(go(remote(sq8.at[0], sq8.at[k], es.at[k], er.at[k], dev)))
    for copy in copies:
        copy.wait_recv()
    code = me.x + 2 * me.y + 4 * me.c

    def at_code(w):
        out = jnp.zeros((8, 128), F32)
        for k in range(8):
            dx, dy, dc = k & 1, (k >> 1) & 1, k >> 2
            src = (
                (me.x + dx - 2 * dx * me.x)
                + 2 * (me.y + dy - 2 * dy * me.y)
                + 4 * (me.c + dc - 2 * dc * me.c)
            )
            out = out + jnp.where(src == w, sq8[k], 0.0)
        return out

    whole = at_code(0)
    for w in range(1, 8):
        whole = whole + at_code(w)
    norm_ref[...] = whole
    remote(peer_out, peer_out, xs.at[0], xr.at[0], me.dev()).wait_recv()
    remote(peer_dx, peer_dx, xs.at[1], xr.at[1], me.dev()).wait_recv()
    remote(peer_small, peer_small, xs.at[2], xr.at[2], me.dev()).wait_recv()
    for copy in waits:
        copy.wait_send()


def reduce_fast(grads, small, own_out, own_dx, rows):
    zyc = (NZ, NY, NC)
    arrays = [small.reshape(zyc + small.shape[1:])]
    arrays += [g.reshape((2,) + zyc + (rows, g.shape[2])) for g in grads]
    index = [
        (4, 0, 4, 0, True),
        (4, 1, 4, 1, True),
        (3, 0, 3, 0, True),
        (3, 1, 3, 1, True),
        (2, 1, 2, 1, True),
        (1, 0, 1, 0, True),
        (1, 1, 1, 1, True),
        (2, 0, 2, 0, True),
        (0, None, 0, None, False),
    ]
    n = len(index)
    out_shape = [
        jax.ShapeDtypeStruct((small.shape[1], small.shape[2] // 2), F32),
    ] + [jax.ShapeDtypeStruct((2, rows, g.shape[2] // 2), F32) for g in grads]
    out_shape += [
        jax.ShapeDtypeStruct(own_out.shape, BF),
        jax.ShapeDtypeStruct(own_dx.shape, BF),
        jax.ShapeDtypeStruct((small.shape[1], small.shape[2] // 2), F32),
        jax.ShapeDtypeStruct((8, 128), F32),
    ]
    bufs = []
    for p, (i, _, _, _, _) in enumerate(index):
        r, w = arrays[i].shape[-2:]
        dt = arrays[i].dtype
        bufs += [pltpu.VMEM((NZ, NY, r, w), dt), pltpu.VMEM((NZ, NY, r, w), dt)]
        if p % 2 == 0:
            bufs += [pltpu.VMEM((NZ, r, w), dt)]
        else:
            bufs += [pltpu.VMEM((NZ, NY, r, w // 2), dt)]
        bufs += [pltpu.VMEM((NZ, r, w // 2), dt), pltpu.VMEM((NZ, r, w // 2), dt)]
    vm = pl.BlockSpec(memory_space=pltpu.VMEM)
    hb = pl.BlockSpec(memory_space=ANY)
    return pl.pallas_call(
        functools.partial(reduce_kernel, 7, len(out_shape), index),
        out_shape=out_shape,
        in_specs=[hb] * 7,
        out_specs=[vm] * 5 + [hb, hb, vm, vm],
        scratch_shapes=bufs
        + [
            pltpu.VMEM((NZ, 8, 128), F32), pltpu.VMEM((8, 8, 128), F32),
            dma(n), dma(n), dma(n), dma(n), dma(n), dma(n), dma(n), dma(n, NZ), dma(n, NZ),
            dma(3), dma(3), dma(NZ), dma(NZ), dma(8), dma(8),
        ],
        compiler_params=pltpu.CompilerParams(
            collective_id=2, has_side_effects=True, vmem_limit_bytes=56 * 2**20
        ),
        name="reduce",
    )(*arrays, own_out, own_dx)


def gather_plain(shards, small, rows):
    def both(v, axis):
        v = lax.all_gather(v, "dp", axis=axis, tiled=True)
        return lax.all_gather(v, "mp", axis=2, tiled=True)

    return [both(small[None], 0)] + [both(v, 1) for v in shards]


def reduce_plain(grads, small, own_out, own_dx, rows):
    def both(v, axis, wide):
        v = lax.psum_scatter(v.astype(F32), "mp", scatter_dimension=wide, tiled=True)
        return lax.psum_scatter(v, "dp", scatter_dimension=axis, tiled=True)

    small_sum = both(small, 0, 2)[0]
    sums = [both(g, 1, 2) for g in grads]
    ox = 1 - lax.axis_index("mp")
    swap = [(0, 1), (1, 0)]
    peer_out = lax.ppermute(own_out, "mp", swap)
    peer_dx = lax.ppermute(own_dx, "mp", swap)
    peer_small = lax.ppermute(small_sum, "mp", swap)
    squares = sum(squared(g) for g in sums) + squared(small_sum[:-4])
    total = lax.psum(squares, ("dp", "mp"))
    return [small_sum] + sums + [peer_out, peer_dx, peer_small, jnp.full((8, 128), total)]


def local(
    tokens, cotangent, lengths, doc_ids, doc_rows,
    w_qkv, m_qkv, v_qkv, w_attn, m_attn, v_attn, w_inner, m_inner, v_inner,
    w_outer, m_outer, v_outer, w_proj, m_proj, v_proj, vectors, m_vectors, v_vectors,
):
    mp = lax.axis_index("mp")
    n_dp, n_mp = lax.axis_size("dp"), lax.axis_size("mp")
    fast = n_dp == NZ * NY * NC and n_mp == NX
    seqs = lengths.shape[0]
    all_rows, width = tokens.shape
    seq_len = all_rows // seqs
    full = seqs // 2
    n_full, n_half = full * seq_len, seq_len // 2
    n_own = n_full + n_half
    heads = width // HEAD_DIM
    rows = w_qkv.shape[1]
    half_w, half_ff = w_qkv.shape[2], w_inner.shape[1]
    ff = 2 * half_ff
    score_scale = HEAD_DIM ** (-0.5)

    def two(v):
        return v.reshape(rows, 2, half_ff // 2).transpose(1, 0, 2)

    qk_s = w_qkv[:2].astype(BF)
    va_s = jnp.stack([w_qkv[2], w_attn]).astype(BF)
    inner_s = two(w_inner.astype(BF))
    outer_s = two(w_outer.astype(BF))
    vec_pad = jnp.pad(vectors, ((0, 16 - vectors.shape[0]), (0, 128 - vectors.shape[1])))
    half_rows = rows // 2
    proj_half = lax.dynamic_slice_in_dim(w_proj, mp * half_rows, half_rows, 0)
    small_s = jnp.concatenate([proj_half, vec_pad], axis=0)
    gather = gather_fast if fast else gather_plain
    small_g, qk, va, inner, outer = gather([qk_s, va_s, inner_s, outer_s], small_s, rows)
    small_g = small_g.reshape(n_dp, half_rows + 16, 2, 128)
    proj = small_g[:, :half_rows].transpose(0, 2, 1, 3).reshape(width, 128).astype(BF)
    nvec, vec_lanes = vectors.shape
    vec = small_g[:, half_rows : half_rows + nvec, :, :vec_lanes].transpose(1, 0, 2, 3).reshape(nvec, width)
    qk = qk.reshape(2, width, width)
    va = va.reshape(2, width, width)
    inner = inner.reshape(2, width, half_ff)
    outer = outer.reshape(2, width, half_ff)
    ff_rows = nvec - 8
    b_inner = (
        vec[5 : 5 + ff_rows].reshape(2, 2, half_ff // 2).transpose(1, 0, 2).reshape(2, half_ff)
    )
    bias_attn, gain_one, shift_one = vec[2], vec[3], vec[4]
    bias_outer, gain_two, shift_two = vec[5 + ff_rows], vec[6 + ff_rows], vec[7 + ff_rows]

    a0 = mp * n_own + mp * 0
    a0 = mp * (n_full + seq_len)
    h0 = n_full + mp * n_half
    o0 = n_full + (1 - mp) * n_half

    def own_rows(v):
        return jnp.concatenate(
            [lax.dynamic_slice_in_dim(v, a0, n_full, 0), lax.dynamic_slice_in_dim(v, h0, n_half, 0)]
        )

    x_own = own_rows(tokens)
    x_all = jnp.concatenate([x_own, lax.dynamic_slice_in_dim(tokens, o0, n_half, 0)])
    cot = own_rows(cotangent)
    my_seqs = jnp.concatenate([mp * (full + 1) + jnp.arange(full), jnp.array([full])])
    my_len = lengths[my_seqs]
    pos = jnp.arange(seq_len)
    pos_last = jnp.where(pos < n_half, pos + mp * n_half, pos - n_half + (1 - mp) * n_half)
    valid_full = pos[None, :] < my_len[:full, None]
    valid_last = pos_last[None, :] < my_len[full:, None]

    q = (jnp.dot(x_own, qk[0], preferred_element_type=F32) + vec[0]).astype(BF)
    k = jnp.dot(x_all, qk[1], preferred_element_type=F32).astype(BF)
    v = (jnp.dot(x_all, va[0], preferred_element_type=F32) + vec[1]).astype(BF)

    def split(t, first):
        return (
            t[:n_full].reshape(full, seq_len, heads, HEAD_DIM),
            t[n_full:].reshape(1, first, heads, HEAD_DIM),
        )

    qs, ks, vs = split(q, n_half), split(k, seq_len), split(v, seq_len)
    valids = (valid_full, valid_last)
    lses, outs = [], []

    def scores(qh, kh, valid):
        raw = jnp.einsum("gqhe,gkhe->ghqk", qh, kh, preferred_element_type=F32) * score_scale
        return jnp.where(valid[:, None, None, :], raw, -1000000000.0)

    for qh, kh, vh, valid in zip(qs, ks, vs, valids):
        s = scores(qh, kh, valid)
        top = jnp.max(s, axis=-1, keepdims=True)
        lse = top + jnp.log(jnp.sum(jnp.exp(s - top), axis=-1, keepdims=True))
        pb = jnp.exp(s - lse).astype(BF)
        o = jnp.einsum("ghqk,gkhe->gqhe", pb, vh, preferred_element_type=F32)
        outs.append(o.reshape(-1, width).astype(BF))
        lses.append(lse)
    mixed = jnp.concatenate(outs)
    attn = jnp.einsum("te,de->td", mixed, va[1], preferred_element_type=F32)
    z1 = x_own.astype(F32) + attn + bias_attn
    normed, norm_one_back = jax.vjp(layer_norm, z1, gain_one, shift_one)
    normed_low = normed.astype(BF)
    pre = jnp.einsum("td,hdf->htf", normed_low, inner, preferred_element_type=F32) + b_inner[:, None, :]
    act, gelu_back = jax.vjp(gelu_exact, pre)
    act_low = act.astype(BF)
    f_out = jnp.einsum("htf,hdf->td", act_low, outer, preferred_element_type=F32)
    z2 = normed + f_out + bias_outer
    output, norm_two_back = jax.vjp(layer_norm, z2, gain_two, shift_two)
    out_own = output.astype(BF)

    n_mine = full + 1
    mine = jnp.where((jnp.arange(n_mine) < full) | (mp == 0), 1.0, 0.0).astype(F32)
    cls_low = out_own[:: seq_len][:n_mine]
    docs = doc_rows[my_seqs].astype(F32)
    ids = doc_ids[my_seqs]
    query = jnp.dot(cls_low, proj, preferred_element_type=F32).astype(BF)
    query_float = query.astype(F32)
    doc_scores = jnp.einsum("gp,gkp->gk", query_float, docs, precision=highest_mode) * retrieval_scale
    soft = jax.nn.softmax(doc_scores, axis=-1)
    target = (jnp.arange(doc_scores.shape[1]) == 0).astype(F32)
    score_grad = (soft - target[None, :]) * retrieval_scale * mine[:, None]
    query_grad = jnp.einsum("gk,gkp->gp", score_grad, docs, precision=highest_mode).astype(BF)
    row_grads = score_grad[:, :, None] * query_float[:, None, :]
    cls_grad = jnp.einsum("gp,dp->gd", query_grad, proj, preferred_element_type=F32)
    proj_grad = jnp.einsum("gd,gp->dp", cls_low, query_grad, preferred_element_type=F32)
    table_rows = TAB_DEV * n_dp
    one_hot = (jnp.arange(table_rows)[:, None] == ids.reshape(1, -1)).astype(F32)
    table_local = jnp.dot(one_hot, row_grads.reshape(-1, row_grads.shape[2]), precision=highest_mode)

    dy = cot.astype(F32)
    first_rows = jnp.arange(n_mine) * seq_len
    dy = dy.at[first_rows].add(cls_grad)
    dz2, dg2, dc2 = norm_two_back(dy)
    df = dz2.astype(BF)
    dg = jnp.einsum("td,hdf->htf", df, outer, preferred_element_type=F32)
    g_outer = jnp.einsum("td,htf->hdf", df, act_low, preferred_element_type=F32).astype(BF)
    (du,) = gelu_back(dg)
    du = du.astype(BF)
    g_inner = jnp.einsum("td,htf->hdf", normed_low, du, preferred_element_type=F32).astype(BF)
    dh1 = jnp.einsum("htf,hdf->td", du, inner, preferred_element_type=F32) + dz2
    dz1, dg1, dc1 = norm_one_back(dh1)
    da = dz1.astype(BF)
    do = jnp.dot(da, va[1], preferred_element_type=F32).astype(BF)
    g_attn = jnp.einsum("td,te->de", da, mixed, preferred_element_type=F32)
    dos = split(do, n_half)
    dqs, dks, dvs = [], [], []
    for qh, kh, vh, doh, valid, lse in zip(qs, ks, vs, dos, valids, lses):
        probs = jnp.exp(scores(qh, kh, valid) - lse)
        dp_ = jnp.einsum("gqhe,gkhe->ghqk", doh, vh, preferred_element_type=F32)
        delta = jnp.sum(probs * dp_, axis=-1, keepdims=True)
        ds_ = (probs * (dp_ - delta)).astype(BF)
        dqs.append((jnp.einsum("ghqk,gkhe->gqhe", ds_, kh, preferred_element_type=F32) * score_scale).reshape(-1, width))
        dks.append((jnp.einsum("ghqk,gqhe->gkhe", ds_, qh, preferred_element_type=F32) * score_scale).reshape(-1, width))
        dvs.append(jnp.einsum("ghqk,gqhe->gkhe", probs.astype(BF), doh, preferred_element_type=F32).reshape(-1, width))
    dq = jnp.concatenate(dqs).astype(BF)
    dk = jnp.concatenate(dks).astype(BF)
    dv = jnp.concatenate(dvs).astype(BF)
    g_q = jnp.einsum("td,te->de", x_own, dq, preferred_element_type=F32)
    g_k = jnp.einsum("td,te->de", x_all, dk, preferred_element_type=F32)
    g_v = jnp.einsum("td,te->de", x_all, dv, preferred_element_type=F32)
    g_qk = jnp.stack([g_q, g_k]).astype(BF)
    g_va = jnp.stack([g_v, g_attn]).astype(BF)
    dx_own = jnp.einsum("te,de->td", dq, qk[0], preferred_element_type=F32) + dz1
    dx_all = jnp.einsum("te,de->td", dk, qk[1], preferred_element_type=F32)
    dx_all = dx_all + jnp.einsum("te,de->td", dv, va[0], preferred_element_type=F32)
    dx = jnp.concatenate([dx_all[:n_own] + dx_own, dx_all[n_own:]]).astype(BF)
    db_inner = jnp.sum(du.astype(F32), axis=1)
    db_inner = db_inner.reshape(2, 2, half_ff // 2).transpose(1, 0, 2).reshape(ff_rows, width)
    vec_grad = jnp.concatenate(
        [
            jnp.stack(
                [
                    jnp.sum(dq.astype(F32), axis=0),
                    jnp.sum(dv.astype(F32), axis=0),
                    jnp.sum(dz1, axis=0),
                    dg1,
                    dc1,
                ]
            ),
            db_inner,
            jnp.stack([jnp.sum(dz2, axis=0), dg2, dc2]),
        ]
    )
    vg = vec_grad.reshape(nvec, n_dp, 2, vec_lanes).transpose(1, 0, 2, 3)
    vg = jnp.pad(vg, ((0, 0), (0, 0), (0, 0), (0, 128 - vec_lanes))).reshape(n_dp, nvec, 256)
    pg = proj_grad.reshape(n_dp, 2, half_rows, 128).transpose(0, 2, 1, 3).reshape(n_dp, half_rows, 256)
    tg = table_local.reshape(n_dp, 2, TAB_DEV // 2, 128).transpose(0, 2, 1, 3).reshape(n_dp, TAB_DEV // 2, 256)
    small = jnp.concatenate([pg, vg, tg], axis=1)

    reduce = reduce_fast if fast else reduce_plain
    (small_r, qk_r, va_r, inner_r, outer_r, peer_out, peer_dx, peer_small, total) = reduce(
        [g_qk, g_va, g_inner, g_outer], small, out_own, dx, rows
    )

    def whole_rows(own, peer):
        lo = jnp.where(mp == 0, own[:n_own], peer[:n_own])
        hi = jnp.where(mp == 0, peer[:n_own], own[:n_own])
        return lo, hi

    lo, hi = whole_rows(out_own, peer_out)
    out_tokens = jnp.concatenate([lo, hi[n_full:], hi[:n_full]])
    lo, hi = whole_rows(dx.astype(F32), peer_dx.astype(F32))
    tail = jnp.where(mp == 0, dx[n_own:], peer_dx[n_own:]).astype(F32)
    tail_hi = jnp.where(mp == 0, peer_dx[n_own:], dx[n_own:]).astype(F32)
    input_grad = jnp.concatenate(
        [lo[:n_full], lo[n_full:] + tail_hi, hi[n_full:] + tail, hi[:n_full]]
    )

    def both_halves(at, count):
        mine_, peer_ = small_r[at : at + count], peer_small[at : at + count]
        return jnp.concatenate(
            [jnp.where(mp == 0, mine_, peer_), jnp.where(mp == 0, peer_, mine_)]
        )

    proj_r = both_halves(0, half_rows)
    table_grad = both_halves(half_rows + nvec, TAB_DEV // 2)
    vector_r = small_r[half_rows : half_rows + nvec, :vec_lanes]
    qkv_r = jnp.stack([qk_r[0], qk_r[1], va_r[0]])
    attn_r = va_r[1]

    def back(v):
        return v.transpose(1, 0, 2).reshape(rows, half_ff)

    inner_r, outer_r = back(inner_r), back(outer_r)
    grad_norm = jnp.sqrt(total[0, 0])
    clip = clip_norm / jnp.maximum(grad_norm, clip_norm)
    results = [out_tokens, input_grad, grad_norm]
    for w, m, s, g, dec, rate in (
        (w_qkv, m_qkv, v_qkv, qkv_r, decay_rate, learn_rate),
        (w_attn, m_attn, v_attn, attn_r, decay_rate, learn_rate),
        (w_inner, m_inner, v_inner, inner_r, decay_rate, learn_rate),
        (w_outer, m_outer, v_outer, outer_r, decay_rate, learn_rate),
        (w_proj, m_proj, v_proj, proj_r, decay_rate, learn_rate),
        (vectors, m_vectors, v_vectors, vector_r, 0.0, vector_rate),
    ):
        results += list(adamw_update(w, m, s, g * clip, dec, rate))
    return tuple(results) + (table_grad,)


def solution(mesh):
    mat = P("dp", "mp")
    rep = P("dp", None)
    qkv = P(None, "dp", "mp")
    vec = P(None, ("dp", "mp"))
    placed = (rep, rep, P("dp"), rep, P("dp", None, None), qkv, qkv, qkv)
    placed += (mat,) * 9 + (rep,) * 3 + (vec,) * 3
    given = (rep, rep, P(), qkv, qkv, qkv) + (mat,) * 9 + (rep,) * 3 + (vec,) * 3 + (rep,)
    return jax.shard_map(local, mesh=mesh, in_specs=placed, out_specs=given, check_vma=False)
```

```python
import functools

import jax
import jax.numpy as jnp
from jax import lax
from jax.experimental import pallas as pl
from jax.experimental.pallas import tpu as pltpu
from jax.sharding import PartitionSpec as P

HEAD_DIM = 64
STEP = 10
TAB_DEV = 8
MESH = pl.DeviceIdType.MESH
ANY = pl.ANY
BF = jnp.bfloat16
F32 = jnp.float32
NZ, NY, NC, NX = 4, 2, 2, 2

highest_mode = lax.Precision.HIGHEST
retrieval_scale = 0.17677669529663687
ln_epsilon = 1e-12
beta_first = 0.9
beta_second = 0.999
learn_rate = 0.05
vector_rate = 0.5
decay_rate = 0.01
adam_epsilon = 1e-08
clip_norm = 1.0


def layer_norm(values, gain_row, shift_row):
    centre = jnp.mean(values, axis=-1, keepdims=True)
    centred = values - centre
    spread = jnp.mean(centred * centred, axis=-1, keepdims=True)
    return centred * lax.rsqrt(spread + ln_epsilon) * gain_row + shift_row


def gelu_exact(values):
    return jax.nn.gelu(values, approximate=False)


def adamw_update(weight, moment, second, gradient, decay_factor, step_rate):
    moment_new = beta_first * moment + (1.0 - beta_first) * gradient
    second_new = beta_second * second + (1.0 - beta_second) * gradient * gradient
    first_hat = moment_new / (1.0 - beta_first**STEP)
    second_hat = second_new / (1.0 - beta_second**STEP)
    weight_new = weight - step_rate * (
        first_hat / (jnp.sqrt(second_hat) + adam_epsilon) + decay_factor * weight
    )
    return (moment_new, second_new, weight_new)


def squared(values):
    return jnp.sum(values * values)


class Place:
    def __init__(self):
        dp = lax.axis_index("dp")
        self.x = lax.axis_index("mp")
        self.c = lax.rem(dp, NC)
        self.y = lax.rem(dp // NC, NY)
        self.z = dp // (NC * NY)

    def dev(self, z=None, y=None, c=None, x=None):
        z = self.z if z is None else z
        y = self.y if y is None else y
        c = self.c if c is None else c
        x = self.x if x is None else x
        return ((z * NY + y) * NC + c, x)

    def others(self):
        out = [self.dev(z=lax.rem(self.z + k, NZ)) for k in range(1, NZ)]
        out.append(self.dev(x=1 - self.x))
        out.append(self.dev(y=1 - self.y))
        out.append(self.dev(c=1 - self.c))
        return out

    def eights(self):
        out = []
        for k in range(1, 8):
            dx, dy, dc = k & 1, (k >> 1) & 1, k >> 2
            out.append(
                self.dev(
                    x=self.x + dx - 2 * dx * self.x,
                    y=self.y + dy - 2 * dy * self.y,
                    c=self.c + dc - 2 * dc * self.c,
                )
            )
        return out


def greet(devices):
    barrier = pltpu.get_barrier_semaphore()
    for d in devices:
        pl.semaphore_signal(barrier, inc=1, device_id=d, device_id_type=MESH)
    pl.semaphore_wait(barrier, len(devices))


def remote(src, dst, ssem, rsem, dev):
    return pltpu.make_async_remote_copy(
        src_ref=src, dst_ref=dst, send_sem=ssem, recv_sem=rsem, device_id=dev, device_id_type=MESH
    )


def cols(x, half):
    return pl.ds(pl.multiple_of(x * half, 128), half)


def dma(*shape):
    return pltpu.SemaphoreType.DMA(shape)


def mm(a, b):
    return jnp.dot(a, b, preferred_element_type=F32)


def mm_nt(a, b):
    return lax.dot_general(a, b, (((1,), (1,)), ((), ())), preferred_element_type=F32)


def mm_tn(a, b):
    return lax.dot_general(a, b, (((0,), (0,)), ((), ())), preferred_element_type=F32)


def flat(value):
    return value.reshape(-1, value.shape[-1])


def lanes(i, n=128):
    return pl.ds(pl.multiple_of(i * n, 128), n)


def rows_at(i, n, at=0):
    return pl.ds(pl.multiple_of(at + i * n, 16), n)


def each(n, body):
    lax.fori_loop(0, n, lambda i, c: (body(i), c)[1], 0)


class Gather:
    def __init__(self, me, pieces, sems):
        self.me, self.pieces = me, pieces
        self.lsem, self.zs, self.zr, self.s1, self.r1, self.s2, self.r2, self.ds, self.dr = sems
        self.waits, self.locs = [], {}

    def go(self, copy):
        copy.start()
        self.waits.append(copy)

    def step1(self, p):
        me = self.me
        src, dst = self.pieces[p]
        blk = dst.at[me.z, me.y, me.c, :, cols(me.x, dst.shape[-1] // 2)]
        loc = pltpu.make_async_copy(src, blk, self.lsem.at[p])
        loc.start()
        self.locs[p] = loc
        for k in range(1, NZ):
            dev = me.dev(z=lax.rem(me.z + k, NZ))
            self.go(remote(src, blk, self.zs.at[p, k], self.zr.at[p, k], dev))

    def part(self, p, stage, c):
        me, dst = self.me, self.pieces[p][1]
        half = dst.shape[-1] // 2
        own, other = cols(me.x, half), cols(1 - me.x, half)
        if stage == "z":
            return dst.at[:, me.y, c, :, own]
        if p % 2 == 0:
            if stage == "in1":
                return dst.at[:, me.y, c, :, other]
            if stage == "out2":
                return dst.at[:, me.y, c]
            return dst.at[:, 1 - me.y, c]
        if stage == "in1":
            return dst.at[:, 1 - me.y, c, :, own]
        if stage == "out2":
            return dst.at[:, :, c, :, own]
        return dst.at[:, :, c, :, other]

    def first(self, p):
        return self.me.dev(x=1 - self.me.x) if p % 2 == 0 else self.me.dev(y=1 - self.me.y)

    def second(self, p):
        return self.me.dev(y=1 - self.me.y) if p % 2 == 0 else self.me.dev(x=1 - self.me.x)

    def cross(self, p, ref, which):
        self.go(remote(ref, ref, self.ds.at[p, which], self.dr.at[p, which], self.me.dev(c=1 - self.me.c)))

    def arrived(self, ref, ssem, rsem):
        remote(ref, ref, ssem, rsem, self.me.dev(c=1 - self.me.c)).wait_recv()

    def step2(self, p):
        me, dst = self.me, self.pieces[p][1]
        self.locs[p].wait()
        for k in range(1, NZ):
            blk = dst.at[lax.rem(me.z + NZ - k, NZ), me.y, me.c, :, cols(me.x, dst.shape[-1] // 2)]
            self.arrived(blk, self.zs.at[p, k], self.zr.at[p, k])
        have = self.part(p, "z", me.c)
        self.go(remote(have, have, self.s1.at[p], self.r1.at[p], self.first(p)))
        self.cross(p, have, 0)

    def step3(self, p):
        got = self.part(p, "in1", self.me.c)
        self.arrived(got, self.s1.at[p], self.r1.at[p])
        have = self.part(p, "out2", self.me.c)
        self.go(remote(have, have, self.s2.at[p], self.r2.at[p], self.second(p)))
        self.cross(p, got, 1)

    def step4(self, p):
        got = self.part(p, "in2", self.me.c)
        self.arrived(got, self.s2.at[p], self.r2.at[p])
        self.cross(p, got, 2)

    def step5(self, p):
        for which, stage in enumerate(("z", "in1", "in2")):
            self.arrived(self.part(p, stage, 1 - self.me.c), self.ds.at[p, which], self.dr.at[p, which])

    def tick(self, t, ahead):
        n = len(self.pieces)
        if t < n:
            self.step2(t)
            if t + ahead < n:
                self.step1(t + ahead)
        if 0 <= t - 1 < n:
            self.step3(t - 1)
        if 0 <= t - 2 < n:
            self.step4(t - 2)
        if 0 <= t - 3 < n:
            self.step5(t - 3)

    def end(self):
        for copy in self.waits:
            copy.wait_send()


def norm_rows(z_ref, r_ref, n_rows, put):
    step = 48

    def body(i):
        at = rows_at(i, step)
        z = z_ref[at, :]
        centred = z - jnp.mean(z, axis=-1, keepdims=True)
        spread = jnp.mean(centred * centred, axis=-1, keepdims=True)
        root = lax.rsqrt(spread + ln_epsilon)
        hat = centred * root
        z_ref[at, :] = hat
        r_ref[at, :] = jnp.broadcast_to(root, (step, 128))
        put(at, hat)

    each(n_rows // step, body)


def forward_kernel(*refs):
    (lens, tokens, w_qkv, w_attn, w_inner, w_outer, w_proj, vectors) = refs[:8]
    outs = refs[8:28]
    scr = refs[28:]
    (small_s, qk_s, va_s, inner_s, outer_s, small_g, qk, va, inner, outer) = scr[:10]
    (x_all, q, k, v, p_ab, p_c, o, xh1, r1, g, gp, xh2, r2, out_own, proj, vec, h1b, vecp, bias_ff) = scr[10:29]
    gsems, tsem, osem = scr[29:38], scr[38], scr[39]
    me = Place()
    mp = me.x
    n_all, width = x_all.shape
    n_own = q.shape[0]
    seq = p_ab.shape[1]
    half_seq = seq // 2
    full = (n_own - half_seq) // seq
    n_full = full * seq
    half_ff = inner.shape[-1]
    rows = qk_s.shape[1]
    half_rows = rows // 2

    starts = (
        (mp * (n_full + seq), 0, n_full),
        (n_full + mp * half_seq, n_full, half_seq),
        (n_full + (1 - mp) * half_seq, n_own, half_seq),
    )
    loads = []
    for i, (at, to, n) in enumerate(starts):
        cp = pltpu.make_async_copy(
            tokens.at[pl.ds(pl.multiple_of(at, 16), n)], x_all.at[pl.ds(to, n)], tsem.at[i]
        )
        cp.start()
        loads.append(cp)

    vecp[...] = jnp.zeros_like(vecp)
    nvec, nlane = vectors.shape
    vecp[0:nvec, 0:nlane] = vectors[...]
    small_s[0:half_rows] = w_proj[pl.ds(pl.multiple_of(mp * half_rows, 8), half_rows), :]
    small_s[half_rows : half_rows + nlane] = jnp.transpose(vecp[...])[0:nlane]
    qk_s[...] = w_qkv[0:2].astype(BF)
    va_s[0] = w_qkv[2].astype(BF)
    va_s[1] = w_attn[...].astype(BF)
    hf = half_ff // 2
    for h in range(2):
        inner_s[h] = w_inner[:, h * hf : (h + 1) * hf].astype(BF)
        outer_s[h] = w_outer[:, h * hf : (h + 1) * hf].astype(BF)

    greet(me.others())
    pieces = [
        (small_s, small_g),
        (qk_s.at[0], qk.at[0]),
        (qk_s.at[1], qk.at[1]),
        (va_s.at[0], va.at[0]),
        (va_s.at[1], va.at[1]),
        (inner_s.at[0], inner.at[0]),
        (inner_s.at[1], inner.at[1]),
        (outer_s.at[0], outer.at[0]),
        (outer_s.at[1], outer.at[1]),
    ]
    net = Gather(me, pieces, gsems)
    ahead = 3
    for p in range(ahead):
        net.step1(p)
    tick = lambda t: net.tick(t, ahead)
    saves = []

    def save(i, ref):
        cp = pltpu.make_async_copy(ref, outs[i], osem.at[i])
        cp.start()
        saves.append(cp)

    for cp in loads:
        cp.wait()
    save(4, x_all)
    for t in range(4):
        tick(t)
    big = []
    for z in range(NZ):
        for y in range(NY):
            for c in range(NC):
                for x in range(NX):
                    blk = small_g[z, y, c, :, x * 128 : (x + 1) * 128]
                    d = ((z * NY + y) * NC + c) * NX + x
                    proj[d * half_rows : (d + 1) * half_rows] = blk[:half_rows]
                    big.append(blk[half_rows : half_rows + nlane])
    vec[...] = jnp.transpose(jnp.concatenate(big, axis=0))[0 : vec.shape[0]]
    for h in range(2):
        for x in range(NX):
            bias_ff[h : h + 1, x * width : (x + 1) * width] = vec[5 + NX * x + h : 6 + NX * x + h, :]
    save(17, proj)
    save(18, vec)

    def project(w_ref, src_rows, dst, bias):
        n_tile = 256

        def body(i):
            w = flat(w_ref[:, :, :, :, lanes(i, n_tile)])
            r = mm(x_all[0:src_rows], w)
            if bias is not None:
                r = r + vec[bias : bias + 1, lanes(i, n_tile)]
            dst[:, lanes(i, n_tile)] = r.astype(BF)

        each(width // n_tile, body)

    tick(4)
    project(qk.at[0], n_own, q, 0)
    tick(5)
    project(qk.at[1], n_all, k, None)
    save(0, qk)
    tick(6)
    project(va.at[0], n_all, v, 1)
    save(5, q)
    save(6, k)
    save(7, v)

    lane = lax.broadcasted_iota(jnp.int32, (1, 128), 1)
    head_lo = jnp.where(lane < HEAD_DIM, 1.0, 0.0)
    head_mask = (head_lo.astype(BF), (1.0 - head_lo).astype(BF))
    pos = lax.broadcasted_iota(jnp.int32, (1, seq), 1)

    def attend(q0, nq, k0, hp, length, place, p_ref, p_at):
        qp = q[pl.ds(pl.multiple_of(q0, 16), nq), lanes(hp)]
        kp = k[pl.ds(pl.multiple_of(k0, 16), seq), lanes(hp)]
        vp = v[pl.ds(pl.multiple_of(k0, 16), seq), lanes(hp)]
        got = []
        for h in range(2):
            s = mm_nt(qp * head_mask[h], kp) * (HEAD_DIM**-0.5)
            s = jnp.where(place < length, s, -1000000000.0)
            e = jnp.exp(s - jnp.max(s, axis=-1, keepdims=True))
            pb = (e * (1.0 / jnp.sum(e, axis=-1, keepdims=True))).astype(BF)
            p_ref[p_at + h] = pb
            got.append(mm(pb, vp))
        mixed = jnp.where(lane < HEAD_DIM, got[0], got[1])
        o[pl.ds(pl.multiple_of(q0, 16), nq), lanes(hp)] = mixed.astype(BF)

    pairs = width // 128
    for s in range(full):
        length = lens[mp * (full + 1) + s]
        each(pairs, lambda hp: attend(s * seq, seq, s * seq, hp, length, pos, p_ab, s * 2 * pairs + 2 * hp))
        tick(7 + s)
    length = lens[full]
    pos_c = jnp.where(pos < half_seq, pos + mp * half_seq, pos - half_seq + (1 - mp) * half_seq)
    each(pairs, lambda hp: attend(n_full, half_seq, n_full, hp, length, pos_c, p_c, 2 * hp))
    save(8, p_ab)
    save(9, p_c)
    save(10, o)
    tick(7 + full)

    tile = 240
    tiles = n_own // tile

    def attn_out(i):
        a = mm_nt(o[rows_at(i, tile), :], flat(va[1]))
        xh1[rows_at(i, tile), :] = x_all[rows_at(i, tile), :].astype(F32) + a + vec[2:3, :]

    each(tiles, attn_out)
    save(1, va)

    def put_h1(at, hat):
        h1b[at, :] = (hat * vec[3:4, :] + vec[4:5, :]).astype(BF)

    norm_rows(xh1, r1, n_own, put_h1)
    save(11, xh1)
    save(12, r1)
    tick(8 + full)

    def feed(h):
        n_tile = 256

        def body(i):
            w = flat(inner[h, :, :, :, :, lanes(i, n_tile)])
            for t in range(tiles):
                at = pl.ds(t * tile, tile)
                u = mm(h1b[at, :], w)
                u = u + bias_ff[h : h + 1, lanes(i, n_tile)]
                tail = 0.5 * (1.0 + lax.erf(u * 0.7071067811865476))
                g[h, at, lanes(i, n_tile)] = (u * tail).astype(BF)
                slope = tail + u * (0.3989422804014327 * jnp.exp(-0.5 * u * u))
                gp[h, at, lanes(i, n_tile)] = slope.astype(BF)

        each(half_ff // n_tile, body)

    feed(0)
    tick(9 + full)
    feed(1)
    for t in range(10 + full, len(pieces) + 3):
        tick(t)
    save(2, inner)
    save(13, g)
    save(14, gp)

    def ff_out(i):
        at = rows_at(i, tile)
        f = mm_nt(g[0, at, :], flat(outer[0])) + mm_nt(g[1, at, :], flat(outer[1]))
        h1 = xh1[at, :] * vec[3:4, :] + vec[4:5, :]
        xh2[at, :] = h1 + f + vec[9:10, :]

    each(tiles, ff_out)
    save(3, outer)

    def put_y(at, hat):
        out_own[at, :] = (hat * vec[10:11, :] + vec[11:12, :]).astype(BF)

    norm_rows(xh2, r2, n_own, put_y)
    save(15, xh2)
    save(16, r2)
    save(19, out_own)
    net.end()
    for cp in saves:
        cp.wait()


def forward_fast(lengths, tokens, w_qkv, w_attn, w_inner, w_outer, w_proj, vectors):
    seqs = lengths.shape[0]
    all_rows, width = tokens.shape
    seq = all_rows // seqs
    full = seqs // 2
    n_own = full * seq + seq // 2
    n_all = n_own + seq // 2
    rows, half_ff = w_qkv.shape[1], w_inner.shape[1]
    heads = width // HEAD_DIM
    zyc = (NZ, NY, NC)
    small_rows = rows // 2 + vectors.shape[1]
    weights = [
        ((2,) + zyc + (rows, width), BF),
        ((2,) + zyc + (rows, width), BF),
        ((2,) + zyc + (rows, half_ff), BF),
        ((2,) + zyc + (rows, half_ff), BF),
    ]
    kept = [
        ((n_all, width), BF),
        ((n_own, width), BF),
        ((n_all, width), BF),
        ((n_all, width), BF),
        ((full * heads, seq, seq), BF),
        ((heads, seq // 2, seq), BF),
        ((n_own, width), BF),
        ((n_own, width), F32),
        ((n_own, 128), F32),
        ((2, n_own, half_ff), BF),
        ((2, n_own, half_ff), BF),
        ((n_own, width), F32),
        ((n_own, 128), F32),
        ((width, 128), F32),
        ((16, width), F32),
        ((n_own, width), BF),
    ]
    order = kept[:13] + [kept[15], kept[13], kept[14]]
    scratch = [
        ((small_rows, 128), F32),
        ((2, rows, width // 2), BF),
        ((2, rows, width // 2), BF),
        ((2, rows, half_ff // 2), BF),
        ((2, rows, half_ff // 2), BF),
        (zyc + (small_rows, 256), F32),
    ] + weights + order + [((n_own, width), BF), ((128, 128), F32), ((8, half_ff), F32)]
    n = 9
    vm = pl.BlockSpec(memory_space=pltpu.VMEM)
    hb = pl.BlockSpec(memory_space=ANY)
    sm = pl.BlockSpec(memory_space=pltpu.SMEM)
    return pl.pallas_call(
        forward_kernel,
        out_shape=[jax.ShapeDtypeStruct(s, d) for s, d in weights + kept],
        in_specs=[sm, hb] + [vm] * 6,
        out_specs=[hb] * 20,
        scratch_shapes=[pltpu.VMEM(s, d) for s, d in scratch]
        + [
            dma(n), dma(n, NZ), dma(n, NZ), dma(n), dma(n), dma(n), dma(n), dma(n, 3), dma(n, 3),
            dma(3), dma(20),
        ],
        compiler_params=pltpu.CompilerParams(
            collective_id=1, has_side_effects=True, vmem_limit_bytes=60 * 2**20
        ),
        name="forward",
    )(lengths, tokens, w_qkv, w_attn, w_inner, w_outer, w_proj, vectors)


def reduce_kernel(n_in, n_out, index, *refs):
    ins, outs = refs[:n_in], refs[n_in : n_in + n_out]
    rest = refs[n_in + n_out :]
    nb = len(index)
    bufs, rest = rest[: 5 * nb], rest[5 * nb :]
    sq4, sq8, lsem, ds, dr, s1, r1, s2, r2, zs, zr, xs, xr, qs, qr, es, er = rest
    send_out, send_dx = ins[-2:]
    peer_out, peer_dx, peer_small, norm_ref = outs[-4:]
    me = Place()
    greet(me.others() + me.eights())
    n = len(index)
    waits = []

    def go(copy):
        copy.start()
        waits.append(copy)
        return copy

    oc, oy, ox = 1 - me.c, 1 - me.y, 1 - me.x
    pieces = []
    for p, (i, li, o, lo, sx) in enumerate(index):
        src = ins[i] if li is None else ins[i].at[li]
        dst = outs[o] if lo is None else outs[o].at[lo]
        pieces.append((src, dst) + tuple(bufs[5 * p : 5 * p + 5]))

    def step1(p):
        src, _, own, got1, _, _, _ = pieces[p]
        go(remote(src.at[:, :, oc], got1, ds.at[p], dr.at[p], me.dev(c=oc)))
        loc = pltpu.make_async_copy(src.at[:, :, me.c], own, lsem.at[p])
        loc.start()
        return loc

    def half(ref):
        return ref.shape[-1] // 2

    def step2(p, loc):
        _, _, own, got1, got2, got3, got4 = pieces[p]
        loc.wait()
        remote(got1, got1, ds.at[p], dr.at[p], me.dev()).wait_recv()
        own[...] = own[...] + got1[...]
        if p % 2 == 0:
            go(remote(own.at[:, oy], got2, s1.at[p], r1.at[p], me.dev(y=oy)))
        else:
            go(remote(own.at[:, :, :, cols(ox, half(own))], got2, s1.at[p], r1.at[p], me.dev(x=ox)))

    def step3(p):
        _, _, own, _, got2, got3, _ = pieces[p]
        remote(got2, got2, s1.at[p], r1.at[p], me.dev()).wait_recv()
        h = half(own)
        if p % 2 == 0:
            own[:, me.y] = own[:, me.y] + got2[...]
            go(remote(own.at[:, me.y, :, cols(ox, h)], got3, s2.at[p], r2.at[p], me.dev(x=ox)))
        else:
            own[:, :, :, cols(me.x, h)] = own[:, :, :, cols(me.x, h)] + got2[...]
            go(remote(own.at[:, oy, :, cols(me.x, h)], got3, s2.at[p], r2.at[p], me.dev(y=oy)))

    def step4(p):
        _, _, own, _, _, got3, got4 = pieces[p]
        remote(got3, got3, s2.at[p], r2.at[p], me.dev()).wait_recv()
        h = half(own)
        mine = cols(me.x, h)
        own[:, me.y, :, mine] = own[:, me.y, :, mine] + got3[...]
        for k in range(1, NZ):
            tz = lax.rem(me.z + k, NZ)
            go(remote(own.at[tz, me.y, :, mine], got4.at[k], zs.at[p, k], zr.at[p, k], me.dev(z=tz)))

    def step5(p):
        _, dst, own, _, _, _, got4 = pieces[p]
        for k in range(1, NZ):
            remote(got4.at[k], got4.at[k], zs.at[p, k], zr.at[p, k], me.dev()).wait_recv()
        total = own[me.z, me.y, :, cols(me.x, half(own))].astype(F32)
        for k in range(1, NZ):
            total = total + got4[k].astype(F32)
        dst[...] = total
        return jnp.sum(total * total, keepdims=True)

    go(remote(send_out, peer_out, xs.at[0], xr.at[0], me.dev(x=ox)))
    locs = {}
    ahead = 2
    total = jnp.zeros((1, 1), F32)
    for p in range(min(ahead, n)):
        locs[p] = step1(p)
    for t in range(n + 3):
        if t < n:
            step2(t, locs[t])
            if t + ahead < n:
                locs[t + ahead] = step1(t + ahead)
        if 0 <= t - 1 < n:
            step3(t - 1)
        if 0 <= t - 2 < n:
            step4(t - 2)
        if 0 <= t - 3 < n:
            p = t - 3
            part = step5(p)
            if index[p][4]:
                total = total + part
    go(remote(send_dx, peer_dx, xs.at[1], xr.at[1], me.dev(x=ox)))
    small = outs[index[-1][2]]
    go(remote(small, peer_small, xs.at[2], xr.at[2], me.dev(x=ox)))
    row = lax.broadcasted_iota(jnp.int32, small.shape, 0)
    keep = jnp.where(row < 36, small[...], 0.0)
    total = total + jnp.sum(keep * keep, keepdims=True)
    sq4[0] = jnp.broadcast_to(total, (8, 128))
    copies = []
    for k in range(1, NZ):
        c = remote(sq4.at[0], sq4.at[k], qs.at[k], qr.at[k], me.dev(z=lax.rem(me.z + k, NZ)))
        copies.append(go(c))
    for k in range(1, NZ):
        copies[k - 1].wait_recv()
    def at_z(z):
        out = jnp.zeros((8, 128), F32)
        for k in range(NZ):
            src = lax.rem(me.z + NZ - k, NZ)
            out = out + jnp.where(src == z, sq4[k], 0.0)
        return out
    group = at_z(0) + at_z(1) + at_z(2) + at_z(3)
    sq8[0] = group
    copies = []
    for k, dev in enumerate(me.eights(), 1):
        copies.append(go(remote(sq8.at[0], sq8.at[k], es.at[k], er.at[k], dev)))
    for copy in copies:
        copy.wait_recv()
    code = me.x + 2 * me.y + 4 * me.c

    def at_code(w):
        out = jnp.zeros((8, 128), F32)
        for k in range(8):
            dx, dy, dc = k & 1, (k >> 1) & 1, k >> 2
            src = (
                (me.x + dx - 2 * dx * me.x)
                + 2 * (me.y + dy - 2 * dy * me.y)
                + 4 * (me.c + dc - 2 * dc * me.c)
            )
            out = out + jnp.where(src == w, sq8[k], 0.0)
        return out

    whole = at_code(0)
    for w in range(1, 8):
        whole = whole + at_code(w)
    norm_ref[...] = whole
    remote(peer_out, peer_out, xs.at[0], xr.at[0], me.dev()).wait_recv()
    remote(peer_dx, peer_dx, xs.at[1], xr.at[1], me.dev()).wait_recv()
    remote(peer_small, peer_small, xs.at[2], xr.at[2], me.dev()).wait_recv()
    for copy in waits:
        copy.wait_send()


def reduce_fast(grads, small, own_out, own_dx, rows):
    zyc = (NZ, NY, NC)
    arrays = [small.reshape(zyc + small.shape[1:])]
    arrays += [g.reshape((2,) + zyc + (rows, g.shape[2])) for g in grads]
    index = [
        (4, 0, 4, 0, True),
        (4, 1, 4, 1, True),
        (3, 0, 3, 0, True),
        (3, 1, 3, 1, True),
        (2, 1, 2, 1, True),
        (1, 0, 1, 0, True),
        (1, 1, 1, 1, True),
        (2, 0, 2, 0, True),
        (0, None, 0, None, False),
    ]
    n = len(index)
    out_shape = [
        jax.ShapeDtypeStruct((small.shape[1], small.shape[2] // 2), F32),
    ] + [jax.ShapeDtypeStruct((2, rows, g.shape[2] // 2), F32) for g in grads]
    out_shape += [
        jax.ShapeDtypeStruct(own_out.shape, BF),
        jax.ShapeDtypeStruct(own_dx.shape, BF),
        jax.ShapeDtypeStruct((small.shape[1], small.shape[2] // 2), F32),
        jax.ShapeDtypeStruct((8, 128), F32),
    ]
    bufs = []
    for p, (i, _, _, _, _) in enumerate(index):
        r, w = arrays[i].shape[-2:]
        dt = arrays[i].dtype
        bufs += [pltpu.VMEM((NZ, NY, r, w), dt), pltpu.VMEM((NZ, NY, r, w), dt)]
        if p % 2 == 0:
            bufs += [pltpu.VMEM((NZ, r, w), dt)]
        else:
            bufs += [pltpu.VMEM((NZ, NY, r, w // 2), dt)]
        bufs += [pltpu.VMEM((NZ, r, w // 2), dt), pltpu.VMEM((NZ, r, w // 2), dt)]
    vm = pl.BlockSpec(memory_space=pltpu.VMEM)
    hb = pl.BlockSpec(memory_space=ANY)
    return pl.pallas_call(
        functools.partial(reduce_kernel, 7, len(out_shape), index),
        out_shape=out_shape,
        in_specs=[hb] * 7,
        out_specs=[vm] * 5 + [hb, hb, vm, vm],
        scratch_shapes=bufs
        + [
            pltpu.VMEM((NZ, 8, 128), F32), pltpu.VMEM((8, 8, 128), F32),
            dma(n), dma(n), dma(n), dma(n), dma(n), dma(n), dma(n), dma(n, NZ), dma(n, NZ),
            dma(3), dma(3), dma(NZ), dma(NZ), dma(8), dma(8),
        ],
        compiler_params=pltpu.CompilerParams(
            collective_id=2, has_side_effects=True, vmem_limit_bytes=56 * 2**20
        ),
        name="reduce",
    )(*arrays, own_out, own_dx)


def gather_plain(shards, small, rows):
    def both(v, axis):
        v = lax.all_gather(v, "dp", axis=axis, tiled=True)
        return lax.all_gather(v, "mp", axis=2, tiled=True)

    return [both(small[None], 0)] + [both(v, 1) for v in shards]


def reduce_plain(grads, small, own_out, own_dx, rows):
    def both(v, axis, wide):
        v = lax.psum_scatter(v.astype(F32), "mp", scatter_dimension=wide, tiled=True)
        return lax.psum_scatter(v, "dp", scatter_dimension=axis, tiled=True)

    small_sum = both(small, 0, 2)[0]
    sums = [both(g, 1, 2) for g in grads]
    ox = 1 - lax.axis_index("mp")
    swap = [(0, 1), (1, 0)]
    peer_out = lax.ppermute(own_out, "mp", swap)
    peer_dx = lax.ppermute(own_dx, "mp", swap)
    peer_small = lax.ppermute(small_sum, "mp", swap)
    squares = sum(squared(g) for g in sums) + squared(small_sum[:-4])
    total = lax.psum(squares, ("dp", "mp"))
    return [small_sum] + sums + [peer_out, peer_dx, peer_small, jnp.full((8, 128), total)]


def forward_plain(lengths, tokens, w_qkv, w_attn, w_inner, w_outer, w_proj, vectors):
    mp = lax.axis_index("mp")
    n_dp = lax.axis_size("dp")
    seqs = lengths.shape[0]
    all_rows, width = tokens.shape
    seq_len = all_rows // seqs
    full = seqs // 2
    n_full, n_half = full * seq_len, seq_len // 2
    n_own = n_full + n_half
    heads = width // HEAD_DIM
    rows, half_ff = w_qkv.shape[1], w_inner.shape[1]
    nvec, vec_lanes = vectors.shape
    half_rows = rows // 2
    score_scale = HEAD_DIM ** (-0.5)

    def two(v):
        return v.reshape(rows, 2, half_ff // 2).transpose(1, 0, 2)

    qk_s = w_qkv[:2].astype(BF)
    va_s = jnp.stack([w_qkv[2], w_attn]).astype(BF)
    vec_pad = jnp.pad(vectors, ((0, 0), (0, 128 - vec_lanes)))
    proj_half = lax.dynamic_slice_in_dim(w_proj, mp * half_rows, half_rows, 0)
    small_s = jnp.concatenate([proj_half, vec_pad], axis=0)
    small_g, qk, va, inner, outer = gather_plain(
        [qk_s, va_s, two(w_inner.astype(BF)), two(w_outer.astype(BF))], small_s, rows
    )
    small_g = small_g.reshape(n_dp, half_rows + nvec, 2, 128)
    proj = small_g[:, :half_rows].transpose(0, 2, 1, 3).reshape(width, 128)
    vec = small_g[:, half_rows:, :, :vec_lanes].transpose(1, 0, 2, 3).reshape(nvec, width)
    ff_rows = nvec - 8
    b_inner = vec[5 : 5 + ff_rows].reshape(2, 2, half_ff // 2).transpose(1, 0, 2).reshape(2, half_ff)

    a0 = mp * (n_full + seq_len)
    h0 = n_full + mp * n_half
    o0 = n_full + (1 - mp) * n_half
    x_all = jnp.concatenate(
        [
            lax.dynamic_slice_in_dim(tokens, a0, n_full, 0),
            lax.dynamic_slice_in_dim(tokens, h0, n_half, 0),
            lax.dynamic_slice_in_dim(tokens, o0, n_half, 0),
        ]
    )
    x_own = x_all[:n_own]
    my_seqs = jnp.concatenate([mp * (full + 1) + jnp.arange(full), jnp.array([full])])
    my_len = lengths[my_seqs]
    pos = jnp.arange(seq_len)
    pos_last = jnp.where(pos < n_half, pos + mp * n_half, pos - n_half + (1 - mp) * n_half)
    valids = (pos[None, :] < my_len[:full, None], pos_last[None, :] < my_len[full:, None])

    q = (jnp.dot(x_own, qk[0], preferred_element_type=F32) + vec[0]).astype(BF)
    k = jnp.dot(x_all, qk[1], preferred_element_type=F32).astype(BF)
    v = (jnp.dot(x_all, va[0], preferred_element_type=F32) + vec[1]).astype(BF)
    probs, outs = [], []
    for qh, kh, vh, valid in zip(*(halves(t, n_full, seq_len) for t in (q, k, v)), valids):
        s = jnp.einsum("gqhe,gkhe->ghqk", qh, kh, preferred_element_type=F32) * score_scale
        s = jnp.where(valid[:, None, None, :], s, -1000000000.0)
        pb = jax.nn.softmax(s, axis=-1).astype(BF)
        o = jnp.einsum("ghqk,gkhe->gqhe", pb, vh, preferred_element_type=F32)
        outs.append(o.reshape(-1, width).astype(BF))
        probs.append(pb.reshape((-1,) + pb.shape[2:]))
    mixed = jnp.concatenate(outs)

    def norm(z):
        centred = z - jnp.mean(z, axis=-1, keepdims=True)
        root = lax.rsqrt(jnp.mean(centred * centred, axis=-1, keepdims=True) + ln_epsilon)
        return centred * root, jnp.broadcast_to(root, (n_own, 128))

    attn = jnp.einsum("te,de->td", mixed, va[1], preferred_element_type=F32)
    xh1, r1 = norm(x_own.astype(F32) + attn + vec[2])
    h1 = xh1 * vec[3] + vec[4]
    u = jnp.einsum("td,hdf->htf", h1.astype(BF), inner, preferred_element_type=F32) + b_inner[:, None, :]
    tail = 0.5 * (1.0 + lax.erf(u * 0.7071067811865476))
    g = (u * tail).astype(BF)
    gp = (tail + u * (0.3989422804014327 * jnp.exp(-0.5 * u * u))).astype(BF)
    f = jnp.einsum("htf,hdf->td", g, outer, preferred_element_type=F32)
    xh2, r2 = norm(h1 + f + vec[5 + ff_rows])
    out_own = (xh2 * vec[6 + ff_rows] + vec[7 + ff_rows]).astype(BF)
    vec = jnp.pad(vec, ((0, 16 - nvec), (0, 0)))
    return [qk, va, inner, outer, x_all, q, k, v, *probs, mixed, xh1, r1, g, gp, xh2, r2, proj, vec, out_own]


def halves(t, n_full, seq_len):
    heads = t.shape[1] // HEAD_DIM
    last = t.shape[0] - n_full
    return (
        t[:n_full].reshape(n_full // seq_len, seq_len, heads, HEAD_DIM),
        t[n_full:].reshape(1, last, heads, HEAD_DIM),
    )


def local(
    tokens, cotangent, lengths, doc_ids, doc_rows,
    w_qkv, m_qkv, v_qkv, w_attn, m_attn, v_attn, w_inner, m_inner, v_inner,
    w_outer, m_outer, v_outer, w_proj, m_proj, v_proj, vectors, m_vectors, v_vectors,
):
    mp = lax.axis_index("mp")
    n_dp, n_mp = lax.axis_size("dp"), lax.axis_size("mp")
    fast = n_dp == NZ * NY * NC and n_mp == NX
    seqs = lengths.shape[0]
    all_rows, width = tokens.shape
    seq_len = all_rows // seqs
    full = seqs // 2
    n_full, n_half = full * seq_len, seq_len // 2
    n_own = n_full + n_half
    rows, half_ff = w_qkv.shape[1], w_inner.shape[1]
    half_rows = rows // 2
    nvec, vec_lanes = vectors.shape
    ff_rows = nvec - 8
    score_scale = HEAD_DIM ** (-0.5)

    forward = forward_fast if fast else forward_plain
    saved = forward(lengths, tokens, w_qkv, w_attn, w_inner, w_outer, w_proj, vectors)
    (qk, va, inner, outer, x_all, q, k, v, p_ab, p_c, mixed, xh1, r1, act_low, slope, xh2, r2, proj, vec, out_own) = saved
    qk = qk.reshape(2, width, width)
    va = va.reshape(2, width, width)
    inner = inner.reshape(2, width, half_ff)
    outer = outer.reshape(2, width, half_ff)
    x_own = x_all[:n_own]
    proj = proj.astype(BF)
    a0 = mp * (n_full + seq_len)
    h0 = n_full + mp * n_half
    cot = jnp.concatenate(
        [lax.dynamic_slice_in_dim(cotangent, a0, n_full, 0), lax.dynamic_slice_in_dim(cotangent, h0, n_half, 0)]
    )
    my_seqs = jnp.concatenate([mp * (full + 1) + jnp.arange(full), jnp.array([full])])

    n_mine = full + 1
    mine = jnp.where((jnp.arange(n_mine) < full) | (mp == 0), 1.0, 0.0).astype(F32)
    cls_low = out_own[:: seq_len][:n_mine]
    docs = doc_rows[my_seqs].astype(F32)
    ids = doc_ids[my_seqs]
    query = jnp.dot(cls_low, proj, preferred_element_type=F32).astype(BF)
    query_float = query.astype(F32)
    doc_scores = jnp.einsum("gp,gkp->gk", query_float, docs, precision=highest_mode) * retrieval_scale
    soft = jax.nn.softmax(doc_scores, axis=-1)
    target = (jnp.arange(doc_scores.shape[1]) == 0).astype(F32)
    score_grad = (soft - target[None, :]) * retrieval_scale * mine[:, None]
    query_grad = jnp.einsum("gk,gkp->gp", score_grad, docs, precision=highest_mode).astype(BF)
    row_grads = score_grad[:, :, None] * query_float[:, None, :]
    cls_grad = jnp.einsum("gp,dp->gd", query_grad, proj, preferred_element_type=F32)
    proj_grad = jnp.einsum("gd,gp->dp", cls_low, query_grad, preferred_element_type=F32)
    table_rows = TAB_DEV * n_dp
    one_hot = (jnp.arange(table_rows)[:, None] == ids.reshape(1, -1)).astype(F32)
    table_local = jnp.dot(one_hot, row_grads.reshape(-1, row_grads.shape[2]), precision=highest_mode)

    def norm_back(dy, hat, root, gain):
        e = dy * gain
        back_ = e - jnp.mean(e, axis=-1, keepdims=True) - hat * jnp.mean(e * hat, axis=-1, keepdims=True)
        return back_ * root[:, :1], jnp.sum(dy * hat, axis=0), jnp.sum(dy, axis=0)

    dy = cot.astype(F32)
    first_rows = jnp.arange(n_mine) * seq_len
    dy = dy.at[first_rows].add(cls_grad)
    dz2, dg2, dc2 = norm_back(dy, xh2, r2, vec[6 + ff_rows])
    df = dz2.astype(BF)
    dg = jnp.einsum("td,hdf->htf", df, outer, preferred_element_type=F32)
    g_outer = jnp.einsum("td,htf->hdf", df, act_low, preferred_element_type=F32).astype(BF)
    du = (dg * slope.astype(F32)).astype(BF)
    normed_low = (xh1 * vec[3] + vec[4]).astype(BF)
    g_inner = jnp.einsum("td,htf->hdf", normed_low, du, preferred_element_type=F32).astype(BF)
    dh1 = jnp.einsum("htf,hdf->td", du, inner, preferred_element_type=F32) + dz2
    dz1, dg1, dc1 = norm_back(dh1, xh1, r1, vec[3])
    da = dz1.astype(BF)
    do = jnp.dot(da, va[1], preferred_element_type=F32).astype(BF)
    g_attn = jnp.einsum("td,te->de", da, mixed, preferred_element_type=F32)
    dqs, dks, dvs = [], [], []
    probs_of = (p_ab.reshape(full, -1, seq_len, seq_len), p_c.reshape(1, -1, n_half, seq_len))
    for qh, kh, vh, doh, pb in zip(*(halves(t, n_full, seq_len) for t in (q, k, v, do)), probs_of):
        probs = pb.astype(F32)
        dp_ = jnp.einsum("gqhe,gkhe->ghqk", doh, vh, preferred_element_type=F32)
        delta = jnp.sum(probs * dp_, axis=-1, keepdims=True)
        ds_ = (probs * (dp_ - delta)).astype(BF)
        dqs.append((jnp.einsum("ghqk,gkhe->gqhe", ds_, kh, preferred_element_type=F32) * score_scale).reshape(-1, width))
        dks.append((jnp.einsum("ghqk,gqhe->gkhe", ds_, qh, preferred_element_type=F32) * score_scale).reshape(-1, width))
        dvs.append(jnp.einsum("ghqk,gqhe->gkhe", pb, doh, preferred_element_type=F32).reshape(-1, width))
    dq = jnp.concatenate(dqs).astype(BF)
    dk = jnp.concatenate(dks).astype(BF)
    dv = jnp.concatenate(dvs).astype(BF)
    g_q = jnp.einsum("td,te->de", x_own, dq, preferred_element_type=F32)
    g_k = jnp.einsum("td,te->de", x_all, dk, preferred_element_type=F32)
    g_v = jnp.einsum("td,te->de", x_all, dv, preferred_element_type=F32)
    g_qk = jnp.stack([g_q, g_k]).astype(BF)
    g_va = jnp.stack([g_v, g_attn]).astype(BF)
    dx_own = jnp.einsum("te,de->td", dq, qk[0], preferred_element_type=F32) + dz1
    dx_all = jnp.einsum("te,de->td", dk, qk[1], preferred_element_type=F32)
    dx_all = dx_all + jnp.einsum("te,de->td", dv, va[0], preferred_element_type=F32)
    dx = jnp.concatenate([dx_all[:n_own] + dx_own, dx_all[n_own:]]).astype(BF)
    db_inner = jnp.sum(du.astype(F32), axis=1)
    db_inner = db_inner.reshape(2, 2, half_ff // 2).transpose(1, 0, 2).reshape(ff_rows, width)
    vec_grad = jnp.concatenate(
        [
            jnp.stack(
                [
                    jnp.sum(dq.astype(F32), axis=0),
                    jnp.sum(dv.astype(F32), axis=0),
                    jnp.sum(dz1, axis=0),
                    dg1,
                    dc1,
                ]
            ),
            db_inner,
            jnp.stack([jnp.sum(dz2, axis=0), dg2, dc2]),
        ]
    )
    vg = vec_grad.reshape(nvec, n_dp, 2, vec_lanes).transpose(1, 0, 2, 3)
    vg = jnp.pad(vg, ((0, 0), (0, 0), (0, 0), (0, 128 - vec_lanes))).reshape(n_dp, nvec, 256)
    pg = proj_grad.reshape(n_dp, 2, half_rows, 128).transpose(0, 2, 1, 3).reshape(n_dp, half_rows, 256)
    tg = table_local.reshape(n_dp, 2, TAB_DEV // 2, 128).transpose(0, 2, 1, 3).reshape(n_dp, TAB_DEV // 2, 256)
    small = jnp.concatenate([pg, vg, tg], axis=1)

    reduce = reduce_fast if fast else reduce_plain
    (small_r, qk_r, va_r, inner_r, outer_r, peer_out, peer_dx, peer_small, total) = reduce(
        [g_qk, g_va, g_inner, g_outer], small, out_own, dx, rows
    )

    def whole_rows(own, peer):
        lo = jnp.where(mp == 0, own[:n_own], peer[:n_own])
        hi = jnp.where(mp == 0, peer[:n_own], own[:n_own])
        return lo, hi

    lo, hi = whole_rows(out_own, peer_out)
    out_tokens = jnp.concatenate([lo, hi[n_full:], hi[:n_full]])
    lo, hi = whole_rows(dx.astype(F32), peer_dx.astype(F32))
    tail = jnp.where(mp == 0, dx[n_own:], peer_dx[n_own:]).astype(F32)
    tail_hi = jnp.where(mp == 0, peer_dx[n_own:], dx[n_own:]).astype(F32)
    input_grad = jnp.concatenate(
        [lo[:n_full], lo[n_full:] + tail_hi, hi[n_full:] + tail, hi[:n_full]]
    )

    def both_halves(at, count):
        mine_, peer_ = small_r[at : at + count], peer_small[at : at + count]
        return jnp.concatenate(
            [jnp.where(mp == 0, mine_, peer_), jnp.where(mp == 0, peer_, mine_)]
        )

    proj_r = both_halves(0, half_rows)
    table_grad = both_halves(half_rows + nvec, TAB_DEV // 2)
    vector_r = small_r[half_rows : half_rows + nvec, :vec_lanes]
    qkv_r = jnp.stack([qk_r[0], qk_r[1], va_r[0]])
    attn_r = va_r[1]

    def back(v):
        return v.transpose(1, 0, 2).reshape(rows, half_ff)

    inner_r, outer_r = back(inner_r), back(outer_r)
    grad_norm = jnp.sqrt(total[0, 0])
    clip = clip_norm / jnp.maximum(grad_norm, clip_norm)
    results = [out_tokens, input_grad, grad_norm]
    for w, m, s, g, dec, rate in (
        (w_qkv, m_qkv, v_qkv, qkv_r, decay_rate, learn_rate),
        (w_attn, m_attn, v_attn, attn_r, decay_rate, learn_rate),
        (w_inner, m_inner, v_inner, inner_r, decay_rate, learn_rate),
        (w_outer, m_outer, v_outer, outer_r, decay_rate, learn_rate),
        (w_proj, m_proj, v_proj, proj_r, decay_rate, learn_rate),
        (vectors, m_vectors, v_vectors, vector_r, 0.0, vector_rate),
    ):
        results += list(adamw_update(w, m, s, g * clip, dec, rate))
    return tuple(results) + (table_grad,)


def solution(mesh):
    mat = P("dp", "mp")
    rep = P("dp", None)
    qkv = P(None, "dp", "mp")
    vec = P(None, ("dp", "mp"))
    placed = (rep, rep, P("dp"), rep, P("dp", None, None), qkv, qkv, qkv)
    placed += (mat,) * 9 + (rep,) * 3 + (vec,) * 3
    given = (rep, rep, P(), qkv, qkv, qkv) + (mat,) * 9 + (rep,) * 3 + (vec,) * 3 + (rep,)
    return jax.shard_map(local, mesh=mesh, in_specs=placed, out_specs=given, check_vma=False)
```

```python
import functools

import jax
import jax.numpy as jnp
from jax import lax
from jax.experimental import pallas as pl
from jax.experimental.pallas import tpu as pltpu
from jax.sharding import PartitionSpec as P

HEAD_DIM = 64
STEP = 10
TAB_DEV = 8
MESH = pl.DeviceIdType.MESH
ANY = pl.ANY
BF = jnp.bfloat16
F32 = jnp.float32
NZ, NY, NC, NX = 4, 2, 2, 2

highest_mode = lax.Precision.HIGHEST
retrieval_scale = 0.17677669529663687
ln_epsilon = 1e-12
beta_first = 0.9
beta_second = 0.999
learn_rate = 0.05
vector_rate = 0.5
decay_rate = 0.01
adam_epsilon = 1e-08
clip_norm = 1.0


def layer_norm(values, gain_row, shift_row):
    centre = jnp.mean(values, axis=-1, keepdims=True)
    centred = values - centre
    spread = jnp.mean(centred * centred, axis=-1, keepdims=True)
    return centred * lax.rsqrt(spread + ln_epsilon) * gain_row + shift_row


def gelu_exact(values):
    return jax.nn.gelu(values, approximate=False)


def adamw_update(weight, moment, second, gradient, decay_factor, step_rate):
    moment_new = beta_first * moment + (1.0 - beta_first) * gradient
    second_new = beta_second * second + (1.0 - beta_second) * gradient * gradient
    first_hat = moment_new / (1.0 - beta_first**STEP)
    second_hat = second_new / (1.0 - beta_second**STEP)
    weight_new = weight - step_rate * (
        first_hat / (jnp.sqrt(second_hat) + adam_epsilon) + decay_factor * weight
    )
    return (moment_new, second_new, weight_new)


def squared(values):
    return jnp.sum(values * values)


class Place:
    def __init__(self):
        dp = lax.axis_index("dp")
        self.x = lax.axis_index("mp")
        self.c = lax.rem(dp, NC)
        self.y = lax.rem(dp // NC, NY)
        self.z = dp // (NC * NY)

    def dev(self, z=None, y=None, c=None, x=None):
        z = self.z if z is None else z
        y = self.y if y is None else y
        c = self.c if c is None else c
        x = self.x if x is None else x
        return ((z * NY + y) * NC + c, x)

    def others(self):
        out = [self.dev(z=lax.rem(self.z + k, NZ)) for k in range(1, NZ)]
        out.append(self.dev(x=1 - self.x))
        out.append(self.dev(y=1 - self.y))
        out.append(self.dev(c=1 - self.c))
        return out

    def eights(self):
        out = []
        for k in range(1, 8):
            dx, dy, dc = k & 1, (k >> 1) & 1, k >> 2
            out.append(
                self.dev(
                    x=self.x + dx - 2 * dx * self.x,
                    y=self.y + dy - 2 * dy * self.y,
                    c=self.c + dc - 2 * dc * self.c,
                )
            )
        return out


def greet(devices):
    barrier = pltpu.get_barrier_semaphore()
    for d in devices:
        pl.semaphore_signal(barrier, inc=1, device_id=d, device_id_type=MESH)
    pl.semaphore_wait(barrier, len(devices))


def remote(src, dst, ssem, rsem, dev):
    return pltpu.make_async_remote_copy(
        src_ref=src, dst_ref=dst, send_sem=ssem, recv_sem=rsem, device_id=dev, device_id_type=MESH
    )


def cols(x, half):
    return pl.ds(pl.multiple_of(x * half, 128), half)


def dma(*shape):
    return pltpu.SemaphoreType.DMA(shape)


def mm(a, b):
    return jnp.dot(a, b, preferred_element_type=F32)


def mm_nt(a, b):
    return lax.dot_general(a, b, (((1,), (1,)), ((), ())), preferred_element_type=F32)


def mm_tn(a, b):
    return lax.dot_general(a, b, (((0,), (0,)), ((), ())), preferred_element_type=F32)


def flat(value):
    return value.reshape(-1, value.shape[-1])


def lanes(i, n=128):
    return pl.ds(pl.multiple_of(i * n, 128), n)


def rows_at(i, n, at=0):
    return pl.ds(pl.multiple_of(at + i * n, 16), n)


def each(n, body):
    lax.fori_loop(0, n, lambda i, c: (body(i), c)[1], 0)


class Gather:
    def __init__(self, me, pieces, sems):
        self.me, self.pieces = me, pieces
        self.lsem, self.zs, self.zr, self.s1, self.r1, self.s2, self.r2, self.ds, self.dr = sems
        self.waits, self.locs = [], {}

    def go(self, copy):
        copy.start()
        self.waits.append(copy)

    def step1(self, p):
        me = self.me
        src, dst = self.pieces[p]
        blk = dst.at[me.z, me.y, me.c, :, cols(me.x, dst.shape[-1] // 2)]
        loc = pltpu.make_async_copy(src, blk, self.lsem.at[p])
        loc.start()
        self.locs[p] = loc
        for k in range(1, NZ):
            dev = me.dev(z=lax.rem(me.z + k, NZ))
            self.go(remote(src, blk, self.zs.at[p, k], self.zr.at[p, k], dev))

    def part(self, p, stage, c):
        me, dst = self.me, self.pieces[p][1]
        half = dst.shape[-1] // 2
        own, other = cols(me.x, half), cols(1 - me.x, half)
        if stage == "z":
            return dst.at[:, me.y, c, :, own]
        if p % 2 == 0:
            if stage == "in1":
                return dst.at[:, me.y, c, :, other]
            if stage == "out2":
                return dst.at[:, me.y, c]
            return dst.at[:, 1 - me.y, c]
        if stage == "in1":
            return dst.at[:, 1 - me.y, c, :, own]
        if stage == "out2":
            return dst.at[:, :, c, :, own]
        return dst.at[:, :, c, :, other]

    def first(self, p):
        return self.me.dev(x=1 - self.me.x) if p % 2 == 0 else self.me.dev(y=1 - self.me.y)

    def second(self, p):
        return self.me.dev(y=1 - self.me.y) if p % 2 == 0 else self.me.dev(x=1 - self.me.x)

    def cross(self, p, ref, which):
        self.go(remote(ref, ref, self.ds.at[p, which], self.dr.at[p, which], self.me.dev(c=1 - self.me.c)))

    def arrived(self, ref, ssem, rsem):
        remote(ref, ref, ssem, rsem, self.me.dev(c=1 - self.me.c)).wait_recv()

    def step2(self, p):
        me, dst = self.me, self.pieces[p][1]
        self.locs[p].wait()
        for k in range(1, NZ):
            blk = dst.at[lax.rem(me.z + NZ - k, NZ), me.y, me.c, :, cols(me.x, dst.shape[-1] // 2)]
            self.arrived(blk, self.zs.at[p, k], self.zr.at[p, k])
        have = self.part(p, "z", me.c)
        self.go(remote(have, have, self.s1.at[p], self.r1.at[p], self.first(p)))
        self.cross(p, have, 0)

    def step3(self, p):
        got = self.part(p, "in1", self.me.c)
        self.arrived(got, self.s1.at[p], self.r1.at[p])
        have = self.part(p, "out2", self.me.c)
        self.go(remote(have, have, self.s2.at[p], self.r2.at[p], self.second(p)))
        self.cross(p, got, 1)

    def step4(self, p):
        got = self.part(p, "in2", self.me.c)
        self.arrived(got, self.s2.at[p], self.r2.at[p])
        self.cross(p, got, 2)

    def step5(self, p):
        for which, stage in enumerate(("z", "in1", "in2")):
            self.arrived(self.part(p, stage, 1 - self.me.c), self.ds.at[p, which], self.dr.at[p, which])

    def tick(self, t, ahead):
        n = len(self.pieces)
        if t < n:
            self.step2(t)
            if t + ahead < n:
                self.step1(t + ahead)
        if 0 <= t - 1 < n:
            self.step3(t - 1)
        if 0 <= t - 2 < n:
            self.step4(t - 2)
        if 0 <= t - 3 < n:
            self.step5(t - 3)

    def end(self):
        for copy in self.waits:
            copy.wait_send()


def norm_rows(z_ref, r_ref, n_rows, put):
    step = 48

    def body(i):
        at = rows_at(i, step)
        z = z_ref[at, :]
        centred = z - jnp.mean(z, axis=-1, keepdims=True)
        spread = jnp.mean(centred * centred, axis=-1, keepdims=True)
        root = lax.rsqrt(spread + ln_epsilon)
        hat = centred * root
        z_ref[at, :] = hat
        r_ref[at, :] = jnp.broadcast_to(root, (step, 128))
        put(at, hat)

    each(n_rows // step, body)


def forward_kernel(*refs):
    (lens, tokens, w_qkv, w_attn, w_inner, w_outer, w_proj, vectors) = refs[:8]
    outs = refs[8:27]
    scr = refs[27:]
    (small_s, qk_s, va_s, inner_s, outer_s, small_g, qk, va, inner, outer) = scr[:10]
    (xt, q, k, v, p, o, xh1, r1, g, gp, xh2, r2, out_own, proj, vec, x_all, h1b, vecp, bias_ff) = scr[10:29]
    gsems, tsem, osem = scr[29:38], scr[38], scr[39]
    me = Place()
    mp = me.x
    n_all, width = x_all.shape
    n_own = q.shape[0]
    half_seq = n_all - n_own
    seq = 2 * half_seq
    full = (n_own - half_seq) // seq
    n_full = full * seq
    half_ff = inner.shape[-1]
    rows = qk_s.shape[1]
    half_rows = rows // 2

    starts = (
        (mp * (n_full + seq), 0, n_full),
        (n_full + mp * half_seq, n_full, half_seq),
        (n_full + (1 - mp) * half_seq, n_own, half_seq),
    )
    loads = []
    for i, (at, to, n) in enumerate(starts):
        cp = pltpu.make_async_copy(
            tokens.at[pl.ds(pl.multiple_of(at, 16), n)], x_all.at[pl.ds(to, n)], tsem.at[i]
        )
        cp.start()
        loads.append(cp)

    vecp[...] = jnp.zeros_like(vecp)
    nvec, nlane = vectors.shape
    vecp[0:nvec, 0:nlane] = vectors[...]
    small_s[0:half_rows] = w_proj[pl.ds(pl.multiple_of(mp * half_rows, 8), half_rows), :]
    small_s[half_rows : half_rows + nlane] = jnp.transpose(vecp[...])[0:nlane]
    qk_s[...] = w_qkv[0:2].astype(BF)
    va_s[0] = w_qkv[2].astype(BF)
    va_s[1] = w_attn[...].astype(BF)
    hf = half_ff // 2
    for h in range(2):
        inner_s[h] = w_inner[:, h * hf : (h + 1) * hf].astype(BF)
        outer_s[h] = w_outer[:, h * hf : (h + 1) * hf].astype(BF)

    greet(me.others())
    pieces = [
        (small_s, small_g),
        (qk_s.at[0], qk.at[0]),
        (qk_s.at[1], qk.at[1]),
        (va_s.at[0], va.at[0]),
        (va_s.at[1], va.at[1]),
        (inner_s.at[0], inner.at[0]),
        (inner_s.at[1], inner.at[1]),
        (outer_s.at[0], outer.at[0]),
        (outer_s.at[1], outer.at[1]),
    ]
    net = Gather(me, pieces, gsems)
    ahead = 3
    for i in range(ahead):
        net.step1(i)
    tick = lambda t: net.tick(t, ahead)
    saves = []

    def save(i, ref):
        cp = pltpu.make_async_copy(ref, outs[i], osem.at[i])
        cp.start()
        saves.append(cp)

    for cp in loads:
        cp.wait()

    def x_turn(i):
        xt[rows_at(i, 256), :] = jnp.transpose(x_all[:, lanes(i, 256)])

    each(width // 256, x_turn)
    save(4, xt)
    for t in range(4):
        tick(t)
    big = []
    for z in range(NZ):
        for y in range(NY):
            for c in range(NC):
                for x in range(NX):
                    blk = small_g[z, y, c, :, x * 128 : (x + 1) * 128]
                    d = ((z * NY + y) * NC + c) * NX + x
                    proj[d * half_rows : (d + 1) * half_rows] = blk[:half_rows]
                    big.append(blk[half_rows : half_rows + nlane])
    vec[...] = jnp.transpose(jnp.concatenate(big, axis=0))[0 : vec.shape[0]]
    for h in range(2):
        for x in range(NX):
            bias_ff[h : h + 1, x * width : (x + 1) * width] = vec[5 + NX * x + h : 6 + NX * x + h, :]
    save(16, proj)
    save(17, vec)

    def project(w_ref, src_rows, dst, bias):
        n_tile = 256

        def body(i):
            w = flat(w_ref[:, :, :, :, lanes(i, n_tile)])
            r = mm(x_all[0:src_rows], w)
            if bias is not None:
                r = r + vec[bias : bias + 1, lanes(i, n_tile)]
            dst[:, lanes(i, n_tile)] = r.astype(BF)

        each(width // n_tile, body)

    tick(4)
    project(qk.at[0], n_own, q, 0)
    tick(5)
    project(qk.at[1], n_all, k, None)
    save(0, qk)
    tick(6)
    project(va.at[0], n_all, v, 1)
    save(5, q)
    save(6, k)
    save(7, v)

    lane = lax.broadcasted_iota(jnp.int32, (1, 128), 1)
    head_lo = jnp.where(lane < HEAD_DIM, 1.0, 0.0)
    head_mask = (head_lo.astype(BF), (1.0 - head_lo).astype(BF))
    pos = lax.broadcasted_iota(jnp.int32, (1, seq), 1)

    def attend(q0, nq, k0, slab, length, place):
        at_q = pl.ds(pl.multiple_of(q0, 16), nq)
        at_k = pl.ds(pl.multiple_of(k0, 16), seq)
        for pair in range(2):
            l = lanes(2 * slab + pair)
            qp, kp, vp = q[at_q, l], k[at_k, l], v[at_k, l]
            got = []
            for h in range(2):
                s = mm_nt(qp * head_mask[h], kp) * (HEAD_DIM**-0.5)
                s = jnp.where(place < length, s, -1000000000.0)
                e = jnp.exp(s - jnp.max(s, axis=-1, keepdims=True))
                pb = (e * (1.0 / jnp.sum(e, axis=-1, keepdims=True))).astype(BF)
                j = 384 * (2 * pair + h)
                p[slab, at_q, j : j + seq] = pb
                got.append(mm(pb, vp))
            o[at_q, l] = jnp.where(lane < HEAD_DIM, got[0], got[1]).astype(BF)

    slabs = p.shape[0]
    for s in range(full):
        length = lens[mp * (full + 1) + s]
        each(slabs, lambda i: attend(s * seq, seq, s * seq, i, length, pos))
        tick(7 + s)
    length = lens[full]
    pos_c = jnp.where(pos < half_seq, pos + mp * half_seq, pos - half_seq + (1 - mp) * half_seq)
    each(slabs, lambda i: attend(n_full, half_seq, n_full, i, length, pos_c))
    save(8, p)
    save(9, o)
    tick(7 + full)

    tile = 240
    tiles = n_own // tile

    def attn_out(i):
        a = mm_nt(o[rows_at(i, tile), :], flat(va[1]))
        xh1[rows_at(i, tile), :] = x_all[rows_at(i, tile), :].astype(F32) + a + vec[2:3, :]

    each(tiles, attn_out)
    save(1, va)

    def put_h1(at, hat):
        h1b[at, :] = (hat * vec[3:4, :] + vec[4:5, :]).astype(BF)

    norm_rows(xh1, r1, n_own, put_h1)
    save(10, xh1)
    save(11, r1)
    tick(8 + full)

    def feed(h):
        n_tile = 256

        def body(i):
            w = flat(inner[h, :, :, :, :, lanes(i, n_tile)])
            for t in range(tiles):
                at = pl.ds(t * tile, tile)
                u = mm(h1b[at, :], w)
                u = u + bias_ff[h : h + 1, lanes(i, n_tile)]
                tail = 0.5 * (1.0 + lax.erf(u * 0.7071067811865476))
                g[h, at, lanes(i, n_tile)] = (u * tail).astype(BF)
                slope = tail + u * (0.3989422804014327 * jnp.exp(-0.5 * u * u))
                gp[h, at, lanes(i, n_tile)] = slope.astype(BF)

        each(half_ff // n_tile, body)

    feed(0)
    tick(9 + full)
    feed(1)
    for t in range(10 + full, len(pieces) + 3):
        tick(t)
    save(2, inner)
    save(12, g)
    save(13, gp)

    def ff_out(i):
        at = rows_at(i, tile)
        f = mm_nt(g[0, at, :], flat(outer[0])) + mm_nt(g[1, at, :], flat(outer[1]))
        h1 = xh1[at, :] * vec[3:4, :] + vec[4:5, :]
        xh2[at, :] = h1 + f + vec[9:10, :]

    each(tiles, ff_out)
    save(3, outer)

    def put_y(at, hat):
        out_own[at, :] = (hat * vec[10:11, :] + vec[11:12, :]).astype(BF)

    norm_rows(xh2, r2, n_own, put_y)
    save(14, xh2)
    save(15, r2)
    save(18, out_own)
    net.end()
    for cp in saves:
        cp.wait()


def forward_fast(lengths, tokens, w_qkv, w_attn, w_inner, w_outer, w_proj, vectors):
    seqs = lengths.shape[0]
    all_rows, width = tokens.shape
    seq = all_rows // seqs
    full = seqs // 2
    n_own = full * seq + seq // 2
    n_all = n_own + seq // 2
    rows, half_ff = w_qkv.shape[1], w_inner.shape[1]
    heads = width // HEAD_DIM
    zyc = (NZ, NY, NC)
    small_rows = rows // 2 + vectors.shape[1]
    weights = [
        ((2,) + zyc + (rows, width), BF),
        ((2,) + zyc + (rows, width), BF),
        ((2,) + zyc + (rows, half_ff), BF),
        ((2,) + zyc + (rows, half_ff), BF),
    ]
    kept = [
        ((width, n_all), BF),
        ((n_own, width), BF),
        ((n_all, width), BF),
        ((n_all, width), BF),
        ((heads // 4, n_own, 4 * 384), BF),
        ((n_own, width), BF),
        ((n_own, width), F32),
        ((n_own, 128), F32),
        ((2, n_own, half_ff), BF),
        ((2, n_own, half_ff), BF),
        ((n_own, width), F32),
        ((n_own, 128), F32),
        ((width, 128), F32),
        ((16, width), F32),
        ((n_own, width), BF),
    ]
    order = kept[:12] + [kept[14], kept[12], kept[13]]
    scratch = [
        ((small_rows, 128), F32),
        ((2, rows, width // 2), BF),
        ((2, rows, width // 2), BF),
        ((2, rows, half_ff // 2), BF),
        ((2, rows, half_ff // 2), BF),
        (zyc + (small_rows, 256), F32),
    ]
    scratch += weights + order
    scratch += [((n_all, width), BF), ((n_own, width), BF), ((128, 128), F32), ((8, half_ff), F32)]
    n = 9
    vm = pl.BlockSpec(memory_space=pltpu.VMEM)
    hb = pl.BlockSpec(memory_space=ANY)
    sm = pl.BlockSpec(memory_space=pltpu.SMEM)
    return pl.pallas_call(
        forward_kernel,
        out_shape=[jax.ShapeDtypeStruct(s, d) for s, d in weights + kept],
        in_specs=[sm, hb] + [vm] * 6,
        out_specs=[hb] * 19,
        scratch_shapes=[pltpu.VMEM(s, d) for s, d in scratch]
        + [
            dma(n), dma(n, NZ), dma(n, NZ), dma(n), dma(n), dma(n), dma(n), dma(n, 3), dma(n, 3),
            dma(3), dma(20),
        ],
        compiler_params=pltpu.CompilerParams(
            collective_id=1, has_side_effects=True, vmem_limit_bytes=60 * 2**20
        ),
        name="forward",
    )(lengths, tokens, w_qkv, w_attn, w_inner, w_outer, w_proj, vectors)


class Reduce:
    def __init__(self, me, pieces, sems):
        self.me, self.pieces = me, pieces
        self.ds, self.dr, self.s1, self.r1, self.s2, self.r2, self.zs, self.zr = sems
        self.waits = []
        self.squares = jnp.zeros((1, 1), F32)

    def go(self, copy):
        copy.start()
        self.waits.append(copy)

    def arrived(self, ref, ssem, rsem):
        remote(ref, ref, ssem, rsem, self.me.dev(c=1 - self.me.c)).wait_recv()

    def step1(self, p):
        src, got1 = self.pieces[p][2], self.pieces[p][3]
        oc = 1 - self.me.c
        self.go(remote(src.at[:, :, oc], got1, self.ds.at[p], self.dr.at[p], self.me.dev(c=oc)))

    def step2(self, p):
        route, _, src, got1, got2, _, _ = self.pieces[p]
        me = self.me
        c, half = me.c, src.shape[-1] // 2
        self.arrived(got1, self.ds.at[p], self.dr.at[p])

        def add(z):
            for y in range(NY):
                src[z, y, c] = src[z, y, c] + got1[z, y]

        each(NZ, add)
        if route == "y":
            part, dev = src.at[:, 1 - me.y, c], me.dev(y=1 - me.y)
        else:
            part, dev = src.at[:, :, c, :, cols(1 - me.x, half)], me.dev(x=1 - me.x)
        self.go(remote(part, got2, self.s1.at[p], self.r1.at[p], dev))

    def step3(self, p):
        route, _, src, _, got2, got3, _ = self.pieces[p]
        me = self.me
        c, half = me.c, src.shape[-1] // 2
        mine = cols(me.x, half)
        self.arrived(got2, self.s1.at[p], self.r1.at[p])
        if route == "y":

            def add(z):
                src[z, me.y, c] = src[z, me.y, c] + got2[z]

            each(NZ, add)
            part, dev = src.at[:, me.y, c, :, cols(1 - me.x, half)], me.dev(x=1 - me.x)
        else:

            def add(z):
                for y in range(NY):
                    src[z, y, c, :, mine] = src[z, y, c, :, mine] + got2[z, y]

            each(NZ, add)
            part, dev = src.at[:, 1 - me.y, c, :, mine], me.dev(y=1 - me.y)
        self.go(remote(part, got3, self.s2.at[p], self.r2.at[p], dev))

    def step4(self, p):
        _, _, src, _, _, got3, got4 = self.pieces[p]
        me = self.me
        c, mine = me.c, cols(me.x, src.shape[-1] // 2)
        self.arrived(got3, self.s2.at[p], self.r2.at[p])

        def add(z):
            src[z, me.y, c, :, mine] = src[z, me.y, c, :, mine] + got3[z]

        each(NZ, add)
        for k in range(1, NZ):
            tz = lax.rem(me.z + k, NZ)
            part = src.at[tz, me.y, c, :, mine]
            self.go(remote(part, got4.at[k], self.zs.at[p, k], self.zr.at[p, k], me.dev(z=tz)))

    def step5(self, p, counted=True):
        _, dst, src, _, _, _, got4 = self.pieces[p]
        me = self.me
        for k in range(1, NZ):
            self.arrived(got4.at[k], self.zs.at[p, k], self.zr.at[p, k])
        total = src[me.z, me.y, me.c, :, cols(me.x, src.shape[-1] // 2)].astype(F32)
        for k in range(1, NZ):
            total = total + got4[k].astype(F32)
        dst[...] = total
        if counted:
            self.squares = self.squares + jnp.sum(total * total, keepdims=True)

    def end(self):
        for copy in self.waits:
            copy.wait_send()


routes = ("x", "y", "x", "x", "x", "y", "y", "y", "y")


def all_squares(me, net, total, sq4, sq8, sems):
    qs, qr, es, er = sems
    sq4[0] = jnp.broadcast_to(total, (8, 128))
    copies = []
    for k in range(1, NZ):
        copies.append(remote(sq4.at[0], sq4.at[k], qs.at[k], qr.at[k], me.dev(z=lax.rem(me.z + k, NZ))))
    for copy in copies:
        net.go(copy)
    for copy in copies:
        copy.wait_recv()

    def at_z(z):
        out = jnp.zeros((8, 128), F32)
        for k in range(NZ):
            out = out + jnp.where(lax.rem(me.z + NZ - k, NZ) == z, sq4[k], 0.0)
        return out

    sq8[0] = at_z(0) + at_z(1) + at_z(2) + at_z(3)
    copies = []
    for k, dev in enumerate(me.eights(), 1):
        copies.append(remote(sq8.at[0], sq8.at[k], es.at[k], er.at[k], dev))
    for copy in copies:
        net.go(copy)
    for copy in copies:
        copy.wait_recv()

    def at_code(w):
        out = jnp.zeros((8, 128), F32)
        for k in range(8):
            dx, dy, dc = k & 1, (k >> 1) & 1, k >> 2
            src = (
                (me.x + dx - 2 * dx * me.x)
                + 2 * (me.y + dy - 2 * dy * me.y)
                + 4 * (me.c + dc - 2 * dc * me.c)
            )
            out = out + jnp.where(src == w, sq8[k], 0.0)
        return out

    whole = at_code(0)
    for w in range(1, 8):
        whole = whole + at_code(w)
    return whole


def fold(value):
    return jnp.sum(value.reshape(-1, 8, value.shape[-1]), axis=0)


def norm_back_rows(n_rows, get_dy, hat_ref, root_ref, gain, put, acc):
    step = 48

    def body(i):
        at = rows_at(i, step)
        dy, hat = get_dy(i, at), hat_ref[at, :]
        e = dy * gain
        root = root_ref[at, 0:1]
        m1 = jnp.mean(e, axis=-1, keepdims=True)
        m2 = jnp.mean(e * hat, axis=-1, keepdims=True)
        dz = (e - m1 - hat * m2) * root
        acc[0] = acc[0] + fold(dy * hat)
        acc[1] = acc[1] + fold(dy)
        acc[2] = acc[2] + fold(dz)
        hat_ref[at, :] = dz
        put(at, dz)

    each(n_rows // step, body)


def backward_kernel(*refs):
    doc_ids, cotangent, doc_rows = refs[:3]
    (qk_h, va_h, inner_h, outer_h, xt_h, q_h, k_h, v_h, p_h, o_h, xh1_h, r1_h, g_h, gp_h, xh2_h, r2_h, proj_h, vec_h, out_h) = refs[3:22]
    outs = refs[22:32]
    small_r, qk_r, va_r, inner_r, outer_r, dx, peer_out, peer_dx, peer_small, norm_ref = outs
    scr = list(refs[32:])

    def take(n):
        got = scr[:n]
        del scr[:n]
        return got

    (inner, outer, attn, xt, q, k, v, o, xh1, gg, xh2, r2, proj, vec, cls_in, cot, df, dft) = take(18)
    (cls_grad, acc1, acc2, ffacc, vg, small) = take(6)
    grads = take(4)
    bufs = take(9 * 4)
    sq4, sq8 = take(2)
    lsem, rsems, xs, xr, qsems = take(1)[0], take(8), *take(2), take(4)
    do, da, dat, h1t, r1 = cot, df, dft, dft, r2
    me = Place()
    mp = me.x
    n_all, width = dx.shape
    n_own = q.shape[0]
    half_seq = n_all - n_own
    seq = 2 * half_seq
    n_full = n_own - half_seq
    full = n_full // seq
    half_ff = inner.shape[-1]
    other = me.dev(x=1 - mp)

    for i in range(4):
        grads.append(inner.at[i // 2, :, :, :, :, pl.ds(width * (i % 2), width)])
    copies = {}

    def load(name, i, src, dst):
        cp = pltpu.make_async_copy(src, dst, lsem.at[i])
        cp.start()
        copies[name] = cp

    def need(*names):
        for name in names:
            copies[name].wait()

    load("vec", 0, vec_h, vec)
    load("proj", 1, proj_h, proj)
    for s in range(full + 1):
        load("cls%d" % s, 2 + s, out_h.at[pl.ds(s * seq, 16)], cls_in.at[s])
    load("cot0", 5, cotangent.at[pl.ds(pl.multiple_of(mp * (n_full + seq), 16), n_full)], cot.at[pl.ds(0, n_full)])
    load("cot1", 6, cotangent.at[pl.ds(pl.multiple_of(n_full + mp * half_seq, 16), half_seq)], cot.at[pl.ds(n_full, half_seq)])
    load("xh2", 7, xh2_h, xh2)
    load("r2", 8, r2_h, r2)
    load("g", 9, g_h, gg.at[pl.ds(0, 2)])
    load("outer", 10, outer_h, outer)
    load("gp", 11, gp_h, gg.at[pl.ds(2, 2)])
    load("xh1", 12, xh1_h, xh1)
    load("inner", 14, inner_h, inner)
    load("attn", 15, va_h.at[1], attn)
    load("o", 16, o_h, o)
    load("q", 17, q_h, q)
    load("k", 18, k_h, k)
    load("v", 19, v_h, v)
    load("xt", 20, xt_h, xt)

    greet(me.others() + me.eights())
    pieces = []
    dsts = [outer_r.at[0], outer_r.at[1], inner_r.at[0], inner_r.at[1], va_r.at[1], va_r.at[0], qk_r.at[0], qk_r.at[1], small_r]
    for p in range(9):
        src = grads[p] if p < 8 else small
        pieces.append((routes[p], dsts[p], src) + tuple(bufs[4 * p : 4 * p + 4]))
    net = Reduce(me, pieces, rsems)
    send_out = remote(out_h, peer_out, xs.at[0], xr.at[0], other)
    net.go(send_out)

    vg[...] = jnp.zeros_like(vg)
    small[...] = jnp.zeros_like(small)
    acc1[...] = jnp.zeros_like(acc1)
    acc2[...] = jnp.zeros_like(acc2)
    ffacc[...] = jnp.zeros_like(ffacc)
    need("vec", "proj", *["cls%d" % s for s in range(full + 1)])
    row16 = lax.broadcasted_iota(jnp.int32, (16, 1), 0)
    cls = jnp.zeros((16, width), F32)
    for s in range(full + 1):
        cls = jnp.where(row16 == s, cls_in[s].astype(F32)[0:1], cls)
    cls = cls.astype(BF)
    proj_low = proj[...].astype(BF)
    query = mm(cls, proj_low).astype(BF).astype(F32)
    row8 = lax.broadcasted_iota(jnp.int32, (8, 1), 0)
    dcq = jnp.zeros((16, 128), F32)
    row_grads = []
    cands = doc_ids.shape[1]
    seq_ids = [mp * (full + 1) + s for s in range(full)] + [full]
    for s in range(full + 1):
        docs = doc_rows[seq_ids[s]].astype(F32)
        mine = 1.0 if s < full else jnp.where(mp == 0, 1.0, 0.0)
        query_s = query[s : s + 1]
        score = jnp.sum(query_s * docs, axis=-1, keepdims=True) * retrieval_scale
        e = jnp.exp(score - jnp.max(score, axis=0, keepdims=True))
        soft = e / jnp.sum(e, axis=0, keepdims=True)
        sg = (soft - jnp.where(row8 == 0, 1.0, 0.0)) * (retrieval_scale * mine)
        dcq = jnp.where(row16 == s, jnp.sum(sg * docs, axis=0, keepdims=True), dcq)
        row_grads.append(sg * query_s)
    dcq = dcq.astype(BF)
    cls_grad[...] = mm_nt(dcq, proj_low)
    proj[...] = mm_tn(cls, dcq)

    per = seq // 48
    row48 = lax.broadcasted_iota(jnp.int32, (48, 1), 0)

    def get_dy(i, at):
        first = (row48 == 0) & (lax.rem(i, per) == 0)
        return cot[at, :].astype(F32) + jnp.where(first, cls_grad[pl.ds(i // per, 1), :], 0.0)

    def put_df(at, dz):
        df[at, :] = dz.astype(BF)

    need("cot0", "cot1", "xh2", "r2")
    norm_back_rows(n_own, get_dy, xh2, r2, vec[10:11, :], put_df, acc2)

    def turn(src, dst, n_rows):
        def body(i):
            dst[rows_at(i, 256), 0:n_rows] = jnp.transpose(src[:, lanes(i, 256)])

        each(width // 256, body)

    load("r1", 13, r1_h, r1)
    turn(df, dft, n_own)
    n_tile = 256
    shape5 = (NZ, NY, NC, width // (NZ * NY * NC))

    def weight_grad(left, right, dst, n):
        def body(i):
            r = mm(left(), right(lanes(i, n_tile)))
            dst[:, :, :, :, lanes(i, n_tile)] = r.astype(BF).reshape(shape5 + (n_tile,))

        each(n // n_tile, body)

    need("g")
    for h in range(2):
        weight_grad(lambda: dft[:, 0:n_own], lambda l: gg[h, :, l], grads[h], half_ff)
        net.step1(h)

    need("outer", "gp")
    tile = 240
    tiles = n_own // tile

    def hidden(h):
        def body(i):
            w = flat(outer[h, :, :, :, :, lanes(i, n_tile)])
            for t in range(tiles):
                at = pl.ds(t * tile, tile)
                du = (mm(df[at, :], w) * gg[2 + h, at, lanes(i, n_tile)].astype(F32)).astype(BF)
                gg[2 + h, at, lanes(i, n_tile)] = du
                ffacc[h, :, lanes(i, n_tile)] = ffacc[h, :, lanes(i, n_tile)] + fold(du.astype(F32))

        each(half_ff // n_tile, body)

    hidden(0)
    net.step2(0)
    hidden(1)
    net.step2(1)
    net.step3(0)
    load("p0", 21, p_h.at[0], gg.at[0])
    load("p1", 22, p_h.at[1], gg.at[1])
    load("wq", 23, qk_h.at[0], outer.at[0, :, :, :, :, pl.ds(0, width)])
    load("wk", 24, qk_h.at[1], outer.at[0, :, :, :, :, pl.ds(width, width)])
    load("wv", 25, va_h.at[0], outer.at[1, :, :, :, :, pl.ds(0, width)])
    need("xh1", "r1")

    def h1_turn(i):
        l = lanes(i, 256)
        h1 = (xh1[:, l] * vec[3:4, l] + vec[4:5, l]).astype(BF)
        h1t[rows_at(i, 256), 0:n_own] = jnp.transpose(h1)

    each(width // 256, h1_turn)
    for h in range(2):
        weight_grad(lambda: h1t[:, 0:n_own], lambda l: gg[2 + h, :, l], grads[2 + h], half_ff)
        net.step1(2 + h)
    net.step2(2)
    net.step3(1)
    net.step4(0)
    need("inner")

    def hidden_back(i):
        at = rows_at(i, tile)
        d = mm_nt(gg[2, at, :], flat(inner[0])) + mm_nt(gg[3, at, :], flat(inner[1]))
        xh2[at, :] = d + xh2[at, :]

    each(tiles, hidden_back)
    load("p2", 26, p_h.at[2], gg.at[2])
    net.step2(3)
    net.step3(2)
    net.step4(1)
    net.step5(0)

    norm_back_rows(n_own, lambda i, at: xh2[at, :], xh1, r1, vec[3:4, :], put_df, acc1)
    need("attn", "o")

    def mixed_back(i):
        do[:, lanes(i, n_tile)] = mm(da[...], flat(attn[:, :, :, :, lanes(i, n_tile)])).astype(BF)

    each(width // n_tile, mixed_back)
    turn(da, dat, n_own)
    weight_grad(lambda: dat[:, 0:n_own], lambda l: o[:, l], grads[4], width)
    net.step1(4)

    need("q", "k", "v", "p0", "p1", "p2")
    lane = lax.broadcasted_iota(jnp.int32, (1, 128), 1)
    head_lo = jnp.where(lane < HEAD_DIM, 1.0, 0.0)
    head_mask = (head_lo.astype(BF), (1.0 - head_lo).astype(BF))
    scale = HEAD_DIM**-0.5

    def attend(q0, nq, k0, slab):
        at_q = pl.ds(pl.multiple_of(q0, 16), nq)
        at_k = pl.ds(pl.multiple_of(k0, 16), seq)
        for pair in range(2):
            l = lanes(2 * slab + pair)
            qp, kp, vp, dop = q[at_q, l], k[at_k, l], v[at_k, l], do[at_q, l]
            got = []
            for h in range(2):
                j = 384 * (2 * pair + h)
                pb = gg[slab, at_q, j : j + seq]
                p = pb.astype(F32)
                pd = p * mm_nt(dop * head_mask[h], vp)
                ds = (pd - p * jnp.sum(pd, axis=-1, keepdims=True)).astype(BF)
                got.append((mm(ds, kp) * scale, mm_tn(ds, qp) * scale, mm_tn(pb, dop)))
            low = lane < HEAD_DIM
            q[at_q, l] = jnp.where(low, got[0][0], got[1][0]).astype(BF)
            k[at_k, l] = jnp.where(low, got[0][1], got[1][1]).astype(BF)
            v[at_k, l] = jnp.where(low, got[0][2], got[1][2]).astype(BF)

    slabs = p_h.shape[0]

    def tokens_back(at, own):
        d = mm_nt(k[at, :], flat(outer[0, :, :, :, :, width : 2 * width]))
        d = d + mm_nt(v[at, :], flat(outer[1, :, :, :, :, 0:width]))
        if own:
            d = d + mm_nt(q[at, :], flat(outer[0, :, :, :, :, 0:width])) + xh1[at, :]
            o[at, :] = d.astype(BF)
        else:
            df[0:half_seq, :] = d.astype(BF)

    keeps = []

    def send_dx(i, src, at):
        net.go(remote(src, peer_dx.at[at], xs.at[1 + i], xr.at[1 + i], other))
        cp = pltpu.make_async_copy(src, dx.at[at], lsem.at[27 + i])
        cp.start()
        keeps.append(cp)

    need("wq", "wk", "wv")
    for s in range(full):
        each(slabs, lambda i: attend(s * seq, seq, s * seq, i))
        tokens_back(pl.ds(s * seq, seq), True)
        send_dx(s, o.at[pl.ds(s * seq, seq)], pl.ds(s * seq, seq))
        if s == 0:
            net.step2(4)
            net.step3(3)
            net.step4(2)
            net.step5(1)
        else:
            net.step3(4)
            net.step4(3)
            net.step5(2)
    each(slabs, lambda i: attend(n_full, half_seq, n_full, i))
    need("xt")
    weight_grad(lambda: xt[...], lambda l: v[:, l], grads[5], width)
    net.step1(5)
    weight_grad(lambda: xt[:, 0:n_own], lambda l: q[:, l], grads[6], width)
    net.step1(6)
    net.step2(5)
    net.step4(4)
    net.step5(3)
    weight_grad(lambda: xt[...], lambda l: k[:, l], grads[7], width)
    net.step1(7)
    net.step2(6)
    net.step3(5)
    net.step5(4)
    tokens_back(pl.ds(n_full, half_seq), True)
    tokens_back(pl.ds(n_own, half_seq), False)
    send_dx(full, o.at[pl.ds(n_full, half_seq)], pl.ds(n_full, half_seq))
    send_dx(full + 1, df.at[pl.ds(0, half_seq)], pl.ds(n_own, half_seq))

    vg[0:1, :] = jnp.sum(q[...].astype(F32), axis=0, keepdims=True)
    vg[1:2, :] = jnp.sum(v[...].astype(F32), axis=0, keepdims=True)
    vg[2:3, :] = jnp.sum(acc1[2], axis=0, keepdims=True)
    vg[3:4, :] = jnp.sum(acc1[0], axis=0, keepdims=True)
    vg[4:5, :] = jnp.sum(acc1[1], axis=0, keepdims=True)
    for h in range(2):
        both = jnp.sum(ffacc[h], axis=0, keepdims=True)
        for x in range(NX):
            vg[5 + NX * x + h : 6 + NX * x + h, :] = both[:, x * width : (x + 1) * width]
    vg[9:10, :] = jnp.sum(acc2[2], axis=0, keepdims=True)
    vg[10:11, :] = jnp.sum(acc2[0], axis=0, keepdims=True)
    vg[11:12, :] = jnp.sum(acc2[1], axis=0, keepdims=True)
    turned = jnp.transpose(vg[...])
    n_dev = NZ * NY * NC * NX
    table_row = lax.broadcasted_iota(jnp.int32, (TAB_DEV * n_dev // NX, 1), 0)
    table = jnp.zeros((TAB_DEV * n_dev // NX, 128), F32)
    for s in range(full + 1):
        for i in range(cands):
            table = table + jnp.where(table_row == doc_ids[seq_ids[s], i], row_grads[s][i : i + 1], 0.0)
    hr = width // n_dev
    for z in range(NZ):
        for y in range(NY):
            for c in range(NC):
                dp = (z * NY + y) * NC + c
                for x in range(NX):
                    d = dp * NX + x
                    l = slice(x * 128, (x + 1) * 128)
                    small[z, y, c, 0:hr, l] = proj[d * hr : (d + 1) * hr]
                    small[z, y, c, hr : 2 * hr, l] = turned[d * hr : (d + 1) * hr]
                    t0 = dp * TAB_DEV + x * (TAB_DEV // NX)
                    small[z, y, c, 2 * hr : 2 * hr + TAB_DEV // NX, l] = table[t0 : t0 + TAB_DEV // NX]
    net.step1(8)
    net.step2(7)
    net.step3(6)
    net.step4(5)
    net.step2(8)
    net.step3(7)
    net.step4(6)
    net.step3(8)
    net.step4(7)
    net.step5(5)
    net.step4(8)
    net.step5(6)
    net.step5(7)
    net.step5(8, False)
    net.go(remote(small_r, peer_small, xs.at[5], xr.at[5], other))
    count = small_r[0 : 2 * hr, :]
    total = net.squares + jnp.sum(count * count, keepdims=True)
    norm_ref[...] = all_squares(me, net, total, sq4, sq8, qsems)
    parts = [pl.ds(0, seq), pl.ds(seq, seq), pl.ds(n_full, half_seq), pl.ds(n_own, half_seq)]
    for i, ref in enumerate([peer_out] + [peer_dx.at[at] for at in parts] + [peer_small]):
        net.arrived(ref, xs.at[i], xr.at[i])
    for cp in keeps:
        cp.wait()
    net.end()


def backward_fast(doc_ids, cotangent, doc_rows, saved, rows):
    (qk, va, inner, outer, xt, q, k, v, p, o, xh1, r1, g, gp, xh2, r2, proj, vec, out_own) = saved
    n_own, width = q.shape
    n_all = k.shape[0]
    half_ff = inner.shape[-1]
    zyc = (NZ, NY, NC)
    hr = rows // NX
    small_rows = 2 * hr + 8
    ins = [doc_ids, cotangent, doc_rows] + list(saved)
    out_shape = [
        ((small_rows, 128), F32),
        ((2, rows, width // 2), F32),
        ((2, rows, width // 2), F32),
        ((2, rows, half_ff // 2), F32),
        ((2, rows, half_ff // 2), F32),
        ((n_all, width), BF),
        ((n_own, width), BF),
        ((n_all, width), BF),
        ((small_rows, 128), F32),
        ((8, 128), F32),
    ]
    like = lambda a: (a.shape, a.dtype)
    wide = width // 128 * 128
    scratch = [
        like(inner), like(outer), (va.shape[1:], BF), like(xt), like(q), like(k), like(v), like(o),
        like(xh1), ((4,) + g.shape[1:], BF), like(xh2), like(r2), like(proj), like(vec),
        ((3, 16, width), BF), ((n_own, width), BF), ((n_own, width), BF),
        ((width, wide), BF),
        ((16, width), F32), ((3, 8, width), F32), ((3, 8, width), F32), ((2, 8, half_ff), F32),
        ((128, width), F32), (zyc + (small_rows, 256), F32),
    ]
    sizes = [half_ff] * 4 + [width] * 4
    scratch += [(zyc + (rows, w), BF) for w in sizes[:4]]
    for i, (r, w, dt) in enumerate([(rows, w, BF) for w in sizes] + [(small_rows, 256, F32)]):
        scratch.append(((NZ, NY, r, w), dt))
        scratch.append((((NZ, r, w) if routes[i] == "y" else (NZ, NY, r, w // 2)), dt))
        scratch.append(((NZ, r, w // 2), dt))
        scratch.append(((NZ, r, w // 2), dt))
    scratch += [((NZ, 8, 128), F32), ((8, 8, 128), F32)]
    vm = pl.BlockSpec(memory_space=pltpu.VMEM)
    hb = pl.BlockSpec(memory_space=ANY)
    sm = pl.BlockSpec(memory_space=pltpu.SMEM)
    n = 9
    return pl.pallas_call(
        backward_kernel,
        out_shape=[jax.ShapeDtypeStruct(s, d) for s, d in out_shape],
        in_specs=[sm, hb, vm] + [hb] * 19,
        out_specs=[vm] * 5 + [hb, hb, hb, vm, vm],
        scratch_shapes=[pltpu.VMEM(s, d) for s, d in scratch]
        + [
            dma(31), dma(n), dma(n), dma(n), dma(n), dma(n), dma(n), dma(n, NZ), dma(n, NZ),
            dma(6), dma(6), dma(NZ), dma(NZ), dma(8), dma(8),
        ],
        compiler_params=pltpu.CompilerParams(
            collective_id=2, has_side_effects=True, vmem_limit_bytes=63 * 2**20
        ),
        name="backward",
    )(*ins)


def gather_plain(shards, small, rows):
    def both(v, axis):
        v = lax.all_gather(v, "dp", axis=axis, tiled=True)
        return lax.all_gather(v, "mp", axis=2, tiled=True)

    return [both(small[None], 0)] + [both(v, 1) for v in shards]


def reduce_plain(grads, small, own_out, own_dx, rows):
    def both(v, axis, wide):
        v = lax.psum_scatter(v.astype(F32), "mp", scatter_dimension=wide, tiled=True)
        return lax.psum_scatter(v, "dp", scatter_dimension=axis, tiled=True)

    small_sum = both(small, 0, 2)[0]
    sums = [both(g, 1, 2) for g in grads]
    ox = 1 - lax.axis_index("mp")
    swap = [(0, 1), (1, 0)]
    peer_out = lax.ppermute(own_out, "mp", swap)
    peer_dx = lax.ppermute(own_dx, "mp", swap)
    peer_small = lax.ppermute(small_sum, "mp", swap)
    squares = sum(squared(g) for g in sums) + squared(small_sum[:-4])
    total = lax.psum(squares, ("dp", "mp"))
    return [small_sum] + sums + [peer_out, peer_dx, peer_small, jnp.full((8, 128), total)]


def forward_plain(lengths, tokens, w_qkv, w_attn, w_inner, w_outer, w_proj, vectors):
    mp = lax.axis_index("mp")
    n_dp = lax.axis_size("dp")
    seqs = lengths.shape[0]
    all_rows, width = tokens.shape
    seq_len = all_rows // seqs
    full = seqs // 2
    n_full, n_half = full * seq_len, seq_len // 2
    n_own = n_full + n_half
    heads = width // HEAD_DIM
    rows, half_ff = w_qkv.shape[1], w_inner.shape[1]
    nvec, vec_lanes = vectors.shape
    half_rows = rows // 2
    score_scale = HEAD_DIM ** (-0.5)

    def two(v):
        return v.reshape(rows, 2, half_ff // 2).transpose(1, 0, 2)

    qk_s = w_qkv[:2].astype(BF)
    va_s = jnp.stack([w_qkv[2], w_attn]).astype(BF)
    vec_pad = jnp.pad(vectors, ((0, 0), (0, 128 - vec_lanes)))
    proj_half = lax.dynamic_slice_in_dim(w_proj, mp * half_rows, half_rows, 0)
    small_s = jnp.concatenate([proj_half, vec_pad], axis=0)
    small_g, qk, va, inner, outer = gather_plain(
        [qk_s, va_s, two(w_inner.astype(BF)), two(w_outer.astype(BF))], small_s, rows
    )
    small_g = small_g.reshape(n_dp, half_rows + nvec, 2, 128)
    proj = small_g[:, :half_rows].transpose(0, 2, 1, 3).reshape(width, 128)
    vec = small_g[:, half_rows:, :, :vec_lanes].transpose(1, 0, 2, 3).reshape(nvec, width)
    ff_rows = nvec - 8
    b_inner = vec[5 : 5 + ff_rows].reshape(2, 2, half_ff // 2).transpose(1, 0, 2).reshape(2, half_ff)

    a0 = mp * (n_full + seq_len)
    h0 = n_full + mp * n_half
    o0 = n_full + (1 - mp) * n_half
    x_all = jnp.concatenate(
        [
            lax.dynamic_slice_in_dim(tokens, a0, n_full, 0),
            lax.dynamic_slice_in_dim(tokens, h0, n_half, 0),
            lax.dynamic_slice_in_dim(tokens, o0, n_half, 0),
        ]
    )
    x_own = x_all[:n_own]
    my_seqs = jnp.concatenate([mp * (full + 1) + jnp.arange(full), jnp.array([full])])
    my_len = lengths[my_seqs]
    pos = jnp.arange(seq_len)
    pos_last = jnp.where(pos < n_half, pos + mp * n_half, pos - n_half + (1 - mp) * n_half)
    valids = (pos[None, :] < my_len[:full, None], pos_last[None, :] < my_len[full:, None])

    q = (jnp.dot(x_own, qk[0], preferred_element_type=F32) + vec[0]).astype(BF)
    k = jnp.dot(x_all, qk[1], preferred_element_type=F32).astype(BF)
    v = (jnp.dot(x_all, va[0], preferred_element_type=F32) + vec[1]).astype(BF)
    probs, outs = [], []
    for qh, kh, vh, valid in zip(*(halves(t, n_full, seq_len) for t in (q, k, v)), valids):
        s = jnp.einsum("gqhe,gkhe->ghqk", qh, kh, preferred_element_type=F32) * score_scale
        s = jnp.where(valid[:, None, None, :], s, -1000000000.0)
        pb = jax.nn.softmax(s, axis=-1).astype(BF)
        o = jnp.einsum("ghqk,gkhe->gqhe", pb, vh, preferred_element_type=F32)
        outs.append(o.reshape(-1, width).astype(BF))
        probs.append(pb.reshape((-1,) + pb.shape[2:]))
    mixed = jnp.concatenate(outs)

    def norm(z):
        centred = z - jnp.mean(z, axis=-1, keepdims=True)
        root = lax.rsqrt(jnp.mean(centred * centred, axis=-1, keepdims=True) + ln_epsilon)
        return centred * root, jnp.broadcast_to(root, (n_own, 128))

    attn = jnp.einsum("te,de->td", mixed, va[1], preferred_element_type=F32)
    xh1, r1 = norm(x_own.astype(F32) + attn + vec[2])
    h1 = xh1 * vec[3] + vec[4]
    u = jnp.einsum("td,hdf->htf", h1.astype(BF), inner, preferred_element_type=F32) + b_inner[:, None, :]
    tail = 0.5 * (1.0 + lax.erf(u * 0.7071067811865476))
    g = (u * tail).astype(BF)
    gp = (tail + u * (0.3989422804014327 * jnp.exp(-0.5 * u * u))).astype(BF)
    f = jnp.einsum("htf,hdf->td", g, outer, preferred_element_type=F32)
    xh2, r2 = norm(h1 + f + vec[5 + ff_rows])
    out_own = (xh2 * vec[6 + ff_rows] + vec[7 + ff_rows]).astype(BF)
    vec = jnp.pad(vec, ((0, 16 - nvec), (0, 0)))
    return [qk, va, inner, outer, x_all, q, k, v, *probs, mixed, xh1, r1, g, gp, xh2, r2, proj, vec, out_own]


def halves(t, n_full, seq_len):
    heads = t.shape[1] // HEAD_DIM
    last = t.shape[0] - n_full
    return (
        t[:n_full].reshape(n_full // seq_len, seq_len, heads, HEAD_DIM),
        t[n_full:].reshape(1, last, heads, HEAD_DIM),
    )


def pass_plain(lengths, tokens, cotangent, doc_ids, doc_rows, w_qkv, w_attn, w_inner, w_outer, w_proj, vectors):
    mp = lax.axis_index("mp")
    n_dp, n_mp = lax.axis_size("dp"), lax.axis_size("mp")
    seqs = lengths.shape[0]
    all_rows, width = tokens.shape
    seq_len = all_rows // seqs
    full = seqs // 2
    n_full, n_half = full * seq_len, seq_len // 2
    n_own = n_full + n_half
    rows, half_ff = w_qkv.shape[1], w_inner.shape[1]
    half_rows = rows // 2
    nvec, vec_lanes = vectors.shape
    ff_rows = nvec - 8
    score_scale = HEAD_DIM ** (-0.5)

    saved = forward_plain(lengths, tokens, w_qkv, w_attn, w_inner, w_outer, w_proj, vectors)
    (qk, va, inner, outer, x_all, q, k, v, p_ab, p_c, mixed, xh1, r1, act_low, slope, xh2, r2, proj, vec, out_own) = saved
    qk = qk.reshape(2, width, width)
    va = va.reshape(2, width, width)
    inner = inner.reshape(2, width, half_ff)
    outer = outer.reshape(2, width, half_ff)
    x_own = x_all[:n_own]
    proj = proj.astype(BF)
    a0 = mp * (n_full + seq_len)
    h0 = n_full + mp * n_half
    cot = jnp.concatenate(
        [lax.dynamic_slice_in_dim(cotangent, a0, n_full, 0), lax.dynamic_slice_in_dim(cotangent, h0, n_half, 0)]
    )
    my_seqs = jnp.concatenate([mp * (full + 1) + jnp.arange(full), jnp.array([full])])

    n_mine = full + 1
    mine = jnp.where((jnp.arange(n_mine) < full) | (mp == 0), 1.0, 0.0).astype(F32)
    cls_low = out_own[:: seq_len][:n_mine]
    docs = doc_rows[my_seqs].astype(F32)
    ids = doc_ids[my_seqs]
    query = jnp.dot(cls_low, proj, preferred_element_type=F32).astype(BF)
    query_float = query.astype(F32)
    doc_scores = jnp.einsum("gp,gkp->gk", query_float, docs, precision=highest_mode) * retrieval_scale
    soft = jax.nn.softmax(doc_scores, axis=-1)
    target = (jnp.arange(doc_scores.shape[1]) == 0).astype(F32)
    score_grad = (soft - target[None, :]) * retrieval_scale * mine[:, None]
    query_grad = jnp.einsum("gk,gkp->gp", score_grad, docs, precision=highest_mode).astype(BF)
    row_grads = score_grad[:, :, None] * query_float[:, None, :]
    cls_grad = jnp.einsum("gp,dp->gd", query_grad, proj, preferred_element_type=F32)
    proj_grad = jnp.einsum("gd,gp->dp", cls_low, query_grad, preferred_element_type=F32)
    table_rows = TAB_DEV * n_dp
    one_hot = (jnp.arange(table_rows)[:, None] == ids.reshape(1, -1)).astype(F32)
    table_local = jnp.dot(one_hot, row_grads.reshape(-1, row_grads.shape[2]), precision=highest_mode)

    def norm_back(dy, hat, root, gain):
        e = dy * gain
        back_ = e - jnp.mean(e, axis=-1, keepdims=True) - hat * jnp.mean(e * hat, axis=-1, keepdims=True)
        return back_ * root[:, :1], jnp.sum(dy * hat, axis=0), jnp.sum(dy, axis=0)

    dy = cot.astype(F32)
    first_rows = jnp.arange(n_mine) * seq_len
    dy = dy.at[first_rows].add(cls_grad)
    dz2, dg2, dc2 = norm_back(dy, xh2, r2, vec[6 + ff_rows])
    df = dz2.astype(BF)
    dg = jnp.einsum("td,hdf->htf", df, outer, preferred_element_type=F32)
    g_outer = jnp.einsum("td,htf->hdf", df, act_low, preferred_element_type=F32).astype(BF)
    du = (dg * slope.astype(F32)).astype(BF)
    normed_low = (xh1 * vec[3] + vec[4]).astype(BF)
    g_inner = jnp.einsum("td,htf->hdf", normed_low, du, preferred_element_type=F32).astype(BF)
    dh1 = jnp.einsum("htf,hdf->td", du, inner, preferred_element_type=F32) + dz2
    dz1, dg1, dc1 = norm_back(dh1, xh1, r1, vec[3])
    da = dz1.astype(BF)
    do = jnp.dot(da, va[1], preferred_element_type=F32).astype(BF)
    g_attn = jnp.einsum("td,te->de", da, mixed, preferred_element_type=F32)
    dqs, dks, dvs = [], [], []
    probs_of = (p_ab.reshape(full, -1, seq_len, seq_len), p_c.reshape(1, -1, n_half, seq_len))
    for qh, kh, vh, doh, pb in zip(*(halves(t, n_full, seq_len) for t in (q, k, v, do)), probs_of):
        probs = pb.astype(F32)
        dp_ = jnp.einsum("gqhe,gkhe->ghqk", doh, vh, preferred_element_type=F32)
        delta = jnp.sum(probs * dp_, axis=-1, keepdims=True)
        ds_ = (probs * (dp_ - delta)).astype(BF)
        dqs.append((jnp.einsum("ghqk,gkhe->gqhe", ds_, kh, preferred_element_type=F32) * score_scale).reshape(-1, width))
        dks.append((jnp.einsum("ghqk,gqhe->gkhe", ds_, qh, preferred_element_type=F32) * score_scale).reshape(-1, width))
        dvs.append(jnp.einsum("ghqk,gqhe->gkhe", pb, doh, preferred_element_type=F32).reshape(-1, width))
    dq = jnp.concatenate(dqs).astype(BF)
    dk = jnp.concatenate(dks).astype(BF)
    dv = jnp.concatenate(dvs).astype(BF)
    g_q = jnp.einsum("td,te->de", x_own, dq, preferred_element_type=F32)
    g_k = jnp.einsum("td,te->de", x_all, dk, preferred_element_type=F32)
    g_v = jnp.einsum("td,te->de", x_all, dv, preferred_element_type=F32)
    g_qk = jnp.stack([g_q, g_k]).astype(BF)
    g_va = jnp.stack([g_v, g_attn]).astype(BF)
    dx_own = jnp.einsum("te,de->td", dq, qk[0], preferred_element_type=F32) + dz1
    dx_all = jnp.einsum("te,de->td", dk, qk[1], preferred_element_type=F32)
    dx_all = dx_all + jnp.einsum("te,de->td", dv, va[0], preferred_element_type=F32)
    dx = jnp.concatenate([dx_all[:n_own] + dx_own, dx_all[n_own:]]).astype(BF)
    db_inner = jnp.sum(du.astype(F32), axis=1)
    db_inner = db_inner.reshape(2, 2, half_ff // 2).transpose(1, 0, 2).reshape(ff_rows, width)
    vec_grad = jnp.concatenate(
        [
            jnp.stack(
                [
                    jnp.sum(dq.astype(F32), axis=0),
                    jnp.sum(dv.astype(F32), axis=0),
                    jnp.sum(dz1, axis=0),
                    dg1,
                    dc1,
                ]
            ),
            db_inner,
            jnp.stack([jnp.sum(dz2, axis=0), dg2, dc2]),
        ]
    )
    vg = vec_grad.reshape(nvec, n_dp, 2, vec_lanes).transpose(1, 0, 2, 3)
    vg = jnp.pad(vg, ((0, 0), (0, 0), (0, 0), (0, 128 - vec_lanes))).reshape(n_dp, nvec, 256)
    pg = proj_grad.reshape(n_dp, 2, half_rows, 128).transpose(0, 2, 1, 3).reshape(n_dp, half_rows, 256)
    tg = table_local.reshape(n_dp, 2, TAB_DEV // 2, 128).transpose(0, 2, 1, 3).reshape(n_dp, TAB_DEV // 2, 256)
    small = jnp.concatenate([pg, vg, tg], axis=1)

    return out_own, dx, *reduce_plain([g_qk, g_va, g_inner, g_outer], small, out_own, dx, rows)


def local(
    tokens, cotangent, lengths, doc_ids, doc_rows,
    w_qkv, m_qkv, v_qkv, w_attn, m_attn, v_attn, w_inner, m_inner, v_inner,
    w_outer, m_outer, v_outer, w_proj, m_proj, v_proj, vectors, m_vectors, v_vectors,
):
    mp = lax.axis_index("mp")
    n_dp, n_mp = lax.axis_size("dp"), lax.axis_size("mp")
    fast = n_dp == NZ * NY * NC and n_mp == NX
    seqs = lengths.shape[0]
    all_rows, width = tokens.shape
    seq_len = all_rows // seqs
    full = seqs // 2
    n_full, n_half = full * seq_len, seq_len // 2
    n_own = n_full + n_half
    rows, half_ff = w_qkv.shape[1], w_inner.shape[1]
    half_rows = rows // 2
    nvec, vec_lanes = vectors.shape
    ff_rows = nvec - 8
    score_scale = HEAD_DIM ** (-0.5)

    if fast:
        saved = forward_fast(lengths, tokens, w_qkv, w_attn, w_inner, w_outer, w_proj, vectors)
        out_own = saved[-1]
        (small_r, qk_r, va_r, inner_r, outer_r, dx, peer_out, peer_dx, peer_small, total) = backward_fast(
            doc_ids, cotangent, doc_rows, saved, rows
        )
        vector_r = small_r[half_rows : half_rows + vec_lanes, :nvec].T
        table_at = half_rows + vec_lanes
    else:
        (out_own, dx, small_r, qk_r, va_r, inner_r, outer_r, peer_out, peer_dx, peer_small, total) = pass_plain(
            lengths, tokens, cotangent, doc_ids, doc_rows, w_qkv, w_attn, w_inner, w_outer, w_proj, vectors
        )
        vector_r = small_r[half_rows : half_rows + nvec, :vec_lanes]
        table_at = half_rows + nvec

    def whole_rows(own, peer):
        lo = jnp.where(mp == 0, own[:n_own], peer[:n_own])
        hi = jnp.where(mp == 0, peer[:n_own], own[:n_own])
        return lo, hi

    lo, hi = whole_rows(out_own, peer_out)
    out_tokens = jnp.concatenate([lo, hi[n_full:], hi[:n_full]])
    lo, hi = whole_rows(dx.astype(F32), peer_dx.astype(F32))
    tail = jnp.where(mp == 0, dx[n_own:], peer_dx[n_own:]).astype(F32)
    tail_hi = jnp.where(mp == 0, peer_dx[n_own:], dx[n_own:]).astype(F32)
    input_grad = jnp.concatenate(
        [lo[:n_full], lo[n_full:] + tail_hi, hi[n_full:] + tail, hi[:n_full]]
    )

    def both_halves(at, count):
        mine_, peer_ = small_r[at : at + count], peer_small[at : at + count]
        return jnp.concatenate(
            [jnp.where(mp == 0, mine_, peer_), jnp.where(mp == 0, peer_, mine_)]
        )

    proj_r = both_halves(0, half_rows)
    table_grad = both_halves(table_at, TAB_DEV // 2)
    qkv_r = jnp.stack([qk_r[0], qk_r[1], va_r[0]])
    attn_r = va_r[1]

    def back(v):
        return v.transpose(1, 0, 2).reshape(rows, half_ff)

    inner_r, outer_r = back(inner_r), back(outer_r)
    grad_norm = jnp.sqrt(total[0, 0])
    clip = clip_norm / jnp.maximum(grad_norm, clip_norm)
    results = [out_tokens, input_grad, grad_norm]
    for w, m, s, g, dec, rate in (
        (w_qkv, m_qkv, v_qkv, qkv_r, decay_rate, learn_rate),
        (w_attn, m_attn, v_attn, attn_r, decay_rate, learn_rate),
        (w_inner, m_inner, v_inner, inner_r, decay_rate, learn_rate),
        (w_outer, m_outer, v_outer, outer_r, decay_rate, learn_rate),
        (w_proj, m_proj, v_proj, proj_r, decay_rate, learn_rate),
        (vectors, m_vectors, v_vectors, vector_r, 0.0, vector_rate),
    ):
        results += list(adamw_update(w, m, s, g * clip, dec, rate))
    return tuple(results) + (table_grad,)


def solution(mesh):
    mat = P("dp", "mp")
    rep = P("dp", None)
    qkv = P(None, "dp", "mp")
    vec = P(None, ("dp", "mp"))
    placed = (rep, rep, P("dp"), rep, P("dp", None, None), qkv, qkv, qkv)
    placed += (mat,) * 9 + (rep,) * 3 + (vec,) * 3
    given = (rep, rep, P(), qkv, qkv, qkv) + (mat,) * 9 + (rep,) * 3 + (vec,) * 3 + (rep,)
    return jax.shard_map(local, mesh=mesh, in_specs=placed, out_specs=given, check_vma=False)
```

```python
import functools

import jax
import jax.numpy as jnp
from jax import lax
from jax.experimental import pallas as pl
from jax.experimental.pallas import tpu as pltpu
from jax.sharding import PartitionSpec as P

HEAD_DIM = 64
STEP = 10
TAB_DEV = 8
MESH = pl.DeviceIdType.MESH
ANY = pl.ANY
BF = jnp.bfloat16
F32 = jnp.float32
NZ, NY, NC, NX = 4, 2, 2, 2

highest_mode = lax.Precision.HIGHEST
retrieval_scale = 0.17677669529663687
ln_epsilon = 1e-12
beta_first = 0.9
beta_second = 0.999
learn_rate = 0.05
vector_rate = 0.5
decay_rate = 0.01
adam_epsilon = 1e-08
clip_norm = 1.0


def layer_norm(values, gain_row, shift_row):
    centre = jnp.mean(values, axis=-1, keepdims=True)
    centred = values - centre
    spread = jnp.mean(centred * centred, axis=-1, keepdims=True)
    return centred * lax.rsqrt(spread + ln_epsilon) * gain_row + shift_row


def gelu_exact(values):
    return jax.nn.gelu(values, approximate=False)


def adamw_update(weight, moment, second, gradient, decay_factor, step_rate):
    moment_new = beta_first * moment + (1.0 - beta_first) * gradient
    second_new = beta_second * second + (1.0 - beta_second) * gradient * gradient
    first_hat = moment_new / (1.0 - beta_first**STEP)
    second_hat = second_new / (1.0 - beta_second**STEP)
    weight_new = weight - step_rate * (
        first_hat / (jnp.sqrt(second_hat) + adam_epsilon) + decay_factor * weight
    )
    return (moment_new, second_new, weight_new)


def squared(values):
    return jnp.sum(values * values)


class Place:
    def __init__(self):
        dp = lax.axis_index("dp")
        self.x = lax.axis_index("mp")
        self.c = lax.rem(dp, NC)
        self.y = lax.rem(dp // NC, NY)
        self.z = dp // (NC * NY)

    def dev(self, z=None, y=None, c=None, x=None):
        z = self.z if z is None else z
        y = self.y if y is None else y
        c = self.c if c is None else c
        x = self.x if x is None else x
        return ((z * NY + y) * NC + c, x)

    def others(self):
        out = [self.dev(z=lax.rem(self.z + k, NZ)) for k in range(1, NZ)]
        out.append(self.dev(x=1 - self.x))
        out.append(self.dev(y=1 - self.y))
        out.append(self.dev(c=1 - self.c))
        return out

    def eights(self):
        out = []
        for k in range(1, 8):
            dx, dy, dc = k & 1, (k >> 1) & 1, k >> 2
            out.append(
                self.dev(
                    x=self.x + dx - 2 * dx * self.x,
                    y=self.y + dy - 2 * dy * self.y,
                    c=self.c + dc - 2 * dc * self.c,
                )
            )
        return out


def greet(devices):
    barrier = pltpu.get_barrier_semaphore()
    for d in devices:
        pl.semaphore_signal(barrier, inc=1, device_id=d, device_id_type=MESH)
    pl.semaphore_wait(barrier, len(devices))


def remote(src, dst, ssem, rsem, dev):
    return pltpu.make_async_remote_copy(
        src_ref=src, dst_ref=dst, send_sem=ssem, recv_sem=rsem, device_id=dev, device_id_type=MESH
    )


def cols(x, half):
    return pl.ds(pl.multiple_of(x * half, 128), half)


def dma(*shape):
    return pltpu.SemaphoreType.DMA(shape)


def mm(a, b):
    return jnp.dot(a, b, preferred_element_type=F32)


def mm_nt(a, b):
    return lax.dot_general(a, b, (((1,), (1,)), ((), ())), preferred_element_type=F32)


def mm_tn(a, b):
    return lax.dot_general(a, b, (((0,), (0,)), ((), ())), preferred_element_type=F32)


def flat(value):
    return value.reshape(-1, value.shape[-1])


def lanes(i, n=128):
    return pl.ds(pl.multiple_of(i * n, 128), n)


def rows_at(i, n, at=0):
    return pl.ds(pl.multiple_of(at + i * n, 16), n)


def each(n, body):
    lax.fori_loop(0, n, lambda i, c: (body(i), c)[1], 0)


gather_routes = "xxyxyxyxy"


class Gather:
    def __init__(self, me, pieces, sems):
        self.me, self.pieces = me, pieces
        self.lsem, self.zs, self.zr, self.s1, self.r1, self.s2, self.r2, self.ds, self.dr = sems
        self.waits, self.locs = [], {}

    def go(self, copy):
        copy.start()
        self.waits.append(copy)

    def step1(self, p):
        me = self.me
        src, dst = self.pieces[p]
        blk = dst.at[me.z, me.y, me.c, :, cols(me.x, dst.shape[-1] // 2)]
        loc = pltpu.make_async_copy(src, blk, self.lsem.at[p])
        loc.start()
        self.locs[p] = loc
        for k in range(1, NZ):
            dev = me.dev(z=lax.rem(me.z + k, NZ))
            self.go(remote(src, blk, self.zs.at[p, k], self.zr.at[p, k], dev))

    def part(self, p, stage, c):
        me, dst = self.me, self.pieces[p][1]
        half = dst.shape[-1] // 2
        own, other = cols(me.x, half), cols(1 - me.x, half)
        if stage == "z":
            return dst.at[:, me.y, c, :, own]
        if gather_routes[p] == "x":
            if stage == "in1":
                return dst.at[:, me.y, c, :, other]
            if stage == "out2":
                return dst.at[:, me.y, c]
            return dst.at[:, 1 - me.y, c]
        if stage == "in1":
            return dst.at[:, 1 - me.y, c, :, own]
        if stage == "out2":
            return dst.at[:, :, c, :, own]
        return dst.at[:, :, c, :, other]

    def first(self, p):
        return self.me.dev(x=1 - self.me.x) if gather_routes[p] == "x" else self.me.dev(y=1 - self.me.y)

    def second(self, p):
        return self.me.dev(y=1 - self.me.y) if gather_routes[p] == "x" else self.me.dev(x=1 - self.me.x)

    def cross(self, p, ref, which):
        self.go(remote(ref, ref, self.ds.at[p, which], self.dr.at[p, which], self.me.dev(c=1 - self.me.c)))

    def arrived(self, ref, ssem, rsem):
        remote(ref, ref, ssem, rsem, self.me.dev(c=1 - self.me.c)).wait_recv()

    def step2(self, p):
        me, dst = self.me, self.pieces[p][1]
        self.locs[p].wait()
        for k in range(1, NZ):
            blk = dst.at[lax.rem(me.z + NZ - k, NZ), me.y, me.c, :, cols(me.x, dst.shape[-1] // 2)]
            self.arrived(blk, self.zs.at[p, k], self.zr.at[p, k])
        have = self.part(p, "z", me.c)
        self.go(remote(have, have, self.s1.at[p], self.r1.at[p], self.first(p)))
        self.cross(p, have, 0)

    def step3(self, p):
        got = self.part(p, "in1", self.me.c)
        self.arrived(got, self.s1.at[p], self.r1.at[p])
        have = self.part(p, "out2", self.me.c)
        self.go(remote(have, have, self.s2.at[p], self.r2.at[p], self.second(p)))
        self.cross(p, got, 1)

    def step4(self, p):
        got = self.part(p, "in2", self.me.c)
        self.arrived(got, self.s2.at[p], self.r2.at[p])
        self.cross(p, got, 2)

    def step5(self, p):
        for which, stage in enumerate(("z", "in1", "in2")):
            self.arrived(self.part(p, stage, 1 - self.me.c), self.ds.at[p, which], self.dr.at[p, which])

    def end(self):
        for copy in self.waits:
            copy.wait_send()


def norm_rows(z_ref, r_ref, n_rows, put):
    step = 48

    def body(i):
        at = rows_at(i, step)
        z = z_ref[at, :]
        centred = z - jnp.mean(z, axis=-1, keepdims=True)
        spread = jnp.mean(centred * centred, axis=-1, keepdims=True)
        root = lax.rsqrt(spread + ln_epsilon)
        hat = centred * root
        z_ref[at, :] = hat
        r_ref[at, :] = jnp.broadcast_to(root, (step, 128))
        put(at, hat)

    each(n_rows // step, body)


def forward_kernel(*refs):
    (lens, tokens, w_qkv, w_attn, w_inner, w_outer, w_proj, vectors) = refs[:8]
    outs = refs[8:27]
    scr = refs[27:]
    (small_s, qk_s, va_s, inner_s, outer_s, small_g, qk, va, inner, outer) = scr[:10]
    (xt, q, k, v, p, o, xh1, r1, g, gp, xh2, r2, out_own, proj, vec, x_all, h1b, vecp, bias_ff) = scr[10:29]
    gsems, tsem, osem = scr[29:38], scr[38], scr[39]
    me = Place()
    mp = me.x
    n_all, width = x_all.shape
    n_own = q.shape[0]
    half_seq = n_all - n_own
    seq = 2 * half_seq
    full = (n_own - half_seq) // seq
    n_full = full * seq
    half_ff = inner.shape[-1]
    rows = qk_s.shape[1]
    half_rows = rows // 2

    starts = (
        (mp * (n_full + seq), 0, n_full),
        (n_full + mp * half_seq, n_full, half_seq),
        (n_full + (1 - mp) * half_seq, n_own, half_seq),
    )
    loads = []
    for i, (at, to, n) in enumerate(starts):
        cp = pltpu.make_async_copy(
            tokens.at[pl.ds(pl.multiple_of(at, 16), n)], x_all.at[pl.ds(to, n)], tsem.at[i]
        )
        cp.start()
        loads.append(cp)

    vecp[...] = jnp.zeros_like(vecp)
    nvec, nlane = vectors.shape
    vecp[0:nvec, 0:nlane] = vectors[...]
    small_s[0:half_rows] = w_proj[pl.ds(pl.multiple_of(mp * half_rows, 8), half_rows), :]
    small_s[half_rows : half_rows + nlane] = jnp.transpose(vecp[...])[0:nlane]
    qk_s[...] = w_qkv[0:2].astype(BF)
    va_s[0] = w_qkv[2].astype(BF)
    va_s[1] = w_attn[...].astype(BF)
    hf = half_ff // 2
    for h in range(2):
        inner_s[h] = w_inner[:, h * hf : (h + 1) * hf].astype(BF)
        outer_s[h] = w_outer[:, h * hf : (h + 1) * hf].astype(BF)

    greet(me.others())
    pieces = [
        (small_s, small_g),
        (qk_s.at[0], qk.at[0]),
        (qk_s.at[1], qk.at[1]),
        (va_s.at[0], va.at[0]),
        (va_s.at[1], va.at[1]),
        (inner_s.at[0], inner.at[0]),
        (inner_s.at[1], inner.at[1]),
        (outer_s.at[0], outer.at[0]),
        (outer_s.at[1], outer.at[1]),
    ]
    net = Gather(me, pieces, gsems)
    groups = ((0, 1, 2), (3, 4), (5, 6), (7, 8))

    def go(step, i):
        for piece in groups[i]:
            (net.step1, net.step2, net.step3, net.step4, net.step5)[step - 1](piece)

    go(1, 0)
    go(1, 1)
    saves = []

    def save(i, ref):
        cp = pltpu.make_async_copy(ref, outs[i], osem.at[i])
        cp.start()
        saves.append(cp)

    for cp in loads:
        cp.wait()

    def x_turn(i):
        xt[rows_at(i, 256), :] = jnp.transpose(x_all[:, lanes(i, 256)])

    each(width // 256, x_turn)
    save(4, xt)
    go(2, 0)
    go(1, 2)
    go(3, 0)
    go(2, 1)
    go(1, 3)
    go(4, 0)
    go(3, 1)
    go(2, 2)
    go(5, 0)
    big = []
    for z in range(NZ):
        for y in range(NY):
            for c in range(NC):
                for x in range(NX):
                    blk = small_g[z, y, c, :, x * 128 : (x + 1) * 128]
                    d = ((z * NY + y) * NC + c) * NX + x
                    proj[d * half_rows : (d + 1) * half_rows] = blk[:half_rows]
                    big.append(blk[half_rows : half_rows + nlane])
    vec[...] = jnp.transpose(jnp.concatenate(big, axis=0))[0 : vec.shape[0]]
    for h in range(2):
        for x in range(NX):
            bias_ff[h : h + 1, x * width : (x + 1) * width] = vec[5 + NX * x + h : 6 + NX * x + h, :]
    save(16, proj)
    save(17, vec)

    def project(w_ref, src_rows, dst, bias):
        n_tile = 256

        def body(i):
            w = flat(w_ref[:, :, :, :, lanes(i, n_tile)])
            r = mm(x_all[0:src_rows], w)
            if bias is not None:
                r = r + vec[bias : bias + 1, lanes(i, n_tile)]
            dst[:, lanes(i, n_tile)] = r.astype(BF)

        each(width // n_tile, body)

    project(qk.at[0], n_own, q, 0)
    project(qk.at[1], n_all, k, None)
    save(0, qk)
    go(4, 1)
    go(2, 3)
    go(5, 1)
    project(va.at[0], n_all, v, 1)
    save(5, q)
    save(6, k)
    save(7, v)

    lane = lax.broadcasted_iota(jnp.int32, (1, 128), 1)
    head_lo = jnp.where(lane < HEAD_DIM, 1.0, 0.0)
    head_mask = (head_lo.astype(BF), (1.0 - head_lo).astype(BF))
    pos = lax.broadcasted_iota(jnp.int32, (1, seq), 1)

    def attend(q0, nq, k0, slab, length, place):
        at_q = pl.ds(pl.multiple_of(q0, 16), nq)
        at_k = pl.ds(pl.multiple_of(k0, 16), seq)
        for pair in range(2):
            l = lanes(2 * slab + pair)
            qp, kp, vp = q[at_q, l], k[at_k, l], v[at_k, l]
            got = []
            for h in range(2):
                s = mm_nt(qp * head_mask[h], kp) * (HEAD_DIM**-0.5)
                s = jnp.where(place < length, s, -1000000000.0)
                e = jnp.exp(s - jnp.max(s, axis=-1, keepdims=True))
                pb = (e * (1.0 / jnp.sum(e, axis=-1, keepdims=True))).astype(BF)
                j = 384 * (2 * pair + h)
                p[slab, at_q, j : j + seq] = pb
                got.append(mm(pb, vp))
            o[at_q, l] = jnp.where(lane < HEAD_DIM, got[0], got[1]).astype(BF)

    slabs = p.shape[0]
    for s in range(full):
        length = lens[mp * (full + 1) + s]
        each(slabs, lambda i: attend(s * seq, seq, s * seq, i, length, pos))
        go(3, 2 + s)
    length = lens[full]
    pos_c = jnp.where(pos < half_seq, pos + mp * half_seq, pos - half_seq + (1 - mp) * half_seq)
    each(slabs, lambda i: attend(n_full, half_seq, n_full, i, length, pos_c))
    save(8, p)
    save(9, o)

    tile = 240
    tiles = n_own // tile

    def attn_out(i):
        a = mm_nt(o[rows_at(i, tile), :], flat(va[1]))
        xh1[rows_at(i, tile), :] = x_all[rows_at(i, tile), :].astype(F32) + a + vec[2:3, :]

    each(tiles, attn_out)
    save(1, va)

    def put_h1(at, hat):
        h1b[at, :] = (hat * vec[3:4, :] + vec[4:5, :]).astype(BF)

    norm_rows(xh1, r1, n_own, put_h1)
    save(10, xh1)
    save(11, r1)
    go(4, 2)
    go(5, 2)

    def feed(h):
        n_tile = 256

        def body(i):
            w = flat(inner[h, :, :, :, :, lanes(i, n_tile)])
            for t in range(tiles):
                at = pl.ds(t * tile, tile)
                u = mm(h1b[at, :], w)
                u = u + bias_ff[h : h + 1, lanes(i, n_tile)]
                tail = 0.5 * (1.0 + lax.erf(u * 0.7071067811865476))
                g[h, at, lanes(i, n_tile)] = (u * tail).astype(BF)
                slope = tail + u * (0.3989422804014327 * jnp.exp(-0.5 * u * u))
                gp[h, at, lanes(i, n_tile)] = slope.astype(BF)

        each(half_ff // n_tile, body)

    feed(0)
    feed(1)
    go(4, 3)
    go(5, 3)
    save(2, inner)
    save(12, g)
    save(13, gp)

    def ff_out(i):
        at = rows_at(i, tile)
        f = mm_nt(g[0, at, :], flat(outer[0])) + mm_nt(g[1, at, :], flat(outer[1]))
        h1 = xh1[at, :] * vec[3:4, :] + vec[4:5, :]
        xh2[at, :] = h1 + f + vec[9:10, :]

    each(tiles, ff_out)
    save(3, outer)

    def put_y(at, hat):
        out_own[at, :] = (hat * vec[10:11, :] + vec[11:12, :]).astype(BF)

    norm_rows(xh2, r2, n_own, put_y)
    save(14, xh2)
    save(15, r2)
    save(18, out_own)
    net.end()
    for cp in saves:
        cp.wait()


def forward_fast(lengths, tokens, w_qkv, w_attn, w_inner, w_outer, w_proj, vectors):
    seqs = lengths.shape[0]
    all_rows, width = tokens.shape
    seq = all_rows // seqs
    full = seqs // 2
    n_own = full * seq + seq // 2
    n_all = n_own + seq // 2
    rows, half_ff = w_qkv.shape[1], w_inner.shape[1]
    heads = width // HEAD_DIM
    zyc = (NZ, NY, NC)
    small_rows = rows // 2 + vectors.shape[1]
    weights = [
        ((2,) + zyc + (rows, width), BF),
        ((2,) + zyc + (rows, width), BF),
        ((2,) + zyc + (rows, half_ff), BF),
        ((2,) + zyc + (rows, half_ff), BF),
    ]
    kept = [
        ((width, n_all), BF),
        ((n_own, width), BF),
        ((n_all, width), BF),
        ((n_all, width), BF),
        ((heads // 4, n_own, 4 * 384), BF),
        ((n_own, width), BF),
        ((n_own, width), F32),
        ((n_own, 128), F32),
        ((2, n_own, half_ff), BF),
        ((2, n_own, half_ff), BF),
        ((n_own, width), F32),
        ((n_own, 128), F32),
        ((width, 128), F32),
        ((16, width), F32),
        ((n_own, width), BF),
    ]
    order = kept[:12] + [kept[14], kept[12], kept[13]]
    scratch = [
        ((small_rows, 128), F32),
        ((2, rows, width // 2), BF),
        ((2, rows, width // 2), BF),
        ((2, rows, half_ff // 2), BF),
        ((2, rows, half_ff // 2), BF),
        (zyc + (small_rows, 256), F32),
    ]
    scratch += weights + order
    scratch += [((n_all, width), BF), ((n_own, width), BF), ((128, 128), F32), ((8, half_ff), F32)]
    n = 9
    vm = pl.BlockSpec(memory_space=pltpu.VMEM)
    hb = pl.BlockSpec(memory_space=ANY)
    sm = pl.BlockSpec(memory_space=pltpu.SMEM)
    return pl.pallas_call(
        forward_kernel,
        out_shape=[jax.ShapeDtypeStruct(s, d) for s, d in weights + kept],
        in_specs=[sm, hb] + [vm] * 6,
        out_specs=[hb] * 19,
        scratch_shapes=[pltpu.VMEM(s, d) for s, d in scratch]
        + [
            dma(n), dma(n, NZ), dma(n, NZ), dma(n), dma(n), dma(n), dma(n), dma(n, 3), dma(n, 3),
            dma(3), dma(20),
        ],
        compiler_params=pltpu.CompilerParams(
            collective_id=1, has_side_effects=True, vmem_limit_bytes=60 * 2**20
        ),
        name="forward",
    )(lengths, tokens, w_qkv, w_attn, w_inner, w_outer, w_proj, vectors)


class Reduce:
    def __init__(self, me, pieces, sems):
        self.me, self.pieces = me, pieces
        self.ds, self.dr, self.s1, self.r1, self.s2, self.r2, self.zs, self.zr = sems
        self.waits = []
        self.squares = jnp.zeros((1, 1), F32)

    def go(self, copy):
        copy.start()
        self.waits.append(copy)

    def arrived(self, ref, ssem, rsem):
        remote(ref, ref, ssem, rsem, self.me.dev(c=1 - self.me.c)).wait_recv()

    def step1(self, p):
        src, got1 = self.pieces[p][2], self.pieces[p][3]
        oc = 1 - self.me.c
        self.go(remote(src.at[:, :, oc], got1, self.ds.at[p], self.dr.at[p], self.me.dev(c=oc)))

    def step2(self, p):
        route, _, src, got1, got2, _, _ = self.pieces[p]
        me = self.me
        c, half = me.c, src.shape[-1] // 2
        self.arrived(got1, self.ds.at[p], self.dr.at[p])

        def add(z):
            for y in range(NY):
                src[z, y, c] = src[z, y, c] + got1[z, y]

        each(NZ, add)
        if route == "y":
            part, dev = src.at[:, 1 - me.y, c], me.dev(y=1 - me.y)
        else:
            part, dev = src.at[:, :, c, :, cols(1 - me.x, half)], me.dev(x=1 - me.x)
        self.go(remote(part, got2, self.s1.at[p], self.r1.at[p], dev))

    def step3(self, p):
        route, _, src, _, got2, got3, _ = self.pieces[p]
        me = self.me
        c, half = me.c, src.shape[-1] // 2
        mine = cols(me.x, half)
        self.arrived(got2, self.s1.at[p], self.r1.at[p])
        if route == "y":

            def add(z):
                src[z, me.y, c] = src[z, me.y, c] + got2[z]

            each(NZ, add)
            part, dev = src.at[:, me.y, c, :, cols(1 - me.x, half)], me.dev(x=1 - me.x)
        else:

            def add(z):
                for y in range(NY):
                    src[z, y, c, :, mine] = src[z, y, c, :, mine] + got2[z, y]

            each(NZ, add)
            part, dev = src.at[:, 1 - me.y, c, :, mine], me.dev(y=1 - me.y)
        self.go(remote(part, got3, self.s2.at[p], self.r2.at[p], dev))

    def step4(self, p):
        _, _, src, _, _, got3, got4 = self.pieces[p]
        me = self.me
        c, mine = me.c, cols(me.x, src.shape[-1] // 2)
        self.arrived(got3, self.s2.at[p], self.r2.at[p])

        def add(z):
            src[z, me.y, c, :, mine] = src[z, me.y, c, :, mine] + got3[z]

        each(NZ, add)
        for k in range(1, NZ):
            tz = lax.rem(me.z + k, NZ)
            part = src.at[tz, me.y, c, :, mine]
            self.go(remote(part, got4.at[k], self.zs.at[p, k], self.zr.at[p, k], me.dev(z=tz)))

    def step5(self, p, counted=True):
        _, dst, src, _, _, _, got4 = self.pieces[p]
        me = self.me
        for k in range(1, NZ):
            self.arrived(got4.at[k], self.zs.at[p, k], self.zr.at[p, k])
        total = src[me.z, me.y, me.c, :, cols(me.x, src.shape[-1] // 2)].astype(F32)
        for k in range(1, NZ):
            total = total + got4[k].astype(F32)
        dst[...] = total
        if counted:
            self.squares = self.squares + jnp.sum(total * total, keepdims=True)

    def end(self):
        for copy in self.waits:
            copy.wait_send()


routes = "yyyyyyyyy"


def all_squares(me, net, total, sq4, sq8, sems):
    qs, qr, es, er = sems
    sq4[0] = jnp.broadcast_to(total, (8, 128))
    copies = []
    for k in range(1, NZ):
        copies.append(remote(sq4.at[0], sq4.at[k], qs.at[k], qr.at[k], me.dev(z=lax.rem(me.z + k, NZ))))
    for copy in copies:
        net.go(copy)
    for copy in copies:
        copy.wait_recv()

    def at_z(z):
        out = jnp.zeros((8, 128), F32)
        for k in range(NZ):
            out = out + jnp.where(lax.rem(me.z + NZ - k, NZ) == z, sq4[k], 0.0)
        return out

    sq8[0] = at_z(0) + at_z(1) + at_z(2) + at_z(3)
    copies = []
    for k, dev in enumerate(me.eights(), 1):
        copies.append(remote(sq8.at[0], sq8.at[k], es.at[k], er.at[k], dev))
    for copy in copies:
        net.go(copy)
    for copy in copies:
        copy.wait_recv()

    def at_code(w):
        out = jnp.zeros((8, 128), F32)
        for k in range(8):
            dx, dy, dc = k & 1, (k >> 1) & 1, k >> 2
            src = (
                (me.x + dx - 2 * dx * me.x)
                + 2 * (me.y + dy - 2 * dy * me.y)
                + 4 * (me.c + dc - 2 * dc * me.c)
            )
            out = out + jnp.where(src == w, sq8[k], 0.0)
        return out

    whole = at_code(0)
    for w in range(1, 8):
        whole = whole + at_code(w)
    return whole


def fold(value):
    return jnp.sum(value.reshape(-1, 8, value.shape[-1]), axis=0)


def norm_back_rows(n_rows, get_dy, hat_ref, root_ref, gain, put, acc):
    step = 48

    def body(i):
        at = rows_at(i, step)
        dy, hat = get_dy(i, at), hat_ref[at, :]
        e = dy * gain
        root = root_ref[at, 0:1]
        m1 = jnp.mean(e, axis=-1, keepdims=True)
        m2 = jnp.mean(e * hat, axis=-1, keepdims=True)
        dz = (e - m1 - hat * m2) * root
        acc[0] = acc[0] + fold(dy * hat)
        acc[1] = acc[1] + fold(dy)
        acc[2] = acc[2] + fold(dz)
        hat_ref[at, :] = dz
        put(at, dz)

    each(n_rows // step, body)


def backward_kernel(*refs):
    doc_ids, cotangent, doc_rows = refs[:3]
    (qk_h, va_h, inner_h, outer_h, xt_h, q_h, k_h, v_h, p_h, o_h, xh1_h, r1_h, g_h, gp_h, xh2_h, r2_h, proj_h, vec_h, out_h) = refs[3:22]
    outs = refs[22:32]
    small_r, qk_r, va_r, inner_r, outer_r, dx, peer_out, peer_dx, peer_small, norm_ref = outs
    scr = list(refs[32:])

    def take(n):
        got = scr[:n]
        del scr[:n]
        return got

    (inner, outer, attn, xt, q, k, v, o, xh1, gg, xh2, r2, proj, vec, cls_in, cot, df, dft) = take(18)
    (cls_grad, acc1, acc2, ffacc, vg, small) = take(6)
    grads = take(4)
    bufs = take(9 * 4)
    sq4, sq8 = take(2)
    lsem, rsems, xs, xr, qsems = take(1)[0], take(8), *take(2), take(4)
    do, da, dat, h1t, r1 = cot, df, dft, dft, r2
    me = Place()
    mp = me.x
    n_all, width = dx.shape
    n_own = q.shape[0]
    half_seq = n_all - n_own
    seq = 2 * half_seq
    n_full = n_own - half_seq
    full = n_full // seq
    half_ff = inner.shape[-1]
    other = me.dev(x=1 - mp)

    for i in range(4):
        grads.append(inner.at[i // 2, :, :, :, :, pl.ds(width * (i % 2), width)])
    copies = {}

    def load(name, i, src, dst):
        cp = pltpu.make_async_copy(src, dst, lsem.at[i])
        cp.start()
        copies[name] = cp

    def need(*names):
        for name in names:
            copies[name].wait()

    load("vec", 0, vec_h, vec)
    load("proj", 1, proj_h, proj)
    for s in range(full + 1):
        load("cls%d" % s, 2 + s, out_h.at[pl.ds(s * seq, 16)], cls_in.at[s])
    load("cot0", 5, cotangent.at[pl.ds(pl.multiple_of(mp * (n_full + seq), 16), n_full)], cot.at[pl.ds(0, n_full)])
    load("cot1", 6, cotangent.at[pl.ds(pl.multiple_of(n_full + mp * half_seq, 16), half_seq)], cot.at[pl.ds(n_full, half_seq)])
    load("xh2", 7, xh2_h, xh2)
    load("r2", 8, r2_h, r2)
    load("g", 9, g_h, gg.at[pl.ds(0, 2)])
    load("outer", 10, outer_h, outer)
    load("gp", 11, gp_h, gg.at[pl.ds(2, 2)])
    load("xh1", 12, xh1_h, xh1)
    load("inner", 14, inner_h, inner)
    load("attn", 15, va_h.at[1], attn)
    load("o", 16, o_h, o)
    load("q", 17, q_h, q)
    load("k", 18, k_h, k)
    load("v", 19, v_h, v)
    load("xt", 20, xt_h, xt)

    greet(me.others() + me.eights())
    pieces = []
    dsts = [outer_r.at[0], outer_r.at[1], inner_r.at[0], inner_r.at[1], va_r.at[1], va_r.at[0], qk_r.at[0], qk_r.at[1], small_r]
    for p in range(9):
        src = grads[p] if p < 8 else small
        pieces.append((routes[p], dsts[p], src) + tuple(bufs[4 * p : 4 * p + 4]))
    net = Reduce(me, pieces, rsems)
    send_out = remote(out_h, peer_out, xs.at[0], xr.at[0], other)
    net.go(send_out)

    vg[...] = jnp.zeros_like(vg)
    small[...] = jnp.zeros_like(small)
    acc1[...] = jnp.zeros_like(acc1)
    acc2[...] = jnp.zeros_like(acc2)
    ffacc[...] = jnp.zeros_like(ffacc)
    need("vec", "proj", *["cls%d" % s for s in range(full + 1)])
    row16 = lax.broadcasted_iota(jnp.int32, (16, 1), 0)
    cls = jnp.zeros((16, width), F32)
    for s in range(full + 1):
        cls = jnp.where(row16 == s, cls_in[s].astype(F32)[0:1], cls)
    cls = cls.astype(BF)
    proj_low = proj[...].astype(BF)
    query = mm(cls, proj_low).astype(BF).astype(F32)
    row8 = lax.broadcasted_iota(jnp.int32, (8, 1), 0)
    dcq = jnp.zeros((16, 128), F32)
    row_grads = []
    cands = doc_ids.shape[1]
    seq_ids = [mp * (full + 1) + s for s in range(full)] + [full]
    for s in range(full + 1):
        docs = doc_rows[seq_ids[s]].astype(F32)
        mine = 1.0 if s < full else jnp.where(mp == 0, 1.0, 0.0)
        query_s = query[s : s + 1]
        score = jnp.sum(query_s * docs, axis=-1, keepdims=True) * retrieval_scale
        e = jnp.exp(score - jnp.max(score, axis=0, keepdims=True))
        soft = e / jnp.sum(e, axis=0, keepdims=True)
        sg = (soft - jnp.where(row8 == 0, 1.0, 0.0)) * (retrieval_scale * mine)
        dcq = jnp.where(row16 == s, jnp.sum(sg * docs, axis=0, keepdims=True), dcq)
        row_grads.append(sg * query_s)
    dcq = dcq.astype(BF)
    cls_grad[...] = mm_nt(dcq, proj_low)
    proj[...] = mm_tn(cls, dcq)

    per = seq // 48
    row48 = lax.broadcasted_iota(jnp.int32, (48, 1), 0)

    def get_dy(i, at):
        first = (row48 == 0) & (lax.rem(i, per) == 0)
        return cot[at, :].astype(F32) + jnp.where(first, cls_grad[pl.ds(i // per, 1), :], 0.0)

    def put_df(at, dz):
        df[at, :] = dz.astype(BF)

    need("cot0", "cot1", "xh2", "r2")
    norm_back_rows(n_own, get_dy, xh2, r2, vec[10:11, :], put_df, acc2)

    def turn(src, dst, n_rows):
        def body(i):
            dst[rows_at(i, 256), 0:n_rows] = jnp.transpose(src[:, lanes(i, 256)])

        each(width // 256, body)

    load("r1", 13, r1_h, r1)
    turn(df, dft, n_own)
    n_tile = 256
    shape5 = (NZ, NY, NC, width // (NZ * NY * NC))

    def weight_grad(left, right, dst, n):
        def body(i):
            r = mm(left(), right(lanes(i, n_tile)))
            dst[:, :, :, :, lanes(i, n_tile)] = r.astype(BF).reshape(shape5 + (n_tile,))

        each(n // n_tile, body)

    need("g")
    for h in range(2):
        weight_grad(lambda: dft[:, 0:n_own], lambda l: gg[h, :, l], grads[h], half_ff)
        net.step1(h)

    need("outer", "gp")
    tile = 240
    tiles = n_own // tile

    def hidden(h):
        def body(i):
            w = flat(outer[h, :, :, :, :, lanes(i, n_tile)])
            for t in range(tiles):
                at = pl.ds(t * tile, tile)
                du = (mm(df[at, :], w) * gg[2 + h, at, lanes(i, n_tile)].astype(F32)).astype(BF)
                gg[2 + h, at, lanes(i, n_tile)] = du
                ffacc[h, :, lanes(i, n_tile)] = ffacc[h, :, lanes(i, n_tile)] + fold(du.astype(F32))

        each(half_ff // n_tile, body)

    hidden(0)
    net.step2(0)
    hidden(1)
    net.step2(1)
    net.step3(0)
    load("p0", 21, p_h.at[0], gg.at[0])
    load("p1", 22, p_h.at[1], gg.at[1])
    load("wq", 23, qk_h.at[0], outer.at[0, :, :, :, :, pl.ds(0, width)])
    load("wk", 24, qk_h.at[1], outer.at[0, :, :, :, :, pl.ds(width, width)])
    load("wv", 25, va_h.at[0], outer.at[1, :, :, :, :, pl.ds(0, width)])
    need("xh1", "r1")

    def h1_turn(i):
        l = lanes(i, 256)
        h1 = (xh1[:, l] * vec[3:4, l] + vec[4:5, l]).astype(BF)
        h1t[rows_at(i, 256), 0:n_own] = jnp.transpose(h1)

    each(width // 256, h1_turn)
    for h in range(2):
        weight_grad(lambda: h1t[:, 0:n_own], lambda l: gg[2 + h, :, l], grads[2 + h], half_ff)
        net.step1(2 + h)
    net.step2(2)
    net.step3(1)
    net.step4(0)
    need("inner")

    def hidden_back(i):
        at = rows_at(i, tile)
        d = mm_nt(gg[2, at, :], flat(inner[0])) + mm_nt(gg[3, at, :], flat(inner[1]))
        xh2[at, :] = d + xh2[at, :]

    each(tiles, hidden_back)
    load("p2", 26, p_h.at[2], gg.at[2])
    net.step2(3)
    net.step3(2)
    net.step4(1)
    net.step5(0)

    norm_back_rows(n_own, lambda i, at: xh2[at, :], xh1, r1, vec[3:4, :], put_df, acc1)
    need("attn", "o")

    def mixed_back(i):
        do[:, lanes(i, n_tile)] = mm(da[...], flat(attn[:, :, :, :, lanes(i, n_tile)])).astype(BF)

    each(width // n_tile, mixed_back)
    turn(da, dat, n_own)
    weight_grad(lambda: dat[:, 0:n_own], lambda l: o[:, l], grads[4], width)
    net.step1(4)

    need("q", "k", "v", "p0", "p1", "p2")
    lane = lax.broadcasted_iota(jnp.int32, (1, 128), 1)
    head_lo = jnp.where(lane < HEAD_DIM, 1.0, 0.0)
    head_mask = (head_lo.astype(BF), (1.0 - head_lo).astype(BF))
    scale = HEAD_DIM**-0.5

    def attend(q0, nq, k0, slab):
        at_q = pl.ds(pl.multiple_of(q0, 16), nq)
        at_k = pl.ds(pl.multiple_of(k0, 16), seq)
        for pair in range(2):
            l = lanes(2 * slab + pair)
            qp, kp, vp, dop = q[at_q, l], k[at_k, l], v[at_k, l], do[at_q, l]
            got = []
            for h in range(2):
                j = 384 * (2 * pair + h)
                pb = gg[slab, at_q, j : j + seq]
                p = pb.astype(F32)
                pd = p * mm_nt(dop * head_mask[h], vp)
                ds = (pd - p * jnp.sum(pd, axis=-1, keepdims=True)).astype(BF)
                got.append((mm(ds, kp) * scale, mm_tn(ds, qp) * scale, mm_tn(pb, dop)))
            low = lane < HEAD_DIM
            q[at_q, l] = jnp.where(low, got[0][0], got[1][0]).astype(BF)
            k[at_k, l] = jnp.where(low, got[0][1], got[1][1]).astype(BF)
            v[at_k, l] = jnp.where(low, got[0][2], got[1][2]).astype(BF)

    slabs = p_h.shape[0]

    def tokens_back(at, own):
        d = mm_nt(k[at, :], flat(outer[0, :, :, :, :, width : 2 * width]))
        d = d + mm_nt(v[at, :], flat(outer[1, :, :, :, :, 0:width]))
        if own:
            d = d + mm_nt(q[at, :], flat(outer[0, :, :, :, :, 0:width])) + xh1[at, :]
            o[at, :] = d.astype(BF)
        else:
            df[0:half_seq, :] = d.astype(BF)

    keeps = []

    def send_dx(i, src, at):
        net.go(remote(src, peer_dx.at[at], xs.at[1 + i], xr.at[1 + i], other))
        cp = pltpu.make_async_copy(src, dx.at[at], lsem.at[27 + i])
        cp.start()
        keeps.append(cp)

    need("wq", "wk", "wv")
    for s in range(full):
        each(slabs, lambda i: attend(s * seq, seq, s * seq, i))
        tokens_back(pl.ds(s * seq, seq), True)
        send_dx(s, o.at[pl.ds(s * seq, seq)], pl.ds(s * seq, seq))
        if s == 0:
            net.step2(4)
            net.step3(3)
            net.step4(2)
            net.step5(1)
        else:
            net.step3(4)
            net.step4(3)
            net.step5(2)
    each(slabs, lambda i: attend(n_full, half_seq, n_full, i))
    need("xt")
    weight_grad(lambda: xt[...], lambda l: v[:, l], grads[5], width)
    net.step1(5)
    weight_grad(lambda: xt[:, 0:n_own], lambda l: q[:, l], grads[6], width)
    net.step1(6)
    net.step2(5)
    net.step4(4)
    net.step5(3)
    weight_grad(lambda: xt[...], lambda l: k[:, l], grads[7], width)
    net.step1(7)
    net.step2(6)
    net.step3(5)
    net.step5(4)
    tokens_back(pl.ds(n_full, half_seq), True)
    tokens_back(pl.ds(n_own, half_seq), False)
    send_dx(full, o.at[pl.ds(n_full, half_seq)], pl.ds(n_full, half_seq))
    send_dx(full + 1, df.at[pl.ds(0, half_seq)], pl.ds(n_own, half_seq))

    vg[0:1, :] = jnp.sum(q[...].astype(F32), axis=0, keepdims=True)
    vg[1:2, :] = jnp.sum(v[...].astype(F32), axis=0, keepdims=True)
    vg[2:3, :] = jnp.sum(acc1[2], axis=0, keepdims=True)
    vg[3:4, :] = jnp.sum(acc1[0], axis=0, keepdims=True)
    vg[4:5, :] = jnp.sum(acc1[1], axis=0, keepdims=True)
    for h in range(2):
        both = jnp.sum(ffacc[h], axis=0, keepdims=True)
        for x in range(NX):
            vg[5 + NX * x + h : 6 + NX * x + h, :] = both[:, x * width : (x + 1) * width]
    vg[9:10, :] = jnp.sum(acc2[2], axis=0, keepdims=True)
    vg[10:11, :] = jnp.sum(acc2[0], axis=0, keepdims=True)
    vg[11:12, :] = jnp.sum(acc2[1], axis=0, keepdims=True)
    turned = jnp.transpose(vg[...])
    n_dev = NZ * NY * NC * NX
    table_row = lax.broadcasted_iota(jnp.int32, (TAB_DEV * n_dev // NX, 1), 0)
    table = jnp.zeros((TAB_DEV * n_dev // NX, 128), F32)
    for s in range(full + 1):
        for i in range(cands):
            table = table + jnp.where(table_row == doc_ids[seq_ids[s], i], row_grads[s][i : i + 1], 0.0)
    hr = width // n_dev
    for z in range(NZ):
        for y in range(NY):
            for c in range(NC):
                dp = (z * NY + y) * NC + c
                for x in range(NX):
                    d = dp * NX + x
                    l = slice(x * 128, (x + 1) * 128)
                    small[z, y, c, 0:hr, l] = proj[d * hr : (d + 1) * hr]
                    small[z, y, c, hr : 2 * hr, l] = turned[d * hr : (d + 1) * hr]
                    t0 = dp * TAB_DEV + x * (TAB_DEV // NX)
                    small[z, y, c, 2 * hr : 2 * hr + TAB_DEV // NX, l] = table[t0 : t0 + TAB_DEV // NX]
    net.step1(8)
    net.step2(7)
    net.step3(6)
    net.step4(5)
    net.step2(8)
    net.step3(7)
    net.step4(6)
    net.step3(8)
    net.step4(7)
    net.step5(5)
    net.step4(8)
    net.step5(6)
    net.step5(7)
    net.step5(8, False)
    net.go(remote(small_r, peer_small, xs.at[5], xr.at[5], other))
    count = small_r[0 : 2 * hr, :]
    total = net.squares + jnp.sum(count * count, keepdims=True)
    norm_ref[...] = all_squares(me, net, total, sq4, sq8, qsems)
    parts = [pl.ds(0, seq), pl.ds(seq, seq), pl.ds(n_full, half_seq), pl.ds(n_own, half_seq)]
    for i, ref in enumerate([peer_out] + [peer_dx.at[at] for at in parts] + [peer_small]):
        net.arrived(ref, xs.at[i], xr.at[i])
    for cp in keeps:
        cp.wait()
    net.end()


def backward_fast(doc_ids, cotangent, doc_rows, saved, rows):
    (qk, va, inner, outer, xt, q, k, v, p, o, xh1, r1, g, gp, xh2, r2, proj, vec, out_own) = saved
    n_own, width = q.shape
    n_all = k.shape[0]
    half_ff = inner.shape[-1]
    zyc = (NZ, NY, NC)
    hr = rows // NX
    small_rows = 2 * hr + 8
    ins = [doc_ids, cotangent, doc_rows] + list(saved)
    out_shape = [
        ((small_rows, 128), F32),
        ((2, rows, width // 2), F32),
        ((2, rows, width // 2), F32),
        ((2, rows, half_ff // 2), F32),
        ((2, rows, half_ff // 2), F32),
        ((n_all, width), BF),
        ((n_own, width), BF),
        ((n_all, width), BF),
        ((small_rows, 128), F32),
        ((8, 128), F32),
    ]
    like = lambda a: (a.shape, a.dtype)
    wide = width // 128 * 128
    scratch = [
        like(inner), like(outer), (va.shape[1:], BF), like(xt), like(q), like(k), like(v), like(o),
        like(xh1), ((4,) + g.shape[1:], BF), like(xh2), like(r2), like(proj), like(vec),
        ((3, 16, width), BF), ((n_own, width), BF), ((n_own, width), BF),
        ((width, wide), BF),
        ((16, width), F32), ((3, 8, width), F32), ((3, 8, width), F32), ((2, 8, half_ff), F32),
        ((128, width), F32), (zyc + (small_rows, 256), F32),
    ]
    sizes = [half_ff] * 4 + [width] * 4
    scratch += [(zyc + (rows, w), BF) for w in sizes[:4]]
    for i, (r, w, dt) in enumerate([(rows, w, BF) for w in sizes] + [(small_rows, 256, F32)]):
        scratch.append(((NZ, NY, r, w), dt))
        scratch.append((((NZ, r, w) if routes[i] == "y" else (NZ, NY, r, w // 2)), dt))
        scratch.append(((NZ, r, w // 2), dt))
        scratch.append(((NZ, r, w // 2), dt))
    scratch += [((NZ, 8, 128), F32), ((8, 8, 128), F32)]
    vm = pl.BlockSpec(memory_space=pltpu.VMEM)
    hb = pl.BlockSpec(memory_space=ANY)
    sm = pl.BlockSpec(memory_space=pltpu.SMEM)
    n = 9
    return pl.pallas_call(
        backward_kernel,
        out_shape=[jax.ShapeDtypeStruct(s, d) for s, d in out_shape],
        in_specs=[sm, hb, vm] + [hb] * 19,
        out_specs=[vm] * 5 + [hb, hb, hb, vm, vm],
        scratch_shapes=[pltpu.VMEM(s, d) for s, d in scratch]
        + [
            dma(31), dma(n), dma(n), dma(n), dma(n), dma(n), dma(n), dma(n, NZ), dma(n, NZ),
            dma(6), dma(6), dma(NZ), dma(NZ), dma(8), dma(8),
        ],
        compiler_params=pltpu.CompilerParams(
            collective_id=2, has_side_effects=True, vmem_limit_bytes=63 * 2**20
        ),
        name="backward",
    )(*ins)


def finish_kernel(*refs):
    small_r, peer_small, qk_r, va_r, inner_r, outer_r, total = refs[:7]
    out_own, peer_out, dx, peer_dx = refs[7:11]
    params = [refs[11 + 3 * i : 14 + 3 * i] for i in range(6)]
    outs = refs[29:51]
    turn, sem, lo, hi, mid = refs[51:]
    out_tokens, input_grad, norm = outs[0:3]
    news = [outs[3 + 3 * i : 6 + 3 * i] for i in range(6)]
    table_grad = outs[21]
    mp = lax.axis_index("mp")
    n_own = out_own.shape[0]
    n_all = dx.shape[0]
    half_seq = n_all - n_own
    n_full = n_own - half_seq
    seq = 2 * half_seq
    copies = []
    for i, (src, first) in enumerate(((out_own, mp), (peer_out, 1 - mp))):
        at = pl.multiple_of(first * (n_full + seq), 16)
        copies.append((src.at[pl.ds(0, n_full)], out_tokens.at[pl.ds(at, n_full)]))
        at = pl.multiple_of(n_full + first * half_seq, 16)
        copies.append((src.at[pl.ds(n_full, half_seq)], out_tokens.at[pl.ds(at, half_seq)]))
    copies = [pltpu.make_async_copy(s, d, sem.at[i]) for i, (s, d) in enumerate(copies)]
    for cp in copies:
        cp.start()
    lo[...] = dx[0:n_full].astype(F32)
    hi[...] = peer_dx[0:n_full].astype(F32)
    own_mid = dx[n_full:n_own].astype(F32) + peer_dx[n_own:n_all].astype(F32)
    peer_mid = peer_dx[n_full:n_own].astype(F32) + dx[n_own:n_all].astype(F32)
    mid[pl.ds(pl.multiple_of(mp * half_seq, 16), half_seq)] = own_mid
    mid[pl.ds(pl.multiple_of((1 - mp) * half_seq, 16), half_seq)] = peer_mid
    grads = (
        (lo, pl.multiple_of(mp * (n_full + seq), 16), n_full),
        (hi, pl.multiple_of((1 - mp) * (n_full + seq), 16), n_full),
        (mid, n_full, seq),
    )
    for i, (src, at, n) in enumerate(grads):
        cp = pltpu.make_async_copy(src, input_grad.at[pl.ds(at, n)], sem.at[4 + i])
        cp.start()
        copies.append(cp)

    root = jnp.sqrt(total[...])
    norm[0, 0] = jnp.max(root)
    clip = clip_norm / jnp.maximum(root[0:1, 0:1], clip_norm)
    hf = inner_r.shape[-1]
    hr = params[4][0].shape[0] // 2
    nvec, nlane = params[5][0].shape
    tr = table_grad.shape[0] // 2

    def adam(which, at, g, dec, rate):
        w, m, s = (ref[at] for ref in params[which])
        for ref, new in zip(news[which], adamw_update(w, m, s, g * clip, dec, rate)):
            ref[at] = new

    for j in range(3):
        g = qk_r[j] if j < 2 else va_r[0]
        adam(0, (j,), g, decay_rate, learn_rate)
    adam(1, (slice(None), slice(None)), va_r[1], decay_rate, learn_rate)
    for which, ref in ((2, inner_r), (3, outer_r)):
        for h in range(2):
            adam(which, (slice(None), slice(h * hf, (h + 1) * hf)), ref[h], decay_rate, learn_rate)
    turn[...] = jnp.zeros_like(turn)
    turn[0:nlane] = small_r[hr : hr + nlane]
    adam(5, (slice(None), slice(None)), jnp.transpose(turn[...])[0:nvec, 0:nlane], 0.0, vector_rate)
    for block, first in ((small_r, mp), (peer_small, 1 - mp)):
        at = pl.ds(pl.multiple_of(first * hr, 8), hr)
        adam(4, (at, slice(None)), block[0:hr], decay_rate, learn_rate)
    own_t, peer_t = small_r[hr + nlane : hr + nlane + tr], peer_small[hr + nlane : hr + nlane + tr]
    table_grad[0:tr] = jnp.where(mp == 0, own_t, peer_t)
    table_grad[tr : 2 * tr] = jnp.where(mp == 0, peer_t, own_t)
    for cp in copies:
        cp.wait()


def finish_fast(reduced, out_own, params, n_rows):
    (small_r, qk_r, va_r, inner_r, outer_r, dx, peer_out, peer_dx, peer_small, total) = reduced
    n_own, width = out_own.shape
    n_all = dx.shape[0]
    half_seq = n_all - n_own
    like = lambda a: jax.ShapeDtypeStruct(a.shape, a.dtype)
    vm = pl.BlockSpec(memory_space=pltpu.VMEM)
    hb = pl.BlockSpec(memory_space=ANY)
    sm = pl.BlockSpec(memory_space=pltpu.SMEM)
    out_shape = [
        jax.ShapeDtypeStruct((n_rows, width), BF),
        jax.ShapeDtypeStruct((n_rows, width), F32),
        jax.ShapeDtypeStruct((1, 1), F32),
    ]
    out_shape += [like(a) for a in params] + [jax.ShapeDtypeStruct((TAB_DEV, 128), F32)]
    n_full = n_own - half_seq
    outs = pl.pallas_call(
        finish_kernel,
        out_shape=out_shape,
        in_specs=[vm] * 29,
        out_specs=[hb, hb, sm] + [vm] * 19,
        scratch_shapes=[
            pltpu.VMEM((128, 128), F32),
            dma(7),
            pltpu.VMEM((n_full, width), F32),
            pltpu.VMEM((n_full, width), F32),
            pltpu.VMEM((2 * half_seq, width), F32),
        ],
        compiler_params=pltpu.CompilerParams(vmem_limit_bytes=63 * 2**20),
        name="finish",
    )(small_r, peer_small, qk_r, va_r, inner_r, outer_r, total, out_own, peer_out, dx, peer_dx, *params)
    return tuple(outs[:2]) + (outs[2].reshape(()),) + tuple(outs[3:])


def gather_plain(shards, small, rows):
    def both(v, axis):
        v = lax.all_gather(v, "dp", axis=axis, tiled=True)
        return lax.all_gather(v, "mp", axis=2, tiled=True)

    return [both(small[None], 0)] + [both(v, 1) for v in shards]


def reduce_plain(grads, small, own_out, own_dx, rows):
    def both(v, axis, wide):
        v = lax.psum_scatter(v.astype(F32), "mp", scatter_dimension=wide, tiled=True)
        return lax.psum_scatter(v, "dp", scatter_dimension=axis, tiled=True)

    small_sum = both(small, 0, 2)[0]
    sums = [both(g, 1, 2) for g in grads]
    ox = 1 - lax.axis_index("mp")
    swap = [(0, 1), (1, 0)]
    peer_out = lax.ppermute(own_out, "mp", swap)
    peer_dx = lax.ppermute(own_dx, "mp", swap)
    peer_small = lax.ppermute(small_sum, "mp", swap)
    squares = sum(squared(g) for g in sums) + squared(small_sum[:-4])
    total = lax.psum(squares, ("dp", "mp"))
    return [small_sum] + sums + [peer_out, peer_dx, peer_small, jnp.full((8, 128), total)]


def forward_plain(lengths, tokens, w_qkv, w_attn, w_inner, w_outer, w_proj, vectors):
    mp = lax.axis_index("mp")
    n_dp = lax.axis_size("dp")
    seqs = lengths.shape[0]
    all_rows, width = tokens.shape
    seq_len = all_rows // seqs
    full = seqs // 2
    n_full, n_half = full * seq_len, seq_len // 2
    n_own = n_full + n_half
    heads = width // HEAD_DIM
    rows, half_ff = w_qkv.shape[1], w_inner.shape[1]
    nvec, vec_lanes = vectors.shape
    half_rows = rows // 2
    score_scale = HEAD_DIM ** (-0.5)

    def two(v):
        return v.reshape(rows, 2, half_ff // 2).transpose(1, 0, 2)

    qk_s = w_qkv[:2].astype(BF)
    va_s = jnp.stack([w_qkv[2], w_attn]).astype(BF)
    vec_pad = jnp.pad(vectors, ((0, 0), (0, 128 - vec_lanes)))
    proj_half = lax.dynamic_slice_in_dim(w_proj, mp * half_rows, half_rows, 0)
    small_s = jnp.concatenate([proj_half, vec_pad], axis=0)
    small_g, qk, va, inner, outer = gather_plain(
        [qk_s, va_s, two(w_inner.astype(BF)), two(w_outer.astype(BF))], small_s, rows
    )
    small_g = small_g.reshape(n_dp, half_rows + nvec, 2, 128)
    proj = small_g[:, :half_rows].transpose(0, 2, 1, 3).reshape(width, 128)
    vec = small_g[:, half_rows:, :, :vec_lanes].transpose(1, 0, 2, 3).reshape(nvec, width)
    ff_rows = nvec - 8
    b_inner = vec[5 : 5 + ff_rows].reshape(2, 2, half_ff // 2).transpose(1, 0, 2).reshape(2, half_ff)

    a0 = mp * (n_full + seq_len)
    h0 = n_full + mp * n_half
    o0 = n_full + (1 - mp) * n_half
    x_all = jnp.concatenate(
        [
            lax.dynamic_slice_in_dim(tokens, a0, n_full, 0),
            lax.dynamic_slice_in_dim(tokens, h0, n_half, 0),
            lax.dynamic_slice_in_dim(tokens, o0, n_half, 0),
        ]
    )
    x_own = x_all[:n_own]
    my_seqs = jnp.concatenate([mp * (full + 1) + jnp.arange(full), jnp.array([full])])
    my_len = lengths[my_seqs]
    pos = jnp.arange(seq_len)
    pos_last = jnp.where(pos < n_half, pos + mp * n_half, pos - n_half + (1 - mp) * n_half)
    valids = (pos[None, :] < my_len[:full, None], pos_last[None, :] < my_len[full:, None])

    q = (jnp.dot(x_own, qk[0], preferred_element_type=F32) + vec[0]).astype(BF)
    k = jnp.dot(x_all, qk[1], preferred_element_type=F32).astype(BF)
    v = (jnp.dot(x_all, va[0], preferred_element_type=F32) + vec[1]).astype(BF)
    probs, outs = [], []
    for qh, kh, vh, valid in zip(*(halves(t, n_full, seq_len) for t in (q, k, v)), valids):
        s = jnp.einsum("gqhe,gkhe->ghqk", qh, kh, preferred_element_type=F32) * score_scale
        s = jnp.where(valid[:, None, None, :], s, -1000000000.0)
        pb = jax.nn.softmax(s, axis=-1).astype(BF)
        o = jnp.einsum("ghqk,gkhe->gqhe", pb, vh, preferred_element_type=F32)
        outs.append(o.reshape(-1, width).astype(BF))
        probs.append(pb.reshape((-1,) + pb.shape[2:]))
    mixed = jnp.concatenate(outs)

    def norm(z):
        centred = z - jnp.mean(z, axis=-1, keepdims=True)
        root = lax.rsqrt(jnp.mean(centred * centred, axis=-1, keepdims=True) + ln_epsilon)
        return centred * root, jnp.broadcast_to(root, (n_own, 128))

    attn = jnp.einsum("te,de->td", mixed, va[1], preferred_element_type=F32)
    xh1, r1 = norm(x_own.astype(F32) + attn + vec[2])
    h1 = xh1 * vec[3] + vec[4]
    u = jnp.einsum("td,hdf->htf", h1.astype(BF), inner, preferred_element_type=F32) + b_inner[:, None, :]
    tail = 0.5 * (1.0 + lax.erf(u * 0.7071067811865476))
    g = (u * tail).astype(BF)
    gp = (tail + u * (0.3989422804014327 * jnp.exp(-0.5 * u * u))).astype(BF)
    f = jnp.einsum("htf,hdf->td", g, outer, preferred_element_type=F32)
    xh2, r2 = norm(h1 + f + vec[5 + ff_rows])
    out_own = (xh2 * vec[6 + ff_rows] + vec[7 + ff_rows]).astype(BF)
    vec = jnp.pad(vec, ((0, 16 - nvec), (0, 0)))
    return [qk, va, inner, outer, x_all, q, k, v, *probs, mixed, xh1, r1, g, gp, xh2, r2, proj, vec, out_own]


def halves(t, n_full, seq_len):
    heads = t.shape[1] // HEAD_DIM
    last = t.shape[0] - n_full
    return (
        t[:n_full].reshape(n_full // seq_len, seq_len, heads, HEAD_DIM),
        t[n_full:].reshape(1, last, heads, HEAD_DIM),
    )


def pass_plain(lengths, tokens, cotangent, doc_ids, doc_rows, w_qkv, w_attn, w_inner, w_outer, w_proj, vectors):
    mp = lax.axis_index("mp")
    n_dp, n_mp = lax.axis_size("dp"), lax.axis_size("mp")
    seqs = lengths.shape[0]
    all_rows, width = tokens.shape
    seq_len = all_rows // seqs
    full = seqs // 2
    n_full, n_half = full * seq_len, seq_len // 2
    n_own = n_full + n_half
    rows, half_ff = w_qkv.shape[1], w_inner.shape[1]
    half_rows = rows // 2
    nvec, vec_lanes = vectors.shape
    ff_rows = nvec - 8
    score_scale = HEAD_DIM ** (-0.5)

    saved = forward_plain(lengths, tokens, w_qkv, w_attn, w_inner, w_outer, w_proj, vectors)
    (qk, va, inner, outer, x_all, q, k, v, p_ab, p_c, mixed, xh1, r1, act_low, slope, xh2, r2, proj, vec, out_own) = saved
    qk = qk.reshape(2, width, width)
    va = va.reshape(2, width, width)
    inner = inner.reshape(2, width, half_ff)
    outer = outer.reshape(2, width, half_ff)
    x_own = x_all[:n_own]
    proj = proj.astype(BF)
    a0 = mp * (n_full + seq_len)
    h0 = n_full + mp * n_half
    cot = jnp.concatenate(
        [lax.dynamic_slice_in_dim(cotangent, a0, n_full, 0), lax.dynamic_slice_in_dim(cotangent, h0, n_half, 0)]
    )
    my_seqs = jnp.concatenate([mp * (full + 1) + jnp.arange(full), jnp.array([full])])

    n_mine = full + 1
    mine = jnp.where((jnp.arange(n_mine) < full) | (mp == 0), 1.0, 0.0).astype(F32)
    cls_low = out_own[:: seq_len][:n_mine]
    docs = doc_rows[my_seqs].astype(F32)
    ids = doc_ids[my_seqs]
    query = jnp.dot(cls_low, proj, preferred_element_type=F32).astype(BF)
    query_float = query.astype(F32)
    doc_scores = jnp.einsum("gp,gkp->gk", query_float, docs, precision=highest_mode) * retrieval_scale
    soft = jax.nn.softmax(doc_scores, axis=-1)
    target = (jnp.arange(doc_scores.shape[1]) == 0).astype(F32)
    score_grad = (soft - target[None, :]) * retrieval_scale * mine[:, None]
    query_grad = jnp.einsum("gk,gkp->gp", score_grad, docs, precision=highest_mode).astype(BF)
    row_grads = score_grad[:, :, None] * query_float[:, None, :]
    cls_grad = jnp.einsum("gp,dp->gd", query_grad, proj, preferred_element_type=F32)
    proj_grad = jnp.einsum("gd,gp->dp", cls_low, query_grad, preferred_element_type=F32)
    table_rows = TAB_DEV * n_dp
    one_hot = (jnp.arange(table_rows)[:, None] == ids.reshape(1, -1)).astype(F32)
    table_local = jnp.dot(one_hot, row_grads.reshape(-1, row_grads.shape[2]), precision=highest_mode)

    def norm_back(dy, hat, root, gain):
        e = dy * gain
        back_ = e - jnp.mean(e, axis=-1, keepdims=True) - hat * jnp.mean(e * hat, axis=-1, keepdims=True)
        return back_ * root[:, :1], jnp.sum(dy * hat, axis=0), jnp.sum(dy, axis=0)

    dy = cot.astype(F32)
    first_rows = jnp.arange(n_mine) * seq_len
    dy = dy.at[first_rows].add(cls_grad)
    dz2, dg2, dc2 = norm_back(dy, xh2, r2, vec[6 + ff_rows])
    df = dz2.astype(BF)
    dg = jnp.einsum("td,hdf->htf", df, outer, preferred_element_type=F32)
    g_outer = jnp.einsum("td,htf->hdf", df, act_low, preferred_element_type=F32).astype(BF)
    du = (dg * slope.astype(F32)).astype(BF)
    normed_low = (xh1 * vec[3] + vec[4]).astype(BF)
    g_inner = jnp.einsum("td,htf->hdf", normed_low, du, preferred_element_type=F32).astype(BF)
    dh1 = jnp.einsum("htf,hdf->td", du, inner, preferred_element_type=F32) + dz2
    dz1, dg1, dc1 = norm_back(dh1, xh1, r1, vec[3])
    da = dz1.astype(BF)
    do = jnp.dot(da, va[1], preferred_element_type=F32).astype(BF)
    g_attn = jnp.einsum("td,te->de", da, mixed, preferred_element_type=F32)
    dqs, dks, dvs = [], [], []
    probs_of = (p_ab.reshape(full, -1, seq_len, seq_len), p_c.reshape(1, -1, n_half, seq_len))
    for qh, kh, vh, doh, pb in zip(*(halves(t, n_full, seq_len) for t in (q, k, v, do)), probs_of):
        probs = pb.astype(F32)
        dp_ = jnp.einsum("gqhe,gkhe->ghqk", doh, vh, preferred_element_type=F32)
        delta = jnp.sum(probs * dp_, axis=-1, keepdims=True)
        ds_ = (probs * (dp_ - delta)).astype(BF)
        dqs.append((jnp.einsum("ghqk,gkhe->gqhe", ds_, kh, preferred_element_type=F32) * score_scale).reshape(-1, width))
        dks.append((jnp.einsum("ghqk,gqhe->gkhe", ds_, qh, preferred_element_type=F32) * score_scale).reshape(-1, width))
        dvs.append(jnp.einsum("ghqk,gqhe->gkhe", pb, doh, preferred_element_type=F32).reshape(-1, width))
    dq = jnp.concatenate(dqs).astype(BF)
    dk = jnp.concatenate(dks).astype(BF)
    dv = jnp.concatenate(dvs).astype(BF)
    g_q = jnp.einsum("td,te->de", x_own, dq, preferred_element_type=F32)
    g_k = jnp.einsum("td,te->de", x_all, dk, preferred_element_type=F32)
    g_v = jnp.einsum("td,te->de", x_all, dv, preferred_element_type=F32)
    g_qk = jnp.stack([g_q, g_k]).astype(BF)
    g_va = jnp.stack([g_v, g_attn]).astype(BF)
    dx_own = jnp.einsum("te,de->td", dq, qk[0], preferred_element_type=F32) + dz1
    dx_all = jnp.einsum("te,de->td", dk, qk[1], preferred_element_type=F32)
    dx_all = dx_all + jnp.einsum("te,de->td", dv, va[0], preferred_element_type=F32)
    dx = jnp.concatenate([dx_all[:n_own] + dx_own, dx_all[n_own:]]).astype(BF)
    db_inner = jnp.sum(du.astype(F32), axis=1)
    db_inner = db_inner.reshape(2, 2, half_ff // 2).transpose(1, 0, 2).reshape(ff_rows, width)
    vec_grad = jnp.concatenate(
        [
            jnp.stack(
                [
                    jnp.sum(dq.astype(F32), axis=0),
                    jnp.sum(dv.astype(F32), axis=0),
                    jnp.sum(dz1, axis=0),
                    dg1,
                    dc1,
                ]
            ),
            db_inner,
            jnp.stack([jnp.sum(dz2, axis=0), dg2, dc2]),
        ]
    )
    vg = vec_grad.reshape(nvec, n_dp, 2, vec_lanes).transpose(1, 0, 2, 3)
    vg = jnp.pad(vg, ((0, 0), (0, 0), (0, 0), (0, 128 - vec_lanes))).reshape(n_dp, nvec, 256)
    pg = proj_grad.reshape(n_dp, 2, half_rows, 128).transpose(0, 2, 1, 3).reshape(n_dp, half_rows, 256)
    tg = table_local.reshape(n_dp, 2, TAB_DEV // 2, 128).transpose(0, 2, 1, 3).reshape(n_dp, TAB_DEV // 2, 256)
    small = jnp.concatenate([pg, vg, tg], axis=1)

    return out_own, dx, *reduce_plain([g_qk, g_va, g_inner, g_outer], small, out_own, dx, rows)


def local(
    tokens, cotangent, lengths, doc_ids, doc_rows,
    w_qkv, m_qkv, v_qkv, w_attn, m_attn, v_attn, w_inner, m_inner, v_inner,
    w_outer, m_outer, v_outer, w_proj, m_proj, v_proj, vectors, m_vectors, v_vectors,
):
    mp = lax.axis_index("mp")
    n_dp, n_mp = lax.axis_size("dp"), lax.axis_size("mp")
    fast = n_dp == NZ * NY * NC and n_mp == NX
    seqs = lengths.shape[0]
    all_rows, width = tokens.shape
    seq_len = all_rows // seqs
    full = seqs // 2
    n_full, n_half = full * seq_len, seq_len // 2
    n_own = n_full + n_half
    rows, half_ff = w_qkv.shape[1], w_inner.shape[1]
    half_rows = rows // 2
    nvec, vec_lanes = vectors.shape
    ff_rows = nvec - 8
    score_scale = HEAD_DIM ** (-0.5)

    if fast:
        saved = forward_fast(lengths, tokens, w_qkv, w_attn, w_inner, w_outer, w_proj, vectors)
        reduced = backward_fast(doc_ids, cotangent, doc_rows, saved, rows)
        params = (w_qkv, m_qkv, v_qkv, w_attn, m_attn, v_attn, w_inner, m_inner, v_inner)
        params += (w_outer, m_outer, v_outer, w_proj, m_proj, v_proj, vectors, m_vectors, v_vectors)
        return finish_fast(reduced, saved[-1], params, all_rows)
    if not fast:
        (out_own, dx, small_r, qk_r, va_r, inner_r, outer_r, peer_out, peer_dx, peer_small, total) = pass_plain(
            lengths, tokens, cotangent, doc_ids, doc_rows, w_qkv, w_attn, w_inner, w_outer, w_proj, vectors
        )
        vector_r = small_r[half_rows : half_rows + nvec, :vec_lanes]
        table_at = half_rows + nvec

    def whole_rows(own, peer):
        lo = jnp.where(mp == 0, own[:n_own], peer[:n_own])
        hi = jnp.where(mp == 0, peer[:n_own], own[:n_own])
        return lo, hi

    lo, hi = whole_rows(out_own, peer_out)
    out_tokens = jnp.concatenate([lo, hi[n_full:], hi[:n_full]])
    lo, hi = whole_rows(dx.astype(F32), peer_dx.astype(F32))
    tail = jnp.where(mp == 0, dx[n_own:], peer_dx[n_own:]).astype(F32)
    tail_hi = jnp.where(mp == 0, peer_dx[n_own:], dx[n_own:]).astype(F32)
    input_grad = jnp.concatenate(
        [lo[:n_full], lo[n_full:] + tail_hi, hi[n_full:] + tail, hi[:n_full]]
    )

    def both_halves(at, count):
        mine_, peer_ = small_r[at : at + count], peer_small[at : at + count]
        return jnp.concatenate(
            [jnp.where(mp == 0, mine_, peer_), jnp.where(mp == 0, peer_, mine_)]
        )

    proj_r = both_halves(0, half_rows)
    table_grad = both_halves(table_at, TAB_DEV // 2)
    qkv_r = jnp.stack([qk_r[0], qk_r[1], va_r[0]])
    attn_r = va_r[1]

    def back(v):
        return v.transpose(1, 0, 2).reshape(rows, half_ff)

    inner_r, outer_r = back(inner_r), back(outer_r)
    grad_norm = jnp.sqrt(total[0, 0])
    clip = clip_norm / jnp.maximum(grad_norm, clip_norm)
    results = [out_tokens, input_grad, grad_norm]
    for w, m, s, g, dec, rate in (
        (w_qkv, m_qkv, v_qkv, qkv_r, decay_rate, learn_rate),
        (w_attn, m_attn, v_attn, attn_r, decay_rate, learn_rate),
        (w_inner, m_inner, v_inner, inner_r, decay_rate, learn_rate),
        (w_outer, m_outer, v_outer, outer_r, decay_rate, learn_rate),
        (w_proj, m_proj, v_proj, proj_r, decay_rate, learn_rate),
        (vectors, m_vectors, v_vectors, vector_r, 0.0, vector_rate),
    ):
        results += list(adamw_update(w, m, s, g * clip, dec, rate))
    return tuple(results) + (table_grad,)


def solution(mesh):
    mat = P("dp", "mp")
    rep = P("dp", None)
    qkv = P(None, "dp", "mp")
    vec = P(None, ("dp", "mp"))
    placed = (rep, rep, P("dp"), rep, P("dp", None, None), qkv, qkv, qkv)
    placed += (mat,) * 9 + (rep,) * 3 + (vec,) * 3
    given = (rep, rep, P(), qkv, qkv, qkv) + (mat,) * 9 + (rep,) * 3 + (vec,) * 3 + (rep,)
    return jax.shard_map(local, mesh=mesh, in_specs=placed, out_specs=given, check_vma=False)
```

```python
import functools

import jax
import jax.numpy as jnp
from jax import lax
from jax.experimental import pallas as pl
from jax.experimental.pallas import tpu as pltpu
from jax.sharding import PartitionSpec as P

HEAD_DIM = 64
STEP = 10
TAB_DEV = 8
MESH = pl.DeviceIdType.MESH
ANY = pl.ANY
BF = jnp.bfloat16
F32 = jnp.float32
NZ, NY, NC, NX = 4, 2, 2, 2

highest_mode = lax.Precision.HIGHEST
retrieval_scale = 0.17677669529663687
ln_epsilon = 1e-12
beta_first = 0.9
beta_second = 0.999
learn_rate = 0.05
vector_rate = 0.5
decay_rate = 0.01
adam_epsilon = 1e-08
clip_norm = 1.0


def layer_norm(values, gain_row, shift_row):
    centre = jnp.mean(values, axis=-1, keepdims=True)
    centred = values - centre
    spread = jnp.mean(centred * centred, axis=-1, keepdims=True)
    return centred * lax.rsqrt(spread + ln_epsilon) * gain_row + shift_row


def gelu_exact(values):
    return jax.nn.gelu(values, approximate=False)


def adamw_update(weight, moment, second, gradient, decay_factor, step_rate):
    moment_new = beta_first * moment + (1.0 - beta_first) * gradient
    second_new = beta_second * second + (1.0 - beta_second) * gradient * gradient
    first_hat = moment_new / (1.0 - beta_first**STEP)
    second_hat = second_new / (1.0 - beta_second**STEP)
    weight_new = weight - step_rate * (
        first_hat / (jnp.sqrt(second_hat) + adam_epsilon) + decay_factor * weight
    )
    return (moment_new, second_new, weight_new)


def squared(values):
    return jnp.sum(values * values)


class Place:
    def __init__(self):
        dp = lax.axis_index("dp")
        self.x = lax.axis_index("mp")
        self.c = lax.rem(dp, NC)
        self.y = lax.rem(dp // NC, NY)
        self.z = dp // (NC * NY)

    def dev(self, z=None, y=None, c=None, x=None):
        z = self.z if z is None else z
        y = self.y if y is None else y
        c = self.c if c is None else c
        x = self.x if x is None else x
        return ((z * NY + y) * NC + c, x)

    def others(self):
        out = [self.dev(z=lax.rem(self.z + k, NZ)) for k in range(1, NZ)]
        out.append(self.dev(x=1 - self.x))
        out.append(self.dev(y=1 - self.y))
        out.append(self.dev(c=1 - self.c))
        return out

    def eights(self):
        out = []
        for k in range(1, 8):
            dx, dy, dc = k & 1, (k >> 1) & 1, k >> 2
            out.append(
                self.dev(
                    x=self.x + dx - 2 * dx * self.x,
                    y=self.y + dy - 2 * dy * self.y,
                    c=self.c + dc - 2 * dc * self.c,
                )
            )
        return out


def greet(devices):
    barrier = pltpu.get_barrier_semaphore()
    for d in devices:
        pl.semaphore_signal(barrier, inc=1, device_id=d, device_id_type=MESH)
    pl.semaphore_wait(barrier, len(devices))


def greet_send(devices):
    barrier = pltpu.get_barrier_semaphore()
    for d in devices:
        pl.semaphore_signal(barrier, inc=1, device_id=d, device_id_type=MESH)


def greet_wait(count):
    pl.semaphore_wait(pltpu.get_barrier_semaphore(), count)


def remote(src, dst, ssem, rsem, dev):
    return pltpu.make_async_remote_copy(
        src_ref=src, dst_ref=dst, send_sem=ssem, recv_sem=rsem, device_id=dev, device_id_type=MESH
    )


def cols(x, half):
    return pl.ds(pl.multiple_of(x * half, 128), half)


def dma(*shape):
    return pltpu.SemaphoreType.DMA(shape)


def mm(a, b):
    return jnp.dot(a, b, preferred_element_type=F32)


def mm_nt(a, b):
    return lax.dot_general(a, b, (((1,), (1,)), ((), ())), preferred_element_type=F32)


def mm_tn(a, b):
    return lax.dot_general(a, b, (((0,), (0,)), ((), ())), preferred_element_type=F32)


def flat(value):
    return value.reshape(-1, value.shape[-1])


def lanes(i, n=128):
    return pl.ds(pl.multiple_of(i * n, 128), n)


def rows_at(i, n, at=0):
    return pl.ds(pl.multiple_of(at + i * n, 16), n)


def each(n, body):
    lax.fori_loop(0, n, lambda i, c: (body(i), c)[1], 0)


gather_orders = ("zxy", "zxy", "zyx", "zxy", "zyx", "zxy", "zyx", "zxy", "zyx", "zxy", "zyx", "zxy", "xyz", "yxz", "zyx")


class Gather:
    def __init__(self, me, pieces, sems):
        self.me, self.pieces = me, pieces
        self.lsem, self.ss, self.rs, self.ds, self.dr = sems
        self.waits, self.locs = [], {}

    def region(self, p, stage, c, **at):
        dst, me, done = self.pieces[p][1], self.me, gather_orders[p][:stage]
        half = dst.shape[-1] // 2
        z = at.get("z", None if "z" in done else me.z)
        y = at.get("y", None if "y" in done else me.y)
        x = at.get("x", None if "x" in done else me.x)
        zs = slice(None) if z is None else pl.ds(0, NZ - 1) if z == "three" else pl.ds(z, 1)
        ys = slice(None) if y is None else pl.ds(y, 1)
        xs = slice(None) if x is None else cols(x, half)
        return dst.at[zs, ys, c, :, xs]

    def bulk(self, p, stage, c):
        axis = gather_orders[p][stage]
        return self.region(p, stage, c, z="three") if axis == "z" else self.coming(p, stage, c)[0]

    def coming(self, p, stage, c):
        me, axis = self.me, gather_orders[p][stage]
        if axis == "z":
            return [self.region(p, stage, c, z=lax.rem(me.z + NZ - k, NZ)) for k in range(1, NZ)]
        return [self.region(p, stage, c, **{axis: 1 - (me.y if axis == "y" else me.x)})]

    def send(self, p, stage):
        me, axis = self.me, gather_orders[p][stage]
        src, dst = self.pieces[p]
        if stage == 0:
            to = dst.at[me.z, me.y, me.c, :, cols(me.x, dst.shape[-1] // 2)]
        else:
            src = to = self.region(p, stage, me.c)
        if axis == "z":
            devs = [me.dev(z=lax.rem(me.z + k, NZ)) for k in range(1, NZ)]
        else:
            devs = [me.dev(**{axis: 1 - (me.y if axis == "y" else me.x)})]
        for dev in devs:
            remote(src, to, self.ss.at[p, stage], self.rs.at[p, stage], dev).start()
        self.waits.append((self.bulk(p, stage, me.c), self.ss.at[p, stage]))

    def arrived(self, ref, sem):
        remote(ref, ref, sem, sem, self.me.dev(c=1 - self.me.c)).wait_recv()

    def receive(self, p, stage):
        self.arrived(self.bulk(p, stage, self.me.c), self.rs.at[p, stage])

    def crossing(self, p, stage, c):
        if stage == 0:
            ref = self.region(p, 1, c)
            return [ref], ref
        return self.coming(p, stage, c), self.bulk(p, stage, c)

    def cross(self, p, stage):
        refs, whole = self.crossing(p, stage, self.me.c)
        for ref in refs:
            remote(ref, ref, self.ds.at[p, stage], self.dr.at[p, stage], self.me.dev(c=1 - self.me.c)).start()
        self.waits.append((whole, self.ds.at[p, stage]))

    def step1(self, p):
        me = self.me
        src, dst = self.pieces[p]
        self.send(p, 0)
        blk = dst.at[me.z, me.y, me.c, :, cols(me.x, dst.shape[-1] // 2)]
        loc = pltpu.make_async_copy(src, blk, self.lsem.at[p])
        loc.start()
        self.locs[p] = loc

    def step2(self, p):
        self.locs[p].wait()
        self.receive(p, 0)
        self.send(p, 1)
        self.cross(p, 0)

    def step3(self, p):
        self.receive(p, 1)
        self.send(p, 2)
        self.cross(p, 1)

    def step4(self, p):
        self.receive(p, 2)
        self.cross(p, 2)

    def step5(self, p):
        for stage in range(3):
            self.arrived(self.crossing(p, stage, 1 - self.me.c)[1], self.dr.at[p, stage])

    def end(self):
        for ref, sem in self.waits:
            remote(ref, ref, sem, sem, self.me.dev(c=1 - self.me.c)).wait_send()


def norm_rows(z_ref, r_ref, n_rows, put):
    step = 48

    def body(i):
        at = rows_at(i, step)
        z = z_ref[at, :]
        centred = z - jnp.mean(z, axis=-1, keepdims=True)
        spread = jnp.mean(centred * centred, axis=-1, keepdims=True)
        root = lax.rsqrt(spread + ln_epsilon)
        hat = centred * root
        z_ref[at, :] = hat
        r_ref[at, :] = jnp.broadcast_to(root, (step, 128))
        put(at, hat)

    each(n_rows // step, body)


def forward_kernel(*refs):
    (lens, tokens, w_qkv, w_attn, w_inner, w_outer, w_proj, vectors) = refs[:8]
    outs = refs[8:27]
    scr = refs[27:]
    (vec_s, proj_s, qk_s, va_s, inner_s, outer_s, vec_g, proj_g, qk, va, inner, outer) = scr[:12]
    (xt, q, k, v, p, o, xh1, r1, g, gp, xh2, r2, out_own, proj, vec, x_all, h1b, vecp, bias_ff) = scr[12:31]
    gsems, tsem, osem = scr[31:36], scr[36], scr[37]
    me = Place()
    mp = me.x
    n_all, width = x_all.shape
    n_own = q.shape[0]
    half_seq = n_all - n_own
    seq = 2 * half_seq
    full = (n_own - half_seq) // seq
    n_full = full * seq
    half_ff = inner.shape[-1]
    rows = qk_s.shape[1]
    half_rows = rows // 2

    starts = (
        (mp * (n_full + seq), 0, n_full),
        (n_full + mp * half_seq, n_full, half_seq),
        (n_full + (1 - mp) * half_seq, n_own, half_seq),
    )
    loads = []
    for i, (at, to, n) in enumerate(starts):
        cp = pltpu.make_async_copy(
            tokens.at[pl.ds(pl.multiple_of(at, 16), n)], x_all.at[pl.ds(to, n)], tsem.at[i]
        )
        cp.start()
        loads.append(cp)

    greet_send(me.others())
    vecp[...] = jnp.zeros_like(vecp)
    nvec, nlane = vectors.shape
    vecp[0:nvec, 0:nlane] = vectors[...]
    proj_s[...] = w_proj[pl.ds(pl.multiple_of(mp * half_rows, 8), half_rows), :]
    vec_s[...] = jnp.transpose(vecp[...])[0:nlane]
    qk_s[...] = w_qkv[0:2].astype(BF)
    va_s[0] = w_qkv[2].astype(BF)
    va_s[1] = w_attn[...].astype(BF)
    hf = half_ff // 2
    for h in range(2):
        inner_s[h] = w_inner[:, h * hf : (h + 1) * hf].astype(BF)
        outer_s[h] = w_outer[:, h * hf : (h + 1) * hf].astype(BF)

    greet_wait(len(me.others()))
    row_cut = 32
    pieces = [
        (vec_s, vec_g),
        (qk_s.at[0], qk.at[0]),
        (qk_s.at[1], qk.at[1]),
        (va_s.at[0, pl.ds(0, row_cut)], va.at[0, :, :, :, pl.ds(0, row_cut)]),
        (va_s.at[0, pl.ds(row_cut, rows - row_cut)], va.at[0, :, :, :, pl.ds(row_cut, rows - row_cut)]),
        (va_s.at[1], va.at[1]),
    ]
    for shard, whole in ((inner_s, inner), (outer_s, outer)):
        for h in range(2):
            for j in range(2):
                src = shard.at[h, :, pl.ds(j * (hf // 2), hf // 2)]
                pieces.append((src, whole.at[h, :, :, :, :, pl.ds(j * hf, hf)]))
    pieces.append((proj_s, proj_g))
    net = Gather(me, pieces, gsems)

    def go(step, *members):
        for piece in members:
            (net.step1, net.step2, net.step3, net.step4, net.step5)[step - 1](piece)

    go(1, 0, 1, 2, 12, 13)
    saves = []

    def save(i, ref):
        cp = pltpu.make_async_copy(ref, outs[i], osem.at[i])
        cp.start()
        saves.append(cp)

    for cp in loads:
        cp.wait()

    def x_turn(i):
        xt[rows_at(i, 256), :] = jnp.transpose(x_all[:, lanes(i, 256)])

    each(width // 256, x_turn)
    save(4, xt)
    go(2, 0)
    go(1, 3, 4)
    go(2, 1, 12, 13)
    go(1, 5)
    go(2, 2)
    go(1, 6)
    go(3, 0, 1)
    go(2, 3)
    go(3, 2)
    go(1, 7)
    go(2, 4)
    go(4, 0)
    go(5, 0)
    big = []
    for z in range(NZ):
        for y in range(NY):
            for c in range(NC):
                for x in range(NX):
                    big.append(vec_g[z, y, c, :, x * 128 : (x + 1) * 128])
    vec[...] = jnp.transpose(jnp.concatenate(big, axis=0))[0 : vec.shape[0]]
    for h in range(2):
        for x in range(NX):
            for j in range(2):
                row = vec[5 + NX * x + h : 6 + NX * x + h, j * (hf // 2) : (j + 1) * (hf // 2)]
                bias_ff[h : h + 1, j * hf + x * (hf // 2) : j * hf + (x + 1) * (hf // 2)] = row
    save(17, vec)

    def project(w_ref, src_rows, dst, bias):
        n_tile = 256

        def body(i):
            w = flat(w_ref[:, :, :, :, lanes(i, n_tile)])
            r = mm(x_all[0:src_rows], w)
            if bias is not None:
                r = r + vec[bias : bias + 1, lanes(i, n_tile)]
            dst[:, lanes(i, n_tile)] = r.astype(BF)

        each(width // n_tile, body)

    go(3, 3)
    go(4, 1)
    go(3, 4)
    go(2, 5)
    go(1, 8)
    go(4, 2)
    go(5, 1)
    project(qk.at[0], n_own, q, 0)
    go(5, 2)
    go(2, 6)
    go(1, 9)
    project(qk.at[1], n_all, k, None)
    save(0, qk)
    go(4, 3, 4)
    go(3, 5)
    go(5, 3, 4)
    project(va.at[0], n_all, v, 1)
    go(3, 6)
    go(2, 7)
    go(1, 10)
    save(5, q)
    save(6, k)
    save(7, v)

    lane = lax.broadcasted_iota(jnp.int32, (1, 128), 1)
    head_lo = jnp.where(lane < HEAD_DIM, 1.0, 0.0)
    head_mask = (head_lo.astype(BF), (1.0 - head_lo).astype(BF))
    pos = lax.broadcasted_iota(jnp.int32, (1, seq), 1)

    def attend(q0, nq, k0, slab, length, place):
        at_q = pl.ds(pl.multiple_of(q0, 16), nq)
        at_k = pl.ds(pl.multiple_of(k0, 16), seq)
        for pair in range(2):
            l = lanes(2 * slab + pair)
            qp, kp, vp = q[at_q, l], k[at_k, l], v[at_k, l]
            got = []
            for h in range(2):
                s = mm_nt(qp * head_mask[h], kp) * (HEAD_DIM**-0.5)
                s = jnp.where(place < length, s, -1000000000.0)
                e = jnp.exp(s - jnp.max(s, axis=-1, keepdims=True))
                pb = (e * (1.0 / jnp.sum(e, axis=-1, keepdims=True))).astype(BF)
                j = 384 * (2 * pair + h)
                p[slab, at_q, j : j + seq] = pb
                got.append(mm(pb, vp))
            o[at_q, l] = jnp.where(lane < HEAD_DIM, got[0], got[1]).astype(BF)

    slabs = p.shape[0]
    jobs = [[(2, 8), (1, 11, 14), (3, 12)], [], [(2, 9)], [(4, 5, 6), (3, 13)], [(2, 10)], [(3, 7, 8), (5, 5, 6)]]
    for s in range(full):
        length = lens[mp * (full + 1) + s]
        for i in range(slabs):
            attend(s * seq, seq, s * seq, i, length, pos)
            for job in jobs[3 * s + i]:
                go(*job)
    length = lens[full]
    pos_c = jnp.where(pos < half_seq, pos + mp * half_seq, pos - half_seq + (1 - mp) * half_seq)
    for i in range(slabs):
        attend(n_full, half_seq, n_full, i, length, pos_c)
        if i == 0:
            go(2, 11)
    go(2, 14)
    save(8, p)
    save(9, o)

    tile = 240
    tiles = n_own // tile

    def attn_out(i):
        a = mm_nt(o[rows_at(i, tile), :], flat(va[1]))
        xh1[rows_at(i, tile), :] = x_all[rows_at(i, tile), :].astype(F32) + a + vec[2:3, :]

    each(tiles, attn_out)
    go(4, 7, 8)
    save(1, va)

    def put_h1(at, hat):
        h1b[at, :] = (hat * vec[3:4, :] + vec[4:5, :]).astype(BF)

    norm_rows(xh1, r1, n_own, put_h1)
    save(10, xh1)
    save(11, r1)
    go(5, 7)
    go(3, 9, 10)

    def feed(h):
        n_tile = 256

        def body(i):
            w = flat(inner[h, :, :, :, :, lanes(i, n_tile)])
            for t in range(tiles):
                at = pl.ds(t * tile, tile)
                u = mm(h1b[at, :], w)
                u = u + bias_ff[h : h + 1, lanes(i, n_tile)]
                tail = 0.5 * (1.0 + lax.erf(u * 0.7071067811865476))
                g[h, at, lanes(i, n_tile)] = (u * tail).astype(BF)
                slope = tail + u * (0.3989422804014327 * jnp.exp(-0.5 * u * u))
                gp[h, at, lanes(i, n_tile)] = slope.astype(BF)

        each(half_ff // n_tile, body)

    feed(0)
    go(5, 8)
    go(3, 11, 14)
    go(4, 9)
    go(5, 9)
    feed(1)
    go(4, 10, 12, 11, 13)
    go(5, 10, 12, 11, 13)
    save(2, inner)
    save(12, g)
    save(13, gp)

    def ff_out(i):
        at = rows_at(i, tile)
        f = mm_nt(g[0, at, :], flat(outer[0])) + mm_nt(g[1, at, :], flat(outer[1]))
        h1 = xh1[at, :] * vec[3:4, :] + vec[4:5, :]
        xh2[at, :] = h1 + f + vec[9:10, :]

    each(tiles, ff_out)
    save(3, outer)
    go(4, 14)
    go(5, 14)
    for d in range(NZ * NY * NC * NX):
        block = proj_g[d // 8, d // 4 % 2, d // 2 % 2, :, d % 2 * 128 : (d % 2 + 1) * 128]
        proj[d * half_rows : (d + 1) * half_rows] = block
    save(16, proj)

    def put_y(at, hat):
        out_own[at, :] = (hat * vec[10:11, :] + vec[11:12, :]).astype(BF)

    norm_rows(xh2, r2, n_own, put_y)
    save(14, xh2)
    save(15, r2)
    save(18, out_own)
    net.end()
    for cp in saves:
        cp.wait()


def forward_fast(lengths, tokens, w_qkv, w_attn, w_inner, w_outer, w_proj, vectors):
    seqs = lengths.shape[0]
    all_rows, width = tokens.shape
    seq = all_rows // seqs
    full = seqs // 2
    n_own = full * seq + seq // 2
    n_all = n_own + seq // 2
    rows, half_ff = w_qkv.shape[1], w_inner.shape[1]
    heads = width // HEAD_DIM
    zyc = (NZ, NY, NC)
    hr, nlane = rows // 2, vectors.shape[1]
    weights = [
        ((2,) + zyc + (rows, width), BF),
        ((2,) + zyc + (rows, width), BF),
        ((2,) + zyc + (rows, half_ff), BF),
        ((2,) + zyc + (rows, half_ff), BF),
    ]
    kept = [
        ((width, n_all), BF),
        ((n_own, width), BF),
        ((n_all, width), BF),
        ((n_all, width), BF),
        ((heads // 4, n_own, 4 * 384), BF),
        ((n_own, width), BF),
        ((n_own, width), F32),
        ((n_own, 128), F32),
        ((2, n_own, half_ff), BF),
        ((2, n_own, half_ff), BF),
        ((n_own, width), F32),
        ((n_own, 128), F32),
        ((width, 128), F32),
        ((16, width), F32),
        ((n_own, width), BF),
    ]
    order = kept[:12] + [kept[14], kept[12], kept[13]]
    scratch = [
        ((nlane, 128), F32),
        ((hr, 128), F32),
        ((2, rows, width // 2), BF),
        ((2, rows, width // 2), BF),
        ((2, rows, half_ff // 2), BF),
        ((2, rows, half_ff // 2), BF),
        (zyc + (nlane, 256), F32),
        (zyc + (hr, 256), F32),
    ]
    scratch += weights + order
    scratch += [((n_all, width), BF), ((n_own, width), BF), ((128, 128), F32), ((8, half_ff), F32)]
    n = 15
    vm = pl.BlockSpec(memory_space=pltpu.VMEM)
    hb = pl.BlockSpec(memory_space=ANY)
    sm = pl.BlockSpec(memory_space=pltpu.SMEM)
    return pl.pallas_call(
        forward_kernel,
        out_shape=[jax.ShapeDtypeStruct(s, d) for s, d in weights + kept],
        in_specs=[sm, hb] + [vm] * 6,
        out_specs=[hb] * 19,
        scratch_shapes=[pltpu.VMEM(s, d) for s, d in scratch]
        + [
            dma(n), dma(n, 3), dma(n, 3), dma(n, 3), dma(n, 3),
            dma(3), dma(20),
        ],
        compiler_params=pltpu.CompilerParams(
            collective_id=1, has_side_effects=True, vmem_limit_bytes=60 * 2**20
        ),
        name="forward",
    )(lengths, tokens, w_qkv, w_attn, w_inner, w_outer, w_proj, vectors)


class Reduce:
    def __init__(self, me, pieces, sems):
        self.me, self.pieces = me, pieces
        self.ds, self.dr, self.ss, self.rs = sems
        self.waits = []
        self.squares = jnp.zeros((1, 1), F32)

    def go(self, copy):
        copy.start()
        self.waits.append(copy)

    def arrived(self, ref, ssem, rsem):
        remote(ref, ref, ssem, rsem, self.me.dev(c=1 - self.me.c)).wait_recv()

    def region(self, p, stage, **at):
        order, src = self.pieces[p][0], self.pieces[p][2]
        me, done = self.me, order[:stage]
        half = src.shape[-1] // 2
        z = at.get("z", me.z if "z" in done else None)
        y = at.get("y", me.y if "y" in done else None)
        x = at.get("x", me.x if "x" in done else None)
        zs = slice(None) if z is None else pl.ds(0, NZ - 1) if z == "three" else pl.ds(z, 1)
        ys = slice(None) if y is None else pl.ds(y, 1)
        xs = slice(None) if x is None else cols(x, half)
        return src.at[zs, ys, me.c, :, xs]

    def send(self, p, stage):
        order, got, me = self.pieces[p][0], self.pieces[p][4 + stage], self.me
        ss, rs = self.ss, self.rs
        if order[stage] == "z":
            for k in range(1, NZ):
                tz = lax.rem(me.z + k, NZ)
                part = self.region(p, stage, z=tz)
                remote(part, got.at[pl.ds(k, 1)], ss.at[p, stage], rs.at[p, stage], me.dev(z=tz)).start()
            part = self.region(p, stage, z="three")
            self.waits.append(remote(part, part, ss.at[p, stage], rs.at[p, stage], me.dev(c=1 - me.c)))
        else:
            far = 1 - (me.y if order[stage] == "y" else me.x)
            part = self.region(p, stage, **{order[stage]: far})
            dev = me.dev(**{order[stage]: far})
            self.go(remote(part, got, ss.at[p, stage], rs.at[p, stage], dev))

    def receive(self, p, stage):
        order, got = self.pieces[p][0], self.pieces[p][4 + stage]
        if order[stage] == "z":
            got = got.at[pl.ds(1, NZ - 1)]
        self.arrived(got, self.ss.at[p, stage], self.rs.at[p, stage])

    def add(self, p, stage):
        order, _, src, _, *gots = self.pieces[p]
        got, me = gots[stage], self.me
        done = order[: stage + 1]
        half = src.shape[-1] // 2
        xs = cols(me.x, half) if "x" in done else slice(None)
        ys = [(me.y, 0)] if "y" in done else [(y, y) for y in range(NY)]
        if order[stage] == "z":
            for y, i in ys:
                total = src[me.z, y, me.c, :, xs].astype(F32)
                for k in range(1, NZ):
                    total = total + got[k, i].astype(F32)
                src[me.z, y, me.c, :, xs] = total.astype(src.dtype)
            return

        def one(z):
            for y, i in ys:
                src[z, y, me.c, :, xs] = src[z, y, me.c, :, xs] + got[0 if "z" in done else z, i]

        if "z" in done:
            one(me.z)
        else:
            each(NZ, one)

    def step1(self, p):
        src, got = self.pieces[p][2], self.pieces[p][3]
        oc = 1 - self.me.c
        self.go(remote(src.at[:, :, oc], got, self.ds.at[p], self.dr.at[p], self.me.dev(c=oc)))

    def step2(self, p):
        src, got, c = self.pieces[p][2], self.pieces[p][3], self.me.c
        self.arrived(got, self.ds.at[p], self.dr.at[p])

        def one(z):
            for y in range(NY):
                src[z, y, c] = src[z, y, c] + got[z, y]

        each(NZ, one)
        self.send(p, 0)

    def step3(self, p):
        self.receive(p, 0)
        self.add(p, 0)
        self.send(p, 1)

    def step4(self, p):
        self.receive(p, 1)
        self.add(p, 1)
        self.send(p, 2)

    def step5(self, p, counted=None):
        order, dst, src, _, *gots = self.pieces[p]
        me = self.me
        self.receive(p, 2)
        total = src[me.z, me.y, me.c, :, cols(me.x, src.shape[-1] // 2)].astype(F32)
        for k in range(1, NZ) if order[2] == "z" else (0,):
            total = total + gots[2][k, 0].astype(F32)
        dst[...] = total
        total = total[:counted]
        self.squares = self.squares + jnp.sum(total * total, keepdims=True)

    def end(self):
        for copy in self.waits:
            copy.wait_send()


def got_shapes(order, r, w):
    out, done = [], ""
    for axis in order:
        done += axis
        nz = NZ if axis == "z" or "z" not in done else 1
        out.append((nz, 1 if "y" in done else NY, r, w // 2 if "x" in done else w))
    return out


orders = ("zyx", "zyx", "yxz", "yxz", "yxz", "yxz", "yzx", "yzx", "yzx", "yzx", "yxz", "yxz", "yxz", "yxz")


def all_squares(me, net, total, sq4, sq8, sems):
    qs, qr, es, er = sems
    sq4[0] = jnp.broadcast_to(total, (8, 128))
    copies = []
    for k in range(1, NZ):
        copies.append(remote(sq4.at[0], sq4.at[k], qs.at[k], qr.at[k], me.dev(z=lax.rem(me.z + k, NZ))))
    for copy in copies:
        net.go(copy)
    for copy in copies:
        copy.wait_recv()

    def at_z(z):
        out = jnp.zeros((8, 128), F32)
        for k in range(NZ):
            out = out + jnp.where(lax.rem(me.z + NZ - k, NZ) == z, sq4[k], 0.0)
        return out

    sq8[0] = at_z(0) + at_z(1) + at_z(2) + at_z(3)
    copies = []
    for k, dev in enumerate(me.eights(), 1):
        copies.append(remote(sq8.at[0], sq8.at[k], es.at[k], er.at[k], dev))
    for copy in copies:
        net.go(copy)
    for copy in copies:
        copy.wait_recv()

    def at_code(w):
        out = jnp.zeros((8, 128), F32)
        for k in range(8):
            dx, dy, dc = k & 1, (k >> 1) & 1, k >> 2
            src = (
                (me.x + dx - 2 * dx * me.x)
                + 2 * (me.y + dy - 2 * dy * me.y)
                + 4 * (me.c + dc - 2 * dc * me.c)
            )
            out = out + jnp.where(src == w, sq8[k], 0.0)
        return out

    whole = at_code(0)
    for w in range(1, 8):
        whole = whole + at_code(w)
    return whole


def fold(value):
    return jnp.sum(value.reshape(-1, 8, value.shape[-1]), axis=0)


def norm_back_rows(n_rows, get_dy, hat_ref, root_ref, gain, put, acc):
    step = 48

    def body(i):
        at = rows_at(i, step)
        dy, hat = get_dy(i, at), hat_ref[at, :]
        e = dy * gain
        root = root_ref[at, 0:1]
        m1 = jnp.mean(e, axis=-1, keepdims=True)
        m2 = jnp.mean(e * hat, axis=-1, keepdims=True)
        dz = (e - m1 - hat * m2) * root
        acc[0] = acc[0] + fold(dy * hat)
        acc[1] = acc[1] + fold(dy)
        acc[2] = acc[2] + fold(dz)
        hat_ref[at, :] = dz
        put(at, dz)

    each(n_rows // step, body)


def backward_kernel(*refs):
    doc_ids, cotangent, doc_rows = refs[:3]
    (qk_h, va_h, inner_h, outer_h, xt_h, q_h, k_h, v_h, p_h, o_h, xh1_h, r1_h, g_h, gp_h, xh2_h, r2_h, proj_h, vec_h, out_h) = refs[3:22]
    outs = refs[22:32]
    small_r, qk_r, va_r, inner_r, outer_r, dx, peer_out, peer_dx, peer_small, norm_ref = outs
    scr = list(refs[32:])

    def take(n):
        got = scr[:n]
        del scr[:n]
        return got

    (inner, outer, attn, xt, q, k, v, o, xh1, gg, xh2, r2, proj, vec, cls_in, cot, df, dft) = take(18)
    (cls_grad, acc1, acc2, ffacc, vg, early, late) = take(7)
    grads = take(4)
    bufs = take(14 * 4)
    sq4, sq8 = take(2)
    lsem, rsems, xs, xr, qsems = take(1)[0], take(4), *take(2), take(4)
    do, da, dat, h1t, r1 = cot, df, dft, dft, r2
    me = Place()
    mp = me.x
    n_all, width = dx.shape
    n_own = q.shape[0]
    half_seq = n_all - n_own
    seq = 2 * half_seq
    n_full = n_own - half_seq
    full = n_full // seq
    half_ff = inner.shape[-1]
    other = me.dev(x=1 - mp)

    for i in range(4):
        grads.append(inner.at[i // 2, :, :, :, :, pl.ds(width * (i % 2), width)])
    copies = {}

    def load(name, i, src, dst):
        cp = pltpu.make_async_copy(src, dst, lsem.at[i])
        cp.start()
        copies[name] = cp

    def need(*names):
        for name in names:
            copies[name].wait()

    load("vec", 0, vec_h, vec)
    load("proj", 1, proj_h, proj)
    for s in range(full + 1):
        load("cls%d" % s, 2 + s, out_h.at[pl.ds(s * seq, 16)], cls_in.at[s])
    load("cot0", 5, cotangent.at[pl.ds(pl.multiple_of(mp * (n_full + seq), 16), n_full)], cot.at[pl.ds(0, n_full)])
    load("cot1", 6, cotangent.at[pl.ds(pl.multiple_of(n_full + mp * half_seq, 16), half_seq)], cot.at[pl.ds(n_full, half_seq)])
    load("xh2", 7, xh2_h, xh2)
    load("r2", 8, r2_h, r2)
    load("g", 9, g_h, gg.at[pl.ds(0, 2)])
    load("outer", 10, outer_h, outer)
    load("gp", 11, gp_h, gg.at[pl.ds(2, 2)])
    load("xh1", 12, xh1_h, xh1)
    load("inner", 14, inner_h, inner)
    load("attn", 15, va_h.at[1], attn)
    load("o", 16, o_h, o)
    load("q", 17, q_h, q)
    load("k", 18, k_h, k)
    load("v", 19, v_h, v)
    load("xt", 20, xt_h, xt)

    greet(me.others() + me.eights())
    pieces = []
    hr = width // (NZ * NY * NC * NX)
    n_early = early.shape[3]
    hf = half_ff // 2
    dsts, srcs = [], []
    for i, ref in enumerate((outer_r, inner_r)):
        for h in range(2):
            for j in range(2):
                dsts.append(ref.at[h, :, pl.ds(j * (hf // 2), hf // 2)])
                srcs.append(grads[2 * i + h].at[:, :, :, :, pl.ds(j * hf, hf)])
    dsts += [va_r.at[1], va_r.at[0], qk_r.at[0], qk_r.at[1]]
    dsts += [small_r.at[pl.ds(0, n_early)], small_r.at[pl.ds(n_early, hr)]]
    srcs += grads[4:] + [early, late]
    for i in range(14):
        pieces.append((orders[i], dsts[i], srcs[i]) + tuple(bufs[4 * i : 4 * i + 4]))
    net = Reduce(me, pieces, rsems)

    def go(step, *members):
        for piece in members:
            if step == 5 and piece == 12:
                net.step5(piece, hr)
            else:
                (net.step1, net.step2, net.step3, net.step4, net.step5)[step - 1](piece)

    send_out = remote(out_h, peer_out, xs.at[0], xr.at[0], other)
    net.go(send_out)

    vg[...] = jnp.zeros_like(vg)
    early[...] = jnp.zeros_like(early)
    acc1[...] = jnp.zeros_like(acc1)
    acc2[...] = jnp.zeros_like(acc2)
    ffacc[...] = jnp.zeros_like(ffacc)
    need("vec", "proj", *["cls%d" % s for s in range(full + 1)])
    row16 = lax.broadcasted_iota(jnp.int32, (16, 1), 0)
    cls = jnp.zeros((16, width), F32)
    for s in range(full + 1):
        cls = jnp.where(row16 == s, cls_in[s].astype(F32)[0:1], cls)
    cls = cls.astype(BF)
    proj_low = proj[...].astype(BF)
    query = mm(cls, proj_low).astype(BF).astype(F32)
    row8 = lax.broadcasted_iota(jnp.int32, (8, 1), 0)
    dcq = jnp.zeros((16, 128), F32)
    row_grads = []
    cands = doc_ids.shape[1]
    seq_ids = [mp * (full + 1) + s for s in range(full)] + [full]
    for s in range(full + 1):
        docs = doc_rows[seq_ids[s]].astype(F32)
        mine = 1.0 if s < full else jnp.where(mp == 0, 1.0, 0.0)
        query_s = query[s : s + 1]
        score = jnp.sum(query_s * docs, axis=-1, keepdims=True) * retrieval_scale
        e = jnp.exp(score - jnp.max(score, axis=0, keepdims=True))
        soft = e / jnp.sum(e, axis=0, keepdims=True)
        sg = (soft - jnp.where(row8 == 0, 1.0, 0.0)) * (retrieval_scale * mine)
        dcq = jnp.where(row16 == s, jnp.sum(sg * docs, axis=0, keepdims=True), dcq)
        row_grads.append(sg * query_s)
    dcq = dcq.astype(BF)
    cls_grad[...] = mm_nt(dcq, proj_low)
    proj_grad = mm_tn(cls, dcq)
    n_dev = NZ * NY * NC * NX
    table_row = lax.broadcasted_iota(jnp.int32, (TAB_DEV * n_dev // NX, 1), 0)
    table = jnp.zeros((TAB_DEV * n_dev // NX, 128), F32)
    for s in range(full + 1):
        for i in range(cands):
            table = table + jnp.where(table_row == doc_ids[seq_ids[s], i], row_grads[s][i : i + 1], 0.0)
    tr = TAB_DEV // NX
    for d in range(n_dev):
        z, y, c, x = d // 8, d // 4 % 2, d // 2 % 2, d % 2
        l = slice(x * 128, (x + 1) * 128)
        t0 = (d // 2) * TAB_DEV + x * tr
        early[z, y, c, 0:hr, l] = proj_grad[d * hr : (d + 1) * hr]
        early[z, y, c, hr : hr + tr, l] = table[t0 : t0 + tr]
    go(1, 12)

    per = seq // 48
    row48 = lax.broadcasted_iota(jnp.int32, (48, 1), 0)

    def get_dy(i, at):
        first = (row48 == 0) & (lax.rem(i, per) == 0)
        return cot[at, :].astype(F32) + jnp.where(first, cls_grad[pl.ds(i // per, 1), :], 0.0)

    def put_df(at, dz):
        df[at, :] = dz.astype(BF)

    need("cot0", "cot1", "xh2", "r2")
    norm_back_rows(n_own, get_dy, xh2, r2, vec[10:11, :], put_df, acc2)

    def turn(src, dst, n_rows):
        def body(i):
            dst[rows_at(i, 256), 0:n_rows] = jnp.transpose(src[:, lanes(i, 256)])

        each(width // 256, body)

    load("r1", 13, r1_h, r1)
    turn(df, dft, n_own)
    go(2, 12)
    n_tile = 256
    shape5 = (NZ, NY, NC, width // (NZ * NY * NC))

    def weight_grad(left, right, dst, n):
        def body(i):
            r = mm(left(), right(lanes(i, n_tile)))
            dst[:, :, :, :, lanes(i, n_tile)] = r.astype(BF).reshape(shape5 + (n_tile,))

        each(n // n_tile, body)

    need("g")
    for h in range(2):
        weight_grad(lambda: dft[:, 0:n_own], lambda l: gg[h, :, l], grads[h], half_ff)
        go(1, 2 * h, 2 * h + 1)
    go(2, 0, 1)

    need("outer", "gp")
    tile = 240
    tiles = n_own // tile

    def hidden(h):
        def body(i):
            w = flat(outer[h, :, :, :, :, lanes(i, n_tile)])
            for t in range(tiles):
                at = pl.ds(t * tile, tile)
                du = (mm(df[at, :], w) * gg[2 + h, at, lanes(i, n_tile)].astype(F32)).astype(BF)
                gg[2 + h, at, lanes(i, n_tile)] = du
                ffacc[h, :, lanes(i, n_tile)] = ffacc[h, :, lanes(i, n_tile)] + fold(du.astype(F32))

        each(half_ff // n_tile, body)

    hidden(0)
    go(2, 2, 3)
    go(3, 12)
    hidden(1)
    load("p0", 21, p_h.at[0], gg.at[0])
    load("p1", 22, p_h.at[1], gg.at[1])
    load("wq", 23, qk_h.at[0], outer.at[0, :, :, :, :, pl.ds(0, width)])
    load("wk", 24, qk_h.at[1], outer.at[0, :, :, :, :, pl.ds(width, width)])
    load("wv", 25, va_h.at[0], outer.at[1, :, :, :, :, pl.ds(0, width)])
    need("xh1", "r1")

    def h1_turn(i):
        l = lanes(i, 256)
        h1 = (xh1[:, l] * vec[3:4, l] + vec[4:5, l]).astype(BF)
        h1t[rows_at(i, 256), 0:n_own] = jnp.transpose(h1)

    each(width // 256, h1_turn)
    for h in range(2):
        weight_grad(lambda: h1t[:, 0:n_own], lambda l: gg[2 + h, :, l], grads[2 + h], half_ff)
        go(1, 4 + 2 * h, 5 + 2 * h)
    go(2, 4, 5)
    need("inner")

    def hidden_back(i):
        at = rows_at(i, tile)
        d = mm_nt(gg[2, at, :], flat(inner[0])) + mm_nt(gg[3, at, :], flat(inner[1]))
        xh2[at, :] = d + xh2[at, :]

    each(tiles, hidden_back)
    load("p2", 26, p_h.at[2], gg.at[2])
    go(2, 6, 7)
    go(3, 2)

    norm_back_rows(n_own, lambda i, at: xh2[at, :], xh1, r1, vec[3:4, :], put_df, acc1)
    go(3, 3)
    need("attn", "o")

    def mixed_back(i):
        do[:, lanes(i, n_tile)] = mm(da[...], flat(attn[:, :, :, :, lanes(i, n_tile)])).astype(BF)

    each(width // n_tile, mixed_back)
    turn(da, dat, n_own)
    weight_grad(lambda: dat[:, 0:n_own], lambda l: o[:, l], grads[4], width)
    go(1, 8)

    need("q", "k", "v", "p0", "p1", "p2")
    lane = lax.broadcasted_iota(jnp.int32, (1, 128), 1)
    head_lo = jnp.where(lane < HEAD_DIM, 1.0, 0.0)
    head_mask = (head_lo.astype(BF), (1.0 - head_lo).astype(BF))
    scale = HEAD_DIM**-0.5

    def attend(q0, nq, k0, slab):
        at_q = pl.ds(pl.multiple_of(q0, 16), nq)
        at_k = pl.ds(pl.multiple_of(k0, 16), seq)
        for pair in range(2):
            l = lanes(2 * slab + pair)
            qp, kp, vp, dop = q[at_q, l], k[at_k, l], v[at_k, l], do[at_q, l]
            got = []
            for h in range(2):
                j = 384 * (2 * pair + h)
                pb = gg[slab, at_q, j : j + seq]
                p = pb.astype(F32)
                pd = p * mm_nt(dop * head_mask[h], vp)
                ds = (pd - p * jnp.sum(pd, axis=-1, keepdims=True)).astype(BF)
                got.append((mm(ds, kp) * scale, mm_tn(ds, qp) * scale, mm_tn(pb, dop)))
            low = lane < HEAD_DIM
            q[at_q, l] = jnp.where(low, got[0][0], got[1][0]).astype(BF)
            k[at_k, l] = jnp.where(low, got[0][1], got[1][1]).astype(BF)
            v[at_k, l] = jnp.where(low, got[0][2], got[1][2]).astype(BF)

    slabs = p_h.shape[0]

    def tokens_back(at, own):
        d = mm_nt(k[at, :], flat(outer[0, :, :, :, :, width : 2 * width]))
        d = d + mm_nt(v[at, :], flat(outer[1, :, :, :, :, 0:width]))
        if own:
            d = d + mm_nt(q[at, :], flat(outer[0, :, :, :, :, 0:width])) + xh1[at, :]
            o[at, :] = d.astype(BF)
        else:
            df[0:half_seq, :] = d.astype(BF)

    keeps = []

    def send_dx(i, src, at):
        net.go(remote(src, peer_dx.at[at], xs.at[1 + i], xr.at[1 + i], other))
        cp = pltpu.make_async_copy(src, dx.at[at], lsem.at[27 + i])
        cp.start()
        keeps.append(cp)

    need("wq", "wk", "wv")
    for s in range(full):
        for i in range(slabs):
            attend(s * seq, seq, s * seq, i)
            if s == 0:
                (lambda: (go(2, 8), go(4, 12)), lambda: (go(3, 4), go(4, 2)), lambda: (go(3, 0, 1), go(4, 3)))[i]()
            else:
                (lambda: (go(3, 5), go(4, 4)), lambda: None, lambda: go(5, 2, 3))[i]()
        tokens_back(pl.ds(s * seq, seq), True)
        send_dx(s, o.at[pl.ds(s * seq, seq)], pl.ds(s * seq, seq))
    for i in range(slabs):
        attend(n_full, half_seq, n_full, i)
        (lambda: go(3, 6), lambda: None, lambda: (go(3, 7), go(4, 5)))[i]()
    need("xt")
    weight_grad(lambda: xt[...], lambda l: v[:, l], grads[5], width)
    go(1, 9)
    go(5, 4)
    weight_grad(lambda: xt[:, 0:n_own], lambda l: q[:, l], grads[6], width)
    go(1, 10)
    go(2, 9)
    go(4, 0, 1)
    weight_grad(lambda: xt[...], lambda l: k[:, l], grads[7], width)
    go(1, 11)
    go(2, 10)
    tokens_back(pl.ds(n_full, half_seq), True)
    tokens_back(pl.ds(n_own, half_seq), False)
    send_dx(full, o.at[pl.ds(n_full, half_seq)], pl.ds(n_full, half_seq))
    send_dx(full + 1, df.at[pl.ds(0, half_seq)], pl.ds(n_own, half_seq))

    vg[0:1, :] = jnp.sum(q[...].astype(F32), axis=0, keepdims=True)
    vg[1:2, :] = jnp.sum(v[...].astype(F32), axis=0, keepdims=True)
    vg[2:3, :] = jnp.sum(acc1[2], axis=0, keepdims=True)
    vg[3:4, :] = jnp.sum(acc1[0], axis=0, keepdims=True)
    vg[4:5, :] = jnp.sum(acc1[1], axis=0, keepdims=True)
    for h in range(2):
        both = jnp.sum(ffacc[h], axis=0, keepdims=True)
        for x in range(NX):
            for j in range(2):
                at = j * hf + x * (hf // 2)
                vg[5 + NX * x + h : 6 + NX * x + h, j * (hf // 2) : (j + 1) * (hf // 2)] = both[:, at : at + hf // 2]
    vg[9:10, :] = jnp.sum(acc2[2], axis=0, keepdims=True)
    vg[10:11, :] = jnp.sum(acc2[0], axis=0, keepdims=True)
    vg[11:12, :] = jnp.sum(acc2[1], axis=0, keepdims=True)
    turned = jnp.transpose(vg[...])
    for d in range(n_dev):
        z, y, c, x = d // 8, d // 4 % 2, d // 2 % 2, d % 2
        late[z, y, c, :, x * 128 : (x + 1) * 128] = turned[d * hr : (d + 1) * hr]
    go(1, 13)
    go(2, 11)
    go(3, 8)
    go(2, 13)
    go(5, 5)
    go(4, 6, 7)
    go(5, 12, 0, 1)
    go(4, 8)
    go(3, 9)
    go(5, 6, 7)
    go(3, 10)
    go(4, 9)
    go(5, 8)
    go(4, 10)
    go(3, 11)
    go(5, 9)
    go(3, 13)
    go(4, 11)
    go(5, 10)
    go(4, 13)
    go(5, 11, 13)
    net.go(remote(small_r, peer_small, xs.at[5], xr.at[5], other))
    norm_ref[...] = all_squares(me, net, net.squares, sq4, sq8, qsems)
    parts = [pl.ds(0, seq), pl.ds(seq, seq), pl.ds(n_full, half_seq), pl.ds(n_own, half_seq)]
    for i, ref in enumerate([peer_out] + [peer_dx.at[at] for at in parts] + [peer_small]):
        net.arrived(ref, xs.at[i], xr.at[i])
    for cp in keeps:
        cp.wait()
    net.end()


def backward_fast(doc_ids, cotangent, doc_rows, saved, rows):
    (qk, va, inner, outer, xt, q, k, v, p, o, xh1, r1, g, gp, xh2, r2, proj, vec, out_own) = saved
    n_own, width = q.shape
    n_all = k.shape[0]
    half_ff = inner.shape[-1]
    zyc = (NZ, NY, NC)
    hr = rows // NX
    n_early = hr + 8
    small_rows = n_early + hr
    ins = [doc_ids, cotangent, doc_rows] + list(saved)
    out_shape = [
        ((small_rows, 128), F32),
        ((2, rows, width // 2), F32),
        ((2, rows, width // 2), F32),
        ((2, rows, half_ff // 2), F32),
        ((2, rows, half_ff // 2), F32),
        ((n_all, width), BF),
        ((n_own, width), BF),
        ((n_all, width), BF),
        ((small_rows, 128), F32),
        ((8, 128), F32),
    ]
    like = lambda a: (a.shape, a.dtype)
    wide = width // 128 * 128
    scratch = [
        like(inner), like(outer), (va.shape[1:], BF), like(xt), like(q), like(k), like(v), like(o),
        like(xh1), ((4,) + g.shape[1:], BF), like(xh2), like(r2), like(proj), like(vec),
        ((3, 16, width), BF), ((n_own, width), BF), ((n_own, width), BF),
        ((width, wide), BF),
        ((16, width), F32), ((3, 8, width), F32), ((3, 8, width), F32), ((2, 8, half_ff), F32),
        ((128, width), F32), (zyc + (n_early, 256), F32), (zyc + (hr, 256), F32),
    ]
    sizes = [half_ff] * 4 + [width] * 4
    scratch += [(zyc + (rows, w), BF) for w in sizes[:4]]
    smalls = [(n_early, 256, F32), (hr, 256, F32)]
    for i, (r, w, dt) in enumerate([(rows, width, BF)] * 12 + smalls):
        scratch += [((NZ, NY, r, w), dt)] + [(shape, dt) for shape in got_shapes(orders[i], r, w)]
    scratch += [((NZ, 8, 128), F32), ((8, 8, 128), F32)]
    vm = pl.BlockSpec(memory_space=pltpu.VMEM)
    hb = pl.BlockSpec(memory_space=ANY)
    sm = pl.BlockSpec(memory_space=pltpu.SMEM)
    n = 14
    return pl.pallas_call(
        backward_kernel,
        out_shape=[jax.ShapeDtypeStruct(s, d) for s, d in out_shape],
        in_specs=[sm, hb, vm] + [hb] * 19,
        out_specs=[vm] * 5 + [hb, hb, hb, vm, vm],
        scratch_shapes=[pltpu.VMEM(s, d) for s, d in scratch]
        + [
            dma(31), dma(n), dma(n), dma(n, 3), dma(n, 3),
            dma(6), dma(6), dma(NZ), dma(NZ), dma(8), dma(8),
        ],
        compiler_params=pltpu.CompilerParams(
            collective_id=2, has_side_effects=True, vmem_limit_bytes=63 * 2**20
        ),
        name="backward",
    )(*ins)


def finish_kernel(*refs):
    small_r, peer_small, qk_r, va_r, inner_r, outer_r, total = refs[:7]
    out_own, peer_out, dx, peer_dx = refs[7:11]
    params = [refs[11 + 3 * i : 14 + 3 * i] for i in range(6)]
    outs = refs[29:51]
    turn, sem, lo, hi, mid = refs[51:]
    out_tokens, input_grad, norm = outs[0:3]
    news = [outs[3 + 3 * i : 6 + 3 * i] for i in range(6)]
    table_grad = outs[21]
    mp = lax.axis_index("mp")
    n_own = out_own.shape[0]
    n_all = dx.shape[0]
    half_seq = n_all - n_own
    n_full = n_own - half_seq
    seq = 2 * half_seq
    copies = []
    for i, (src, first) in enumerate(((out_own, mp), (peer_out, 1 - mp))):
        at = pl.multiple_of(first * (n_full + seq), 16)
        copies.append((src.at[pl.ds(0, n_full)], out_tokens.at[pl.ds(at, n_full)]))
        at = pl.multiple_of(n_full + first * half_seq, 16)
        copies.append((src.at[pl.ds(n_full, half_seq)], out_tokens.at[pl.ds(at, half_seq)]))
    copies = [pltpu.make_async_copy(s, d, sem.at[i]) for i, (s, d) in enumerate(copies)]
    for cp in copies:
        cp.start()
    lo[...] = dx[0:n_full].astype(F32)
    hi[...] = peer_dx[0:n_full].astype(F32)
    own_mid = dx[n_full:n_own].astype(F32) + peer_dx[n_own:n_all].astype(F32)
    peer_mid = peer_dx[n_full:n_own].astype(F32) + dx[n_own:n_all].astype(F32)
    mid[pl.ds(pl.multiple_of(mp * half_seq, 16), half_seq)] = own_mid
    mid[pl.ds(pl.multiple_of((1 - mp) * half_seq, 16), half_seq)] = peer_mid
    grads = (
        (lo, pl.multiple_of(mp * (n_full + seq), 16), n_full),
        (hi, pl.multiple_of((1 - mp) * (n_full + seq), 16), n_full),
        (mid, n_full, seq),
    )
    for i, (src, at, n) in enumerate(grads):
        cp = pltpu.make_async_copy(src, input_grad.at[pl.ds(at, n)], sem.at[4 + i])
        cp.start()
        copies.append(cp)

    root = jnp.sqrt(total[...])
    norm[0, 0] = jnp.max(root)
    clip = clip_norm / jnp.maximum(root[0:1, 0:1], clip_norm)
    hf = inner_r.shape[-1]
    hr = params[4][0].shape[0] // 2
    nvec, nlane = params[5][0].shape
    tr = table_grad.shape[0] // 2

    def adam(which, at, g, dec, rate):
        w, m, s = (ref[at] for ref in params[which])
        for ref, new in zip(news[which], adamw_update(w, m, s, g * clip, dec, rate)):
            ref[at] = new

    for j in range(3):
        g = qk_r[j] if j < 2 else va_r[0]
        adam(0, (j,), g, decay_rate, learn_rate)
    adam(1, (slice(None), slice(None)), va_r[1], decay_rate, learn_rate)
    for which, ref in ((2, inner_r), (3, outer_r)):
        for h in range(2):
            adam(which, (slice(None), slice(h * hf, (h + 1) * hf)), ref[h], decay_rate, learn_rate)
    turn[...] = jnp.zeros_like(turn)
    turn[0:nlane] = small_r[hr + 8 : hr + 8 + nlane]
    adam(5, (slice(None), slice(None)), jnp.transpose(turn[...])[0:nvec, 0:nlane], 0.0, vector_rate)
    for block, first in ((small_r, mp), (peer_small, 1 - mp)):
        at = pl.ds(pl.multiple_of(first * hr, 8), hr)
        adam(4, (at, slice(None)), block[0:hr], decay_rate, learn_rate)
    own_t, peer_t = small_r[hr : hr + tr], peer_small[hr : hr + tr]
    table_grad[0:tr] = jnp.where(mp == 0, own_t, peer_t)
    table_grad[tr : 2 * tr] = jnp.where(mp == 0, peer_t, own_t)
    for cp in copies:
        cp.wait()


def finish_fast(reduced, out_own, params, n_rows):
    (small_r, qk_r, va_r, inner_r, outer_r, dx, peer_out, peer_dx, peer_small, total) = reduced
    n_own, width = out_own.shape
    n_all = dx.shape[0]
    half_seq = n_all - n_own
    like = lambda a: jax.ShapeDtypeStruct(a.shape, a.dtype)
    vm = pl.BlockSpec(memory_space=pltpu.VMEM)
    hb = pl.BlockSpec(memory_space=ANY)
    sm = pl.BlockSpec(memory_space=pltpu.SMEM)
    out_shape = [
        jax.ShapeDtypeStruct((n_rows, width), BF),
        jax.ShapeDtypeStruct((n_rows, width), F32),
        jax.ShapeDtypeStruct((1, 1), F32),
    ]
    out_shape += [like(a) for a in params] + [jax.ShapeDtypeStruct((TAB_DEV, 128), F32)]
    n_full = n_own - half_seq
    outs = pl.pallas_call(
        finish_kernel,
        out_shape=out_shape,
        in_specs=[vm] * 29,
        out_specs=[hb, hb, sm] + [vm] * 19,
        scratch_shapes=[
            pltpu.VMEM((128, 128), F32),
            dma(7),
            pltpu.VMEM((n_full, width), F32),
            pltpu.VMEM((n_full, width), F32),
            pltpu.VMEM((2 * half_seq, width), F32),
        ],
        compiler_params=pltpu.CompilerParams(vmem_limit_bytes=63 * 2**20),
        name="finish",
    )(small_r, peer_small, qk_r, va_r, inner_r, outer_r, total, out_own, peer_out, dx, peer_dx, *params)
    return tuple(outs[:2]) + (outs[2].reshape(()),) + tuple(outs[3:])


def gather_plain(shards, small, rows):
    def both(v, axis):
        v = lax.all_gather(v, "dp", axis=axis, tiled=True)
        return lax.all_gather(v, "mp", axis=2, tiled=True)

    return [both(small[None], 0)] + [both(v, 1) for v in shards]


def reduce_plain(grads, small, own_out, own_dx, rows):
    def both(v, axis, wide):
        v = lax.psum_scatter(v.astype(F32), "mp", scatter_dimension=wide, tiled=True)
        return lax.psum_scatter(v, "dp", scatter_dimension=axis, tiled=True)

    small_sum = both(small, 0, 2)[0]
    sums = [both(g, 1, 2) for g in grads]
    ox = 1 - lax.axis_index("mp")
    swap = [(0, 1), (1, 0)]
    peer_out = lax.ppermute(own_out, "mp", swap)
    peer_dx = lax.ppermute(own_dx, "mp", swap)
    peer_small = lax.ppermute(small_sum, "mp", swap)
    squares = sum(squared(g) for g in sums) + squared(small_sum[:-4])
    total = lax.psum(squares, ("dp", "mp"))
    return [small_sum] + sums + [peer_out, peer_dx, peer_small, jnp.full((8, 128), total)]


def forward_plain(lengths, tokens, w_qkv, w_attn, w_inner, w_outer, w_proj, vectors):
    mp = lax.axis_index("mp")
    n_dp = lax.axis_size("dp")
    seqs = lengths.shape[0]
    all_rows, width = tokens.shape
    seq_len = all_rows // seqs
    full = seqs // 2
    n_full, n_half = full * seq_len, seq_len // 2
    n_own = n_full + n_half
    heads = width // HEAD_DIM
    rows, half_ff = w_qkv.shape[1], w_inner.shape[1]
    nvec, vec_lanes = vectors.shape
    half_rows = rows // 2
    score_scale = HEAD_DIM ** (-0.5)

    def two(v):
        return v.reshape(rows, 2, half_ff // 2).transpose(1, 0, 2)

    qk_s = w_qkv[:2].astype(BF)
    va_s = jnp.stack([w_qkv[2], w_attn]).astype(BF)
    vec_pad = jnp.pad(vectors, ((0, 0), (0, 128 - vec_lanes)))
    proj_half = lax.dynamic_slice_in_dim(w_proj, mp * half_rows, half_rows, 0)
    small_s = jnp.concatenate([proj_half, vec_pad], axis=0)
    small_g, qk, va, inner, outer = gather_plain(
        [qk_s, va_s, two(w_inner.astype(BF)), two(w_outer.astype(BF))], small_s, rows
    )
    small_g = small_g.reshape(n_dp, half_rows + nvec, 2, 128)
    proj = small_g[:, :half_rows].transpose(0, 2, 1, 3).reshape(width, 128)
    vec = small_g[:, half_rows:, :, :vec_lanes].transpose(1, 0, 2, 3).reshape(nvec, width)
    ff_rows = nvec - 8
    b_inner = vec[5 : 5 + ff_rows].reshape(2, 2, half_ff // 2).transpose(1, 0, 2).reshape(2, half_ff)

    a0 = mp * (n_full + seq_len)
    h0 = n_full + mp * n_half
    o0 = n_full + (1 - mp) * n_half
    x_all = jnp.concatenate(
        [
            lax.dynamic_slice_in_dim(tokens, a0, n_full, 0),
            lax.dynamic_slice_in_dim(tokens, h0, n_half, 0),
            lax.dynamic_slice_in_dim(tokens, o0, n_half, 0),
        ]
    )
    x_own = x_all[:n_own]
    my_seqs = jnp.concatenate([mp * (full + 1) + jnp.arange(full), jnp.array([full])])
    my_len = lengths[my_seqs]
    pos = jnp.arange(seq_len)
    pos_last = jnp.where(pos < n_half, pos + mp * n_half, pos - n_half + (1 - mp) * n_half)
    valids = (pos[None, :] < my_len[:full, None], pos_last[None, :] < my_len[full:, None])

    q = (jnp.dot(x_own, qk[0], preferred_element_type=F32) + vec[0]).astype(BF)
    k = jnp.dot(x_all, qk[1], preferred_element_type=F32).astype(BF)
    v = (jnp.dot(x_all, va[0], preferred_element_type=F32) + vec[1]).astype(BF)
    probs, outs = [], []
    for qh, kh, vh, valid in zip(*(halves(t, n_full, seq_len) for t in (q, k, v)), valids):
        s = jnp.einsum("gqhe,gkhe->ghqk", qh, kh, preferred_element_type=F32) * score_scale
        s = jnp.where(valid[:, None, None, :], s, -1000000000.0)
        pb = jax.nn.softmax(s, axis=-1).astype(BF)
        o = jnp.einsum("ghqk,gkhe->gqhe", pb, vh, preferred_element_type=F32)
        outs.append(o.reshape(-1, width).astype(BF))
        probs.append(pb.reshape((-1,) + pb.shape[2:]))
    mixed = jnp.concatenate(outs)

    def norm(z):
        centred = z - jnp.mean(z, axis=-1, keepdims=True)
        root = lax.rsqrt(jnp.mean(centred * centred, axis=-1, keepdims=True) + ln_epsilon)
        return centred * root, jnp.broadcast_to(root, (n_own, 128))

    attn = jnp.einsum("te,de->td", mixed, va[1], preferred_element_type=F32)
    xh1, r1 = norm(x_own.astype(F32) + attn + vec[2])
    h1 = xh1 * vec[3] + vec[4]
    u = jnp.einsum("td,hdf->htf", h1.astype(BF), inner, preferred_element_type=F32) + b_inner[:, None, :]
    tail = 0.5 * (1.0 + lax.erf(u * 0.7071067811865476))
    g = (u * tail).astype(BF)
    gp = (tail + u * (0.3989422804014327 * jnp.exp(-0.5 * u * u))).astype(BF)
    f = jnp.einsum("htf,hdf->td", g, outer, preferred_element_type=F32)
    xh2, r2 = norm(h1 + f + vec[5 + ff_rows])
    out_own = (xh2 * vec[6 + ff_rows] + vec[7 + ff_rows]).astype(BF)
    vec = jnp.pad(vec, ((0, 16 - nvec), (0, 0)))
    return [qk, va, inner, outer, x_all, q, k, v, *probs, mixed, xh1, r1, g, gp, xh2, r2, proj, vec, out_own]


def halves(t, n_full, seq_len):
    heads = t.shape[1] // HEAD_DIM
    last = t.shape[0] - n_full
    return (
        t[:n_full].reshape(n_full // seq_len, seq_len, heads, HEAD_DIM),
        t[n_full:].reshape(1, last, heads, HEAD_DIM),
    )


def pass_plain(lengths, tokens, cotangent, doc_ids, doc_rows, w_qkv, w_attn, w_inner, w_outer, w_proj, vectors):
    mp = lax.axis_index("mp")
    n_dp, n_mp = lax.axis_size("dp"), lax.axis_size("mp")
    seqs = lengths.shape[0]
    all_rows, width = tokens.shape
    seq_len = all_rows // seqs
    full = seqs // 2
    n_full, n_half = full * seq_len, seq_len // 2
    n_own = n_full + n_half
    rows, half_ff = w_qkv.shape[1], w_inner.shape[1]
    half_rows = rows // 2
    nvec, vec_lanes = vectors.shape
    ff_rows = nvec - 8
    score_scale = HEAD_DIM ** (-0.5)

    saved = forward_plain(lengths, tokens, w_qkv, w_attn, w_inner, w_outer, w_proj, vectors)
    (qk, va, inner, outer, x_all, q, k, v, p_ab, p_c, mixed, xh1, r1, act_low, slope, xh2, r2, proj, vec, out_own) = saved
    qk = qk.reshape(2, width, width)
    va = va.reshape(2, width, width)
    inner = inner.reshape(2, width, half_ff)
    outer = outer.reshape(2, width, half_ff)
    x_own = x_all[:n_own]
    proj = proj.astype(BF)
    a0 = mp * (n_full + seq_len)
    h0 = n_full + mp * n_half
    cot = jnp.concatenate(
        [lax.dynamic_slice_in_dim(cotangent, a0, n_full, 0), lax.dynamic_slice_in_dim(cotangent, h0, n_half, 0)]
    )
    my_seqs = jnp.concatenate([mp * (full + 1) + jnp.arange(full), jnp.array([full])])

    n_mine = full + 1
    mine = jnp.where((jnp.arange(n_mine) < full) | (mp == 0), 1.0, 0.0).astype(F32)
    cls_low = out_own[:: seq_len][:n_mine]
    docs = doc_rows[my_seqs].astype(F32)
    ids = doc_ids[my_seqs]
    query = jnp.dot(cls_low, proj, preferred_element_type=F32).astype(BF)
    query_float = query.astype(F32)
    doc_scores = jnp.einsum("gp,gkp->gk", query_float, docs, precision=highest_mode) * retrieval_scale
    soft = jax.nn.softmax(doc_scores, axis=-1)
    target = (jnp.arange(doc_scores.shape[1]) == 0).astype(F32)
    score_grad = (soft - target[None, :]) * retrieval_scale * mine[:, None]
    query_grad = jnp.einsum("gk,gkp->gp", score_grad, docs, precision=highest_mode).astype(BF)
    row_grads = score_grad[:, :, None] * query_float[:, None, :]
    cls_grad = jnp.einsum("gp,dp->gd", query_grad, proj, preferred_element_type=F32)
    proj_grad = jnp.einsum("gd,gp->dp", cls_low, query_grad, preferred_element_type=F32)
    table_rows = TAB_DEV * n_dp
    one_hot = (jnp.arange(table_rows)[:, None] == ids.reshape(1, -1)).astype(F32)
    table_local = jnp.dot(one_hot, row_grads.reshape(-1, row_grads.shape[2]), precision=highest_mode)

    def norm_back(dy, hat, root, gain):
        e = dy * gain
        back_ = e - jnp.mean(e, axis=-1, keepdims=True) - hat * jnp.mean(e * hat, axis=-1, keepdims=True)
        return back_ * root[:, :1], jnp.sum(dy * hat, axis=0), jnp.sum(dy, axis=0)

    dy = cot.astype(F32)
    first_rows = jnp.arange(n_mine) * seq_len
    dy = dy.at[first_rows].add(cls_grad)
    dz2, dg2, dc2 = norm_back(dy, xh2, r2, vec[6 + ff_rows])
    df = dz2.astype(BF)
    dg = jnp.einsum("td,hdf->htf", df, outer, preferred_element_type=F32)
    g_outer = jnp.einsum("td,htf->hdf", df, act_low, preferred_element_type=F32).astype(BF)
    du = (dg * slope.astype(F32)).astype(BF)
    normed_low = (xh1 * vec[3] + vec[4]).astype(BF)
    g_inner = jnp.einsum("td,htf->hdf", normed_low, du, preferred_element_type=F32).astype(BF)
    dh1 = jnp.einsum("htf,hdf->td", du, inner, preferred_element_type=F32) + dz2
    dz1, dg1, dc1 = norm_back(dh1, xh1, r1, vec[3])
    da = dz1.astype(BF)
    do = jnp.dot(da, va[1], preferred_element_type=F32).astype(BF)
    g_attn = jnp.einsum("td,te->de", da, mixed, preferred_element_type=F32)
    dqs, dks, dvs = [], [], []
    probs_of = (p_ab.reshape(full, -1, seq_len, seq_len), p_c.reshape(1, -1, n_half, seq_len))
    for qh, kh, vh, doh, pb in zip(*(halves(t, n_full, seq_len) for t in (q, k, v, do)), probs_of):
        probs = pb.astype(F32)
        dp_ = jnp.einsum("gqhe,gkhe->ghqk", doh, vh, preferred_element_type=F32)
        delta = jnp.sum(probs * dp_, axis=-1, keepdims=True)
        ds_ = (probs * (dp_ - delta)).astype(BF)
        dqs.append((jnp.einsum("ghqk,gkhe->gqhe", ds_, kh, preferred_element_type=F32) * score_scale).reshape(-1, width))
        dks.append((jnp.einsum("ghqk,gqhe->gkhe", ds_, qh, preferred_element_type=F32) * score_scale).reshape(-1, width))
        dvs.append(jnp.einsum("ghqk,gqhe->gkhe", pb, doh, preferred_element_type=F32).reshape(-1, width))
    dq = jnp.concatenate(dqs).astype(BF)
    dk = jnp.concatenate(dks).astype(BF)
    dv = jnp.concatenate(dvs).astype(BF)
    g_q = jnp.einsum("td,te->de", x_own, dq, preferred_element_type=F32)
    g_k = jnp.einsum("td,te->de", x_all, dk, preferred_element_type=F32)
    g_v = jnp.einsum("td,te->de", x_all, dv, preferred_element_type=F32)
    g_qk = jnp.stack([g_q, g_k]).astype(BF)
    g_va = jnp.stack([g_v, g_attn]).astype(BF)
    dx_own = jnp.einsum("te,de->td", dq, qk[0], preferred_element_type=F32) + dz1
    dx_all = jnp.einsum("te,de->td", dk, qk[1], preferred_element_type=F32)
    dx_all = dx_all + jnp.einsum("te,de->td", dv, va[0], preferred_element_type=F32)
    dx = jnp.concatenate([dx_all[:n_own] + dx_own, dx_all[n_own:]]).astype(BF)
    db_inner = jnp.sum(du.astype(F32), axis=1)
    db_inner = db_inner.reshape(2, 2, half_ff // 2).transpose(1, 0, 2).reshape(ff_rows, width)
    vec_grad = jnp.concatenate(
        [
            jnp.stack(
                [
                    jnp.sum(dq.astype(F32), axis=0),
                    jnp.sum(dv.astype(F32), axis=0),
                    jnp.sum(dz1, axis=0),
                    dg1,
                    dc1,
                ]
            ),
            db_inner,
            jnp.stack([jnp.sum(dz2, axis=0), dg2, dc2]),
        ]
    )
    vg = vec_grad.reshape(nvec, n_dp, 2, vec_lanes).transpose(1, 0, 2, 3)
    vg = jnp.pad(vg, ((0, 0), (0, 0), (0, 0), (0, 128 - vec_lanes))).reshape(n_dp, nvec, 256)
    pg = proj_grad.reshape(n_dp, 2, half_rows, 128).transpose(0, 2, 1, 3).reshape(n_dp, half_rows, 256)
    tg = table_local.reshape(n_dp, 2, TAB_DEV // 2, 128).transpose(0, 2, 1, 3).reshape(n_dp, TAB_DEV // 2, 256)
    small = jnp.concatenate([pg, vg, tg], axis=1)

    return out_own, dx, *reduce_plain([g_qk, g_va, g_inner, g_outer], small, out_own, dx, rows)


def local(
    tokens, cotangent, lengths, doc_ids, doc_rows,
    w_qkv, m_qkv, v_qkv, w_attn, m_attn, v_attn, w_inner, m_inner, v_inner,
    w_outer, m_outer, v_outer, w_proj, m_proj, v_proj, vectors, m_vectors, v_vectors,
):
    mp = lax.axis_index("mp")
    n_dp, n_mp = lax.axis_size("dp"), lax.axis_size("mp")
    fast = n_dp == NZ * NY * NC and n_mp == NX
    seqs = lengths.shape[0]
    all_rows, width = tokens.shape
    seq_len = all_rows // seqs
    full = seqs // 2
    n_full, n_half = full * seq_len, seq_len // 2
    n_own = n_full + n_half
    rows, half_ff = w_qkv.shape[1], w_inner.shape[1]
    half_rows = rows // 2
    nvec, vec_lanes = vectors.shape
    ff_rows = nvec - 8
    score_scale = HEAD_DIM ** (-0.5)

    if fast:
        saved = forward_fast(lengths, tokens, w_qkv, w_attn, w_inner, w_outer, w_proj, vectors)
        reduced = backward_fast(doc_ids, cotangent, doc_rows, saved, rows)
        params = (w_qkv, m_qkv, v_qkv, w_attn, m_attn, v_attn, w_inner, m_inner, v_inner)
        params += (w_outer, m_outer, v_outer, w_proj, m_proj, v_proj, vectors, m_vectors, v_vectors)
        return finish_fast(reduced, saved[-1], params, all_rows)
    if not fast:
        (out_own, dx, small_r, qk_r, va_r, inner_r, outer_r, peer_out, peer_dx, peer_small, total) = pass_plain(
            lengths, tokens, cotangent, doc_ids, doc_rows, w_qkv, w_attn, w_inner, w_outer, w_proj, vectors
        )
        vector_r = small_r[half_rows : half_rows + nvec, :vec_lanes]
        table_at = half_rows + nvec

    def whole_rows(own, peer):
        lo = jnp.where(mp == 0, own[:n_own], peer[:n_own])
        hi = jnp.where(mp == 0, peer[:n_own], own[:n_own])
        return lo, hi

    lo, hi = whole_rows(out_own, peer_out)
    out_tokens = jnp.concatenate([lo, hi[n_full:], hi[:n_full]])
    lo, hi = whole_rows(dx.astype(F32), peer_dx.astype(F32))
    tail = jnp.where(mp == 0, dx[n_own:], peer_dx[n_own:]).astype(F32)
    tail_hi = jnp.where(mp == 0, peer_dx[n_own:], dx[n_own:]).astype(F32)
    input_grad = jnp.concatenate(
        [lo[:n_full], lo[n_full:] + tail_hi, hi[n_full:] + tail, hi[:n_full]]
    )

    def both_halves(at, count):
        mine_, peer_ = small_r[at : at + count], peer_small[at : at + count]
        return jnp.concatenate(
            [jnp.where(mp == 0, mine_, peer_), jnp.where(mp == 0, peer_, mine_)]
        )

    proj_r = both_halves(0, half_rows)
    table_grad = both_halves(table_at, TAB_DEV // 2)
    qkv_r = jnp.stack([qk_r[0], qk_r[1], va_r[0]])
    attn_r = va_r[1]

    def back(v):
        return v.transpose(1, 0, 2).reshape(rows, half_ff)

    inner_r, outer_r = back(inner_r), back(outer_r)
    grad_norm = jnp.sqrt(total[0, 0])
    clip = clip_norm / jnp.maximum(grad_norm, clip_norm)
    results = [out_tokens, input_grad, grad_norm]
    for w, m, s, g, dec, rate in (
        (w_qkv, m_qkv, v_qkv, qkv_r, decay_rate, learn_rate),
        (w_attn, m_attn, v_attn, attn_r, decay_rate, learn_rate),
        (w_inner, m_inner, v_inner, inner_r, decay_rate, learn_rate),
        (w_outer, m_outer, v_outer, outer_r, decay_rate, learn_rate),
        (w_proj, m_proj, v_proj, proj_r, decay_rate, learn_rate),
        (vectors, m_vectors, v_vectors, vector_r, 0.0, vector_rate),
    ):
        results += list(adamw_update(w, m, s, g * clip, dec, rate))
    return tuple(results) + (table_grad,)


def solution(mesh):
    mat = P("dp", "mp")
    rep = P("dp", None)
    qkv = P(None, "dp", "mp")
    vec = P(None, ("dp", "mp"))
    placed = (rep, rep, P("dp"), rep, P("dp", None, None), qkv, qkv, qkv)
    placed += (mat,) * 9 + (rep,) * 3 + (vec,) * 3
    given = (rep, rep, P(), qkv, qkv, qkv) + (mat,) * 9 + (rep,) * 3 + (vec,) * 3 + (rep,)
    return jax.shard_map(local, mesh=mesh, in_specs=placed, out_specs=given, check_vma=False)
```

```python
import functools

import jax
import jax.numpy as jnp
from jax import lax
from jax.experimental import pallas as pl
from jax.experimental.pallas import tpu as pltpu
from jax.sharding import PartitionSpec as P

HEAD_DIM = 64
STEP = 10
TAB_DEV = 8
MESH = pl.DeviceIdType.MESH
ANY = pl.ANY
BF = jnp.bfloat16
F32 = jnp.float32
NZ, NY, NC, NX = 4, 2, 2, 2

highest_mode = lax.Precision.HIGHEST
retrieval_scale = 0.17677669529663687
ln_epsilon = 1e-12
beta_first = 0.9
beta_second = 0.999
learn_rate = 0.05
vector_rate = 0.5
decay_rate = 0.01
adam_epsilon = 1e-08
clip_norm = 1.0


def layer_norm(values, gain_row, shift_row):
    centre = jnp.mean(values, axis=-1, keepdims=True)
    centred = values - centre
    spread = jnp.mean(centred * centred, axis=-1, keepdims=True)
    return centred * lax.rsqrt(spread + ln_epsilon) * gain_row + shift_row


def gelu_exact(values):
    return jax.nn.gelu(values, approximate=False)


def adamw_update(weight, moment, second, gradient, decay_factor, step_rate):
    moment_new = beta_first * moment + (1.0 - beta_first) * gradient
    second_new = beta_second * second + (1.0 - beta_second) * gradient * gradient
    first_hat = moment_new / (1.0 - beta_first**STEP)
    second_hat = second_new / (1.0 - beta_second**STEP)
    weight_new = weight - step_rate * (
        first_hat / (jnp.sqrt(second_hat) + adam_epsilon) + decay_factor * weight
    )
    return (moment_new, second_new, weight_new)


def squared(values):
    return jnp.sum(values * values)


class Place:
    def __init__(self):
        dp = lax.axis_index("dp")
        self.x = lax.axis_index("mp")
        self.c = lax.rem(dp, NC)
        self.y = lax.rem(dp // NC, NY)
        self.z = dp // (NC * NY)

    def dev(self, z=None, y=None, c=None, x=None):
        z = self.z if z is None else z
        y = self.y if y is None else y
        c = self.c if c is None else c
        x = self.x if x is None else x
        return ((z * NY + y) * NC + c, x)

    def others(self):
        out = [self.dev(z=lax.rem(self.z + k, NZ)) for k in range(1, NZ)]
        out.append(self.dev(x=1 - self.x))
        out.append(self.dev(y=1 - self.y))
        out.append(self.dev(c=1 - self.c))
        return out

    def eights(self):
        out = []
        for k in range(1, 8):
            dx, dy, dc = k & 1, (k >> 1) & 1, k >> 2
            out.append(
                self.dev(
                    x=self.x + dx - 2 * dx * self.x,
                    y=self.y + dy - 2 * dy * self.y,
                    c=self.c + dc - 2 * dc * self.c,
                )
            )
        return out


def greet(devices):
    barrier = pltpu.get_barrier_semaphore()
    for d in devices:
        pl.semaphore_signal(barrier, inc=1, device_id=d, device_id_type=MESH)
    pl.semaphore_wait(barrier, len(devices))


def greet_send(devices):
    barrier = pltpu.get_barrier_semaphore()
    for d in devices:
        pl.semaphore_signal(barrier, inc=1, device_id=d, device_id_type=MESH)


def greet_wait(count):
    pl.semaphore_wait(pltpu.get_barrier_semaphore(), count)


def remote(src, dst, ssem, rsem, dev):
    return pltpu.make_async_remote_copy(
        src_ref=src, dst_ref=dst, send_sem=ssem, recv_sem=rsem, device_id=dev, device_id_type=MESH
    )


def cols(x, half):
    return pl.ds(pl.multiple_of(x * half, 128), half)


def dma(*shape):
    return pltpu.SemaphoreType.DMA(shape)


def mm(a, b):
    return jnp.dot(a, b, preferred_element_type=F32)


def mm_nt(a, b):
    return lax.dot_general(a, b, (((1,), (1,)), ((), ())), preferred_element_type=F32)


def mm_tn(a, b):
    return lax.dot_general(a, b, (((0,), (0,)), ((), ())), preferred_element_type=F32)


def flat(value):
    return value.reshape(-1, value.shape[-1])


def lanes(i, n=128):
    return pl.ds(pl.multiple_of(i * n, 128), n)


def rows_at(i, n, at=0):
    return pl.ds(pl.multiple_of(at + i * n, 16), n)


def each(n, body):
    lax.fori_loop(0, n, lambda i, c: (body(i), c)[1], 0)


gather_orders = ("zxy", "zxy", "zyx", "zxy", "zyx", "zxy", "zyx", "zxy", "zyx", "zxy", "zyx", "zxy", "xyz", "yxz", "zyx")


def stack_heads(pair, wide=None):
    low = jnp.where(lax.broadcasted_iota(jnp.int32, (1, 128), 1) < HEAD_DIM, 1.0, 0.0)
    parts = []
    for mask in (low, 1.0 - low):
        parts.append(pair * mask.astype(BF))
        if wide is not None:
            parts.append(jnp.zeros((wide - pair.shape[0], 128), BF))
    return jnp.concatenate(parts, axis=0)


class Gather:
    def __init__(self, me, pieces, sems):
        self.me, self.pieces = me, pieces
        self.lsem, self.ss, self.rs, self.ds, self.dr = sems
        self.waits, self.locs = [], {}

    def region(self, p, stage, c, **at):
        dst, me, done = self.pieces[p][1], self.me, gather_orders[p][:stage]
        half = dst.shape[-1] // 2
        z = at.get("z", None if "z" in done else me.z)
        y = at.get("y", None if "y" in done else me.y)
        x = at.get("x", None if "x" in done else me.x)
        zs = slice(None) if z is None else pl.ds(0, NZ - 1) if z == "three" else pl.ds(z, 1)
        ys = slice(None) if y is None else pl.ds(y, 1)
        xs = slice(None) if x is None else cols(x, half)
        return dst.at[zs, ys, c, :, xs]

    def bulk(self, p, stage, c):
        axis = gather_orders[p][stage]
        return self.region(p, stage, c, z="three") if axis == "z" else self.coming(p, stage, c)[0]

    def coming(self, p, stage, c):
        me, axis = self.me, gather_orders[p][stage]
        if axis == "z":
            return [self.region(p, stage, c, z=lax.rem(me.z + NZ - k, NZ)) for k in range(1, NZ)]
        return [self.region(p, stage, c, **{axis: 1 - (me.y if axis == "y" else me.x)})]

    def send(self, p, stage):
        me, axis = self.me, gather_orders[p][stage]
        src, dst = self.pieces[p]
        if stage == 0:
            to = dst.at[me.z, me.y, me.c, :, cols(me.x, dst.shape[-1] // 2)]
        else:
            src = to = self.region(p, stage, me.c)
        if axis == "z":
            devs = [me.dev(z=lax.rem(me.z + k, NZ)) for k in range(1, NZ)]
        else:
            devs = [me.dev(**{axis: 1 - (me.y if axis == "y" else me.x)})]
        for dev in devs:
            remote(src, to, self.ss.at[p, stage], self.rs.at[p, stage], dev).start()
        self.waits.append((self.bulk(p, stage, me.c), self.ss.at[p, stage]))

    def arrived(self, ref, sem):
        remote(ref, ref, sem, sem, self.me.dev(c=1 - self.me.c)).wait_recv()

    def receive(self, p, stage):
        self.arrived(self.bulk(p, stage, self.me.c), self.rs.at[p, stage])

    def crossing(self, p, stage, c):
        if stage == 0:
            ref = self.region(p, 1, c)
            return [ref], ref
        return self.coming(p, stage, c), self.bulk(p, stage, c)

    def cross(self, p, stage):
        refs, whole = self.crossing(p, stage, self.me.c)
        for ref in refs:
            remote(ref, ref, self.ds.at[p, stage], self.dr.at[p, stage], self.me.dev(c=1 - self.me.c)).start()
        self.waits.append((whole, self.ds.at[p, stage]))

    def step1(self, p):
        me = self.me
        src, dst = self.pieces[p]
        self.send(p, 0)
        blk = dst.at[me.z, me.y, me.c, :, cols(me.x, dst.shape[-1] // 2)]
        loc = pltpu.make_async_copy(src, blk, self.lsem.at[p])
        loc.start()
        self.locs[p] = loc

    def step2(self, p):
        self.locs[p].wait()
        self.receive(p, 0)
        self.send(p, 1)
        self.cross(p, 0)

    def step3(self, p):
        self.receive(p, 1)
        self.send(p, 2)
        self.cross(p, 1)

    def step4(self, p):
        self.receive(p, 2)
        self.cross(p, 2)

    def step5(self, p):
        for stage in range(3):
            self.arrived(self.crossing(p, stage, 1 - self.me.c)[1], self.dr.at[p, stage])

    def end(self):
        for ref, sem in self.waits:
            remote(ref, ref, sem, sem, self.me.dev(c=1 - self.me.c)).wait_send()


def norm_rows(z_ref, r_ref, n_rows, put):
    step = 48

    def body(i):
        at = rows_at(i, step)
        z = z_ref[at, :]
        centred = z - jnp.mean(z, axis=-1, keepdims=True)
        spread = jnp.mean(centred * centred, axis=-1, keepdims=True)
        root = lax.rsqrt(spread + ln_epsilon)
        hat = centred * root
        z_ref[at, :] = hat
        r_ref[at, :] = jnp.broadcast_to(root, (step, 128))
        put(at, hat)

    each(n_rows // step, body)


def forward_kernel(*refs):
    (lens, tokens, w_qkv, w_attn, w_inner, w_outer, w_proj, vectors) = refs[:8]
    outs = refs[8:27]
    scr = refs[27:]
    (vec_s, proj_s, qk_s, va_s, inner_s, outer_s, vec_g, proj_g, qk, va, inner, outer) = scr[:12]
    (xt, q, k, v, p, o, xh1, r1, g, gp, xh2, r2, out_own, proj, vec, x_all, h1b, vecp, bias_ff) = scr[12:31]
    gsems, tsem, osem = scr[31:36], scr[36], scr[37]
    me = Place()
    mp = me.x
    n_all, width = x_all.shape
    n_own = q.shape[0]
    half_seq = n_all - n_own
    seq = 2 * half_seq
    full = (n_own - half_seq) // seq
    n_full = full * seq
    half_ff = inner.shape[-1]
    rows = qk_s.shape[1]
    half_rows = rows // 2

    starts = (
        (mp * (n_full + seq), 0, n_full),
        (n_full + mp * half_seq, n_full, half_seq),
        (n_full + (1 - mp) * half_seq, n_own, half_seq),
    )
    loads = []
    for i, (at, to, n) in enumerate(starts):
        cp = pltpu.make_async_copy(
            tokens.at[pl.ds(pl.multiple_of(at, 16), n)], x_all.at[pl.ds(to, n)], tsem.at[i]
        )
        cp.start()
        loads.append(cp)

    greet_send(me.others())
    vecp[...] = jnp.zeros_like(vecp)
    nvec, nlane = vectors.shape
    vecp[0:nvec, 0:nlane] = vectors[...]
    proj_s[...] = w_proj[pl.ds(pl.multiple_of(mp * half_rows, 8), half_rows), :]
    vec_s[...] = jnp.transpose(vecp[...])[0:nlane]
    qk_s[...] = w_qkv[0:2].astype(BF)
    va_s[0] = w_qkv[2].astype(BF)
    va_s[1] = w_attn[...].astype(BF)
    hf = half_ff // 2
    for h in range(2):
        inner_s[h] = w_inner[:, h * hf : (h + 1) * hf].astype(BF)
        outer_s[h] = w_outer[:, h * hf : (h + 1) * hf].astype(BF)

    greet_wait(len(me.others()))
    row_cut = 32
    pieces = [
        (vec_s, vec_g),
        (qk_s.at[0], qk.at[0]),
        (qk_s.at[1], qk.at[1]),
        (va_s.at[0, pl.ds(0, row_cut)], va.at[0, :, :, :, pl.ds(0, row_cut)]),
        (va_s.at[0, pl.ds(row_cut, rows - row_cut)], va.at[0, :, :, :, pl.ds(row_cut, rows - row_cut)]),
        (va_s.at[1], va.at[1]),
    ]
    for shard, whole in ((inner_s, inner), (outer_s, outer)):
        for h in range(2):
            for j in range(2):
                src = shard.at[h, :, pl.ds(j * (hf // 2), hf // 2)]
                pieces.append((src, whole.at[h, :, :, :, :, pl.ds(j * hf, hf)]))
    pieces.append((proj_s, proj_g))
    net = Gather(me, pieces, gsems)

    def go(step, *members):
        for piece in members:
            (net.step1, net.step2, net.step3, net.step4, net.step5)[step - 1](piece)

    go(1, 0, 1, 2, 12, 13)
    saves = []

    def save(i, ref):
        cp = pltpu.make_async_copy(ref, outs[i], osem.at[i])
        cp.start()
        saves.append(cp)

    for cp in loads:
        cp.wait()

    def x_turn(i):
        xt[rows_at(i, 256), :] = jnp.transpose(x_all[:, lanes(i, 256)])

    each(width // 256, x_turn)
    save(4, xt)
    go(2, 0)
    go(1, 3, 4)
    go(2, 1, 12, 13)
    go(1, 5)
    go(2, 2)
    go(1, 6)
    go(3, 0, 1)
    go(2, 3)
    go(3, 2)
    go(1, 7)
    go(2, 4)
    go(4, 0)
    go(5, 0)
    big = []
    for z in range(NZ):
        for y in range(NY):
            for c in range(NC):
                for x in range(NX):
                    big.append(vec_g[z, y, c, :, x * 128 : (x + 1) * 128])
    vec[...] = jnp.transpose(jnp.concatenate(big, axis=0))[0 : vec.shape[0]]
    for h in range(2):
        for x in range(NX):
            for j in range(2):
                row = vec[5 + NX * x + h : 6 + NX * x + h, j * (hf // 2) : (j + 1) * (hf // 2)]
                bias_ff[h : h + 1, j * hf + x * (hf // 2) : j * hf + (x + 1) * (hf // 2)] = row
    save(17, vec)

    def project(w_ref, src_rows, dst, bias):
        n_tile = 256

        def body(i):
            w = flat(w_ref[:, :, :, :, lanes(i, n_tile)])
            r = mm(x_all[0:src_rows], w)
            if bias is not None:
                r = r + vec[bias : bias + 1, lanes(i, n_tile)]
            dst[:, lanes(i, n_tile)] = r.astype(BF)

        each(width // n_tile, body)

    go(3, 3)
    go(4, 1)
    go(3, 4)
    go(2, 5)
    go(1, 8)
    go(4, 2)
    go(5, 1)
    project(qk.at[0], n_own, q, 0)
    go(5, 2)
    go(2, 6)
    go(1, 9)
    project(qk.at[1], n_all, k, None)
    save(0, qk)
    go(4, 3, 4)
    go(3, 5)
    go(2, 7)
    go(3, 6)
    go(1, 10)
    go(5, 3, 4)
    project(va.at[0], n_all, v, 1)
    save(5, q)
    save(6, k)
    save(7, v)

    wide = 384
    pos = lax.broadcasted_iota(jnp.int32, (1, wide), 1)
    beyond = jnp.where(pos < seq, 0, 1 << 20)

    def attend(q0, nq, k0, slab, length, place):
        at_q = pl.ds(pl.multiple_of(q0, 16), nq)
        at_k = pl.ds(pl.multiple_of(k0, 16), seq)
        for pair in range(2):
            l = lanes(2 * slab + pair)
            s = mm_nt(q[at_q, l], stack_heads(k[at_k, l], wide)) * (HEAD_DIM**-0.5)
            both = []
            for h in range(2):
                part = jnp.where(place < length, s[:, h * wide : (h + 1) * wide], -1000000000.0)
                e = jnp.exp(part - jnp.max(part, axis=-1, keepdims=True))
                both.append((e * (1.0 / jnp.sum(e, axis=-1, keepdims=True))).astype(BF))
            pb = jnp.concatenate(both, axis=1)
            p[slab, at_q, 2 * wide * pair : 2 * wide * (pair + 1)] = pb
            o[at_q, l] = mm(pb, stack_heads(v[at_k, l], wide)).astype(BF)

    slabs = p.shape[0]
    jobs = [[(2, 8), (1, 11, 14), (3, 12)], [(3, 7)], [(2, 9)], [(4, 5, 6), (3, 13)], [(2, 10)], [(3, 8), (5, 5, 6)]]
    for s in range(full):
        length = lens[mp * (full + 1) + s]
        for i in range(slabs):
            attend(s * seq, seq, s * seq, i, length, pos + beyond)
            for job in jobs[3 * s + i]:
                go(*job)
    length = lens[full]
    pos_c = jnp.where(pos < half_seq, pos + mp * half_seq, pos - half_seq + (1 - mp) * half_seq) + beyond
    for i in range(slabs):
        attend(n_full, half_seq, n_full, i, length, pos_c)
        if i == 0:
            go(2, 11)
        elif i == 1:
            go(3, 9)
    go(2, 14)
    save(8, p)
    save(9, o)

    tile = 720
    tiles = n_own // tile

    def attn_out(i):
        a = mm_nt(o[rows_at(i, tile), :], flat(va[1]))
        xh1[rows_at(i, tile), :] = x_all[rows_at(i, tile), :].astype(F32) + a + vec[2:3, :]

    each(tiles, attn_out)
    go(4, 7)
    save(1, va)

    def put_h1(at, hat):
        h1b[at, :] = (hat * vec[3:4, :] + vec[4:5, :]).astype(BF)

    norm_rows(xh1, r1, n_own, put_h1)
    save(10, xh1)
    save(11, r1)
    go(5, 7)
    go(3, 10)
    go(4, 8)

    def feed(h):
        n_tile = 256

        def body(i):
            w = flat(inner[h, :, :, :, :, lanes(i, n_tile)])
            for t in range(tiles):
                at = pl.ds(t * tile, tile)
                u = mm(h1b[at, :], w)
                u = u + bias_ff[h : h + 1, lanes(i, n_tile)]
                tail = 0.5 * (1.0 + lax.erf(u * 0.7071067811865476))
                g[h, at, lanes(i, n_tile)] = (u * tail).astype(BF)
                slope = tail + u * (0.3989422804014327 * jnp.exp(-0.5 * u * u))
                gp[h, at, lanes(i, n_tile)] = slope.astype(BF)

        each(half_ff // n_tile, body)

    feed(0)
    go(3, 11)
    go(5, 8)
    go(4, 9)
    go(5, 9)
    feed(1)
    go(3, 14)
    go(4, 10, 12, 11, 13)
    go(5, 10, 12, 11, 13)
    save(2, inner)
    save(12, g)
    save(13, gp)

    def ff_out(i):
        at = rows_at(i, tile)
        f = mm_nt(g[0, at, :], flat(outer[0])) + mm_nt(g[1, at, :], flat(outer[1]))
        h1 = xh1[at, :] * vec[3:4, :] + vec[4:5, :]
        xh2[at, :] = h1 + f + vec[9:10, :]

    each(tiles, ff_out)
    save(3, outer)
    go(4, 14)
    go(5, 14)
    for d in range(NZ * NY * NC * NX):
        block = proj_g[d // 8, d // 4 % 2, d // 2 % 2, :, d % 2 * 128 : (d % 2 + 1) * 128]
        proj[d * half_rows : (d + 1) * half_rows] = block
    save(16, proj)

    def put_y(at, hat):
        out_own[at, :] = (hat * vec[10:11, :] + vec[11:12, :]).astype(BF)

    norm_rows(xh2, r2, n_own, put_y)
    save(14, xh2)
    save(15, r2)
    save(18, out_own)
    net.end()
    for cp in saves:
        cp.wait()


def forward_fast(lengths, tokens, w_qkv, w_attn, w_inner, w_outer, w_proj, vectors):
    seqs = lengths.shape[0]
    all_rows, width = tokens.shape
    seq = all_rows // seqs
    full = seqs // 2
    n_own = full * seq + seq // 2
    n_all = n_own + seq // 2
    rows, half_ff = w_qkv.shape[1], w_inner.shape[1]
    heads = width // HEAD_DIM
    zyc = (NZ, NY, NC)
    hr, nlane = rows // 2, vectors.shape[1]
    weights = [
        ((2,) + zyc + (rows, width), BF),
        ((2,) + zyc + (rows, width), BF),
        ((2,) + zyc + (rows, half_ff), BF),
        ((2,) + zyc + (rows, half_ff), BF),
    ]
    kept = [
        ((width, n_all), BF),
        ((n_own, width), BF),
        ((n_all, width), BF),
        ((n_all, width), BF),
        ((heads // 4, n_own, 4 * 384), BF),
        ((n_own, width), BF),
        ((n_own, width), F32),
        ((n_own, 128), F32),
        ((2, n_own, half_ff), BF),
        ((2, n_own, half_ff), BF),
        ((n_own, width), F32),
        ((n_own, 128), F32),
        ((width, 128), F32),
        ((16, width), F32),
        ((n_own, width), BF),
    ]
    order = kept[:12] + [kept[14], kept[12], kept[13]]
    scratch = [
        ((nlane, 128), F32),
        ((hr, 128), F32),
        ((2, rows, width // 2), BF),
        ((2, rows, width // 2), BF),
        ((2, rows, half_ff // 2), BF),
        ((2, rows, half_ff // 2), BF),
        (zyc + (nlane, 256), F32),
        (zyc + (hr, 256), F32),
    ]
    scratch += weights + order
    scratch += [((n_all, width), BF), ((n_own, width), BF), ((128, 128), F32), ((8, half_ff), F32)]
    n = 15
    vm = pl.BlockSpec(memory_space=pltpu.VMEM)
    hb = pl.BlockSpec(memory_space=ANY)
    sm = pl.BlockSpec(memory_space=pltpu.SMEM)
    return pl.pallas_call(
        forward_kernel,
        out_shape=[jax.ShapeDtypeStruct(s, d) for s, d in weights + kept],
        in_specs=[sm, hb] + [vm] * 6,
        out_specs=[hb] * 19,
        scratch_shapes=[pltpu.VMEM(s, d) for s, d in scratch]
        + [
            dma(n), dma(n, 3), dma(n, 3), dma(n, 3), dma(n, 3),
            dma(3), dma(20),
        ],
        compiler_params=pltpu.CompilerParams(
            collective_id=1, has_side_effects=True, vmem_limit_bytes=60 * 2**20
        ),
        name="forward",
    )(lengths, tokens, w_qkv, w_attn, w_inner, w_outer, w_proj, vectors)


class Reduce:
    def __init__(self, me, pieces, sems):
        self.me, self.pieces = me, pieces
        self.ds, self.dr, self.ss, self.rs = sems
        self.waits = []
        self.squares = jnp.zeros((1, 1), F32)

    def go(self, copy):
        copy.start()
        self.waits.append(copy)

    def arrived(self, ref, ssem, rsem):
        remote(ref, ref, ssem, rsem, self.me.dev(c=1 - self.me.c)).wait_recv()

    def region(self, p, stage, **at):
        order, src = self.pieces[p][0], self.pieces[p][2]
        me, done = self.me, order[:stage]
        half = src.shape[-1] // 2
        z = at.get("z", me.z if "z" in done else None)
        y = at.get("y", me.y if "y" in done else None)
        x = at.get("x", me.x if "x" in done else None)
        zs = slice(None) if z is None else pl.ds(0, NZ - 1) if z == "three" else pl.ds(z, 1)
        ys = slice(None) if y is None else pl.ds(y, 1)
        xs = slice(None) if x is None else cols(x, half)
        return src.at[zs, ys, me.c, :, xs]

    def send(self, p, stage):
        order, got, me = self.pieces[p][0], self.pieces[p][4 + stage], self.me
        ss, rs = self.ss, self.rs
        if order[stage] == "z":
            for k in range(1, NZ):
                tz = lax.rem(me.z + k, NZ)
                part = self.region(p, stage, z=tz)
                remote(part, got.at[pl.ds(k, 1)], ss.at[p, stage], rs.at[p, stage], me.dev(z=tz)).start()
            part = self.region(p, stage, z="three")
            self.waits.append(remote(part, part, ss.at[p, stage], rs.at[p, stage], me.dev(c=1 - me.c)))
        else:
            far = 1 - (me.y if order[stage] == "y" else me.x)
            part = self.region(p, stage, **{order[stage]: far})
            dev = me.dev(**{order[stage]: far})
            self.go(remote(part, got, ss.at[p, stage], rs.at[p, stage], dev))

    def receive(self, p, stage):
        order, got = self.pieces[p][0], self.pieces[p][4 + stage]
        if order[stage] == "z":
            got = got.at[pl.ds(1, NZ - 1)]
        self.arrived(got, self.ss.at[p, stage], self.rs.at[p, stage])

    def add(self, p, stage):
        order, _, src, _, *gots = self.pieces[p]
        got, me = gots[stage], self.me
        done = order[: stage + 1]
        half = src.shape[-1] // 2
        xs = cols(me.x, half) if "x" in done else slice(None)
        ys = [(me.y, 0)] if "y" in done else [(y, y) for y in range(NY)]
        if order[stage] == "z":
            for y, i in ys:
                total = src[me.z, y, me.c, :, xs].astype(F32)
                for k in range(1, NZ):
                    total = total + got[k, i].astype(F32)
                src[me.z, y, me.c, :, xs] = total.astype(src.dtype)
            return

        def one(z):
            for y, i in ys:
                src[z, y, me.c, :, xs] = src[z, y, me.c, :, xs] + got[0 if "z" in done else z, i]

        if "z" in done:
            one(me.z)
        else:
            each(NZ, one)

    def step1(self, p):
        src, got = self.pieces[p][2], self.pieces[p][3]
        oc = 1 - self.me.c
        self.go(remote(src.at[:, :, oc], got, self.ds.at[p], self.dr.at[p], self.me.dev(c=oc)))

    def step2(self, p):
        src, got, c = self.pieces[p][2], self.pieces[p][3], self.me.c
        self.arrived(got, self.ds.at[p], self.dr.at[p])

        def one(z):
            for y in range(NY):
                src[z, y, c] = src[z, y, c] + got[z, y]

        each(NZ, one)
        self.send(p, 0)

    def step3(self, p):
        self.receive(p, 0)
        self.add(p, 0)
        self.send(p, 1)

    def step4(self, p):
        self.receive(p, 1)
        self.add(p, 1)
        self.send(p, 2)

    def step5(self, p, counted=None):
        order, dst, src, _, *gots = self.pieces[p]
        me = self.me
        self.receive(p, 2)
        total = src[me.z, me.y, me.c, :, cols(me.x, src.shape[-1] // 2)].astype(F32)
        for k in range(1, NZ) if order[2] == "z" else (0,):
            total = total + gots[2][k, 0].astype(F32)
        dst[...] = total
        total = total[:counted]
        self.squares = self.squares + jnp.sum(total * total, keepdims=True)

    def end(self):
        for copy in self.waits:
            copy.wait_send()


def got_shapes(order, r, w):
    out, done = [], ""
    for axis in order:
        done += axis
        nz = NZ if axis == "z" or "z" not in done else 1
        out.append((nz, 1 if "y" in done else NY, r, w // 2 if "x" in done else w))
    return out


orders = ("yxz", "yxz", "zyx", "zyx", "yxz", "yxz", "yzx", "yxz", "yxz", "zyx", "yxz", "yxz", "yxz", "yxz")


def all_squares(me, net, total, sq4, sq8, sems):
    qs, qr, es, er = sems
    sq4[0] = jnp.broadcast_to(total, (8, 128))
    copies = []
    for k in range(1, NZ):
        copies.append(remote(sq4.at[0], sq4.at[k], qs.at[k], qr.at[k], me.dev(z=lax.rem(me.z + k, NZ))))
    for copy in copies:
        net.go(copy)
    for copy in copies:
        copy.wait_recv()

    def at_z(z):
        out = jnp.zeros((8, 128), F32)
        for k in range(NZ):
            out = out + jnp.where(lax.rem(me.z + NZ - k, NZ) == z, sq4[k], 0.0)
        return out

    sq8[0] = at_z(0) + at_z(1) + at_z(2) + at_z(3)
    copies = []
    for k, dev in enumerate(me.eights(), 1):
        copies.append(remote(sq8.at[0], sq8.at[k], es.at[k], er.at[k], dev))
    for copy in copies:
        net.go(copy)
    for copy in copies:
        copy.wait_recv()

    def at_code(w):
        out = jnp.zeros((8, 128), F32)
        for k in range(8):
            dx, dy, dc = k & 1, (k >> 1) & 1, k >> 2
            src = (
                (me.x + dx - 2 * dx * me.x)
                + 2 * (me.y + dy - 2 * dy * me.y)
                + 4 * (me.c + dc - 2 * dc * me.c)
            )
            out = out + jnp.where(src == w, sq8[k], 0.0)
        return out

    whole = at_code(0)
    for w in range(1, 8):
        whole = whole + at_code(w)
    return whole


def fold(value):
    return jnp.sum(value.reshape(-1, 8, value.shape[-1]), axis=0)


def norm_back_rows(n_rows, get_dy, hat_ref, root_ref, gain, put, acc):
    step = 48

    def body(i):
        at = rows_at(i, step)
        dy, hat = get_dy(i, at), hat_ref[at, :]
        e = dy * gain
        root = root_ref[at, 0:1]
        m1 = jnp.mean(e, axis=-1, keepdims=True)
        m2 = jnp.mean(e * hat, axis=-1, keepdims=True)
        dz = (e - m1 - hat * m2) * root
        acc[0] = acc[0] + fold(dy * hat)
        acc[1] = acc[1] + fold(dy)
        acc[2] = acc[2] + fold(dz)
        hat_ref[at, :] = dz
        put(at, dz)

    each(n_rows // step, body)


def backward_kernel(*refs):
    doc_ids, cotangent, doc_rows = refs[:3]
    (qk_h, va_h, inner_h, outer_h, xt_h, q_h, k_h, v_h, p_h, o_h, xh1_h, r1_h, g_h, gp_h, xh2_h, r2_h, proj_h, vec_h, out_h) = refs[3:22]
    outs = refs[22:32]
    small_r, qk_r, va_r, inner_r, outer_r, dx, peer_out, peer_dx, peer_small, norm_ref = outs
    scr = list(refs[32:])

    def take(n):
        got = scr[:n]
        del scr[:n]
        return got

    (inner, outer, attn, xt, q, k, v, o, xh1, gg, xh2, r2, proj, vec, cls_in, cot, df, dft) = take(18)
    (cls_grad, acc1, acc2, ffacc, vg, early, late) = take(7)
    grads = take(4)
    bufs = take(14 * 4)
    sq4, sq8 = take(2)
    lsem, rsems, xs, xr, qsems = take(1)[0], take(4), *take(2), take(4)
    do, da, dat, h1t, r1 = cot, df, dft, dft, r2
    me = Place()
    mp = me.x
    n_all, width = dx.shape
    n_own = q.shape[0]
    half_seq = n_all - n_own
    seq = 2 * half_seq
    n_full = n_own - half_seq
    full = n_full // seq
    half_ff = inner.shape[-1]
    other = me.dev(x=1 - mp)

    for i in range(4):
        grads.append(inner.at[i // 2, :, :, :, :, pl.ds(width * (i % 2), width)])
    copies = {}

    def load(name, i, src, dst):
        cp = pltpu.make_async_copy(src, dst, lsem.at[i])
        cp.start()
        copies[name] = cp

    def need(*names):
        for name in names:
            copies[name].wait()

    load("vec", 0, vec_h, vec)
    load("proj", 1, proj_h, proj)
    for s in range(full + 1):
        load("cls%d" % s, 2 + s, out_h.at[pl.ds(s * seq, 16)], cls_in.at[s])
    load("cot0", 5, cotangent.at[pl.ds(pl.multiple_of(mp * (n_full + seq), 16), n_full)], cot.at[pl.ds(0, n_full)])
    load("cot1", 6, cotangent.at[pl.ds(pl.multiple_of(n_full + mp * half_seq, 16), half_seq)], cot.at[pl.ds(n_full, half_seq)])
    load("xh2", 7, xh2_h, xh2)
    load("r2", 8, r2_h, r2)
    load("g", 9, g_h, gg.at[pl.ds(0, 2)])
    load("outer", 10, outer_h, outer)
    load("gp", 11, gp_h, gg.at[pl.ds(2, 2)])
    load("xh1", 12, xh1_h, xh1)
    load("inner", 14, inner_h, inner)
    load("attn", 15, va_h.at[1], attn)
    load("o", 16, o_h, o)
    load("q", 17, q_h, q)
    load("k", 18, k_h, k)
    load("v", 19, v_h, v)
    load("xt", 20, xt_h, xt)

    greet(me.others() + me.eights())
    pieces = []
    hr = width // (NZ * NY * NC * NX)
    n_early = early.shape[3]
    hf = half_ff // 2
    dsts, srcs = [], []
    for i, ref in enumerate((outer_r, inner_r)):
        for h in range(2):
            for j in range(2):
                dsts.append(ref.at[h, :, pl.ds(j * (hf // 2), hf // 2)])
                srcs.append(grads[2 * i + h].at[:, :, :, :, pl.ds(j * hf, hf)])
    dsts += [va_r.at[1], va_r.at[0], qk_r.at[0], qk_r.at[1]]
    dsts += [small_r.at[pl.ds(0, n_early)], small_r.at[pl.ds(n_early, hr)]]
    srcs += grads[4:] + [early, late]
    for i in range(14):
        pieces.append((orders[i], dsts[i], srcs[i]) + tuple(bufs[4 * i : 4 * i + 4]))
    net = Reduce(me, pieces, rsems)

    def go(step, *members):
        for piece in members:
            if step == 5 and piece == 12:
                net.step5(piece, hr)
            else:
                (net.step1, net.step2, net.step3, net.step4, net.step5)[step - 1](piece)

    send_out = remote(out_h, peer_out, xs.at[0], xr.at[0], other)
    net.go(send_out)

    vg[...] = jnp.zeros_like(vg)
    early[...] = jnp.zeros_like(early)
    acc1[...] = jnp.zeros_like(acc1)
    acc2[...] = jnp.zeros_like(acc2)
    ffacc[...] = jnp.zeros_like(ffacc)
    need("vec", "proj", *["cls%d" % s for s in range(full + 1)])
    row16 = lax.broadcasted_iota(jnp.int32, (16, 1), 0)
    cls = jnp.zeros((16, width), F32)
    for s in range(full + 1):
        cls = jnp.where(row16 == s, cls_in[s].astype(F32)[0:1], cls)
    cls = cls.astype(BF)
    proj_low = proj[...].astype(BF)
    query = mm(cls, proj_low).astype(BF).astype(F32)
    row8 = lax.broadcasted_iota(jnp.int32, (8, 1), 0)
    dcq = jnp.zeros((16, 128), F32)
    row_grads = []
    cands = doc_ids.shape[1]
    seq_ids = [mp * (full + 1) + s for s in range(full)] + [full]
    for s in range(full + 1):
        docs = doc_rows[seq_ids[s]].astype(F32)
        mine = 1.0 if s < full else jnp.where(mp == 0, 1.0, 0.0)
        query_s = query[s : s + 1]
        score = jnp.sum(query_s * docs, axis=-1, keepdims=True) * retrieval_scale
        e = jnp.exp(score - jnp.max(score, axis=0, keepdims=True))
        soft = e / jnp.sum(e, axis=0, keepdims=True)
        sg = (soft - jnp.where(row8 == 0, 1.0, 0.0)) * (retrieval_scale * mine)
        dcq = jnp.where(row16 == s, jnp.sum(sg * docs, axis=0, keepdims=True), dcq)
        row_grads.append(sg * query_s)
    dcq = dcq.astype(BF)
    cls_grad[...] = mm_nt(dcq, proj_low)
    proj_grad = mm_tn(cls, dcq)
    n_dev = NZ * NY * NC * NX
    table_row = lax.broadcasted_iota(jnp.int32, (TAB_DEV * n_dev // NX, 1), 0)
    table = jnp.zeros((TAB_DEV * n_dev // NX, 128), F32)
    for s in range(full + 1):
        for i in range(cands):
            table = table + jnp.where(table_row == doc_ids[seq_ids[s], i], row_grads[s][i : i + 1], 0.0)
    tr = TAB_DEV // NX
    for d in range(n_dev):
        z, y, c, x = d // 8, d // 4 % 2, d // 2 % 2, d % 2
        l = slice(x * 128, (x + 1) * 128)
        t0 = (d // 2) * TAB_DEV + x * tr
        early[z, y, c, 0:hr, l] = proj_grad[d * hr : (d + 1) * hr]
        early[z, y, c, hr : hr + tr, l] = table[t0 : t0 + tr]
    go(1, 12)

    per = seq // 48
    row48 = lax.broadcasted_iota(jnp.int32, (48, 1), 0)

    def get_dy(i, at):
        first = (row48 == 0) & (lax.rem(i, per) == 0)
        return cot[at, :].astype(F32) + jnp.where(first, cls_grad[pl.ds(i // per, 1), :], 0.0)

    def put_df(at, dz):
        df[at, :] = dz.astype(BF)

    need("cot0", "cot1", "xh2", "r2")
    norm_back_rows(n_own, get_dy, xh2, r2, vec[10:11, :], put_df, acc2)

    def turn(src, dst, n_rows):
        def body(i):
            dst[rows_at(i, 256), 0:n_rows] = jnp.transpose(src[:, lanes(i, 256)])

        each(width // 256, body)

    load("r1", 13, r1_h, r1)
    turn(df, dft, n_own)
    go(2, 12)
    n_tile = 256
    shape5 = (NZ, NY, NC, width // (NZ * NY * NC))

    def weight_grad(left, right, dst, n, at=0):
        def body(i):
            r = mm(left(), right(lanes(i + at, n_tile)))
            dst[:, :, :, :, lanes(i + at, n_tile)] = r.astype(BF).reshape(shape5 + (n_tile,))

        each(n // n_tile, body)

    need("g")
    for h in range(2):
        for j in range(2):
            weight_grad(lambda: dft[:, 0:n_own], lambda l: gg[h, :, l], grads[h], hf, j * (hf // n_tile))
            i = 2 * h + j
            go(1, i)
            if i > 1:
                go(2, i - 2)

    need("outer", "gp")
    tile = 720
    tiles = n_own // tile

    def hidden(h):
        def body(i):
            w = flat(outer[h, :, :, :, :, lanes(i, n_tile)])
            for t in range(tiles):
                at = pl.ds(t * tile, tile)
                du = (mm(df[at, :], w) * gg[2 + h, at, lanes(i, n_tile)].astype(F32)).astype(BF)
                gg[2 + h, at, lanes(i, n_tile)] = du
                ffacc[h, :, lanes(i, n_tile)] = ffacc[h, :, lanes(i, n_tile)] + fold(du.astype(F32))

        each(half_ff // n_tile, body)

    go(2, 2)
    hidden(0)
    go(2, 3)
    go(3, 12)
    hidden(1)
    load("p0", 21, p_h.at[0], gg.at[0])
    load("p1", 22, p_h.at[1], gg.at[1])
    load("wq", 23, qk_h.at[0], outer.at[0, :, :, :, :, pl.ds(0, width)])
    load("wk", 24, qk_h.at[1], outer.at[0, :, :, :, :, pl.ds(width, width)])
    load("wv", 25, va_h.at[0], outer.at[1, :, :, :, :, pl.ds(0, width)])
    need("xh1", "r1")

    def h1_turn(i):
        l = lanes(i, 256)
        h1 = (xh1[:, l] * vec[3:4, l] + vec[4:5, l]).astype(BF)
        h1t[rows_at(i, 256), 0:n_own] = jnp.transpose(h1)

    each(width // 256, h1_turn)
    for h in range(2):
        for j in range(2):
            weight_grad(lambda: h1t[:, 0:n_own], lambda l: gg[2 + h, :, l], grads[2 + h], hf, j * (hf // n_tile))
            i = 4 + 2 * h + j
            go(1, i)
            if i > 5:
                go(2, i - 2)
            if i == 5:
                go(3, 0)
            if i == 7:
                go(3, 1)
    need("inner")

    def hidden_back(i):
        at = rows_at(i, tile)
        d = mm_nt(gg[2, at, :], flat(inner[0])) + mm_nt(gg[3, at, :], flat(inner[1]))
        xh2[at, :] = d + xh2[at, :]

    each(tiles, hidden_back)
    load("p2", 26, p_h.at[2], gg.at[2])
    go(2, 6, 7)

    norm_back_rows(n_own, lambda i, at: xh2[at, :], xh1, r1, vec[3:4, :], put_df, acc1)
    need("attn", "o")

    def mixed_back(i):
        do[:, lanes(i, n_tile)] = mm(da[...], flat(attn[:, :, :, :, lanes(i, n_tile)])).astype(BF)

    each(width // n_tile, mixed_back)
    turn(da, dat, n_own)
    weight_grad(lambda: dat[:, 0:n_own], lambda l: o[:, l], grads[4], width)
    go(1, 8)
    go(3, 4, 2)

    need("q", "k", "v", "p0", "p1", "p2")
    wide = 384
    scale = HEAD_DIM**-0.5

    def attend(q0, nq, k0, slab):
        at_q = pl.ds(pl.multiple_of(q0, 16), nq)
        at_k = pl.ds(pl.multiple_of(k0, 16), seq)
        for pair in range(2):
            l = lanes(2 * slab + pair)
            qp, kp, dop = q[at_q, l], k[at_k, l], do[at_q, l]
            pb = gg[slab, at_q, 2 * wide * pair : 2 * wide * (pair + 1)]
            p = pb.astype(F32)
            pd = p * mm_nt(dop, stack_heads(v[at_k, l], wide))
            ds, pbs = [], []
            for h in range(2):
                at = slice(h * wide, (h + 1) * wide)
                ds.append((pd[:, at] - p[:, at] * jnp.sum(pd[:, at], axis=-1, keepdims=True)).astype(BF))
                pbs.append(pb[:, h * wide : h * wide + seq])
            q[at_q, l] = (mm(jnp.concatenate(ds, axis=1), stack_heads(kp, wide)) * scale).astype(BF)
            ds = jnp.concatenate([d[:, 0:seq] for d in ds], axis=0)
            k[at_k, l] = (mm_tn(ds, stack_heads(qp)) * scale).astype(BF)
            v[at_k, l] = mm_tn(jnp.concatenate(pbs, axis=0), stack_heads(dop)).astype(BF)

    slabs = p_h.shape[0]

    def tokens_back(at, own):
        d = mm_nt(k[at, :], flat(outer[0, :, :, :, :, width : 2 * width]))
        d = d + mm_nt(v[at, :], flat(outer[1, :, :, :, :, 0:width]))
        if own:
            d = d + mm_nt(q[at, :], flat(outer[0, :, :, :, :, 0:width])) + xh1[at, :]
            o[at, :] = d.astype(BF)
        else:
            df[0:half_seq, :] = d.astype(BF)

    keeps = []

    def send_dx(i, src, at):
        net.go(remote(src, peer_dx.at[at], xs.at[1 + i], xr.at[1 + i], other))
        cp = pltpu.make_async_copy(src, dx.at[at], lsem.at[27 + i])
        cp.start()
        keeps.append(cp)

    need("wq", "wk", "wv")
    for s in range(full):
        for i in range(slabs):
            attend(s * seq, seq, s * seq, i)
            if s == 0:
                (lambda: (go(2, 8), go(4, 0, 1)), lambda: go(3, 5), lambda: (go(3, 3), go(4, 12)))[i]()
            else:
                (lambda: go(4, 4), lambda: go(3, 6), lambda: go(5, 0, 1))[i]()
        tokens_back(pl.ds(s * seq, seq), True)
        size = seq if s == 0 else half_seq
        send_dx(s, o.at[pl.ds(s * seq, size)], pl.ds(s * seq, size))
    for i in range(slabs):
        attend(n_full, half_seq, n_full, i)
        (lambda: go(3, 7), lambda: (go(5, 4), go(4, 5)), lambda: go(4, 2))[i]()
    need("xt")
    weight_grad(lambda: xt[...], lambda l: v[:, l], grads[5], width)
    go(1, 9)
    go(3, 8)
    send_dx(2, o.at[pl.ds(n_full - half_seq, half_seq)], pl.ds(n_full - half_seq, half_seq))
    weight_grad(lambda: xt[:, 0:n_own], lambda l: q[:, l], grads[6], width)
    go(1, 10)
    go(2, 9)
    go(4, 6)
    go(4, 3)
    weight_grad(lambda: xt[...], lambda l: k[:, l], grads[7], width)
    go(1, 11)
    go(2, 10)
    tokens_back(pl.ds(n_full, half_seq), True)
    go(2, 11)
    tokens_back(pl.ds(n_own, half_seq), False)

    vg[0:1, :] = jnp.sum(q[...].astype(F32), axis=0, keepdims=True)
    vg[1:2, :] = jnp.sum(v[...].astype(F32), axis=0, keepdims=True)
    vg[2:3, :] = jnp.sum(acc1[2], axis=0, keepdims=True)
    vg[3:4, :] = jnp.sum(acc1[0], axis=0, keepdims=True)
    vg[4:5, :] = jnp.sum(acc1[1], axis=0, keepdims=True)
    for h in range(2):
        both = jnp.sum(ffacc[h], axis=0, keepdims=True)
        for x in range(NX):
            for j in range(2):
                at = j * hf + x * (hf // 2)
                vg[5 + NX * x + h : 6 + NX * x + h, j * (hf // 2) : (j + 1) * (hf // 2)] = both[:, at : at + hf // 2]
    vg[9:10, :] = jnp.sum(acc2[2], axis=0, keepdims=True)
    vg[10:11, :] = jnp.sum(acc2[0], axis=0, keepdims=True)
    vg[11:12, :] = jnp.sum(acc2[1], axis=0, keepdims=True)
    turned = jnp.transpose(vg[...])
    for d in range(n_dev):
        z, y, c, x = d // 8, d // 4 % 2, d // 2 % 2, d % 2
        late[z, y, c, :, x * 128 : (x + 1) * 128] = turned[d * hr : (d + 1) * hr]
    go(1, 13)
    go(2, 13)
    send_dx(3, o.at[pl.ds(n_full, half_seq)], pl.ds(n_full, half_seq))
    go(4, 7)
    go(5, 5, 12)
    go(4, 8)
    go(3, 10)
    go(3, 11)
    go(3, 9)
    go(4, 10)
    go(3, 13)
    send_dx(4, df.at[pl.ds(0, half_seq)], pl.ds(n_own, half_seq))
    go(4, 9)
    go(4, 11)
    go(4, 13)
    go(5, 2, 3, 6, 7, 8, 10, 9)
    go(5, 11, 13)
    net.go(remote(small_r, peer_small, xs.at[6], xr.at[6], other))
    norm_ref[...] = all_squares(me, net, net.squares, sq4, sq8, qsems)
    parts = [pl.ds(0, seq)] + [pl.ds(seq + i * half_seq, half_seq) for i in range(4)]
    for i, ref in enumerate([peer_out] + [peer_dx.at[at] for at in parts] + [peer_small]):
        net.arrived(ref, xs.at[i], xr.at[i])
    for cp in keeps:
        cp.wait()
    net.end()


def backward_fast(doc_ids, cotangent, doc_rows, saved, rows):
    (qk, va, inner, outer, xt, q, k, v, p, o, xh1, r1, g, gp, xh2, r2, proj, vec, out_own) = saved
    n_own, width = q.shape
    n_all = k.shape[0]
    half_ff = inner.shape[-1]
    zyc = (NZ, NY, NC)
    hr = rows // NX
    n_early = hr + 8
    small_rows = n_early + hr
    ins = [doc_ids, cotangent, doc_rows] + list(saved)
    out_shape = [
        ((small_rows, 128), F32),
        ((2, rows, width // 2), F32),
        ((2, rows, width // 2), F32),
        ((2, rows, half_ff // 2), F32),
        ((2, rows, half_ff // 2), F32),
        ((n_all, width), BF),
        ((n_own, width), BF),
        ((n_all, width), BF),
        ((small_rows, 128), F32),
        ((8, 128), F32),
    ]
    like = lambda a: (a.shape, a.dtype)
    wide = width // 128 * 128
    scratch = [
        like(inner), like(outer), (va.shape[1:], BF), like(xt), like(q), like(k), like(v), like(o),
        like(xh1), ((4,) + g.shape[1:], BF), like(xh2), like(r2), like(proj), like(vec),
        ((3, 16, width), BF), ((n_own, width), BF), ((n_own, width), BF),
        ((width, wide), BF),
        ((16, width), F32), ((3, 8, width), F32), ((3, 8, width), F32), ((2, 8, half_ff), F32),
        ((128, width), F32), (zyc + (n_early, 256), F32), (zyc + (hr, 256), F32),
    ]
    sizes = [half_ff] * 4 + [width] * 4
    scratch += [(zyc + (rows, w), BF) for w in sizes[:4]]
    smalls = [(n_early, 256, F32), (hr, 256, F32)]
    for i, (r, w, dt) in enumerate([(rows, width, BF)] * 12 + smalls):
        scratch += [((NZ, NY, r, w), dt)] + [(shape, dt) for shape in got_shapes(orders[i], r, w)]
    scratch += [((NZ, 8, 128), F32), ((8, 8, 128), F32)]
    vm = pl.BlockSpec(memory_space=pltpu.VMEM)
    hb = pl.BlockSpec(memory_space=ANY)
    sm = pl.BlockSpec(memory_space=pltpu.SMEM)
    n = 14
    return pl.pallas_call(
        backward_kernel,
        out_shape=[jax.ShapeDtypeStruct(s, d) for s, d in out_shape],
        in_specs=[sm, hb, vm] + [hb] * 19,
        out_specs=[vm] * 5 + [hb, hb, hb, vm, vm],
        scratch_shapes=[pltpu.VMEM(s, d) for s, d in scratch]
        + [
            dma(32), dma(n), dma(n), dma(n, 3), dma(n, 3),
            dma(7), dma(7), dma(NZ), dma(NZ), dma(8), dma(8),
        ],
        compiler_params=pltpu.CompilerParams(
            collective_id=2, has_side_effects=True, vmem_limit_bytes=63 * 2**20
        ),
        name="backward",
    )(*ins)


def finish_kernel(*refs):
    small_r, peer_small, qk_r, va_r, inner_r, outer_r, total = refs[:7]
    out_own, peer_out, dx, peer_dx = refs[7:11]
    params = [refs[11 + 3 * i : 14 + 3 * i] for i in range(6)]
    outs = refs[29:51]
    turn, sem, lo, hi, mid = refs[51:]
    out_tokens, input_grad, norm = outs[0:3]
    news = [outs[3 + 3 * i : 6 + 3 * i] for i in range(6)]
    table_grad = outs[21]
    mp = lax.axis_index("mp")
    n_own = out_own.shape[0]
    n_all = dx.shape[0]
    half_seq = n_all - n_own
    n_full = n_own - half_seq
    seq = 2 * half_seq
    copies = []
    for i, (src, first) in enumerate(((out_own, mp), (peer_out, 1 - mp))):
        at = pl.multiple_of(first * (n_full + seq), 16)
        copies.append((src.at[pl.ds(0, n_full)], out_tokens.at[pl.ds(at, n_full)]))
        at = pl.multiple_of(n_full + first * half_seq, 16)
        copies.append((src.at[pl.ds(n_full, half_seq)], out_tokens.at[pl.ds(at, half_seq)]))
    copies = [pltpu.make_async_copy(s, d, sem.at[i]) for i, (s, d) in enumerate(copies)]
    for cp in copies:
        cp.start()
    lo[...] = dx[0:n_full].astype(F32)
    hi[...] = peer_dx[0:n_full].astype(F32)
    own_mid = dx[n_full:n_own].astype(F32) + peer_dx[n_own:n_all].astype(F32)
    peer_mid = peer_dx[n_full:n_own].astype(F32) + dx[n_own:n_all].astype(F32)
    mid[pl.ds(pl.multiple_of(mp * half_seq, 16), half_seq)] = own_mid
    mid[pl.ds(pl.multiple_of((1 - mp) * half_seq, 16), half_seq)] = peer_mid
    grads = (
        (lo, pl.multiple_of(mp * (n_full + seq), 16), n_full),
        (hi, pl.multiple_of((1 - mp) * (n_full + seq), 16), n_full),
        (mid, n_full, seq),
    )
    for i, (src, at, n) in enumerate(grads):
        cp = pltpu.make_async_copy(src, input_grad.at[pl.ds(at, n)], sem.at[4 + i])
        cp.start()
        copies.append(cp)

    root = jnp.sqrt(total[...])
    norm[0, 0] = jnp.max(root)
    clip = clip_norm / jnp.maximum(root[0:1, 0:1], clip_norm)
    hf = inner_r.shape[-1]
    hr = params[4][0].shape[0] // 2
    nvec, nlane = params[5][0].shape
    tr = table_grad.shape[0] // 2

    def adam(which, at, g, dec, rate):
        w, m, s = (ref[at] for ref in params[which])
        for ref, new in zip(news[which], adamw_update(w, m, s, g * clip, dec, rate)):
            ref[at] = new

    for j in range(3):
        g = qk_r[j] if j < 2 else va_r[0]
        adam(0, (j,), g, decay_rate, learn_rate)
    adam(1, (slice(None), slice(None)), va_r[1], decay_rate, learn_rate)
    for which, ref in ((2, inner_r), (3, outer_r)):
        for h in range(2):
            adam(which, (slice(None), slice(h * hf, (h + 1) * hf)), ref[h], decay_rate, learn_rate)
    turn[...] = jnp.zeros_like(turn)
    turn[0:nlane] = small_r[hr + 8 : hr + 8 + nlane]
    adam(5, (slice(None), slice(None)), jnp.transpose(turn[...])[0:nvec, 0:nlane], 0.0, vector_rate)
    for block, first in ((small_r, mp), (peer_small, 1 - mp)):
        at = pl.ds(pl.multiple_of(first * hr, 8), hr)
        adam(4, (at, slice(None)), block[0:hr], decay_rate, learn_rate)
    own_t, peer_t = small_r[hr : hr + tr], peer_small[hr : hr + tr]
    table_grad[0:tr] = jnp.where(mp == 0, own_t, peer_t)
    table_grad[tr : 2 * tr] = jnp.where(mp == 0, peer_t, own_t)
    for cp in copies:
        cp.wait()


def finish_fast(reduced, out_own, params, n_rows):
    (small_r, qk_r, va_r, inner_r, outer_r, dx, peer_out, peer_dx, peer_small, total) = reduced
    n_own, width = out_own.shape
    n_all = dx.shape[0]
    half_seq = n_all - n_own
    like = lambda a: jax.ShapeDtypeStruct(a.shape, a.dtype)
    vm = pl.BlockSpec(memory_space=pltpu.VMEM)
    hb = pl.BlockSpec(memory_space=ANY)
    sm = pl.BlockSpec(memory_space=pltpu.SMEM)
    out_shape = [
        jax.ShapeDtypeStruct((n_rows, width), BF),
        jax.ShapeDtypeStruct((n_rows, width), F32),
        jax.ShapeDtypeStruct((1, 1), F32),
    ]
    out_shape += [like(a) for a in params] + [jax.ShapeDtypeStruct((TAB_DEV, 128), F32)]
    n_full = n_own - half_seq
    outs = pl.pallas_call(
        finish_kernel,
        out_shape=out_shape,
        in_specs=[vm] * 29,
        out_specs=[hb, hb, sm] + [vm] * 19,
        scratch_shapes=[
            pltpu.VMEM((128, 128), F32),
            dma(7),
            pltpu.VMEM((n_full, width), F32),
            pltpu.VMEM((n_full, width), F32),
            pltpu.VMEM((2 * half_seq, width), F32),
        ],
        compiler_params=pltpu.CompilerParams(vmem_limit_bytes=63 * 2**20),
        name="finish",
    )(small_r, peer_small, qk_r, va_r, inner_r, outer_r, total, out_own, peer_out, dx, peer_dx, *params)
    return tuple(outs[:2]) + (outs[2].reshape(()),) + tuple(outs[3:])


def gather_plain(shards, small, rows):
    def both(v, axis):
        v = lax.all_gather(v, "dp", axis=axis, tiled=True)
        return lax.all_gather(v, "mp", axis=2, tiled=True)

    return [both(small[None], 0)] + [both(v, 1) for v in shards]


def reduce_plain(grads, small, own_out, own_dx, rows):
    def both(v, axis, wide):
        v = lax.psum_scatter(v.astype(F32), "mp", scatter_dimension=wide, tiled=True)
        return lax.psum_scatter(v, "dp", scatter_dimension=axis, tiled=True)

    small_sum = both(small, 0, 2)[0]
    sums = [both(g, 1, 2) for g in grads]
    ox = 1 - lax.axis_index("mp")
    swap = [(0, 1), (1, 0)]
    peer_out = lax.ppermute(own_out, "mp", swap)
    peer_dx = lax.ppermute(own_dx, "mp", swap)
    peer_small = lax.ppermute(small_sum, "mp", swap)
    squares = sum(squared(g) for g in sums) + squared(small_sum[:-4])
    total = lax.psum(squares, ("dp", "mp"))
    return [small_sum] + sums + [peer_out, peer_dx, peer_small, jnp.full((8, 128), total)]


def forward_plain(lengths, tokens, w_qkv, w_attn, w_inner, w_outer, w_proj, vectors):
    mp = lax.axis_index("mp")
    n_dp = lax.axis_size("dp")
    seqs = lengths.shape[0]
    all_rows, width = tokens.shape
    seq_len = all_rows // seqs
    full = seqs // 2
    n_full, n_half = full * seq_len, seq_len // 2
    n_own = n_full + n_half
    heads = width // HEAD_DIM
    rows, half_ff = w_qkv.shape[1], w_inner.shape[1]
    nvec, vec_lanes = vectors.shape
    half_rows = rows // 2
    score_scale = HEAD_DIM ** (-0.5)

    def two(v):
        return v.reshape(rows, 2, half_ff // 2).transpose(1, 0, 2)

    qk_s = w_qkv[:2].astype(BF)
    va_s = jnp.stack([w_qkv[2], w_attn]).astype(BF)
    vec_pad = jnp.pad(vectors, ((0, 0), (0, 128 - vec_lanes)))
    proj_half = lax.dynamic_slice_in_dim(w_proj, mp * half_rows, half_rows, 0)
    small_s = jnp.concatenate([proj_half, vec_pad], axis=0)
    small_g, qk, va, inner, outer = gather_plain(
        [qk_s, va_s, two(w_inner.astype(BF)), two(w_outer.astype(BF))], small_s, rows
    )
    small_g = small_g.reshape(n_dp, half_rows + nvec, 2, 128)
    proj = small_g[:, :half_rows].transpose(0, 2, 1, 3).reshape(width, 128)
    vec = small_g[:, half_rows:, :, :vec_lanes].transpose(1, 0, 2, 3).reshape(nvec, width)
    ff_rows = nvec - 8
    b_inner = vec[5 : 5 + ff_rows].reshape(2, 2, half_ff // 2).transpose(1, 0, 2).reshape(2, half_ff)

    a0 = mp * (n_full + seq_len)
    h0 = n_full + mp * n_half
    o0 = n_full + (1 - mp) * n_half
    x_all = jnp.concatenate(
        [
            lax.dynamic_slice_in_dim(tokens, a0, n_full, 0),
            lax.dynamic_slice_in_dim(tokens, h0, n_half, 0),
            lax.dynamic_slice_in_dim(tokens, o0, n_half, 0),
        ]
    )
    x_own = x_all[:n_own]
    my_seqs = jnp.concatenate([mp * (full + 1) + jnp.arange(full), jnp.array([full])])
    my_len = lengths[my_seqs]
    pos = jnp.arange(seq_len)
    pos_last = jnp.where(pos < n_half, pos + mp * n_half, pos - n_half + (1 - mp) * n_half)
    valids = (pos[None, :] < my_len[:full, None], pos_last[None, :] < my_len[full:, None])

    q = (jnp.dot(x_own, qk[0], preferred_element_type=F32) + vec[0]).astype(BF)
    k = jnp.dot(x_all, qk[1], preferred_element_type=F32).astype(BF)
    v = (jnp.dot(x_all, va[0], preferred_element_type=F32) + vec[1]).astype(BF)
    probs, outs = [], []
    for qh, kh, vh, valid in zip(*(halves(t, n_full, seq_len) for t in (q, k, v)), valids):
        s = jnp.einsum("gqhe,gkhe->ghqk", qh, kh, preferred_element_type=F32) * score_scale
        s = jnp.where(valid[:, None, None, :], s, -1000000000.0)
        pb = jax.nn.softmax(s, axis=-1).astype(BF)
        o = jnp.einsum("ghqk,gkhe->gqhe", pb, vh, preferred_element_type=F32)
        outs.append(o.reshape(-1, width).astype(BF))
        probs.append(pb.reshape((-1,) + pb.shape[2:]))
    mixed = jnp.concatenate(outs)

    def norm(z):
        centred = z - jnp.mean(z, axis=-1, keepdims=True)
        root = lax.rsqrt(jnp.mean(centred * centred, axis=-1, keepdims=True) + ln_epsilon)
        return centred * root, jnp.broadcast_to(root, (n_own, 128))

    attn = jnp.einsum("te,de->td", mixed, va[1], preferred_element_type=F32)
    xh1, r1 = norm(x_own.astype(F32) + attn + vec[2])
    h1 = xh1 * vec[3] + vec[4]
    u = jnp.einsum("td,hdf->htf", h1.astype(BF), inner, preferred_element_type=F32) + b_inner[:, None, :]
    tail = 0.5 * (1.0 + lax.erf(u * 0.7071067811865476))
    g = (u * tail).astype(BF)
    gp = (tail + u * (0.3989422804014327 * jnp.exp(-0.5 * u * u))).astype(BF)
    f = jnp.einsum("htf,hdf->td", g, outer, preferred_element_type=F32)
    xh2, r2 = norm(h1 + f + vec[5 + ff_rows])
    out_own = (xh2 * vec[6 + ff_rows] + vec[7 + ff_rows]).astype(BF)
    vec = jnp.pad(vec, ((0, 16 - nvec), (0, 0)))
    return [qk, va, inner, outer, x_all, q, k, v, *probs, mixed, xh1, r1, g, gp, xh2, r2, proj, vec, out_own]


def halves(t, n_full, seq_len):
    heads = t.shape[1] // HEAD_DIM
    last = t.shape[0] - n_full
    return (
        t[:n_full].reshape(n_full // seq_len, seq_len, heads, HEAD_DIM),
        t[n_full:].reshape(1, last, heads, HEAD_DIM),
    )


def pass_plain(lengths, tokens, cotangent, doc_ids, doc_rows, w_qkv, w_attn, w_inner, w_outer, w_proj, vectors):
    mp = lax.axis_index("mp")
    n_dp, n_mp = lax.axis_size("dp"), lax.axis_size("mp")
    seqs = lengths.shape[0]
    all_rows, width = tokens.shape
    seq_len = all_rows // seqs
    full = seqs // 2
    n_full, n_half = full * seq_len, seq_len // 2
    n_own = n_full + n_half
    rows, half_ff = w_qkv.shape[1], w_inner.shape[1]
    half_rows = rows // 2
    nvec, vec_lanes = vectors.shape
    ff_rows = nvec - 8
    score_scale = HEAD_DIM ** (-0.5)

    saved = forward_plain(lengths, tokens, w_qkv, w_attn, w_inner, w_outer, w_proj, vectors)
    (qk, va, inner, outer, x_all, q, k, v, p_ab, p_c, mixed, xh1, r1, act_low, slope, xh2, r2, proj, vec, out_own) = saved
    qk = qk.reshape(2, width, width)
    va = va.reshape(2, width, width)
    inner = inner.reshape(2, width, half_ff)
    outer = outer.reshape(2, width, half_ff)
    x_own = x_all[:n_own]
    proj = proj.astype(BF)
    a0 = mp * (n_full + seq_len)
    h0 = n_full + mp * n_half
    cot = jnp.concatenate(
        [lax.dynamic_slice_in_dim(cotangent, a0, n_full, 0), lax.dynamic_slice_in_dim(cotangent, h0, n_half, 0)]
    )
    my_seqs = jnp.concatenate([mp * (full + 1) + jnp.arange(full), jnp.array([full])])

    n_mine = full + 1
    mine = jnp.where((jnp.arange(n_mine) < full) | (mp == 0), 1.0, 0.0).astype(F32)
    cls_low = out_own[:: seq_len][:n_mine]
    docs = doc_rows[my_seqs].astype(F32)
    ids = doc_ids[my_seqs]
    query = jnp.dot(cls_low, proj, preferred_element_type=F32).astype(BF)
    query_float = query.astype(F32)
    doc_scores = jnp.einsum("gp,gkp->gk", query_float, docs, precision=highest_mode) * retrieval_scale
    soft = jax.nn.softmax(doc_scores, axis=-1)
    target = (jnp.arange(doc_scores.shape[1]) == 0).astype(F32)
    score_grad = (soft - target[None, :]) * retrieval_scale * mine[:, None]
    query_grad = jnp.einsum("gk,gkp->gp", score_grad, docs, precision=highest_mode).astype(BF)
    row_grads = score_grad[:, :, None] * query_float[:, None, :]
    cls_grad = jnp.einsum("gp,dp->gd", query_grad, proj, preferred_element_type=F32)
    proj_grad = jnp.einsum("gd,gp->dp", cls_low, query_grad, preferred_element_type=F32)
    table_rows = TAB_DEV * n_dp
    one_hot = (jnp.arange(table_rows)[:, None] == ids.reshape(1, -1)).astype(F32)
    table_local = jnp.dot(one_hot, row_grads.reshape(-1, row_grads.shape[2]), precision=highest_mode)

    def norm_back(dy, hat, root, gain):
        e = dy * gain
        back_ = e - jnp.mean(e, axis=-1, keepdims=True) - hat * jnp.mean(e * hat, axis=-1, keepdims=True)
        return back_ * root[:, :1], jnp.sum(dy * hat, axis=0), jnp.sum(dy, axis=0)

    dy = cot.astype(F32)
    first_rows = jnp.arange(n_mine) * seq_len
    dy = dy.at[first_rows].add(cls_grad)
    dz2, dg2, dc2 = norm_back(dy, xh2, r2, vec[6 + ff_rows])
    df = dz2.astype(BF)
    dg = jnp.einsum("td,hdf->htf", df, outer, preferred_element_type=F32)
    g_outer = jnp.einsum("td,htf->hdf", df, act_low, preferred_element_type=F32).astype(BF)
    du = (dg * slope.astype(F32)).astype(BF)
    normed_low = (xh1 * vec[3] + vec[4]).astype(BF)
    g_inner = jnp.einsum("td,htf->hdf", normed_low, du, preferred_element_type=F32).astype(BF)
    dh1 = jnp.einsum("htf,hdf->td", du, inner, preferred_element_type=F32) + dz2
    dz1, dg1, dc1 = norm_back(dh1, xh1, r1, vec[3])
    da = dz1.astype(BF)
    do = jnp.dot(da, va[1], preferred_element_type=F32).astype(BF)
    g_attn = jnp.einsum("td,te->de", da, mixed, preferred_element_type=F32)
    dqs, dks, dvs = [], [], []
    probs_of = (p_ab.reshape(full, -1, seq_len, seq_len), p_c.reshape(1, -1, n_half, seq_len))
    for qh, kh, vh, doh, pb in zip(*(halves(t, n_full, seq_len) for t in (q, k, v, do)), probs_of):
        probs = pb.astype(F32)
        dp_ = jnp.einsum("gqhe,gkhe->ghqk", doh, vh, preferred_element_type=F32)
        delta = jnp.sum(probs * dp_, axis=-1, keepdims=True)
        ds_ = (probs * (dp_ - delta)).astype(BF)
        dqs.append((jnp.einsum("ghqk,gkhe->gqhe", ds_, kh, preferred_element_type=F32) * score_scale).reshape(-1, width))
        dks.append((jnp.einsum("ghqk,gqhe->gkhe", ds_, qh, preferred_element_type=F32) * score_scale).reshape(-1, width))
        dvs.append(jnp.einsum("ghqk,gqhe->gkhe", pb, doh, preferred_element_type=F32).reshape(-1, width))
    dq = jnp.concatenate(dqs).astype(BF)
    dk = jnp.concatenate(dks).astype(BF)
    dv = jnp.concatenate(dvs).astype(BF)
    g_q = jnp.einsum("td,te->de", x_own, dq, preferred_element_type=F32)
    g_k = jnp.einsum("td,te->de", x_all, dk, preferred_element_type=F32)
    g_v = jnp.einsum("td,te->de", x_all, dv, preferred_element_type=F32)
    g_qk = jnp.stack([g_q, g_k]).astype(BF)
    g_va = jnp.stack([g_v, g_attn]).astype(BF)
    dx_own = jnp.einsum("te,de->td", dq, qk[0], preferred_element_type=F32) + dz1
    dx_all = jnp.einsum("te,de->td", dk, qk[1], preferred_element_type=F32)
    dx_all = dx_all + jnp.einsum("te,de->td", dv, va[0], preferred_element_type=F32)
    dx = jnp.concatenate([dx_all[:n_own] + dx_own, dx_all[n_own:]]).astype(BF)
    db_inner = jnp.sum(du.astype(F32), axis=1)
    db_inner = db_inner.reshape(2, 2, half_ff // 2).transpose(1, 0, 2).reshape(ff_rows, width)
    vec_grad = jnp.concatenate(
        [
            jnp.stack(
                [
                    jnp.sum(dq.astype(F32), axis=0),
                    jnp.sum(dv.astype(F32), axis=0),
                    jnp.sum(dz1, axis=0),
                    dg1,
                    dc1,
                ]
            ),
            db_inner,
            jnp.stack([jnp.sum(dz2, axis=0), dg2, dc2]),
        ]
    )
    vg = vec_grad.reshape(nvec, n_dp, 2, vec_lanes).transpose(1, 0, 2, 3)
    vg = jnp.pad(vg, ((0, 0), (0, 0), (0, 0), (0, 128 - vec_lanes))).reshape(n_dp, nvec, 256)
    pg = proj_grad.reshape(n_dp, 2, half_rows, 128).transpose(0, 2, 1, 3).reshape(n_dp, half_rows, 256)
    tg = table_local.reshape(n_dp, 2, TAB_DEV // 2, 128).transpose(0, 2, 1, 3).reshape(n_dp, TAB_DEV // 2, 256)
    small = jnp.concatenate([pg, vg, tg], axis=1)

    return out_own, dx, *reduce_plain([g_qk, g_va, g_inner, g_outer], small, out_own, dx, rows)


def local(
    tokens, cotangent, lengths, doc_ids, doc_rows,
    w_qkv, m_qkv, v_qkv, w_attn, m_attn, v_attn, w_inner, m_inner, v_inner,
    w_outer, m_outer, v_outer, w_proj, m_proj, v_proj, vectors, m_vectors, v_vectors,
):
    mp = lax.axis_index("mp")
    n_dp, n_mp = lax.axis_size("dp"), lax.axis_size("mp")
    fast = n_dp == NZ * NY * NC and n_mp == NX
    seqs = lengths.shape[0]
    all_rows, width = tokens.shape
    seq_len = all_rows // seqs
    full = seqs // 2
    n_full, n_half = full * seq_len, seq_len // 2
    n_own = n_full + n_half
    rows, half_ff = w_qkv.shape[1], w_inner.shape[1]
    half_rows = rows // 2
    nvec, vec_lanes = vectors.shape
    ff_rows = nvec - 8
    score_scale = HEAD_DIM ** (-0.5)

    if fast:
        saved = forward_fast(lengths, tokens, w_qkv, w_attn, w_inner, w_outer, w_proj, vectors)
        reduced = backward_fast(doc_ids, cotangent, doc_rows, saved, rows)
        params = (w_qkv, m_qkv, v_qkv, w_attn, m_attn, v_attn, w_inner, m_inner, v_inner)
        params += (w_outer, m_outer, v_outer, w_proj, m_proj, v_proj, vectors, m_vectors, v_vectors)
        return finish_fast(reduced, saved[-1], params, all_rows)
    if not fast:
        (out_own, dx, small_r, qk_r, va_r, inner_r, outer_r, peer_out, peer_dx, peer_small, total) = pass_plain(
            lengths, tokens, cotangent, doc_ids, doc_rows, w_qkv, w_attn, w_inner, w_outer, w_proj, vectors
        )
        vector_r = small_r[half_rows : half_rows + nvec, :vec_lanes]
        table_at = half_rows + nvec

    def whole_rows(own, peer):
        lo = jnp.where(mp == 0, own[:n_own], peer[:n_own])
        hi = jnp.where(mp == 0, peer[:n_own], own[:n_own])
        return lo, hi

    lo, hi = whole_rows(out_own, peer_out)
    out_tokens = jnp.concatenate([lo, hi[n_full:], hi[:n_full]])
    lo, hi = whole_rows(dx.astype(F32), peer_dx.astype(F32))
    tail = jnp.where(mp == 0, dx[n_own:], peer_dx[n_own:]).astype(F32)
    tail_hi = jnp.where(mp == 0, peer_dx[n_own:], dx[n_own:]).astype(F32)
    input_grad = jnp.concatenate(
        [lo[:n_full], lo[n_full:] + tail_hi, hi[n_full:] + tail, hi[:n_full]]
    )

    def both_halves(at, count):
        mine_, peer_ = small_r[at : at + count], peer_small[at : at + count]
        return jnp.concatenate(
            [jnp.where(mp == 0, mine_, peer_), jnp.where(mp == 0, peer_, mine_)]
        )

    proj_r = both_halves(0, half_rows)
    table_grad = both_halves(table_at, TAB_DEV // 2)
    qkv_r = jnp.stack([qk_r[0], qk_r[1], va_r[0]])
    attn_r = va_r[1]

    def back(v):
        return v.transpose(1, 0, 2).reshape(rows, half_ff)

    inner_r, outer_r = back(inner_r), back(outer_r)
    grad_norm = jnp.sqrt(total[0, 0])
    clip = clip_norm / jnp.maximum(grad_norm, clip_norm)
    results = [out_tokens, input_grad, grad_norm]
    for w, m, s, g, dec, rate in (
        (w_qkv, m_qkv, v_qkv, qkv_r, decay_rate, learn_rate),
        (w_attn, m_attn, v_attn, attn_r, decay_rate, learn_rate),
        (w_inner, m_inner, v_inner, inner_r, decay_rate, learn_rate),
        (w_outer, m_outer, v_outer, outer_r, decay_rate, learn_rate),
        (w_proj, m_proj, v_proj, proj_r, decay_rate, learn_rate),
        (vectors, m_vectors, v_vectors, vector_r, 0.0, vector_rate),
    ):
        results += list(adamw_update(w, m, s, g * clip, dec, rate))
    return tuple(results) + (table_grad,)


def solution(mesh):
    mat = P("dp", "mp")
    rep = P("dp", None)
    qkv = P(None, "dp", "mp")
    vec = P(None, ("dp", "mp"))
    placed = (rep, rep, P("dp"), rep, P("dp", None, None), qkv, qkv, qkv)
    placed += (mat,) * 9 + (rep,) * 3 + (vec,) * 3
    given = (rep, rep, P(), qkv, qkv, qkv) + (mat,) * 9 + (rep,) * 3 + (vec,) * 3 + (rep,)
    return jax.shard_map(local, mesh=mesh, in_specs=placed, out_specs=given, check_vma=False)
```

```python
import functools

import jax
import jax.numpy as jnp
from jax import lax
from jax.experimental import pallas as pl
from jax.experimental.pallas import tpu as pltpu
from jax.sharding import PartitionSpec as P

HEAD_DIM = 64
STEP = 10
TAB_DEV = 8
MESH = pl.DeviceIdType.MESH
ANY = pl.ANY
BF = jnp.bfloat16
F32 = jnp.float32
NZ, NY, NC, NX = 4, 2, 2, 2

highest_mode = lax.Precision.HIGHEST
retrieval_scale = 0.17677669529663687
ln_epsilon = 1e-12
beta_first = 0.9
beta_second = 0.999
learn_rate = 0.05
vector_rate = 0.5
decay_rate = 0.01
adam_epsilon = 1e-08
clip_norm = 1.0


def layer_norm(values, gain_row, shift_row):
    centre = jnp.mean(values, axis=-1, keepdims=True)
    centred = values - centre
    spread = jnp.mean(centred * centred, axis=-1, keepdims=True)
    return centred * lax.rsqrt(spread + ln_epsilon) * gain_row + shift_row


def gelu_exact(values):
    return jax.nn.gelu(values, approximate=False)


def adamw_update(weight, moment, second, gradient, decay_factor, step_rate):
    moment_new = beta_first * moment + (1.0 - beta_first) * gradient
    second_new = beta_second * second + (1.0 - beta_second) * gradient * gradient
    first_hat = moment_new / (1.0 - beta_first**STEP)
    second_hat = second_new / (1.0 - beta_second**STEP)
    weight_new = weight - step_rate * (
        first_hat / (jnp.sqrt(second_hat) + adam_epsilon) + decay_factor * weight
    )
    return (moment_new, second_new, weight_new)


def squared(values):
    return jnp.sum(values * values)


class Place:
    def __init__(self):
        dp = lax.axis_index("dp")
        self.x = lax.axis_index("mp")
        self.c = lax.rem(dp, NC)
        self.y = lax.rem(dp // NC, NY)
        self.z = dp // (NC * NY)

    def dev(self, z=None, y=None, c=None, x=None):
        z = self.z if z is None else z
        y = self.y if y is None else y
        c = self.c if c is None else c
        x = self.x if x is None else x
        return ((z * NY + y) * NC + c, x)

    def others(self):
        out = [self.dev(z=lax.rem(self.z + k, NZ)) for k in range(1, NZ)]
        out.append(self.dev(x=1 - self.x))
        out.append(self.dev(y=1 - self.y))
        out.append(self.dev(c=1 - self.c))
        return out

    def eights(self):
        out = []
        for k in range(1, 8):
            dx, dy, dc = k & 1, (k >> 1) & 1, k >> 2
            out.append(
                self.dev(
                    x=self.x + dx - 2 * dx * self.x,
                    y=self.y + dy - 2 * dy * self.y,
                    c=self.c + dc - 2 * dc * self.c,
                )
            )
        return out


def greet(devices):
    barrier = pltpu.get_barrier_semaphore()
    for d in devices:
        pl.semaphore_signal(barrier, inc=1, device_id=d, device_id_type=MESH)
    pl.semaphore_wait(barrier, len(devices))


def greet_send(devices):
    barrier = pltpu.get_barrier_semaphore()
    for d in devices:
        pl.semaphore_signal(barrier, inc=1, device_id=d, device_id_type=MESH)


def greet_wait(count):
    pl.semaphore_wait(pltpu.get_barrier_semaphore(), count)


def remote(src, dst, ssem, rsem, dev):
    return pltpu.make_async_remote_copy(
        src_ref=src, dst_ref=dst, send_sem=ssem, recv_sem=rsem, device_id=dev, device_id_type=MESH
    )


def cols(x, half):
    return pl.ds(pl.multiple_of(x * half, 128), half)


def dma(*shape):
    return pltpu.SemaphoreType.DMA(shape)


def mm(a, b):
    return jnp.dot(a, b, preferred_element_type=F32)


def mm_nt(a, b):
    return lax.dot_general(a, b, (((1,), (1,)), ((), ())), preferred_element_type=F32)


def mm_tn(a, b):
    return lax.dot_general(a, b, (((0,), (0,)), ((), ())), preferred_element_type=F32)


def flat(value):
    return value.reshape(-1, value.shape[-1])


def lanes(i, n=128):
    return pl.ds(pl.multiple_of(i * n, 128), n)


def rows_at(i, n, at=0):
    return pl.ds(pl.multiple_of(at + i * n, 16), n)


def each(n, body):
    lax.fori_loop(0, n, lambda i, c: (body(i), c)[1], 0)


gather_orders = ("zxy", "zxy", "yzx", "zxy", "zyx", "zxy", "zyx", "zxy", "zyx", "zxy", "zyx", "zxy", "xyz", "yxz", "zyx")


def stack_heads(pair, wide=None):
    low = jnp.where(lax.broadcasted_iota(jnp.int32, (1, 128), 1) < HEAD_DIM, 1.0, 0.0)
    parts = []
    for mask in (low, 1.0 - low):
        parts.append(pair * mask.astype(BF))
        if wide is not None:
            parts.append(jnp.zeros((wide - pair.shape[0], 128), BF))
    return jnp.concatenate(parts, axis=0)


class Gather:
    def __init__(self, me, pieces, sems):
        self.me, self.pieces = me, pieces
        self.lsem, self.ss, self.rs, self.ds, self.dr = sems
        self.waits, self.locs = [], {}

    def region(self, p, stage, c, **at):
        dst, me, done = self.pieces[p][1], self.me, gather_orders[p][:stage]
        half = dst.shape[-1] // 2
        z = at.get("z", None if "z" in done else me.z)
        y = at.get("y", None if "y" in done else me.y)
        x = at.get("x", None if "x" in done else me.x)
        zs = slice(None) if z is None else pl.ds(0, NZ - 1) if z == "three" else pl.ds(z, 1)
        ys = slice(None) if y is None else pl.ds(y, 1)
        xs = slice(None) if x is None else cols(x, half)
        return dst.at[zs, ys, c, :, xs]

    def bulk(self, p, stage, c):
        axis = gather_orders[p][stage]
        return self.region(p, stage, c, z="three") if axis == "z" else self.coming(p, stage, c)[0]

    def coming(self, p, stage, c):
        me, axis = self.me, gather_orders[p][stage]
        if axis == "z":
            return [self.region(p, stage, c, z=lax.rem(me.z + NZ - k, NZ)) for k in range(1, NZ)]
        return [self.region(p, stage, c, **{axis: 1 - (me.y if axis == "y" else me.x)})]

    def send(self, p, stage):
        me, axis = self.me, gather_orders[p][stage]
        src, dst = self.pieces[p]
        if stage == 0:
            to = dst.at[me.z, me.y, me.c, :, cols(me.x, dst.shape[-1] // 2)]
        else:
            src = to = self.region(p, stage, me.c)
        if axis == "z":
            devs = [me.dev(z=lax.rem(me.z + k, NZ)) for k in range(1, NZ)]
        else:
            devs = [me.dev(**{axis: 1 - (me.y if axis == "y" else me.x)})]
        for dev in devs:
            remote(src, to, self.ss.at[p, stage], self.rs.at[p, stage], dev).start()
        self.waits.append((self.bulk(p, stage, me.c), self.ss.at[p, stage]))

    def arrived(self, ref, sem):
        remote(ref, ref, sem, sem, self.me.dev(c=1 - self.me.c)).wait_recv()

    def receive(self, p, stage):
        self.arrived(self.bulk(p, stage, self.me.c), self.rs.at[p, stage])

    def crossing(self, p, stage, c):
        if stage == 0:
            ref = self.region(p, 1, c)
            return [ref], ref
        return self.coming(p, stage, c), self.bulk(p, stage, c)

    def cross(self, p, stage):
        refs, whole = self.crossing(p, stage, self.me.c)
        for ref in refs:
            remote(ref, ref, self.ds.at[p, stage], self.dr.at[p, stage], self.me.dev(c=1 - self.me.c)).start()
        self.waits.append((whole, self.ds.at[p, stage]))

    def step1(self, p):
        me = self.me
        src, dst = self.pieces[p]
        self.send(p, 0)
        blk = dst.at[me.z, me.y, me.c, :, cols(me.x, dst.shape[-1] // 2)]
        loc = pltpu.make_async_copy(src, blk, self.lsem.at[p])
        loc.start()
        self.locs[p] = loc

    def step2(self, p):
        self.locs[p].wait()
        self.receive(p, 0)
        self.send(p, 1)
        self.cross(p, 0)

    def step3(self, p):
        self.receive(p, 1)
        self.send(p, 2)
        self.cross(p, 1)

    def step4(self, p):
        self.receive(p, 2)
        self.cross(p, 2)

    def step5(self, p):
        for stage in range(3):
            self.arrived(self.crossing(p, stage, 1 - self.me.c)[1], self.dr.at[p, stage])

    def end(self):
        for ref, sem in self.waits:
            remote(ref, ref, sem, sem, self.me.dev(c=1 - self.me.c)).wait_send()


def norm_rows(z_ref, r_ref, n_rows, put):
    step = 48

    def body(i):
        at = rows_at(i, step)
        z = z_ref[at, :]
        centred = z - jnp.mean(z, axis=-1, keepdims=True)
        spread = jnp.mean(centred * centred, axis=-1, keepdims=True)
        root = lax.rsqrt(spread + ln_epsilon)
        hat = centred * root
        z_ref[at, :] = hat
        r_ref[at, :] = jnp.broadcast_to(root, (step, 128))
        put(at, hat)

    each(n_rows // step, body)


def forward_kernel(*refs):
    (lens, tokens, w_qkv, w_attn, w_inner, w_outer, w_proj, vectors) = refs[:8]
    outs = refs[8:27]
    scr = refs[27:]
    (vec_s, proj_s, qk_s, va_s, inner_s, outer_s, vec_g, proj_g, qk, va, inner, outer) = scr[:12]
    (xt, q, k, v, p, o, xh1, r1, g, gp, xh2, r2, out_own, proj, vec, x_all, h1b, vecp, bias_ff) = scr[12:31]
    gsems, tsem, osem = scr[31:36], scr[36], scr[37]
    me = Place()
    mp = me.x
    n_all, width = x_all.shape
    n_own = q.shape[0]
    half_seq = n_all - n_own
    seq = 2 * half_seq
    full = (n_own - half_seq) // seq
    n_full = full * seq
    half_ff = inner.shape[-1]
    rows = qk_s.shape[1]
    half_rows = rows // 2

    starts = (
        (mp * (n_full + seq), 0, n_full),
        (n_full + mp * half_seq, n_full, half_seq),
        (n_full + (1 - mp) * half_seq, n_own, half_seq),
    )
    loads = []
    for i, (at, to, n) in enumerate(starts):
        cp = pltpu.make_async_copy(
            tokens.at[pl.ds(pl.multiple_of(at, 16), n)], x_all.at[pl.ds(to, n)], tsem.at[i]
        )
        cp.start()
        loads.append(cp)

    greet_send(me.others())
    vecp[...] = jnp.zeros_like(vecp)
    nvec, nlane = vectors.shape
    vecp[0:nvec, 0:nlane] = vectors[...]
    proj_s[...] = w_proj[pl.ds(pl.multiple_of(mp * half_rows, 8), half_rows), :]
    vec_s[...] = jnp.transpose(vecp[...])[0:nlane]
    qk_s[...] = w_qkv[0:2].astype(BF)
    va_s[0] = w_qkv[2].astype(BF)
    va_s[1] = w_attn[...].astype(BF)
    hf = half_ff // 2
    for h in range(2):
        inner_s[h] = w_inner[:, h * hf : (h + 1) * hf].astype(BF)
        outer_s[h] = w_outer[:, h * hf : (h + 1) * hf].astype(BF)

    greet_wait(len(me.others()))
    row_cut = 32
    pieces = [
        (vec_s, vec_g),
        (qk_s.at[0], qk.at[0]),
        (qk_s.at[1], qk.at[1]),
        (va_s.at[0, pl.ds(0, row_cut)], va.at[0, :, :, :, pl.ds(0, row_cut)]),
        (va_s.at[0, pl.ds(row_cut, rows - row_cut)], va.at[0, :, :, :, pl.ds(row_cut, rows - row_cut)]),
        (va_s.at[1], va.at[1]),
    ]
    for shard, whole in ((inner_s, inner), (outer_s, outer)):
        for h in range(2):
            for j in range(2):
                src = shard.at[h, :, pl.ds(j * (hf // 2), hf // 2)]
                pieces.append((src, whole.at[h, :, :, :, :, pl.ds(j * hf, hf)]))
    pieces.append((proj_s, proj_g))
    net = Gather(me, pieces, gsems)

    def go(step, *members):
        for piece in members:
            (net.step1, net.step2, net.step3, net.step4, net.step5)[step - 1](piece)

    go(1, 0, 1, 2, 12, 13)
    saves = []

    def save(i, ref):
        cp = pltpu.make_async_copy(ref, outs[i], osem.at[i])
        cp.start()
        saves.append(cp)

    for cp in loads:
        cp.wait()

    def x_turn(i):
        xt[rows_at(i, 256), :] = jnp.transpose(x_all[:, lanes(i, 256)])

    each(width // 256, x_turn)
    save(4, xt)
    go(2, 2, 0)
    go(1, 3, 4)
    go(2, 1, 12, 13)
    go(1, 5)
    go(3, 0, 1, 2)
    go(1, 6)
    go(2, 3, 4)
    go(1, 7)
    go(4, 0)
    go(5, 0)
    big = []
    for z in range(NZ):
        for y in range(NY):
            for c in range(NC):
                for x in range(NX):
                    big.append(vec_g[z, y, c, :, x * 128 : (x + 1) * 128])
    vec[...] = jnp.transpose(jnp.concatenate(big, axis=0))[0 : vec.shape[0]]
    for h in range(2):
        for x in range(NX):
            for j in range(2):
                row = vec[5 + NX * x + h : 6 + NX * x + h, j * (hf // 2) : (j + 1) * (hf // 2)]
                bias_ff[h : h + 1, j * hf + x * (hf // 2) : j * hf + (x + 1) * (hf // 2)] = row
    save(17, vec)

    def project(w_ref, src_rows, dst, bias):
        n_tile = 256

        def body(i):
            w = flat(w_ref[:, :, :, :, lanes(i, n_tile)])
            r = mm(x_all[0:src_rows], w)
            if bias is not None:
                r = r + vec[bias : bias + 1, lanes(i, n_tile)]
            dst[:, lanes(i, n_tile)] = r.astype(BF)

        each(width // n_tile, body)

    go(3, 3)
    go(4, 1)
    go(3, 4)
    go(2, 5)
    go(1, 8)
    go(4, 2)
    go(5, 1)
    project(qk.at[0], n_own, q, 0)
    go(5, 2)
    go(2, 6)
    go(1, 9)
    project(qk.at[1], n_all, k, None)
    save(0, qk)
    go(4, 3, 4)
    go(3, 5)
    go(5, 3, 4)
    project(va.at[0], n_all, v, 1)
    go(2, 7)
    go(3, 6)
    go(1, 10)
    save(5, q)
    save(6, k)
    save(7, v)

    wide = 384
    pos = lax.broadcasted_iota(jnp.int32, (1, wide), 1)
    beyond = jnp.where(pos < seq, 0, 1 << 20)

    def attend(q0, nq, k0, slab, length, place):
        at_q = pl.ds(pl.multiple_of(q0, 16), nq)
        at_k = pl.ds(pl.multiple_of(k0, 16), seq)
        for pair in range(2):
            l = lanes(2 * slab + pair)
            s = mm_nt(q[at_q, l], stack_heads(k[at_k, l], wide)) * (HEAD_DIM**-0.5)
            both = []
            for h in range(2):
                part = jnp.where(place < length, s[:, h * wide : (h + 1) * wide], -1000000000.0)
                e = jnp.exp(part - jnp.max(part, axis=-1, keepdims=True))
                both.append((e * (1.0 / jnp.sum(e, axis=-1, keepdims=True))).astype(BF))
            pb = jnp.concatenate(both, axis=1)
            p[slab, at_q, 2 * wide * pair : 2 * wide * (pair + 1)] = pb
            o[at_q, l] = mm(pb, stack_heads(v[at_k, l], wide)).astype(BF)

    slabs = p.shape[0]
    jobs = [[(2, 8), (1, 11, 14), (3, 12)], [(3, 7)], [(2, 9)], [(4, 5), (3, 13)], [(2, 10), (4, 6)], [(3, 8), (5, 5, 6)]]
    for s in range(full):
        length = lens[mp * (full + 1) + s]
        for i in range(slabs):
            attend(s * seq, seq, s * seq, i, length, pos + beyond)
            for job in jobs[3 * s + i]:
                go(*job)
    length = lens[full]
    pos_c = jnp.where(pos < half_seq, pos + mp * half_seq, pos - half_seq + (1 - mp) * half_seq) + beyond
    for i in range(slabs):
        attend(n_full, half_seq, n_full, i, length, pos_c)
        if i == 1:
            go(3, 9)
    go(2, 11, 14)
    save(8, p)
    save(9, o)

    tile = 720
    tiles = n_own // tile

    def attn_out(i):
        a = mm_nt(o[rows_at(i, tile), :], flat(va[1]))
        xh1[rows_at(i, tile), :] = x_all[rows_at(i, tile), :].astype(F32) + a + vec[2:3, :]

    each(tiles, attn_out)
    go(4, 7)
    save(1, va)

    def put_h1(at, hat):
        h1b[at, :] = (hat * vec[3:4, :] + vec[4:5, :]).astype(BF)

    norm_rows(xh1, r1, n_own, put_h1)
    save(10, xh1)
    save(11, r1)
    go(5, 7)
    go(3, 10)
    go(4, 8)

    def feed(h):
        n_tile = 256

        def body(i):
            w = flat(inner[h, :, :, :, :, lanes(i, n_tile)])
            for t in range(tiles):
                at = pl.ds(t * tile, tile)
                u = mm(h1b[at, :], w)
                u = u + bias_ff[h : h + 1, lanes(i, n_tile)]
                tail = 0.5 * (1.0 + lax.erf(u * 0.7071067811865476))
                g[h, at, lanes(i, n_tile)] = (u * tail).astype(BF)
                slope = tail + u * (0.3989422804014327 * jnp.exp(-0.5 * u * u))
                gp[h, at, lanes(i, n_tile)] = slope.astype(BF)

        each(half_ff // n_tile, body)

    feed(0)
    go(3, 11)
    go(5, 8)
    go(4, 9)
    go(5, 9)
    feed(1)
    go(3, 14)
    go(4, 10, 12, 11, 13)
    go(5, 10, 12, 11, 13)
    save(2, inner)
    save(12, g)
    save(13, gp)

    def ff_out(i):
        at = rows_at(i, tile)
        f = mm_nt(g[0, at, :], flat(outer[0])) + mm_nt(g[1, at, :], flat(outer[1]))
        h1 = xh1[at, :] * vec[3:4, :] + vec[4:5, :]
        xh2[at, :] = h1 + f + vec[9:10, :]

    each(tiles, ff_out)
    save(3, outer)
    go(4, 14)

    def put_y(at, hat):
        out_own[at, :] = (hat * vec[10:11, :] + vec[11:12, :]).astype(BF)

    norm_rows(xh2, r2, n_own, put_y)
    save(14, xh2)
    save(15, r2)
    save(18, out_own)
    go(5, 14)
    for d in range(NZ * NY * NC * NX):
        block = proj_g[d // 8, d // 4 % 2, d // 2 % 2, :, d % 2 * 128 : (d % 2 + 1) * 128]
        proj[d * half_rows : (d + 1) * half_rows] = block
    save(16, proj)
    net.end()
    for cp in saves:
        cp.wait()


def forward_fast(lengths, tokens, w_qkv, w_attn, w_inner, w_outer, w_proj, vectors):
    seqs = lengths.shape[0]
    all_rows, width = tokens.shape
    seq = all_rows // seqs
    full = seqs // 2
    n_own = full * seq + seq // 2
    n_all = n_own + seq // 2
    rows, half_ff = w_qkv.shape[1], w_inner.shape[1]
    heads = width // HEAD_DIM
    zyc = (NZ, NY, NC)
    hr, nlane = rows // 2, vectors.shape[1]
    weights = [
        ((2,) + zyc + (rows, width), BF),
        ((2,) + zyc + (rows, width), BF),
        ((2,) + zyc + (rows, half_ff), BF),
        ((2,) + zyc + (rows, half_ff), BF),
    ]
    kept = [
        ((width, n_all), BF),
        ((n_own, width), BF),
        ((n_all, width), BF),
        ((n_all, width), BF),
        ((heads // 4, n_own, 4 * 384), BF),
        ((n_own, width), BF),
        ((n_own, width), F32),
        ((n_own, 128), F32),
        ((2, n_own, half_ff), BF),
        ((2, n_own, half_ff), BF),
        ((n_own, width), F32),
        ((n_own, 128), F32),
        ((width, 128), F32),
        ((16, width), F32),
        ((n_own, width), BF),
    ]
    order = kept[:12] + [kept[14], kept[12], kept[13]]
    scratch = [
        ((nlane, 128), F32),
        ((hr, 128), F32),
        ((2, rows, width // 2), BF),
        ((2, rows, width // 2), BF),
        ((2, rows, half_ff // 2), BF),
        ((2, rows, half_ff // 2), BF),
        (zyc + (nlane, 256), F32),
        (zyc + (hr, 256), F32),
    ]
    scratch += weights + order
    scratch += [((n_all, width), BF), ((n_own, width), BF), ((128, 128), F32), ((8, half_ff), F32)]
    n = 15
    vm = pl.BlockSpec(memory_space=pltpu.VMEM)
    hb = pl.BlockSpec(memory_space=ANY)
    sm = pl.BlockSpec(memory_space=pltpu.SMEM)
    return pl.pallas_call(
        forward_kernel,
        out_shape=[jax.ShapeDtypeStruct(s, d) for s, d in weights + kept],
        in_specs=[sm, hb] + [vm] * 6,
        out_specs=[hb] * 19,
        scratch_shapes=[pltpu.VMEM(s, d) for s, d in scratch]
        + [
            dma(n), dma(n, 3), dma(n, 3), dma(n, 3), dma(n, 3),
            dma(3), dma(20),
        ],
        compiler_params=pltpu.CompilerParams(
            collective_id=1, has_side_effects=True, vmem_limit_bytes=60 * 2**20
        ),
        name="forward",
    )(lengths, tokens, w_qkv, w_attn, w_inner, w_outer, w_proj, vectors)


class Reduce:
    def __init__(self, me, pieces, sems):
        self.me, self.pieces = me, pieces
        self.ds, self.dr, self.ss, self.rs = sems
        self.waits = []
        self.squares = jnp.zeros((1, 1), F32)

    def go(self, copy):
        copy.start()
        self.waits.append(copy)

    def arrived(self, ref, ssem, rsem):
        remote(ref, ref, ssem, rsem, self.me.dev(c=1 - self.me.c)).wait_recv()

    def region(self, p, stage, **at):
        order, src = self.pieces[p][0], self.pieces[p][2]
        me, done = self.me, order[:stage]
        half = src.shape[-1] // 2
        z = at.get("z", me.z if "z" in done else None)
        y = at.get("y", me.y if "y" in done else None)
        x = at.get("x", me.x if "x" in done else None)
        zs = slice(None) if z is None else pl.ds(0, NZ - 1) if z == "three" else pl.ds(z, 1)
        ys = slice(None) if y is None else pl.ds(y, 1)
        xs = slice(None) if x is None else cols(x, half)
        return src.at[zs, ys, me.c, :, xs]

    def send(self, p, stage):
        order, got, me = self.pieces[p][0], self.pieces[p][4 + stage], self.me
        ss, rs = self.ss, self.rs
        if order[stage] == "z":
            for k in range(1, NZ):
                tz = lax.rem(me.z + k, NZ)
                part = self.region(p, stage, z=tz)
                remote(part, got.at[pl.ds(k, 1)], ss.at[p, stage], rs.at[p, stage], me.dev(z=tz)).start()
            part = self.region(p, stage, z="three")
            self.waits.append(remote(part, part, ss.at[p, stage], rs.at[p, stage], me.dev(c=1 - me.c)))
        else:
            far = 1 - (me.y if order[stage] == "y" else me.x)
            part = self.region(p, stage, **{order[stage]: far})
            dev = me.dev(**{order[stage]: far})
            self.go(remote(part, got, ss.at[p, stage], rs.at[p, stage], dev))

    def receive(self, p, stage):
        order, got = self.pieces[p][0], self.pieces[p][4 + stage]
        if order[stage] == "z":
            got = got.at[pl.ds(1, NZ - 1)]
        self.arrived(got, self.ss.at[p, stage], self.rs.at[p, stage])

    def add(self, p, stage):
        order, _, src, _, *gots = self.pieces[p]
        got, me = gots[stage], self.me
        done = order[: stage + 1]
        half = src.shape[-1] // 2
        xs = cols(me.x, half) if "x" in done else slice(None)
        ys = [(me.y, 0)] if "y" in done else [(y, y) for y in range(NY)]
        if order[stage] == "z":
            for y, i in ys:
                total = src[me.z, y, me.c, :, xs].astype(F32)
                for k in range(1, NZ):
                    total = total + got[k, i].astype(F32)
                src[me.z, y, me.c, :, xs] = total.astype(src.dtype)
            return

        def one(z):
            for y, i in ys:
                src[z, y, me.c, :, xs] = src[z, y, me.c, :, xs] + got[0 if "z" in done else z, i]

        if "z" in done:
            one(me.z)
        else:
            each(NZ, one)

    def step1(self, p):
        src, got = self.pieces[p][2], self.pieces[p][3]
        oc = 1 - self.me.c
        self.go(remote(src.at[:, :, oc], got, self.ds.at[p], self.dr.at[p], self.me.dev(c=oc)))

    def step2(self, p):
        src, got, c = self.pieces[p][2], self.pieces[p][3], self.me.c
        self.arrived(got, self.ds.at[p], self.dr.at[p])

        def one(z):
            for y in range(NY):
                src[z, y, c] = src[z, y, c] + got[z, y]

        each(NZ, one)
        self.send(p, 0)

    def step3(self, p):
        self.receive(p, 0)
        self.add(p, 0)
        self.send(p, 1)

    def step4(self, p):
        self.receive(p, 1)
        self.add(p, 1)
        self.send(p, 2)

    def step5(self, p, counted=None):
        order, dst, src, _, *gots = self.pieces[p]
        me = self.me
        self.receive(p, 2)
        total = src[me.z, me.y, me.c, :, cols(me.x, src.shape[-1] // 2)].astype(F32)
        for k in range(1, NZ) if order[2] == "z" else (0,):
            total = total + gots[2][k, 0].astype(F32)
        dst[...] = total
        total = total[:counted]
        self.squares = self.squares + jnp.sum(total * total, keepdims=True)

    def end(self):
        for copy in self.waits:
            copy.wait_send()


def got_shapes(order, r, w):
    out, done = [], ""
    for axis in order:
        done += axis
        nz = NZ if axis == "z" or "z" not in done else 1
        out.append((nz, 1 if "y" in done else NY, r, w // 2 if "x" in done else w))
    return out


orders = ("yxz", "yxz", "zyx", "zyx", "yxz", "yxz", "yzx", "yxz", "yxz", "zyx", "yxz", "yxz", "yxz", "yxz")


def all_squares(me, net, total, sq4, sq8, sems):
    qs, qr, es, er = sems
    sq4[0] = jnp.broadcast_to(total, (8, 128))
    copies = []
    for k in range(1, NZ):
        copies.append(remote(sq4.at[0], sq4.at[k], qs.at[k], qr.at[k], me.dev(z=lax.rem(me.z + k, NZ))))
    for copy in copies:
        net.go(copy)
    for copy in copies:
        copy.wait_recv()

    def at_z(z):
        out = jnp.zeros((8, 128), F32)
        for k in range(NZ):
            out = out + jnp.where(lax.rem(me.z + NZ - k, NZ) == z, sq4[k], 0.0)
        return out

    sq8[0] = at_z(0) + at_z(1) + at_z(2) + at_z(3)
    copies = []
    for k, dev in enumerate(me.eights(), 1):
        copies.append(remote(sq8.at[0], sq8.at[k], es.at[k], er.at[k], dev))
    for copy in copies:
        net.go(copy)
    for copy in copies:
        copy.wait_recv()

    def at_code(w):
        out = jnp.zeros((8, 128), F32)
        for k in range(8):
            dx, dy, dc = k & 1, (k >> 1) & 1, k >> 2
            src = (
                (me.x + dx - 2 * dx * me.x)
                + 2 * (me.y + dy - 2 * dy * me.y)
                + 4 * (me.c + dc - 2 * dc * me.c)
            )
            out = out + jnp.where(src == w, sq8[k], 0.0)
        return out

    whole = at_code(0)
    for w in range(1, 8):
        whole = whole + at_code(w)
    return whole


def fold(value):
    return jnp.sum(value.reshape(-1, 8, value.shape[-1]), axis=0)


def norm_back_rows(n_rows, get_dy, hat_ref, root_ref, gain, put, acc):
    step = 48

    def body(i):
        at = rows_at(i, step)
        dy, hat = get_dy(i, at), hat_ref[at, :]
        e = dy * gain
        root = root_ref[at, 0:1]
        m1 = jnp.mean(e, axis=-1, keepdims=True)
        m2 = jnp.mean(e * hat, axis=-1, keepdims=True)
        dz = (e - m1 - hat * m2) * root
        acc[0] = acc[0] + fold(dy * hat)
        acc[1] = acc[1] + fold(dy)
        acc[2] = acc[2] + fold(dz)
        hat_ref[at, :] = dz
        put(at, dz)

    each(n_rows // step, body)


def backward_kernel(*refs):
    doc_ids, cotangent, doc_rows = refs[:3]
    (qk_h, va_h, inner_h, outer_h, xt_h, q_h, k_h, v_h, p_h, o_h, xh1_h, r1_h, g_h, gp_h, xh2_h, r2_h, proj_h, vec_h, out_h) = refs[3:22]
    outs = refs[22:32]
    small_r, qk_r, va_r, inner_r, outer_r, dx, peer_out, peer_dx, peer_small, norm_ref = outs
    scr = list(refs[32:])

    def take(n):
        got = scr[:n]
        del scr[:n]
        return got

    (inner, outer, attn, xt, q, k, v, o, xh1, gg, xh2, r2, proj, vec, cls_in, cot, df, dft) = take(18)
    (cls_grad, acc1, acc2, ffacc, vg, early, late) = take(7)
    grads = take(4)
    bufs = take(14 * 4)
    sq4, sq8 = take(2)
    lsem, rsems, xs, xr, qsems = take(1)[0], take(4), *take(2), take(4)
    do, da, dat, h1t, r1 = cot, df, dft, dft, r2
    me = Place()
    mp = me.x
    n_all, width = dx.shape
    n_own = q.shape[0]
    half_seq = n_all - n_own
    seq = 2 * half_seq
    n_full = n_own - half_seq
    full = n_full // seq
    half_ff = inner.shape[-1]
    other = me.dev(x=1 - mp)

    for i in range(4):
        grads.append(inner.at[i // 2, :, :, :, :, pl.ds(width * (i % 2), width)])
    copies = {}

    def load(name, i, src, dst):
        cp = pltpu.make_async_copy(src, dst, lsem.at[i])
        cp.start()
        copies[name] = cp

    def need(*names):
        for name in names:
            copies[name].wait()

    load("vec", 0, vec_h, vec)
    load("proj", 1, proj_h, proj)
    for s in range(full + 1):
        load("cls%d" % s, 2 + s, out_h.at[pl.ds(s * seq, 16)], cls_in.at[s])
    load("cot0", 5, cotangent.at[pl.ds(pl.multiple_of(mp * (n_full + seq), 16), n_full)], cot.at[pl.ds(0, n_full)])
    load("cot1", 6, cotangent.at[pl.ds(pl.multiple_of(n_full + mp * half_seq, 16), half_seq)], cot.at[pl.ds(n_full, half_seq)])
    load("xh2", 7, xh2_h, xh2)
    load("r2", 8, r2_h, r2)
    load("g", 9, g_h, gg.at[pl.ds(0, 2)])
    load("outer", 10, outer_h, outer)
    load("gp", 11, gp_h, gg.at[pl.ds(2, 2)])
    load("xh1", 12, xh1_h, xh1)
    load("inner", 14, inner_h, inner)
    load("attn", 15, va_h.at[1], attn)
    load("o", 16, o_h, o)
    load("q", 17, q_h, q)
    load("k", 18, k_h, k)
    load("v", 19, v_h, v)
    load("xt", 20, xt_h, xt)

    greet(me.others() + me.eights())
    pieces = []
    hr = width // (NZ * NY * NC * NX)
    n_early = early.shape[3]
    hf = half_ff // 2
    dsts, srcs = [], []
    for i, ref in enumerate((outer_r, inner_r)):
        for h in range(2):
            for j in range(2):
                dsts.append(ref.at[h, :, pl.ds(j * (hf // 2), hf // 2)])
                srcs.append(grads[2 * i + h].at[:, :, :, :, pl.ds(j * hf, hf)])
    dsts += [va_r.at[1], va_r.at[0], qk_r.at[0], qk_r.at[1]]
    dsts += [small_r.at[pl.ds(0, n_early)], small_r.at[pl.ds(n_early, hr)]]
    srcs += grads[4:] + [early, late]
    for i in range(14):
        pieces.append((orders[i], dsts[i], srcs[i]) + tuple(bufs[4 * i : 4 * i + 4]))
    net = Reduce(me, pieces, rsems)

    def go(step, *members):
        for piece in members:
            if step == 5 and piece == 12:
                net.step5(piece, hr)
            else:
                (net.step1, net.step2, net.step3, net.step4, net.step5)[step - 1](piece)

    send_out = remote(out_h, peer_out, xs.at[0], xr.at[0], other)
    net.go(send_out)

    vg[...] = jnp.zeros_like(vg)
    early[...] = jnp.zeros_like(early)
    acc1[...] = jnp.zeros_like(acc1)
    acc2[...] = jnp.zeros_like(acc2)
    ffacc[...] = jnp.zeros_like(ffacc)
    need("vec", "proj", *["cls%d" % s for s in range(full + 1)])
    row16 = lax.broadcasted_iota(jnp.int32, (16, 1), 0)
    cls = jnp.zeros((16, width), F32)
    for s in range(full + 1):
        cls = jnp.where(row16 == s, cls_in[s].astype(F32)[0:1], cls)
    cls = cls.astype(BF)
    proj_low = proj[...].astype(BF)
    query = mm(cls, proj_low).astype(BF).astype(F32)
    row8 = lax.broadcasted_iota(jnp.int32, (8, 1), 0)
    dcq = jnp.zeros((16, 128), F32)
    row_grads = []
    cands = doc_ids.shape[1]
    seq_ids = [mp * (full + 1) + s for s in range(full)] + [full]
    for s in range(full + 1):
        docs = doc_rows[seq_ids[s]].astype(F32)
        mine = 1.0 if s < full else jnp.where(mp == 0, 1.0, 0.0)
        query_s = query[s : s + 1]
        score = jnp.sum(query_s * docs, axis=-1, keepdims=True) * retrieval_scale
        e = jnp.exp(score - jnp.max(score, axis=0, keepdims=True))
        soft = e / jnp.sum(e, axis=0, keepdims=True)
        sg = (soft - jnp.where(row8 == 0, 1.0, 0.0)) * (retrieval_scale * mine)
        dcq = jnp.where(row16 == s, jnp.sum(sg * docs, axis=0, keepdims=True), dcq)
        row_grads.append(sg * query_s)
    dcq = dcq.astype(BF)
    cls_grad[...] = mm_nt(dcq, proj_low)
    proj_grad = mm_tn(cls, dcq)
    n_dev = NZ * NY * NC * NX
    table_row = lax.broadcasted_iota(jnp.int32, (TAB_DEV * n_dev // NX, 1), 0)
    table = jnp.zeros((TAB_DEV * n_dev // NX, 128), F32)
    for s in range(full + 1):
        for i in range(cands):
            table = table + jnp.where(table_row == doc_ids[seq_ids[s], i], row_grads[s][i : i + 1], 0.0)
    tr = TAB_DEV // NX
    for d in range(n_dev):
        z, y, c, x = d // 8, d // 4 % 2, d // 2 % 2, d % 2
        l = slice(x * 128, (x + 1) * 128)
        t0 = (d // 2) * TAB_DEV + x * tr
        early[z, y, c, 0:hr, l] = proj_grad[d * hr : (d + 1) * hr]
        early[z, y, c, hr : hr + tr, l] = table[t0 : t0 + tr]
    go(1, 12)

    per = seq // 48
    row48 = lax.broadcasted_iota(jnp.int32, (48, 1), 0)

    def get_dy(i, at):
        first = (row48 == 0) & (lax.rem(i, per) == 0)
        return cot[at, :].astype(F32) + jnp.where(first, cls_grad[pl.ds(i // per, 1), :], 0.0)

    def put_df(at, dz):
        df[at, :] = dz.astype(BF)

    need("cot0", "cot1", "xh2", "r2")
    norm_back_rows(n_own, get_dy, xh2, r2, vec[10:11, :], put_df, acc2)

    def turn(src, dst, n_rows):
        def body(i):
            dst[rows_at(i, 256), 0:n_rows] = jnp.transpose(src[:, lanes(i, 256)])

        each(width // 256, body)

    load("r1", 13, r1_h, r1)
    turn(df, dft, n_own)
    go(2, 12)
    n_tile = 256
    shape5 = (NZ, NY, NC, width // (NZ * NY * NC))

    def weight_grad(left, right, dst, n, at=0):
        def body(i):
            r = mm(left(), right(lanes(i + at, n_tile)))
            dst[:, :, :, :, lanes(i + at, n_tile)] = r.astype(BF).reshape(shape5 + (n_tile,))

        each(n // n_tile, body)

    need("g")
    for h in range(2):
        for j in range(2):
            weight_grad(lambda: dft[:, 0:n_own], lambda l: gg[h, :, l], grads[h], hf, j * (hf // n_tile))
            i = 2 * h + j
            go(1, i)
            if i > 1:
                go(2, i - 2)

    need("outer", "gp")
    tile = 720
    tiles = n_own // tile

    def hidden(h):
        def body(i):
            w = flat(outer[h, :, :, :, :, lanes(i, n_tile)])
            for t in range(tiles):
                at = pl.ds(t * tile, tile)
                du = (mm(df[at, :], w) * gg[2 + h, at, lanes(i, n_tile)].astype(F32)).astype(BF)
                gg[2 + h, at, lanes(i, n_tile)] = du
                ffacc[h, :, lanes(i, n_tile)] = ffacc[h, :, lanes(i, n_tile)] + fold(du.astype(F32))

        each(half_ff // n_tile, body)

    go(2, 2)
    hidden(0)
    go(2, 3)
    go(3, 12)
    hidden(1)
    load("p0", 21, p_h.at[0], gg.at[0])
    load("p1", 22, p_h.at[1], gg.at[1])
    load("wq", 23, qk_h.at[0], outer.at[0, :, :, :, :, pl.ds(0, width)])
    load("wk", 24, qk_h.at[1], outer.at[0, :, :, :, :, pl.ds(width, width)])
    load("wv", 25, va_h.at[0], outer.at[1, :, :, :, :, pl.ds(0, width)])
    need("xh1", "r1")

    def h1_turn(i):
        l = lanes(i, 256)
        h1 = (xh1[:, l] * vec[3:4, l] + vec[4:5, l]).astype(BF)
        h1t[rows_at(i, 256), 0:n_own] = jnp.transpose(h1)

    each(width // 256, h1_turn)
    for h in range(2):
        for j in range(2):
            weight_grad(lambda: h1t[:, 0:n_own], lambda l: gg[2 + h, :, l], grads[2 + h], hf, j * (hf // n_tile))
            i = 4 + 2 * h + j
            go(1, i)
            if i > 5:
                go(2, i - 2)
            if i == 5:
                go(3, 0)
            if i == 7:
                go(3, 1)
    need("inner")

    def hidden_back(i):
        at = rows_at(i, tile)
        d = mm_nt(gg[2, at, :], flat(inner[0])) + mm_nt(gg[3, at, :], flat(inner[1]))
        xh2[at, :] = d + xh2[at, :]

    each(tiles, hidden_back)
    load("p2", 26, p_h.at[2], gg.at[2])
    go(2, 6, 7)

    norm_back_rows(n_own, lambda i, at: xh2[at, :], xh1, r1, vec[3:4, :], put_df, acc1)
    need("attn", "o")

    def mixed_back(i):
        do[:, lanes(i, n_tile)] = mm(da[...], flat(attn[:, :, :, :, lanes(i, n_tile)])).astype(BF)

    each(width // n_tile, mixed_back)
    turn(da, dat, n_own)
    weight_grad(lambda: dat[:, 0:n_own], lambda l: o[:, l], grads[4], width)
    go(1, 8)
    go(3, 4, 2)

    need("q", "k", "v", "p0", "p1", "p2")
    wide = 384
    scale = HEAD_DIM**-0.5

    def attend(q0, nq, k0, slab):
        at_q = pl.ds(pl.multiple_of(q0, 16), nq)
        at_k = pl.ds(pl.multiple_of(k0, 16), seq)
        for pair in range(2):
            l = lanes(2 * slab + pair)
            qp, kp, dop = q[at_q, l], k[at_k, l], do[at_q, l]
            pb = gg[slab, at_q, 2 * wide * pair : 2 * wide * (pair + 1)]
            p = pb.astype(F32)
            pd = p * mm_nt(dop, stack_heads(v[at_k, l], wide))
            ds, pbs = [], []
            for h in range(2):
                at = slice(h * wide, (h + 1) * wide)
                ds.append((pd[:, at] - p[:, at] * jnp.sum(pd[:, at], axis=-1, keepdims=True)).astype(BF))
                pbs.append(pb[:, h * wide : h * wide + seq])
            q[at_q, l] = (mm(jnp.concatenate(ds, axis=1), stack_heads(kp, wide)) * scale).astype(BF)
            ds = jnp.concatenate([d[:, 0:seq] for d in ds], axis=0)
            k[at_k, l] = (mm_tn(ds, stack_heads(qp)) * scale).astype(BF)
            v[at_k, l] = mm_tn(jnp.concatenate(pbs, axis=0), stack_heads(dop)).astype(BF)

    slabs = p_h.shape[0]

    def tokens_back(at, own):
        d = mm_nt(k[at, :], flat(outer[0, :, :, :, :, width : 2 * width]))
        d = d + mm_nt(v[at, :], flat(outer[1, :, :, :, :, 0:width]))
        if own:
            d = d + mm_nt(q[at, :], flat(outer[0, :, :, :, :, 0:width])) + xh1[at, :]
            o[at, :] = d.astype(BF)
        else:
            df[0:half_seq, :] = d.astype(BF)

    keeps = []

    def send_dx(i, src, at):
        net.go(remote(src, peer_dx.at[at], xs.at[1 + i], xr.at[1 + i], other))
        cp = pltpu.make_async_copy(src, dx.at[at], lsem.at[27 + i])
        cp.start()
        keeps.append(cp)

    need("wq", "wk", "wv")
    for s in range(full):
        for i in range(slabs):
            attend(s * seq, seq, s * seq, i)
            if s == 0:
                (lambda: (go(2, 8), go(4, 0, 1)), lambda: go(3, 5), lambda: (go(3, 3), go(4, 12)))[i]()
            else:
                (lambda: go(4, 4), lambda: go(3, 6), lambda: go(5, 0, 1))[i]()
        tokens_back(pl.ds(s * seq, seq), True)
        size = seq if s == 0 else half_seq
        send_dx(s, o.at[pl.ds(s * seq, size)], pl.ds(s * seq, size))
    for i in range(slabs):
        attend(n_full, half_seq, n_full, i)
        (lambda: go(3, 7), lambda: go(4, 5), lambda: go(4, 2))[i]()
    need("xt")
    weight_grad(lambda: xt[...], lambda l: v[:, l], grads[5], width)
    go(1, 9)
    send_dx(2, o.at[pl.ds(n_full - half_seq, half_seq)], pl.ds(n_full - half_seq, half_seq))
    weight_grad(lambda: xt[:, 0:n_own], lambda l: q[:, l], grads[6], width)
    go(1, 10)
    go(2, 9)
    go(4, 6)
    weight_grad(lambda: xt[...], lambda l: k[:, l], grads[7], width)
    go(1, 11)
    go(2, 10)
    go(3, 8)
    go(4, 3)
    tokens_back(pl.ds(n_full, half_seq), True)
    go(2, 11)
    tokens_back(pl.ds(n_own, half_seq), False)

    vg[0:1, :] = jnp.sum(q[...].astype(F32), axis=0, keepdims=True)
    vg[1:2, :] = jnp.sum(v[...].astype(F32), axis=0, keepdims=True)
    vg[2:3, :] = jnp.sum(acc1[2], axis=0, keepdims=True)
    vg[3:4, :] = jnp.sum(acc1[0], axis=0, keepdims=True)
    vg[4:5, :] = jnp.sum(acc1[1], axis=0, keepdims=True)
    for h in range(2):
        both = jnp.sum(ffacc[h], axis=0, keepdims=True)
        for x in range(NX):
            for j in range(2):
                at = j * hf + x * (hf // 2)
                vg[5 + NX * x + h : 6 + NX * x + h, j * (hf // 2) : (j + 1) * (hf // 2)] = both[:, at : at + hf // 2]
    vg[9:10, :] = jnp.sum(acc2[2], axis=0, keepdims=True)
    vg[10:11, :] = jnp.sum(acc2[0], axis=0, keepdims=True)
    vg[11:12, :] = jnp.sum(acc2[1], axis=0, keepdims=True)
    turned = jnp.transpose(vg[...])
    for d in range(n_dev):
        z, y, c, x = d // 8, d // 4 % 2, d // 2 % 2, d % 2
        late[z, y, c, :, x * 128 : (x + 1) * 128] = turned[d * hr : (d + 1) * hr]
    go(1, 13)
    go(2, 13)
    go(4, 7)
    go(5, 4, 5, 12)
    go(3, 10)
    go(3, 11)
    go(4, 8)
    go(3, 9)
    go(4, 10)
    go(3, 13)
    send_dx(3, o.at[pl.ds(n_full, half_seq)], pl.ds(n_full, half_seq))
    go(4, 9)
    go(4, 11)
    send_dx(4, df.at[pl.ds(0, half_seq)], pl.ds(n_own, half_seq))
    go(4, 13)
    go(5, 2, 3, 6, 7, 8, 10, 9)
    go(5, 11, 13)
    net.go(remote(small_r, peer_small, xs.at[6], xr.at[6], other))
    norm_ref[...] = all_squares(me, net, net.squares, sq4, sq8, qsems)
    parts = [pl.ds(0, seq)] + [pl.ds(seq + i * half_seq, half_seq) for i in range(4)]
    for i, ref in enumerate([peer_out] + [peer_dx.at[at] for at in parts] + [peer_small]):
        net.arrived(ref, xs.at[i], xr.at[i])
    for cp in keeps:
        cp.wait()
    net.end()


def backward_fast(doc_ids, cotangent, doc_rows, saved, rows):
    (qk, va, inner, outer, xt, q, k, v, p, o, xh1, r1, g, gp, xh2, r2, proj, vec, out_own) = saved
    n_own, width = q.shape
    n_all = k.shape[0]
    half_ff = inner.shape[-1]
    zyc = (NZ, NY, NC)
    hr = rows // NX
    n_early = hr + 8
    small_rows = n_early + hr
    ins = [doc_ids, cotangent, doc_rows] + list(saved)
    out_shape = [
        ((small_rows, 128), F32),
        ((2, rows, width // 2), F32),
        ((2, rows, width // 2), F32),
        ((2, rows, half_ff // 2), F32),
        ((2, rows, half_ff // 2), F32),
        ((n_all, width), BF),
        ((n_own, width), BF),
        ((n_all, width), BF),
        ((small_rows, 128), F32),
        ((8, 128), F32),
    ]
    like = lambda a: (a.shape, a.dtype)
    wide = width // 128 * 128
    scratch = [
        like(inner), like(outer), (va.shape[1:], BF), like(xt), like(q), like(k), like(v), like(o),
        like(xh1), ((4,) + g.shape[1:], BF), like(xh2), like(r2), like(proj), like(vec),
        ((3, 16, width), BF), ((n_own, width), BF), ((n_own, width), BF),
        ((width, wide), BF),
        ((16, width), F32), ((3, 8, width), F32), ((3, 8, width), F32), ((2, 8, half_ff), F32),
        ((128, width), F32), (zyc + (n_early, 256), F32), (zyc + (hr, 256), F32),
    ]
    sizes = [half_ff] * 4 + [width] * 4
    scratch += [(zyc + (rows, w), BF) for w in sizes[:4]]
    smalls = [(n_early, 256, F32), (hr, 256, F32)]
    for i, (r, w, dt) in enumerate([(rows, width, BF)] * 12 + smalls):
        scratch += [((NZ, NY, r, w), dt)] + [(shape, dt) for shape in got_shapes(orders[i], r, w)]
    scratch += [((NZ, 8, 128), F32), ((8, 8, 128), F32)]
    vm = pl.BlockSpec(memory_space=pltpu.VMEM)
    hb = pl.BlockSpec(memory_space=ANY)
    sm = pl.BlockSpec(memory_space=pltpu.SMEM)
    n = 14
    return pl.pallas_call(
        backward_kernel,
        out_shape=[jax.ShapeDtypeStruct(s, d) for s, d in out_shape],
        in_specs=[sm, hb, vm] + [hb] * 19,
        out_specs=[vm] * 5 + [hb, hb, hb, vm, vm],
        scratch_shapes=[pltpu.VMEM(s, d) for s, d in scratch]
        + [
            dma(32), dma(n), dma(n), dma(n, 3), dma(n, 3),
            dma(7), dma(7), dma(NZ), dma(NZ), dma(8), dma(8),
        ],
        compiler_params=pltpu.CompilerParams(
            collective_id=2, has_side_effects=True, vmem_limit_bytes=63 * 2**20
        ),
        name="backward",
    )(*ins)


def finish_kernel(*refs):
    small_r, peer_small, qk_r, va_r, inner_r, outer_r, total = refs[:7]
    out_own, peer_out, dx, peer_dx = refs[7:11]
    params = [refs[11 + 3 * i : 14 + 3 * i] for i in range(6)]
    outs = refs[29:51]
    turn, sem, lo, hi, mid = refs[51:]
    out_tokens, input_grad, norm = outs[0:3]
    news = [outs[3 + 3 * i : 6 + 3 * i] for i in range(6)]
    table_grad = outs[21]
    mp = lax.axis_index("mp")
    n_own = out_own.shape[0]
    n_all = dx.shape[0]
    half_seq = n_all - n_own
    n_full = n_own - half_seq
    seq = 2 * half_seq
    copies = []
    for i, (src, first) in enumerate(((out_own, mp), (peer_out, 1 - mp))):
        at = pl.multiple_of(first * (n_full + seq), 16)
        copies.append((src.at[pl.ds(0, n_full)], out_tokens.at[pl.ds(at, n_full)]))
        at = pl.multiple_of(n_full + first * half_seq, 16)
        copies.append((src.at[pl.ds(n_full, half_seq)], out_tokens.at[pl.ds(at, half_seq)]))
    copies = [pltpu.make_async_copy(s, d, sem.at[i]) for i, (s, d) in enumerate(copies)]
    for cp in copies:
        cp.start()
    lo[...] = dx[0:n_full].astype(F32)
    hi[...] = peer_dx[0:n_full].astype(F32)
    own_mid = dx[n_full:n_own].astype(F32) + peer_dx[n_own:n_all].astype(F32)
    peer_mid = peer_dx[n_full:n_own].astype(F32) + dx[n_own:n_all].astype(F32)
    mid[pl.ds(pl.multiple_of(mp * half_seq, 16), half_seq)] = own_mid
    mid[pl.ds(pl.multiple_of((1 - mp) * half_seq, 16), half_seq)] = peer_mid
    grads = (
        (lo, pl.multiple_of(mp * (n_full + seq), 16), n_full),
        (hi, pl.multiple_of((1 - mp) * (n_full + seq), 16), n_full),
        (mid, n_full, seq),
    )
    for i, (src, at, n) in enumerate(grads):
        cp = pltpu.make_async_copy(src, input_grad.at[pl.ds(at, n)], sem.at[4 + i])
        cp.start()
        copies.append(cp)

    root = jnp.sqrt(total[...])
    norm[0, 0] = jnp.max(root)
    clip = clip_norm / jnp.maximum(root[0:1, 0:1], clip_norm)
    hf = inner_r.shape[-1]
    hr = params[4][0].shape[0] // 2
    nvec, nlane = params[5][0].shape
    tr = table_grad.shape[0] // 2

    def adam(which, at, g, dec, rate):
        w, m, s = (ref[at] for ref in params[which])
        for ref, new in zip(news[which], adamw_update(w, m, s, g * clip, dec, rate)):
            ref[at] = new

    for j in range(3):
        g = qk_r[j] if j < 2 else va_r[0]
        adam(0, (j,), g, decay_rate, learn_rate)
    adam(1, (slice(None), slice(None)), va_r[1], decay_rate, learn_rate)
    for which, ref in ((2, inner_r), (3, outer_r)):
        for h in range(2):
            adam(which, (slice(None), slice(h * hf, (h + 1) * hf)), ref[h], decay_rate, learn_rate)
    turn[...] = jnp.zeros_like(turn)
    turn[0:nlane] = small_r[hr + 8 : hr + 8 + nlane]
    adam(5, (slice(None), slice(None)), jnp.transpose(turn[...])[0:nvec, 0:nlane], 0.0, vector_rate)
    for block, first in ((small_r, mp), (peer_small, 1 - mp)):
        at = pl.ds(pl.multiple_of(first * hr, 8), hr)
        adam(4, (at, slice(None)), block[0:hr], decay_rate, learn_rate)
    own_t, peer_t = small_r[hr : hr + tr], peer_small[hr : hr + tr]
    table_grad[0:tr] = jnp.where(mp == 0, own_t, peer_t)
    table_grad[tr : 2 * tr] = jnp.where(mp == 0, peer_t, own_t)
    for cp in copies:
        cp.wait()


def finish_fast(reduced, out_own, params, n_rows):
    (small_r, qk_r, va_r, inner_r, outer_r, dx, peer_out, peer_dx, peer_small, total) = reduced
    n_own, width = out_own.shape
    n_all = dx.shape[0]
    half_seq = n_all - n_own
    like = lambda a: jax.ShapeDtypeStruct(a.shape, a.dtype)
    vm = pl.BlockSpec(memory_space=pltpu.VMEM)
    hb = pl.BlockSpec(memory_space=ANY)
    sm = pl.BlockSpec(memory_space=pltpu.SMEM)
    out_shape = [
        jax.ShapeDtypeStruct((n_rows, width), BF),
        jax.ShapeDtypeStruct((n_rows, width), F32),
        jax.ShapeDtypeStruct((1, 1), F32),
    ]
    out_shape += [like(a) for a in params] + [jax.ShapeDtypeStruct((TAB_DEV, 128), F32)]
    n_full = n_own - half_seq
    outs = pl.pallas_call(
        finish_kernel,
        out_shape=out_shape,
        in_specs=[vm] * 29,
        out_specs=[hb, hb, sm] + [vm] * 19,
        scratch_shapes=[
            pltpu.VMEM((128, 128), F32),
            dma(7),
            pltpu.VMEM((n_full, width), F32),
            pltpu.VMEM((n_full, width), F32),
            pltpu.VMEM((2 * half_seq, width), F32),
        ],
        compiler_params=pltpu.CompilerParams(vmem_limit_bytes=63 * 2**20),
        name="finish",
    )(small_r, peer_small, qk_r, va_r, inner_r, outer_r, total, out_own, peer_out, dx, peer_dx, *params)
    return tuple(outs[:2]) + (outs[2].reshape(()),) + tuple(outs[3:])


def gather_plain(shards, small, rows):
    def both(v, axis):
        v = lax.all_gather(v, "dp", axis=axis, tiled=True)
        return lax.all_gather(v, "mp", axis=2, tiled=True)

    return [both(small[None], 0)] + [both(v, 1) for v in shards]


def reduce_plain(grads, small, own_out, own_dx, rows):
    def both(v, axis, wide):
        v = lax.psum_scatter(v.astype(F32), "mp", scatter_dimension=wide, tiled=True)
        return lax.psum_scatter(v, "dp", scatter_dimension=axis, tiled=True)

    small_sum = both(small, 0, 2)[0]
    sums = [both(g, 1, 2) for g in grads]
    ox = 1 - lax.axis_index("mp")
    swap = [(0, 1), (1, 0)]
    peer_out = lax.ppermute(own_out, "mp", swap)
    peer_dx = lax.ppermute(own_dx, "mp", swap)
    peer_small = lax.ppermute(small_sum, "mp", swap)
    squares = sum(squared(g) for g in sums) + squared(small_sum[:-4])
    total = lax.psum(squares, ("dp", "mp"))
    return [small_sum] + sums + [peer_out, peer_dx, peer_small, jnp.full((8, 128), total)]


def forward_plain(lengths, tokens, w_qkv, w_attn, w_inner, w_outer, w_proj, vectors):
    mp = lax.axis_index("mp")
    n_dp = lax.axis_size("dp")
    seqs = lengths.shape[0]
    all_rows, width = tokens.shape
    seq_len = all_rows // seqs
    full = seqs // 2
    n_full, n_half = full * seq_len, seq_len // 2
    n_own = n_full + n_half
    heads = width // HEAD_DIM
    rows, half_ff = w_qkv.shape[1], w_inner.shape[1]
    nvec, vec_lanes = vectors.shape
    half_rows = rows // 2
    score_scale = HEAD_DIM ** (-0.5)

    def two(v):
        return v.reshape(rows, 2, half_ff // 2).transpose(1, 0, 2)

    qk_s = w_qkv[:2].astype(BF)
    va_s = jnp.stack([w_qkv[2], w_attn]).astype(BF)
    vec_pad = jnp.pad(vectors, ((0, 0), (0, 128 - vec_lanes)))
    proj_half = lax.dynamic_slice_in_dim(w_proj, mp * half_rows, half_rows, 0)
    small_s = jnp.concatenate([proj_half, vec_pad], axis=0)
    small_g, qk, va, inner, outer = gather_plain(
        [qk_s, va_s, two(w_inner.astype(BF)), two(w_outer.astype(BF))], small_s, rows
    )
    small_g = small_g.reshape(n_dp, half_rows + nvec, 2, 128)
    proj = small_g[:, :half_rows].transpose(0, 2, 1, 3).reshape(width, 128)
    vec = small_g[:, half_rows:, :, :vec_lanes].transpose(1, 0, 2, 3).reshape(nvec, width)
    ff_rows = nvec - 8
    b_inner = vec[5 : 5 + ff_rows].reshape(2, 2, half_ff // 2).transpose(1, 0, 2).reshape(2, half_ff)

    a0 = mp * (n_full + seq_len)
    h0 = n_full + mp * n_half
    o0 = n_full + (1 - mp) * n_half
    x_all = jnp.concatenate(
        [
            lax.dynamic_slice_in_dim(tokens, a0, n_full, 0),
            lax.dynamic_slice_in_dim(tokens, h0, n_half, 0),
            lax.dynamic_slice_in_dim(tokens, o0, n_half, 0),
        ]
    )
    x_own = x_all[:n_own]
    my_seqs = jnp.concatenate([mp * (full + 1) + jnp.arange(full), jnp.array([full])])
    my_len = lengths[my_seqs]
    pos = jnp.arange(seq_len)
    pos_last = jnp.where(pos < n_half, pos + mp * n_half, pos - n_half + (1 - mp) * n_half)
    valids = (pos[None, :] < my_len[:full, None], pos_last[None, :] < my_len[full:, None])

    q = (jnp.dot(x_own, qk[0], preferred_element_type=F32) + vec[0]).astype(BF)
    k = jnp.dot(x_all, qk[1], preferred_element_type=F32).astype(BF)
    v = (jnp.dot(x_all, va[0], preferred_element_type=F32) + vec[1]).astype(BF)
    probs, outs = [], []
    for qh, kh, vh, valid in zip(*(halves(t, n_full, seq_len) for t in (q, k, v)), valids):
        s = jnp.einsum("gqhe,gkhe->ghqk", qh, kh, preferred_element_type=F32) * score_scale
        s = jnp.where(valid[:, None, None, :], s, -1000000000.0)
        pb = jax.nn.softmax(s, axis=-1).astype(BF)
        o = jnp.einsum("ghqk,gkhe->gqhe", pb, vh, preferred_element_type=F32)
        outs.append(o.reshape(-1, width).astype(BF))
        probs.append(pb.reshape((-1,) + pb.shape[2:]))
    mixed = jnp.concatenate(outs)

    def norm(z):
        centred = z - jnp.mean(z, axis=-1, keepdims=True)
        root = lax.rsqrt(jnp.mean(centred * centred, axis=-1, keepdims=True) + ln_epsilon)
        return centred * root, jnp.broadcast_to(root, (n_own, 128))

    attn = jnp.einsum("te,de->td", mixed, va[1], preferred_element_type=F32)
    xh1, r1 = norm(x_own.astype(F32) + attn + vec[2])
    h1 = xh1 * vec[3] + vec[4]
    u = jnp.einsum("td,hdf->htf", h1.astype(BF), inner, preferred_element_type=F32) + b_inner[:, None, :]
    tail = 0.5 * (1.0 + lax.erf(u * 0.7071067811865476))
    g = (u * tail).astype(BF)
    gp = (tail + u * (0.3989422804014327 * jnp.exp(-0.5 * u * u))).astype(BF)
    f = jnp.einsum("htf,hdf->td", g, outer, preferred_element_type=F32)
    xh2, r2 = norm(h1 + f + vec[5 + ff_rows])
    out_own = (xh2 * vec[6 + ff_rows] + vec[7 + ff_rows]).astype(BF)
    vec = jnp.pad(vec, ((0, 16 - nvec), (0, 0)))
    return [qk, va, inner, outer, x_all, q, k, v, *probs, mixed, xh1, r1, g, gp, xh2, r2, proj, vec, out_own]


def halves(t, n_full, seq_len):
    heads = t.shape[1] // HEAD_DIM
    last = t.shape[0] - n_full
    return (
        t[:n_full].reshape(n_full // seq_len, seq_len, heads, HEAD_DIM),
        t[n_full:].reshape(1, last, heads, HEAD_DIM),
    )


def pass_plain(lengths, tokens, cotangent, doc_ids, doc_rows, w_qkv, w_attn, w_inner, w_outer, w_proj, vectors):
    mp = lax.axis_index("mp")
    n_dp, n_mp = lax.axis_size("dp"), lax.axis_size("mp")
    seqs = lengths.shape[0]
    all_rows, width = tokens.shape
    seq_len = all_rows // seqs
    full = seqs // 2
    n_full, n_half = full * seq_len, seq_len // 2
    n_own = n_full + n_half
    rows, half_ff = w_qkv.shape[1], w_inner.shape[1]
    half_rows = rows // 2
    nvec, vec_lanes = vectors.shape
    ff_rows = nvec - 8
    score_scale = HEAD_DIM ** (-0.5)

    saved = forward_plain(lengths, tokens, w_qkv, w_attn, w_inner, w_outer, w_proj, vectors)
    (qk, va, inner, outer, x_all, q, k, v, p_ab, p_c, mixed, xh1, r1, act_low, slope, xh2, r2, proj, vec, out_own) = saved
    qk = qk.reshape(2, width, width)
    va = va.reshape(2, width, width)
    inner = inner.reshape(2, width, half_ff)
    outer = outer.reshape(2, width, half_ff)
    x_own = x_all[:n_own]
    proj = proj.astype(BF)
    a0 = mp * (n_full + seq_len)
    h0 = n_full + mp * n_half
    cot = jnp.concatenate(
        [lax.dynamic_slice_in_dim(cotangent, a0, n_full, 0), lax.dynamic_slice_in_dim(cotangent, h0, n_half, 0)]
    )
    my_seqs = jnp.concatenate([mp * (full + 1) + jnp.arange(full), jnp.array([full])])

    n_mine = full + 1
    mine = jnp.where((jnp.arange(n_mine) < full) | (mp == 0), 1.0, 0.0).astype(F32)
    cls_low = out_own[:: seq_len][:n_mine]
    docs = doc_rows[my_seqs].astype(F32)
    ids = doc_ids[my_seqs]
    query = jnp.dot(cls_low, proj, preferred_element_type=F32).astype(BF)
    query_float = query.astype(F32)
    doc_scores = jnp.einsum("gp,gkp->gk", query_float, docs, precision=highest_mode) * retrieval_scale
    soft = jax.nn.softmax(doc_scores, axis=-1)
    target = (jnp.arange(doc_scores.shape[1]) == 0).astype(F32)
    score_grad = (soft - target[None, :]) * retrieval_scale * mine[:, None]
    query_grad = jnp.einsum("gk,gkp->gp", score_grad, docs, precision=highest_mode).astype(BF)
    row_grads = score_grad[:, :, None] * query_float[:, None, :]
    cls_grad = jnp.einsum("gp,dp->gd", query_grad, proj, preferred_element_type=F32)
    proj_grad = jnp.einsum("gd,gp->dp", cls_low, query_grad, preferred_element_type=F32)
    table_rows = TAB_DEV * n_dp
    one_hot = (jnp.arange(table_rows)[:, None] == ids.reshape(1, -1)).astype(F32)
    table_local = jnp.dot(one_hot, row_grads.reshape(-1, row_grads.shape[2]), precision=highest_mode)

    def norm_back(dy, hat, root, gain):
        e = dy * gain
        back_ = e - jnp.mean(e, axis=-1, keepdims=True) - hat * jnp.mean(e * hat, axis=-1, keepdims=True)
        return back_ * root[:, :1], jnp.sum(dy * hat, axis=0), jnp.sum(dy, axis=0)

    dy = cot.astype(F32)
    first_rows = jnp.arange(n_mine) * seq_len
    dy = dy.at[first_rows].add(cls_grad)
    dz2, dg2, dc2 = norm_back(dy, xh2, r2, vec[6 + ff_rows])
    df = dz2.astype(BF)
    dg = jnp.einsum("td,hdf->htf", df, outer, preferred_element_type=F32)
    g_outer = jnp.einsum("td,htf->hdf", df, act_low, preferred_element_type=F32).astype(BF)
    du = (dg * slope.astype(F32)).astype(BF)
    normed_low = (xh1 * vec[3] + vec[4]).astype(BF)
    g_inner = jnp.einsum("td,htf->hdf", normed_low, du, preferred_element_type=F32).astype(BF)
    dh1 = jnp.einsum("htf,hdf->td", du, inner, preferred_element_type=F32) + dz2
    dz1, dg1, dc1 = norm_back(dh1, xh1, r1, vec[3])
    da = dz1.astype(BF)
    do = jnp.dot(da, va[1], preferred_element_type=F32).astype(BF)
    g_attn = jnp.einsum("td,te->de", da, mixed, preferred_element_type=F32)
    dqs, dks, dvs = [], [], []
    probs_of = (p_ab.reshape(full, -1, seq_len, seq_len), p_c.reshape(1, -1, n_half, seq_len))
    for qh, kh, vh, doh, pb in zip(*(halves(t, n_full, seq_len) for t in (q, k, v, do)), probs_of):
        probs = pb.astype(F32)
        dp_ = jnp.einsum("gqhe,gkhe->ghqk", doh, vh, preferred_element_type=F32)
        delta = jnp.sum(probs * dp_, axis=-1, keepdims=True)
        ds_ = (probs * (dp_ - delta)).astype(BF)
        dqs.append((jnp.einsum("ghqk,gkhe->gqhe", ds_, kh, preferred_element_type=F32) * score_scale).reshape(-1, width))
        dks.append((jnp.einsum("ghqk,gqhe->gkhe", ds_, qh, preferred_element_type=F32) * score_scale).reshape(-1, width))
        dvs.append(jnp.einsum("ghqk,gqhe->gkhe", pb, doh, preferred_element_type=F32).reshape(-1, width))
    dq = jnp.concatenate(dqs).astype(BF)
    dk = jnp.concatenate(dks).astype(BF)
    dv = jnp.concatenate(dvs).astype(BF)
    g_q = jnp.einsum("td,te->de", x_own, dq, preferred_element_type=F32)
    g_k = jnp.einsum("td,te->de", x_all, dk, preferred_element_type=F32)
    g_v = jnp.einsum("td,te->de", x_all, dv, preferred_element_type=F32)
    g_qk = jnp.stack([g_q, g_k]).astype(BF)
    g_va = jnp.stack([g_v, g_attn]).astype(BF)
    dx_own = jnp.einsum("te,de->td", dq, qk[0], preferred_element_type=F32) + dz1
    dx_all = jnp.einsum("te,de->td", dk, qk[1], preferred_element_type=F32)
    dx_all = dx_all + jnp.einsum("te,de->td", dv, va[0], preferred_element_type=F32)
    dx = jnp.concatenate([dx_all[:n_own] + dx_own, dx_all[n_own:]]).astype(BF)
    db_inner = jnp.sum(du.astype(F32), axis=1)
    db_inner = db_inner.reshape(2, 2, half_ff // 2).transpose(1, 0, 2).reshape(ff_rows, width)
    vec_grad = jnp.concatenate(
        [
            jnp.stack(
                [
                    jnp.sum(dq.astype(F32), axis=0),
                    jnp.sum(dv.astype(F32), axis=0),
                    jnp.sum(dz1, axis=0),
                    dg1,
                    dc1,
                ]
            ),
            db_inner,
            jnp.stack([jnp.sum(dz2, axis=0), dg2, dc2]),
        ]
    )
    vg = vec_grad.reshape(nvec, n_dp, 2, vec_lanes).transpose(1, 0, 2, 3)
    vg = jnp.pad(vg, ((0, 0), (0, 0), (0, 0), (0, 128 - vec_lanes))).reshape(n_dp, nvec, 256)
    pg = proj_grad.reshape(n_dp, 2, half_rows, 128).transpose(0, 2, 1, 3).reshape(n_dp, half_rows, 256)
    tg = table_local.reshape(n_dp, 2, TAB_DEV // 2, 128).transpose(0, 2, 1, 3).reshape(n_dp, TAB_DEV // 2, 256)
    small = jnp.concatenate([pg, vg, tg], axis=1)

    return out_own, dx, *reduce_plain([g_qk, g_va, g_inner, g_outer], small, out_own, dx, rows)


def local(
    tokens, cotangent, lengths, doc_ids, doc_rows,
    w_qkv, m_qkv, v_qkv, w_attn, m_attn, v_attn, w_inner, m_inner, v_inner,
    w_outer, m_outer, v_outer, w_proj, m_proj, v_proj, vectors, m_vectors, v_vectors,
):
    mp = lax.axis_index("mp")
    n_dp, n_mp = lax.axis_size("dp"), lax.axis_size("mp")
    fast = n_dp == NZ * NY * NC and n_mp == NX
    seqs = lengths.shape[0]
    all_rows, width = tokens.shape
    seq_len = all_rows // seqs
    full = seqs // 2
    n_full, n_half = full * seq_len, seq_len // 2
    n_own = n_full + n_half
    rows, half_ff = w_qkv.shape[1], w_inner.shape[1]
    half_rows = rows // 2
    nvec, vec_lanes = vectors.shape
    ff_rows = nvec - 8
    score_scale = HEAD_DIM ** (-0.5)

    if fast:
        saved = forward_fast(lengths, tokens, w_qkv, w_attn, w_inner, w_outer, w_proj, vectors)
        reduced = backward_fast(doc_ids, cotangent, doc_rows, saved, rows)
        params = (w_qkv, m_qkv, v_qkv, w_attn, m_attn, v_attn, w_inner, m_inner, v_inner)
        params += (w_outer, m_outer, v_outer, w_proj, m_proj, v_proj, vectors, m_vectors, v_vectors)
        return finish_fast(reduced, saved[-1], params, all_rows)
    if not fast:
        (out_own, dx, small_r, qk_r, va_r, inner_r, outer_r, peer_out, peer_dx, peer_small, total) = pass_plain(
            lengths, tokens, cotangent, doc_ids, doc_rows, w_qkv, w_attn, w_inner, w_outer, w_proj, vectors
        )
        vector_r = small_r[half_rows : half_rows + nvec, :vec_lanes]
        table_at = half_rows + nvec

    def whole_rows(own, peer):
        lo = jnp.where(mp == 0, own[:n_own], peer[:n_own])
        hi = jnp.where(mp == 0, peer[:n_own], own[:n_own])
        return lo, hi

    lo, hi = whole_rows(out_own, peer_out)
    out_tokens = jnp.concatenate([lo, hi[n_full:], hi[:n_full]])
    lo, hi = whole_rows(dx.astype(F32), peer_dx.astype(F32))
    tail = jnp.where(mp == 0, dx[n_own:], peer_dx[n_own:]).astype(F32)
    tail_hi = jnp.where(mp == 0, peer_dx[n_own:], dx[n_own:]).astype(F32)
    input_grad = jnp.concatenate(
        [lo[:n_full], lo[n_full:] + tail_hi, hi[n_full:] + tail, hi[:n_full]]
    )

    def both_halves(at, count):
        mine_, peer_ = small_r[at : at + count], peer_small[at : at + count]
        return jnp.concatenate(
            [jnp.where(mp == 0, mine_, peer_), jnp.where(mp == 0, peer_, mine_)]
        )

    proj_r = both_halves(0, half_rows)
    table_grad = both_halves(table_at, TAB_DEV // 2)
    qkv_r = jnp.stack([qk_r[0], qk_r[1], va_r[0]])
    attn_r = va_r[1]

    def back(v):
        return v.transpose(1, 0, 2).reshape(rows, half_ff)

    inner_r, outer_r = back(inner_r), back(outer_r)
    grad_norm = jnp.sqrt(total[0, 0])
    clip = clip_norm / jnp.maximum(grad_norm, clip_norm)
    results = [out_tokens, input_grad, grad_norm]
    for w, m, s, g, dec, rate in (
        (w_qkv, m_qkv, v_qkv, qkv_r, decay_rate, learn_rate),
        (w_attn, m_attn, v_attn, attn_r, decay_rate, learn_rate),
        (w_inner, m_inner, v_inner, inner_r, decay_rate, learn_rate),
        (w_outer, m_outer, v_outer, outer_r, decay_rate, learn_rate),
        (w_proj, m_proj, v_proj, proj_r, decay_rate, learn_rate),
        (vectors, m_vectors, v_vectors, vector_r, 0.0, vector_rate),
    ):
        results += list(adamw_update(w, m, s, g * clip, dec, rate))
    return tuple(results) + (table_grad,)


def solution(mesh):
    mat = P("dp", "mp")
    rep = P("dp", None)
    qkv = P(None, "dp", "mp")
    vec = P(None, ("dp", "mp"))
    placed = (rep, rep, P("dp"), rep, P("dp", None, None), qkv, qkv, qkv)
    placed += (mat,) * 9 + (rep,) * 3 + (vec,) * 3
    given = (rep, rep, P(), qkv, qkv, qkv) + (mat,) * 9 + (rep,) * 3 + (vec,) * 3 + (rep,)
    return jax.shard_map(local, mesh=mesh, in_specs=placed, out_specs=given, check_vma=False)
```

```python
import functools

import jax
import jax.numpy as jnp
from jax import lax
from jax.experimental import pallas as pl
from jax.experimental.pallas import tpu as pltpu
from jax.sharding import PartitionSpec as P

HEAD_DIM = 64
STEP = 10
TAB_DEV = 8
MESH = pl.DeviceIdType.MESH
ANY = pl.ANY
BF = jnp.bfloat16
F32 = jnp.float32
NZ, NY, NC, NX = 4, 2, 2, 2

highest_mode = lax.Precision.HIGHEST
retrieval_scale = 0.17677669529663687
ln_epsilon = 1e-12
beta_first = 0.9
beta_second = 0.999
learn_rate = 0.05
vector_rate = 0.5
decay_rate = 0.01
adam_epsilon = 1e-08
clip_norm = 1.0


def layer_norm(values, gain_row, shift_row):
    centre = jnp.mean(values, axis=-1, keepdims=True)
    centred = values - centre
    spread = jnp.mean(centred * centred, axis=-1, keepdims=True)
    return centred * lax.rsqrt(spread + ln_epsilon) * gain_row + shift_row


def gelu_exact(values):
    return jax.nn.gelu(values, approximate=False)


def adamw_update(weight, moment, second, gradient, decay_factor, step_rate):
    moment_new = beta_first * moment + (1.0 - beta_first) * gradient
    second_new = beta_second * second + (1.0 - beta_second) * gradient * gradient
    first_hat = moment_new / (1.0 - beta_first**STEP)
    second_hat = second_new / (1.0 - beta_second**STEP)
    weight_new = weight - step_rate * (
        first_hat / (jnp.sqrt(second_hat) + adam_epsilon) + decay_factor * weight
    )
    return (moment_new, second_new, weight_new)


def squared(values):
    return jnp.sum(values * values)


class Place:
    def __init__(self):
        dp = lax.axis_index("dp")
        self.x = lax.axis_index("mp")
        self.c = lax.rem(dp, NC)
        self.y = lax.rem(dp // NC, NY)
        self.z = dp // (NC * NY)

    def dev(self, z=None, y=None, c=None, x=None):
        z = self.z if z is None else z
        y = self.y if y is None else y
        c = self.c if c is None else c
        x = self.x if x is None else x
        return ((z * NY + y) * NC + c, x)

    def others(self):
        out = [self.dev(z=lax.rem(self.z + k, NZ)) for k in range(1, NZ)]
        out.append(self.dev(x=1 - self.x))
        out.append(self.dev(y=1 - self.y))
        out.append(self.dev(c=1 - self.c))
        return out

    def eights(self):
        out = []
        for k in range(1, 8):
            dx, dy, dc = k & 1, (k >> 1) & 1, k >> 2
            out.append(
                self.dev(
                    x=self.x + dx - 2 * dx * self.x,
                    y=self.y + dy - 2 * dy * self.y,
                    c=self.c + dc - 2 * dc * self.c,
                )
            )
        return out


def greet(devices):
    barrier = pltpu.get_barrier_semaphore()
    for d in devices:
        pl.semaphore_signal(barrier, inc=1, device_id=d, device_id_type=MESH)
    pl.semaphore_wait(barrier, len(devices))


def greet_send(devices):
    barrier = pltpu.get_barrier_semaphore()
    for d in devices:
        pl.semaphore_signal(barrier, inc=1, device_id=d, device_id_type=MESH)


def greet_wait(count):
    pl.semaphore_wait(pltpu.get_barrier_semaphore(), count)


def remote(src, dst, ssem, rsem, dev):
    return pltpu.make_async_remote_copy(
        src_ref=src, dst_ref=dst, send_sem=ssem, recv_sem=rsem, device_id=dev, device_id_type=MESH
    )


def cols(x, half):
    return pl.ds(pl.multiple_of(x * half, 128), half)


def dma(*shape):
    return pltpu.SemaphoreType.DMA(shape)


def mm(a, b):
    return jnp.dot(a, b, preferred_element_type=F32)


def mm_nt(a, b):
    return lax.dot_general(a, b, (((1,), (1,)), ((), ())), preferred_element_type=F32)


def mm_tn(a, b):
    return lax.dot_general(a, b, (((0,), (0,)), ((), ())), preferred_element_type=F32)


def flat(value):
    return value.reshape(-1, value.shape[-1])


def lanes(i, n=128):
    return pl.ds(pl.multiple_of(i * n, 128), n)


def rows_at(i, n, at=0):
    return pl.ds(pl.multiple_of(at + i * n, 16), n)


def each(n, body):
    lax.fori_loop(0, n, lambda i, c: (body(i), c)[1], 0)


gather_orders = ("zxy", "zxy", "yzx", "zxy", "zyx", "zxy", "zyx", "zxy", "zyx", "zxy", "zyx", "zxy", "xyz", "yxz", "zyx")


def with_jobs(n, body, go, jobs):
    def one(i):
        body(i)
        for at, todo in enumerate(jobs):
            if todo:

                @pl.when(i == at)
                def _(todo=todo):
                    for job in todo:
                        go(*job)

    each(n, one)


def stack_heads(pair, wide=None):
    low = jnp.where(lax.broadcasted_iota(jnp.int32, (1, 128), 1) < HEAD_DIM, 1.0, 0.0)
    parts = []
    for mask in (low, 1.0 - low):
        parts.append(pair * mask.astype(BF))
        if wide is not None:
            parts.append(jnp.zeros((wide - pair.shape[0], 128), BF))
    return jnp.concatenate(parts, axis=0)


class Gather:
    def __init__(self, me, pieces, sems):
        self.me, self.pieces = me, pieces
        self.lsem, self.ss, self.rs, self.ds, self.dr = sems
        self.waits = []

    def region(self, p, stage, c, **at):
        dst, me, done = self.pieces[p][1], self.me, gather_orders[p][:stage]
        half = dst.shape[-1] // 2
        z = at.get("z", None if "z" in done else me.z)
        y = at.get("y", None if "y" in done else me.y)
        x = at.get("x", None if "x" in done else me.x)
        zs = slice(None) if z is None else pl.ds(0, NZ - 1) if z == "three" else pl.ds(z, 1)
        ys = slice(None) if y is None else pl.ds(y, 1)
        xs = slice(None) if x is None else cols(x, half)
        return dst.at[zs, ys, c, :, xs]

    def bulk(self, p, stage, c):
        axis = gather_orders[p][stage]
        return self.region(p, stage, c, z="three") if axis == "z" else self.coming(p, stage, c)[0]

    def coming(self, p, stage, c):
        me, axis = self.me, gather_orders[p][stage]
        if axis == "z":
            return [self.region(p, stage, c, z=lax.rem(me.z + NZ - k, NZ)) for k in range(1, NZ)]
        return [self.region(p, stage, c, **{axis: 1 - (me.y if axis == "y" else me.x)})]

    def send(self, p, stage):
        me, axis = self.me, gather_orders[p][stage]
        src, dst = self.pieces[p]
        if stage == 0:
            to = dst.at[me.z, me.y, me.c, :, cols(me.x, dst.shape[-1] // 2)]
        else:
            src = to = self.region(p, stage, me.c)
        if axis == "z":
            devs = [me.dev(z=lax.rem(me.z + k, NZ)) for k in range(1, NZ)]
        else:
            devs = [me.dev(**{axis: 1 - (me.y if axis == "y" else me.x)})]
        for dev in devs:
            remote(src, to, self.ss.at[p, stage], self.rs.at[p, stage], dev).start()
        self.waits.append((p, stage, False))

    def arrived(self, ref, sem):
        remote(ref, ref, sem, sem, self.me.dev(c=1 - self.me.c)).wait_recv()

    def receive(self, p, stage):
        self.arrived(self.bulk(p, stage, self.me.c), self.rs.at[p, stage])

    def crossing(self, p, stage, c):
        if stage == 0:
            ref = self.region(p, 1, c)
            return [ref], ref
        return self.coming(p, stage, c), self.bulk(p, stage, c)

    def cross(self, p, stage):
        refs = self.crossing(p, stage, self.me.c)[0]
        for ref in refs:
            remote(ref, ref, self.ds.at[p, stage], self.dr.at[p, stage], self.me.dev(c=1 - self.me.c)).start()
        self.waits.append((p, stage, True))

    def own_copy(self, p):
        me = self.me
        src, dst = self.pieces[p]
        blk = dst.at[me.z, me.y, me.c, :, cols(me.x, dst.shape[-1] // 2)]
        return pltpu.make_async_copy(src, blk, self.lsem.at[p])

    def step1(self, p):
        self.send(p, 0)
        self.own_copy(p).start()

    def step2(self, p):
        self.own_copy(p).wait()
        self.receive(p, 0)
        self.send(p, 1)
        self.cross(p, 0)

    def step3(self, p):
        self.receive(p, 1)
        self.send(p, 2)
        self.cross(p, 1)

    def step4(self, p):
        self.receive(p, 2)
        self.cross(p, 2)

    def step5(self, p):
        for stage in range(3):
            self.arrived(self.crossing(p, stage, 1 - self.me.c)[1], self.dr.at[p, stage])

    def end(self):
        c = self.me.c
        for p, stage, over in self.waits:
            ref = self.crossing(p, stage, c)[1] if over else self.bulk(p, stage, c)
            sem = (self.ds if over else self.ss).at[p, stage]
            remote(ref, ref, sem, sem, self.me.dev(c=1 - c)).wait_send()


def norm_rows(z_ref, r_ref, n_rows, put):
    step = 48

    def body(i):
        at = rows_at(i, step)
        z = z_ref[at, :]
        centred = z - jnp.mean(z, axis=-1, keepdims=True)
        spread = jnp.mean(centred * centred, axis=-1, keepdims=True)
        root = lax.rsqrt(spread + ln_epsilon)
        hat = centred * root
        z_ref[at, :] = hat
        r_ref[at, :] = jnp.broadcast_to(root, (step, 128))
        put(at, hat)

    each(n_rows // step, body)


def forward_kernel(*refs):
    (lens, tokens, w_qkv, w_attn, w_inner, w_outer, w_proj, vectors) = refs[:8]
    outs = refs[8:27]
    scr = refs[27:]
    (vec_s, proj_s, qk_s, va_s, inner_s, outer_s, vec_g, proj_g, qk, va, inner, outer) = scr[:12]
    (xt, q, k, v, p, o, xh1, r1, g, gp, xh2, r2, out_own, proj, vec, x_all, h1b, vecp, bias_ff) = scr[12:31]
    gsems, tsem, osem = scr[31:36], scr[36], scr[37]
    me = Place()
    mp = me.x
    n_all, width = x_all.shape
    n_own = q.shape[0]
    half_seq = n_all - n_own
    seq = 2 * half_seq
    full = (n_own - half_seq) // seq
    n_full = full * seq
    half_ff = inner.shape[-1]
    rows = qk_s.shape[1]
    half_rows = rows // 2

    starts = (
        (mp * (n_full + seq), 0, n_full),
        (n_full + mp * half_seq, n_full, half_seq),
        (n_full + (1 - mp) * half_seq, n_own, half_seq),
    )
    loads = []
    for i, (at, to, n) in enumerate(starts):
        cp = pltpu.make_async_copy(
            tokens.at[pl.ds(pl.multiple_of(at, 16), n)], x_all.at[pl.ds(to, n)], tsem.at[i]
        )
        cp.start()
        loads.append(cp)

    greet_send(me.others())
    vecp[...] = jnp.zeros_like(vecp)
    nvec, nlane = vectors.shape
    vecp[0:nvec, 0:nlane] = vectors[...]
    proj_s[...] = w_proj[pl.ds(pl.multiple_of(mp * half_rows, 8), half_rows), :]
    vec_s[...] = jnp.transpose(vecp[...])[0:nlane]
    qk_s[...] = w_qkv[0:2].astype(BF)
    va_s[0] = w_qkv[2].astype(BF)
    va_s[1] = w_attn[...].astype(BF)
    hf = half_ff // 2
    for h in range(2):
        inner_s[h] = w_inner[:, h * hf : (h + 1) * hf].astype(BF)
        outer_s[h] = w_outer[:, h * hf : (h + 1) * hf].astype(BF)

    greet_wait(len(me.others()))
    row_cut = 32
    pieces = [
        (vec_s, vec_g),
        (qk_s.at[0], qk.at[0]),
        (qk_s.at[1], qk.at[1]),
        (va_s.at[0, pl.ds(0, row_cut)], va.at[0, :, :, :, pl.ds(0, row_cut)]),
        (va_s.at[0, pl.ds(row_cut, rows - row_cut)], va.at[0, :, :, :, pl.ds(row_cut, rows - row_cut)]),
        (va_s.at[1], va.at[1]),
    ]
    for shard, whole in ((inner_s, inner), (outer_s, outer)):
        for h in range(2):
            for j in range(2):
                src = shard.at[h, :, pl.ds(j * (hf // 2), hf // 2)]
                pieces.append((src, whole.at[h, :, :, :, :, pl.ds(j * hf, hf)]))
    pieces.append((proj_s, proj_g))
    net = Gather(me, pieces, gsems)

    def go(step, *members):
        for piece in members:
            (net.step1, net.step2, net.step3, net.step4, net.step5)[step - 1](piece)

    go(1, 0, 1, 2, 12, 13)
    saves = []

    def save(i, ref):
        cp = pltpu.make_async_copy(ref, outs[i], osem.at[i])
        cp.start()
        saves.append(cp)

    for cp in loads:
        cp.wait()

    def x_turn(i):
        xt[rows_at(i, 256), :] = jnp.transpose(x_all[:, lanes(i, 256)])

    each(width // 256, x_turn)
    save(4, xt)
    go(2, 2, 0)
    go(1, 3, 4)
    go(2, 1, 12, 13)
    go(1, 5)
    go(3, 0, 1, 2)
    go(1, 6)
    go(2, 3, 4)
    go(1, 7)
    go(4, 0)
    go(5, 0)
    big = []
    for z in range(NZ):
        for y in range(NY):
            for c in range(NC):
                for x in range(NX):
                    big.append(vec_g[z, y, c, :, x * 128 : (x + 1) * 128])
    vec[...] = jnp.transpose(jnp.concatenate(big, axis=0))[0 : vec.shape[0]]
    for h in range(2):
        for x in range(NX):
            for j in range(2):
                row = vec[5 + NX * x + h : 6 + NX * x + h, j * (hf // 2) : (j + 1) * (hf // 2)]
                bias_ff[h : h + 1, j * hf + x * (hf // 2) : j * hf + (x + 1) * (hf // 2)] = row
    save(17, vec)

    def project(w_ref, src_rows, dst, bias):
        n_tile = 256

        def body(i):
            w = flat(w_ref[:, :, :, :, lanes(i, n_tile)])
            r = mm(x_all[0:src_rows], w)
            if bias is not None:
                r = r + vec[bias : bias + 1, lanes(i, n_tile)]
            dst[:, lanes(i, n_tile)] = r.astype(BF)

        each(width // n_tile, body)

    go(3, 3)
    go(4, 1)
    go(3, 4)
    go(2, 5)
    go(1, 8)
    go(4, 2)
    go(5, 1)
    project(qk.at[0], n_own, q, 0)
    go(5, 2)
    go(2, 6)
    go(1, 9)
    project(qk.at[1], n_all, k, None)
    save(0, qk)
    go(4, 3, 4)
    go(3, 5)
    go(5, 3, 4)
    project(va.at[0], n_all, v, 1)
    go(2, 7)
    go(3, 6)
    go(1, 10)
    save(5, q)
    save(6, k)
    save(7, v)

    wide = 384
    pos = lax.broadcasted_iota(jnp.int32, (1, wide), 1)
    beyond = jnp.where(pos < seq, 0, 1 << 20)

    def attend(q0, nq, k0, slab, length, place):
        at_q = pl.ds(pl.multiple_of(q0, 16), nq)
        at_k = pl.ds(pl.multiple_of(k0, 16), seq)
        for pair in range(2):
            l = lanes(2 * slab + pair)
            s = mm_nt(q[at_q, l], stack_heads(k[at_k, l], wide)) * (HEAD_DIM**-0.5)
            both = []
            for h in range(2):
                part = jnp.where(place < length, s[:, h * wide : (h + 1) * wide], -1000000000.0)
                e = jnp.exp(part - jnp.max(part, axis=-1, keepdims=True))
                both.append((e * (1.0 / jnp.sum(e, axis=-1, keepdims=True))).astype(BF))
            pb = jnp.concatenate(both, axis=1)
            p[slab, at_q, 2 * wide * pair : 2 * wide * (pair + 1)] = pb
            o[at_q, l] = mm(pb, stack_heads(v[at_k, l], wide)).astype(BF)

    slabs = p.shape[0]
    jobs = [[(2, 8), (1, 11, 14), (3, 12)], [(3, 7)], [(2, 9)], [(4, 5), (3, 13)], [(2, 10), (4, 6)], [(3, 8), (5, 5, 6)]]
    for s in range(full):
        length = lens[mp * (full + 1) + s]
        with_jobs(slabs, lambda i: attend(s * seq, seq, s * seq, i, length, pos + beyond), go, jobs[3 * s : 3 * s + 3])
    length = lens[full]
    pos_c = jnp.where(pos < half_seq, pos + mp * half_seq, pos - half_seq + (1 - mp) * half_seq) + beyond
    with_jobs(slabs, lambda i: attend(n_full, half_seq, n_full, i, length, pos_c), go, [[], [(3, 9)], []])
    go(2, 11, 14)
    save(8, p)
    save(9, o)

    tile = 720
    tiles = n_own // tile

    def attn_out(i):
        a = mm_nt(o[rows_at(i, tile), :], flat(va[1]))
        xh1[rows_at(i, tile), :] = x_all[rows_at(i, tile), :].astype(F32) + a + vec[2:3, :]

    each(tiles, attn_out)
    go(4, 7)
    save(1, va)

    def put_h1(at, hat):
        h1b[at, :] = (hat * vec[3:4, :] + vec[4:5, :]).astype(BF)

    norm_rows(xh1, r1, n_own, put_h1)
    save(10, xh1)
    save(11, r1)
    go(5, 7)
    go(3, 10)
    go(4, 8)

    def feed(h):
        n_tile = 256

        def body(i):
            w = flat(inner[h, :, :, :, :, lanes(i, n_tile)])
            for t in range(tiles):
                at = pl.ds(t * tile, tile)
                u = mm(h1b[at, :], w)
                u = u + bias_ff[h : h + 1, lanes(i, n_tile)]
                tail = 0.5 * (1.0 + lax.erf(u * 0.7071067811865476))
                g[h, at, lanes(i, n_tile)] = (u * tail).astype(BF)
                slope = tail + u * (0.3989422804014327 * jnp.exp(-0.5 * u * u))
                gp[h, at, lanes(i, n_tile)] = slope.astype(BF)

        each(half_ff // n_tile, body)

    feed(0)
    go(3, 11)
    go(5, 8)
    go(4, 9)
    go(5, 9)
    feed(1)
    go(3, 14)
    go(4, 10, 12, 11, 13)
    go(5, 10, 12, 11, 13)
    save(2, inner)
    save(12, g)
    save(13, gp)

    def ff_out(i):
        at = rows_at(i, tile)
        f = mm_nt(g[0, at, :], flat(outer[0])) + mm_nt(g[1, at, :], flat(outer[1]))
        h1 = xh1[at, :] * vec[3:4, :] + vec[4:5, :]
        xh2[at, :] = h1 + f + vec[9:10, :]

    each(tiles, ff_out)
    save(3, outer)
    go(4, 14)

    def put_y(at, hat):
        out_own[at, :] = (hat * vec[10:11, :] + vec[11:12, :]).astype(BF)

    norm_rows(xh2, r2, n_own, put_y)
    save(14, xh2)
    save(15, r2)
    save(18, out_own)
    go(5, 14)
    for d in range(NZ * NY * NC * NX):
        block = proj_g[d // 8, d // 4 % 2, d // 2 % 2, :, d % 2 * 128 : (d % 2 + 1) * 128]
        proj[d * half_rows : (d + 1) * half_rows] = block
    save(16, proj)
    net.end()
    for cp in saves:
        cp.wait()


def forward_fast(lengths, tokens, w_qkv, w_attn, w_inner, w_outer, w_proj, vectors):
    seqs = lengths.shape[0]
    all_rows, width = tokens.shape
    seq = all_rows // seqs
    full = seqs // 2
    n_own = full * seq + seq // 2
    n_all = n_own + seq // 2
    rows, half_ff = w_qkv.shape[1], w_inner.shape[1]
    heads = width // HEAD_DIM
    zyc = (NZ, NY, NC)
    hr, nlane = rows // 2, vectors.shape[1]
    weights = [
        ((2,) + zyc + (rows, width), BF),
        ((2,) + zyc + (rows, width), BF),
        ((2,) + zyc + (rows, half_ff), BF),
        ((2,) + zyc + (rows, half_ff), BF),
    ]
    kept = [
        ((width, n_all), BF),
        ((n_own, width), BF),
        ((n_all, width), BF),
        ((n_all, width), BF),
        ((heads // 4, n_own, 4 * 384), BF),
        ((n_own, width), BF),
        ((n_own, width), F32),
        ((n_own, 128), F32),
        ((2, n_own, half_ff), BF),
        ((2, n_own, half_ff), BF),
        ((n_own, width), F32),
        ((n_own, 128), F32),
        ((width, 128), F32),
        ((16, width), F32),
        ((n_own, width), BF),
    ]
    order = kept[:12] + [kept[14], kept[12], kept[13]]
    scratch = [
        ((nlane, 128), F32),
        ((hr, 128), F32),
        ((2, rows, width // 2), BF),
        ((2, rows, width // 2), BF),
        ((2, rows, half_ff // 2), BF),
        ((2, rows, half_ff // 2), BF),
        (zyc + (nlane, 256), F32),
        (zyc + (hr, 256), F32),
    ]
    scratch += weights + order
    scratch += [((n_all, width), BF), ((n_own, width), BF), ((128, 128), F32), ((8, half_ff), F32)]
    n = 15
    vm = pl.BlockSpec(memory_space=pltpu.VMEM)
    hb = pl.BlockSpec(memory_space=ANY)
    sm = pl.BlockSpec(memory_space=pltpu.SMEM)
    return pl.pallas_call(
        forward_kernel,
        out_shape=[jax.ShapeDtypeStruct(s, d) for s, d in weights + kept],
        in_specs=[sm, hb] + [vm] * 6,
        out_specs=[hb] * 19,
        scratch_shapes=[pltpu.VMEM(s, d) for s, d in scratch]
        + [
            dma(n), dma(n, 3), dma(n, 3), dma(n, 3), dma(n, 3),
            dma(3), dma(20),
        ],
        compiler_params=pltpu.CompilerParams(
            collective_id=1, has_side_effects=True, vmem_limit_bytes=60 * 2**20
        ),
        name="forward",
    )(lengths, tokens, w_qkv, w_attn, w_inner, w_outer, w_proj, vectors)


class Reduce:
    def __init__(self, me, pieces, sems):
        self.me, self.pieces = me, pieces
        self.ds, self.dr, self.ss, self.rs = sems
        self.waits, self.sent = [], []
        self.squares = jnp.zeros((1, 1), F32)

    def go(self, copy):
        copy.start()
        self.waits.append(copy)

    def arrived(self, ref, ssem, rsem):
        remote(ref, ref, ssem, rsem, self.me.dev(c=1 - self.me.c)).wait_recv()

    def region(self, p, stage, **at):
        order, src = self.pieces[p][0], self.pieces[p][2]
        me, done = self.me, order[:stage]
        half = src.shape[-1] // 2
        z = at.get("z", me.z if "z" in done else None)
        y = at.get("y", me.y if "y" in done else None)
        x = at.get("x", me.x if "x" in done else None)
        zs = slice(None) if z is None else pl.ds(0, NZ - 1) if z == "three" else pl.ds(z, 1)
        ys = slice(None) if y is None else pl.ds(y, 1)
        xs = slice(None) if x is None else cols(x, half)
        return src.at[zs, ys, me.c, :, xs]

    def send(self, p, stage):
        order, got, me = self.pieces[p][0], self.pieces[p][4 + stage], self.me
        ss, rs = self.ss, self.rs
        if order[stage] == "z":
            for k in range(1, NZ):
                tz = lax.rem(me.z + k, NZ)
                part = self.region(p, stage, z=tz)
                remote(part, got.at[pl.ds(k, 1)], ss.at[p, stage], rs.at[p, stage], me.dev(z=tz)).start()
        else:
            far = 1 - (me.y if order[stage] == "y" else me.x)
            part = self.region(p, stage, **{order[stage]: far})
            dev = me.dev(**{order[stage]: far})
            remote(part, got, ss.at[p, stage], rs.at[p, stage], dev).start()
        self.sent.append((p, stage))

    def receive(self, p, stage):
        order, got = self.pieces[p][0], self.pieces[p][4 + stage]
        if order[stage] == "z":
            got = got.at[pl.ds(1, NZ - 1)]
        self.arrived(got, self.ss.at[p, stage], self.rs.at[p, stage])

    def add(self, p, stage):
        order, _, src, _, *gots = self.pieces[p]
        got, me = gots[stage], self.me
        done = order[: stage + 1]
        half = src.shape[-1] // 2
        xs = cols(me.x, half) if "x" in done else slice(None)
        ys = [(me.y, 0)] if "y" in done else [(y, y) for y in range(NY)]
        if order[stage] == "z":
            for y, i in ys:
                total = src[me.z, y, me.c, :, xs].astype(F32)
                for k in range(1, NZ):
                    total = total + got[k, i].astype(F32)
                src[me.z, y, me.c, :, xs] = total.astype(src.dtype)
            return

        def one(z):
            for y, i in ys:
                src[z, y, me.c, :, xs] = src[z, y, me.c, :, xs] + got[0 if "z" in done else z, i]

        if "z" in done:
            one(me.z)
        else:
            each(NZ, one)

    def step1(self, p):
        src, got = self.pieces[p][2], self.pieces[p][3]
        oc = 1 - self.me.c
        remote(src.at[:, :, oc], got, self.ds.at[p], self.dr.at[p], self.me.dev(c=oc)).start()
        self.sent.append((p, None))

    def step2(self, p):
        src, got, c = self.pieces[p][2], self.pieces[p][3], self.me.c
        self.arrived(got, self.ds.at[p], self.dr.at[p])

        def one(z):
            for y in range(NY):
                src[z, y, c] = src[z, y, c] + got[z, y]

        each(NZ, one)
        self.send(p, 0)

    def step3(self, p):
        self.receive(p, 0)
        self.add(p, 0)
        self.send(p, 1)

    def step4(self, p):
        self.receive(p, 1)
        self.add(p, 1)
        self.send(p, 2)

    def step5(self, p, counted=None):
        order, dst, src, _, *gots = self.pieces[p]
        me = self.me
        self.receive(p, 2)
        total = src[me.z, me.y, me.c, :, cols(me.x, src.shape[-1] // 2)].astype(F32)
        for k in range(1, NZ) if order[2] == "z" else (0,):
            total = total + gots[2][k, 0].astype(F32)
        dst[...] = total
        total = total[:counted]
        self.squares = self.squares + jnp.sum(total * total, keepdims=True)

    def end(self):
        oc = 1 - self.me.c
        for p, stage in self.sent:
            if stage is None:
                part, sem = self.pieces[p][2].at[:, :, oc], self.ds.at[p]
            else:
                axis = self.pieces[p][0][stage]
                far = "three" if axis == "z" else 1 - (self.me.y if axis == "y" else self.me.x)
                part, sem = self.region(p, stage, **{axis: far}), self.ss.at[p, stage]
            remote(part, part, sem, sem, self.me.dev(c=oc)).wait_send()
        for copy in self.waits:
            copy.wait_send()


def got_shapes(order, r, w):
    out, done = [], ""
    for axis in order:
        done += axis
        nz = NZ if axis == "z" or "z" not in done else 1
        out.append((nz, 1 if "y" in done else NY, r, w // 2 if "x" in done else w))
    return out


orders = ("yxz", "yxz", "zyx", "zyx", "yxz", "yxz", "yzx", "yxz", "yxz", "zyx", "yxz", "yxz", "yxz", "yxz")


def all_squares(me, net, total, sq4, sq8, sems):
    qs, qr, es, er = sems
    sq4[0] = jnp.broadcast_to(total, (8, 128))
    copies = []
    for k in range(1, NZ):
        copies.append(remote(sq4.at[0], sq4.at[k], qs.at[k], qr.at[k], me.dev(z=lax.rem(me.z + k, NZ))))
    for copy in copies:
        net.go(copy)
    for copy in copies:
        copy.wait_recv()

    def at_z(z):
        out = jnp.zeros((8, 128), F32)
        for k in range(NZ):
            out = out + jnp.where(lax.rem(me.z + NZ - k, NZ) == z, sq4[k], 0.0)
        return out

    sq8[0] = at_z(0) + at_z(1) + at_z(2) + at_z(3)
    copies = []
    for k, dev in enumerate(me.eights(), 1):
        copies.append(remote(sq8.at[0], sq8.at[k], es.at[k], er.at[k], dev))
    for copy in copies:
        net.go(copy)
    for copy in copies:
        copy.wait_recv()

    def at_code(w):
        out = jnp.zeros((8, 128), F32)
        for k in range(8):
            dx, dy, dc = k & 1, (k >> 1) & 1, k >> 2
            src = (
                (me.x + dx - 2 * dx * me.x)
                + 2 * (me.y + dy - 2 * dy * me.y)
                + 4 * (me.c + dc - 2 * dc * me.c)
            )
            out = out + jnp.where(src == w, sq8[k], 0.0)
        return out

    whole = at_code(0)
    for w in range(1, 8):
        whole = whole + at_code(w)
    return whole


def fold(value):
    return jnp.sum(value.reshape(-1, 8, value.shape[-1]), axis=0)


def norm_back_rows(n_rows, get_dy, hat_ref, root_ref, gain, put, acc):
    step = 48

    def body(i):
        at = rows_at(i, step)
        dy, hat = get_dy(i, at), hat_ref[at, :]
        e = dy * gain
        root = root_ref[at, 0:1]
        m1 = jnp.mean(e, axis=-1, keepdims=True)
        m2 = jnp.mean(e * hat, axis=-1, keepdims=True)
        dz = (e - m1 - hat * m2) * root
        acc[0] = acc[0] + fold(dy * hat)
        acc[1] = acc[1] + fold(dy)
        acc[2] = acc[2] + fold(dz)
        hat_ref[at, :] = dz
        put(at, dz)

    each(n_rows // step, body)


def backward_kernel(*refs):
    doc_ids, cotangent, doc_rows = refs[:3]
    (qk_h, va_h, inner_h, outer_h, xt_h, q_h, k_h, v_h, p_h, o_h, xh1_h, r1_h, g_h, gp_h, xh2_h, r2_h, proj_h, vec_h, out_h) = refs[3:22]
    outs = refs[22:32]
    small_r, qk_r, va_r, inner_r, outer_r, dx, peer_out, peer_dx, peer_small, norm_ref = outs
    scr = list(refs[32:])

    def take(n):
        got = scr[:n]
        del scr[:n]
        return got

    (inner, outer, attn, xt, q, k, v, o, xh1, gg, xh2, r2, proj, vec, cls_in, cot, df, dft) = take(18)
    (cls_grad, acc1, acc2, ffacc, vg, early, late) = take(7)
    grads = take(4)
    bufs = take(14 * 4)
    sq4, sq8 = take(2)
    lsem, rsems, xs, xr, qsems = take(1)[0], take(4), *take(2), take(4)
    do, da, dat, h1t, r1 = cot, df, dft, dft, r2
    me = Place()
    mp = me.x
    n_all, width = dx.shape
    n_own = q.shape[0]
    half_seq = n_all - n_own
    seq = 2 * half_seq
    n_full = n_own - half_seq
    full = n_full // seq
    half_ff = inner.shape[-1]
    other = me.dev(x=1 - mp)

    for i in range(4):
        grads.append(inner.at[i // 2, :, :, :, :, pl.ds(width * (i % 2), width)])
    copies = {}

    def load(name, i, src, dst):
        cp = pltpu.make_async_copy(src, dst, lsem.at[i])
        cp.start()
        copies[name] = cp

    def need(*names):
        for name in names:
            copies[name].wait()

    load("vec", 0, vec_h, vec)
    load("proj", 1, proj_h, proj)
    for s in range(full + 1):
        load("cls%d" % s, 2 + s, out_h.at[pl.ds(s * seq, 16)], cls_in.at[s])
    load("cot0", 5, cotangent.at[pl.ds(pl.multiple_of(mp * (n_full + seq), 16), n_full)], cot.at[pl.ds(0, n_full)])
    load("cot1", 6, cotangent.at[pl.ds(pl.multiple_of(n_full + mp * half_seq, 16), half_seq)], cot.at[pl.ds(n_full, half_seq)])
    load("xh2", 7, xh2_h, xh2)
    load("r2", 8, r2_h, r2)
    load("g", 9, g_h, gg.at[pl.ds(0, 2)])
    load("outer", 10, outer_h, outer)
    load("gp", 11, gp_h, gg.at[pl.ds(2, 2)])
    load("xh1", 12, xh1_h, xh1)
    load("inner", 14, inner_h, inner)
    load("attn", 15, va_h.at[1], attn)
    load("o", 16, o_h, o)
    load("q", 17, q_h, q)
    load("k", 18, k_h, k)
    load("v", 19, v_h, v)
    load("xt", 20, xt_h, xt)

    greet(me.others() + me.eights())
    pieces = []
    hr = width // (NZ * NY * NC * NX)
    n_early = early.shape[3]
    hf = half_ff // 2
    dsts, srcs = [], []
    for i, ref in enumerate((outer_r, inner_r)):
        for h in range(2):
            for j in range(2):
                dsts.append(ref.at[h, :, pl.ds(j * (hf // 2), hf // 2)])
                srcs.append(grads[2 * i + h].at[:, :, :, :, pl.ds(j * hf, hf)])
    dsts += [va_r.at[1], va_r.at[0], qk_r.at[0], qk_r.at[1]]
    dsts += [small_r.at[pl.ds(0, n_early)], small_r.at[pl.ds(n_early, hr)]]
    srcs += grads[4:] + [early, late]
    for i in range(14):
        pieces.append((orders[i], dsts[i], srcs[i]) + tuple(bufs[4 * i : 4 * i + 4]))
    net = Reduce(me, pieces, rsems)

    def go(step, *members):
        for piece in members:
            if step == 5 and piece == 12:
                net.step5(piece, hr)
            else:
                (net.step1, net.step2, net.step3, net.step4, net.step5)[step - 1](piece)

    send_out = remote(out_h, peer_out, xs.at[0], xr.at[0], other)
    net.go(send_out)

    vg[...] = jnp.zeros_like(vg)
    early[...] = jnp.zeros_like(early)
    acc1[...] = jnp.zeros_like(acc1)
    acc2[...] = jnp.zeros_like(acc2)
    ffacc[...] = jnp.zeros_like(ffacc)
    need("vec", "proj", *["cls%d" % s for s in range(full + 1)])
    row16 = lax.broadcasted_iota(jnp.int32, (16, 1), 0)
    cls = jnp.zeros((16, width), F32)
    for s in range(full + 1):
        cls = jnp.where(row16 == s, cls_in[s].astype(F32)[0:1], cls)
    cls = cls.astype(BF)
    proj_low = proj[...].astype(BF)
    query = mm(cls, proj_low).astype(BF).astype(F32)
    row8 = lax.broadcasted_iota(jnp.int32, (8, 1), 0)
    dcq = jnp.zeros((16, 128), F32)
    row_grads = []
    cands = doc_ids.shape[1]
    seq_ids = [mp * (full + 1) + s for s in range(full)] + [full]
    for s in range(full + 1):
        docs = doc_rows[seq_ids[s]].astype(F32)
        mine = 1.0 if s < full else jnp.where(mp == 0, 1.0, 0.0)
        query_s = query[s : s + 1]
        score = jnp.sum(query_s * docs, axis=-1, keepdims=True) * retrieval_scale
        e = jnp.exp(score - jnp.max(score, axis=0, keepdims=True))
        soft = e / jnp.sum(e, axis=0, keepdims=True)
        sg = (soft - jnp.where(row8 == 0, 1.0, 0.0)) * (retrieval_scale * mine)
        dcq = jnp.where(row16 == s, jnp.sum(sg * docs, axis=0, keepdims=True), dcq)
        row_grads.append(sg * query_s)
    dcq = dcq.astype(BF)
    cls_grad[...] = mm_nt(dcq, proj_low)
    proj_grad = mm_tn(cls, dcq)
    n_dev = NZ * NY * NC * NX
    table_row = lax.broadcasted_iota(jnp.int32, (TAB_DEV * n_dev // NX, 1), 0)
    table = jnp.zeros((TAB_DEV * n_dev // NX, 128), F32)
    for s in range(full + 1):
        for i in range(cands):
            table = table + jnp.where(table_row == doc_ids[seq_ids[s], i], row_grads[s][i : i + 1], 0.0)
    tr = TAB_DEV // NX
    for d in range(n_dev):
        z, y, c, x = d // 8, d // 4 % 2, d // 2 % 2, d % 2
        l = slice(x * 128, (x + 1) * 128)
        t0 = (d // 2) * TAB_DEV + x * tr
        early[z, y, c, 0:hr, l] = proj_grad[d * hr : (d + 1) * hr]
        early[z, y, c, hr : hr + tr, l] = table[t0 : t0 + tr]
    go(1, 12)

    per = seq // 48
    row48 = lax.broadcasted_iota(jnp.int32, (48, 1), 0)

    def get_dy(i, at):
        first = (row48 == 0) & (lax.rem(i, per) == 0)
        return cot[at, :].astype(F32) + jnp.where(first, cls_grad[pl.ds(i // per, 1), :], 0.0)

    def put_df(at, dz):
        df[at, :] = dz.astype(BF)

    need("cot0", "cot1", "xh2", "r2")
    norm_back_rows(n_own, get_dy, xh2, r2, vec[10:11, :], put_df, acc2)

    def turn(src, dst, n_rows):
        def body(i):
            dst[rows_at(i, 256), 0:n_rows] = jnp.transpose(src[:, lanes(i, 256)])

        each(width // 256, body)

    load("r1", 13, r1_h, r1)
    turn(df, dft, n_own)
    go(2, 12)
    n_tile = 256
    shape5 = (NZ, NY, NC, width // (NZ * NY * NC))

    def weight_grad(left, right, dst, n, at=0):
        def body(i):
            r = mm(left(), right(lanes(i + at, n_tile)))
            dst[:, :, :, :, lanes(i + at, n_tile)] = r.astype(BF).reshape(shape5 + (n_tile,))

        each(n // n_tile, body)

    need("g")
    for h in range(2):
        for j in range(2):
            weight_grad(lambda: dft[:, 0:n_own], lambda l: gg[h, :, l], grads[h], hf, j * (hf // n_tile))
            i = 2 * h + j
            go(1, i)
            if i > 1:
                go(2, i - 2)

    need("outer", "gp")
    tile = 720
    tiles = n_own // tile

    def hidden(h):
        def body(i):
            w = flat(outer[h, :, :, :, :, lanes(i, n_tile)])
            for t in range(tiles):
                at = pl.ds(t * tile, tile)
                du = (mm(df[at, :], w) * gg[2 + h, at, lanes(i, n_tile)].astype(F32)).astype(BF)
                gg[2 + h, at, lanes(i, n_tile)] = du
                ffacc[h, :, lanes(i, n_tile)] = ffacc[h, :, lanes(i, n_tile)] + fold(du.astype(F32))

        each(half_ff // n_tile, body)

    go(2, 2)
    hidden(0)
    go(2, 3)
    go(3, 12)
    hidden(1)
    load("p0", 21, p_h.at[0], gg.at[0])
    load("p1", 22, p_h.at[1], gg.at[1])
    load("wq", 23, qk_h.at[0], outer.at[0, :, :, :, :, pl.ds(0, width)])
    load("wk", 24, qk_h.at[1], outer.at[0, :, :, :, :, pl.ds(width, width)])
    load("wv", 25, va_h.at[0], outer.at[1, :, :, :, :, pl.ds(0, width)])
    need("xh1", "r1")

    def h1_turn(i):
        l = lanes(i, 256)
        h1 = (xh1[:, l] * vec[3:4, l] + vec[4:5, l]).astype(BF)
        h1t[rows_at(i, 256), 0:n_own] = jnp.transpose(h1)

    each(width // 256, h1_turn)
    for h in range(2):
        for j in range(2):
            weight_grad(lambda: h1t[:, 0:n_own], lambda l: gg[2 + h, :, l], grads[2 + h], hf, j * (hf // n_tile))
            i = 4 + 2 * h + j
            go(1, i)
            if i > 5:
                go(2, i - 2)
            if i == 5:
                go(3, 0)
            if i == 7:
                go(3, 1)
    need("inner")

    def hidden_back(i):
        at = rows_at(i, tile)
        d = mm_nt(gg[2, at, :], flat(inner[0])) + mm_nt(gg[3, at, :], flat(inner[1]))
        xh2[at, :] = d + xh2[at, :]

    each(tiles, hidden_back)
    load("p2", 26, p_h.at[2], gg.at[2])
    go(2, 6, 7)

    norm_back_rows(n_own, lambda i, at: xh2[at, :], xh1, r1, vec[3:4, :], put_df, acc1)
    need("attn", "o")

    def mixed_back(i):
        do[:, lanes(i, n_tile)] = mm(da[...], flat(attn[:, :, :, :, lanes(i, n_tile)])).astype(BF)

    each(width // n_tile, mixed_back)
    turn(da, dat, n_own)
    weight_grad(lambda: dat[:, 0:n_own], lambda l: o[:, l], grads[4], width)
    go(1, 8)
    go(3, 4, 2)

    need("q", "k", "v", "p0", "p1", "p2")
    wide = 384
    scale = HEAD_DIM**-0.5

    def attend(q0, nq, k0, slab):
        at_q = pl.ds(pl.multiple_of(q0, 16), nq)
        at_k = pl.ds(pl.multiple_of(k0, 16), seq)
        for pair in range(2):
            l = lanes(2 * slab + pair)
            qp, kp, dop = q[at_q, l], k[at_k, l], do[at_q, l]
            pb = gg[slab, at_q, 2 * wide * pair : 2 * wide * (pair + 1)]
            p = pb.astype(F32)
            pd = p * mm_nt(dop, stack_heads(v[at_k, l], wide))
            ds, pbs = [], []
            for h in range(2):
                at = slice(h * wide, (h + 1) * wide)
                ds.append((pd[:, at] - p[:, at] * jnp.sum(pd[:, at], axis=-1, keepdims=True)).astype(BF))
                pbs.append(pb[:, h * wide : h * wide + seq])
            q[at_q, l] = (mm(jnp.concatenate(ds, axis=1), stack_heads(kp, wide)) * scale).astype(BF)
            ds = jnp.concatenate([d[:, 0:seq] for d in ds], axis=0)
            k[at_k, l] = (mm_tn(ds, stack_heads(qp)) * scale).astype(BF)
            v[at_k, l] = mm_tn(jnp.concatenate(pbs, axis=0), stack_heads(dop)).astype(BF)

    slabs = p_h.shape[0]
    jobs = (
        ([(2, 8), (4, 0, 1)], [(3, 5)], [(3, 3), (4, 12)]),
        ([(4, 4)], [(3, 6)], []),
        ([(3, 7)], [(4, 5)], [(4, 2)]),
    )

    def tokens_back(at, own):
        d = mm_nt(k[at, :], flat(outer[0, :, :, :, :, width : 2 * width]))
        d = d + mm_nt(v[at, :], flat(outer[1, :, :, :, :, 0:width]))
        if own:
            d = d + mm_nt(q[at, :], flat(outer[0, :, :, :, :, 0:width])) + xh1[at, :]
            o[at, :] = d.astype(BF)
        else:
            df[0:half_seq, :] = d.astype(BF)

    keeps = []

    def send_dx(i, src, at):
        net.go(remote(src, peer_dx.at[at], xs.at[1 + i], xr.at[1 + i], other))
        cp = pltpu.make_async_copy(src, dx.at[at], lsem.at[27 + i])
        cp.start()
        keeps.append(cp)

    need("wq", "wk", "wv")
    for s in range(full):
        with_jobs(slabs, lambda i: attend(s * seq, seq, s * seq, i), go, jobs[s])
        tokens_back(pl.ds(s * seq, seq), True)
        size = seq if s == 0 else half_seq
        send_dx(s, o.at[pl.ds(s * seq, size)], pl.ds(s * seq, size))
    with_jobs(slabs, lambda i: attend(n_full, half_seq, n_full, i), go, jobs[full])
    need("xt")
    weight_grad(lambda: xt[...], lambda l: v[:, l], grads[5], width)
    go(1, 9)
    send_dx(2, o.at[pl.ds(n_full - half_seq, half_seq)], pl.ds(n_full - half_seq, half_seq))
    weight_grad(lambda: xt[:, 0:n_own], lambda l: q[:, l], grads[6], width)
    go(1, 10)
    go(2, 9)
    go(4, 6)
    weight_grad(lambda: xt[...], lambda l: k[:, l], grads[7], width)
    go(1, 11)
    go(2, 10)
    go(3, 8)
    go(4, 3)
    tokens_back(pl.ds(n_full, half_seq), True)
    go(2, 11)
    tokens_back(pl.ds(n_own, half_seq), False)

    vg[0:1, :] = jnp.sum(q[...].astype(F32), axis=0, keepdims=True)
    vg[1:2, :] = jnp.sum(v[...].astype(F32), axis=0, keepdims=True)
    vg[2:3, :] = jnp.sum(acc1[2], axis=0, keepdims=True)
    vg[3:4, :] = jnp.sum(acc1[0], axis=0, keepdims=True)
    vg[4:5, :] = jnp.sum(acc1[1], axis=0, keepdims=True)
    for h in range(2):
        both = jnp.sum(ffacc[h], axis=0, keepdims=True)
        for x in range(NX):
            for j in range(2):
                at = j * hf + x * (hf // 2)
                vg[5 + NX * x + h : 6 + NX * x + h, j * (hf // 2) : (j + 1) * (hf // 2)] = both[:, at : at + hf // 2]
    vg[9:10, :] = jnp.sum(acc2[2], axis=0, keepdims=True)
    vg[10:11, :] = jnp.sum(acc2[0], axis=0, keepdims=True)
    vg[11:12, :] = jnp.sum(acc2[1], axis=0, keepdims=True)
    turned = jnp.transpose(vg[...])
    for d in range(n_dev):
        z, y, c, x = d // 8, d // 4 % 2, d // 2 % 2, d % 2
        late[z, y, c, :, x * 128 : (x + 1) * 128] = turned[d * hr : (d + 1) * hr]
    go(1, 13)
    go(2, 13)
    go(4, 7)
    go(5, 0, 1, 4, 5, 12)
    go(3, 10)
    go(3, 11)
    go(4, 8)
    go(3, 9)
    go(4, 10)
    go(3, 13)
    send_dx(3, o.at[pl.ds(n_full, half_seq)], pl.ds(n_full, half_seq))
    go(4, 9)
    go(4, 11)
    send_dx(4, df.at[pl.ds(0, half_seq)], pl.ds(n_own, half_seq))
    go(4, 13)
    go(5, 2, 3, 6, 7, 8, 10, 9)
    go(5, 11, 13)
    net.go(remote(small_r, peer_small, xs.at[6], xr.at[6], other))
    norm_ref[...] = all_squares(me, net, net.squares, sq4, sq8, qsems)
    parts = [pl.ds(0, seq)] + [pl.ds(seq + i * half_seq, half_seq) for i in range(4)]
    for i, ref in enumerate([peer_out] + [peer_dx.at[at] for at in parts] + [peer_small]):
        net.arrived(ref, xs.at[i], xr.at[i])
    for cp in keeps:
        cp.wait()
    net.end()


def backward_fast(doc_ids, cotangent, doc_rows, saved, rows):
    (qk, va, inner, outer, xt, q, k, v, p, o, xh1, r1, g, gp, xh2, r2, proj, vec, out_own) = saved
    n_own, width = q.shape
    n_all = k.shape[0]
    half_ff = inner.shape[-1]
    zyc = (NZ, NY, NC)
    hr = rows // NX
    n_early = hr + 8
    small_rows = n_early + hr
    ins = [doc_ids, cotangent, doc_rows] + list(saved)
    out_shape = [
        ((small_rows, 128), F32),
        ((2, rows, width // 2), F32),
        ((2, rows, width // 2), F32),
        ((2, rows, half_ff // 2), F32),
        ((2, rows, half_ff // 2), F32),
        ((n_all, width), BF),
        ((n_own, width), BF),
        ((n_all, width), BF),
        ((small_rows, 128), F32),
        ((8, 128), F32),
    ]
    like = lambda a: (a.shape, a.dtype)
    wide = width // 128 * 128
    scratch = [
        like(inner), like(outer), (va.shape[1:], BF), like(xt), like(q), like(k), like(v), like(o),
        like(xh1), ((4,) + g.shape[1:], BF), like(xh2), like(r2), like(proj), like(vec),
        ((3, 16, width), BF), ((n_own, width), BF), ((n_own, width), BF),
        ((width, wide), BF),
        ((16, width), F32), ((3, 8, width), F32), ((3, 8, width), F32), ((2, 8, half_ff), F32),
        ((128, width), F32), (zyc + (n_early, 256), F32), (zyc + (hr, 256), F32),
    ]
    sizes = [half_ff] * 4 + [width] * 4
    scratch += [(zyc + (rows, w), BF) for w in sizes[:4]]
    smalls = [(n_early, 256, F32), (hr, 256, F32)]
    for i, (r, w, dt) in enumerate([(rows, width, BF)] * 12 + smalls):
        scratch += [((NZ, NY, r, w), dt)] + [(shape, dt) for shape in got_shapes(orders[i], r, w)]
    scratch += [((NZ, 8, 128), F32), ((8, 8, 128), F32)]
    vm = pl.BlockSpec(memory_space=pltpu.VMEM)
    hb = pl.BlockSpec(memory_space=ANY)
    sm = pl.BlockSpec(memory_space=pltpu.SMEM)
    n = 14
    return pl.pallas_call(
        backward_kernel,
        out_shape=[jax.ShapeDtypeStruct(s, d) for s, d in out_shape],
        in_specs=[sm, hb, vm] + [hb] * 19,
        out_specs=[vm] * 5 + [hb, hb, hb, vm, vm],
        scratch_shapes=[pltpu.VMEM(s, d) for s, d in scratch]
        + [
            dma(32), dma(n), dma(n), dma(n, 3), dma(n, 3),
            dma(7), dma(7), dma(NZ), dma(NZ), dma(8), dma(8),
        ],
        compiler_params=pltpu.CompilerParams(
            collective_id=2, has_side_effects=True, vmem_limit_bytes=63 * 2**20
        ),
        name="backward",
    )(*ins)


def finish_kernel(*refs):
    small_r, peer_small, qk_r, va_r, inner_r, outer_r, total = refs[:7]
    out_own, peer_out, dx, peer_dx = refs[7:11]
    params = [refs[11 + 3 * i : 14 + 3 * i] for i in range(6)]
    outs = refs[29:51]
    turn, sem, lo, hi, mid = refs[51:]
    out_tokens, input_grad, norm = outs[0:3]
    news = [outs[3 + 3 * i : 6 + 3 * i] for i in range(6)]
    table_grad = outs[21]
    mp = lax.axis_index("mp")
    n_own = out_own.shape[0]
    n_all = dx.shape[0]
    half_seq = n_all - n_own
    n_full = n_own - half_seq
    seq = 2 * half_seq
    copies = []
    for i, (src, first) in enumerate(((out_own, mp), (peer_out, 1 - mp))):
        at = pl.multiple_of(first * (n_full + seq), 16)
        copies.append((src.at[pl.ds(0, n_full)], out_tokens.at[pl.ds(at, n_full)]))
        at = pl.multiple_of(n_full + first * half_seq, 16)
        copies.append((src.at[pl.ds(n_full, half_seq)], out_tokens.at[pl.ds(at, half_seq)]))
    copies = [pltpu.make_async_copy(s, d, sem.at[i]) for i, (s, d) in enumerate(copies)]
    for cp in copies:
        cp.start()
    lo[...] = dx[0:n_full].astype(F32)
    hi[...] = peer_dx[0:n_full].astype(F32)
    own_mid = dx[n_full:n_own].astype(F32) + peer_dx[n_own:n_all].astype(F32)
    peer_mid = peer_dx[n_full:n_own].astype(F32) + dx[n_own:n_all].astype(F32)
    mid[pl.ds(pl.multiple_of(mp * half_seq, 16), half_seq)] = own_mid
    mid[pl.ds(pl.multiple_of((1 - mp) * half_seq, 16), half_seq)] = peer_mid
    grads = (
        (lo, pl.multiple_of(mp * (n_full + seq), 16), n_full),
        (hi, pl.multiple_of((1 - mp) * (n_full + seq), 16), n_full),
        (mid, n_full, seq),
    )
    for i, (src, at, n) in enumerate(grads):
        cp = pltpu.make_async_copy(src, input_grad.at[pl.ds(at, n)], sem.at[4 + i])
        cp.start()
        copies.append(cp)

    root = jnp.sqrt(total[...])
    norm[0, 0] = jnp.max(root)
    clip = clip_norm / jnp.maximum(root[0:1, 0:1], clip_norm)
    hf = inner_r.shape[-1]
    hr = params[4][0].shape[0] // 2
    nvec, nlane = params[5][0].shape
    tr = table_grad.shape[0] // 2

    def adam(which, at, g, dec, rate):
        w, m, s = (ref[at] for ref in params[which])
        for ref, new in zip(news[which], adamw_update(w, m, s, g * clip, dec, rate)):
            ref[at] = new

    for j in range(3):
        g = qk_r[j] if j < 2 else va_r[0]
        adam(0, (j,), g, decay_rate, learn_rate)
    adam(1, (slice(None), slice(None)), va_r[1], decay_rate, learn_rate)
    for which, ref in ((2, inner_r), (3, outer_r)):
        for h in range(2):
            adam(which, (slice(None), slice(h * hf, (h + 1) * hf)), ref[h], decay_rate, learn_rate)
    turn[...] = jnp.zeros_like(turn)
    turn[0:nlane] = small_r[hr + 8 : hr + 8 + nlane]
    adam(5, (slice(None), slice(None)), jnp.transpose(turn[...])[0:nvec, 0:nlane], 0.0, vector_rate)
    for block, first in ((small_r, mp), (peer_small, 1 - mp)):
        at = pl.ds(pl.multiple_of(first * hr, 8), hr)
        adam(4, (at, slice(None)), block[0:hr], decay_rate, learn_rate)
    own_t, peer_t = small_r[hr : hr + tr], peer_small[hr : hr + tr]
    table_grad[0:tr] = jnp.where(mp == 0, own_t, peer_t)
    table_grad[tr : 2 * tr] = jnp.where(mp == 0, peer_t, own_t)
    for cp in copies:
        cp.wait()


def finish_fast(reduced, out_own, params, n_rows):
    (small_r, qk_r, va_r, inner_r, outer_r, dx, peer_out, peer_dx, peer_small, total) = reduced
    n_own, width = out_own.shape
    n_all = dx.shape[0]
    half_seq = n_all - n_own
    like = lambda a: jax.ShapeDtypeStruct(a.shape, a.dtype)
    vm = pl.BlockSpec(memory_space=pltpu.VMEM)
    hb = pl.BlockSpec(memory_space=ANY)
    sm = pl.BlockSpec(memory_space=pltpu.SMEM)
    out_shape = [
        jax.ShapeDtypeStruct((n_rows, width), BF),
        jax.ShapeDtypeStruct((n_rows, width), F32),
        jax.ShapeDtypeStruct((1, 1), F32),
    ]
    out_shape += [like(a) for a in params] + [jax.ShapeDtypeStruct((TAB_DEV, 128), F32)]
    n_full = n_own - half_seq
    outs = pl.pallas_call(
        finish_kernel,
        out_shape=out_shape,
        in_specs=[vm] * 29,
        out_specs=[hb, hb, sm] + [vm] * 19,
        scratch_shapes=[
            pltpu.VMEM((128, 128), F32),
            dma(7),
            pltpu.VMEM((n_full, width), F32),
            pltpu.VMEM((n_full, width), F32),
            pltpu.VMEM((2 * half_seq, width), F32),
        ],
        compiler_params=pltpu.CompilerParams(vmem_limit_bytes=63 * 2**20),
        name="finish",
    )(small_r, peer_small, qk_r, va_r, inner_r, outer_r, total, out_own, peer_out, dx, peer_dx, *params)
    return tuple(outs[:2]) + (outs[2].reshape(()),) + tuple(outs[3:])


def gather_plain(shards, small, rows):
    def both(v, axis):
        v = lax.all_gather(v, "dp", axis=axis, tiled=True)
        return lax.all_gather(v, "mp", axis=2, tiled=True)

    return [both(small[None], 0)] + [both(v, 1) for v in shards]


def reduce_plain(grads, small, own_out, own_dx, rows):
    def both(v, axis, wide):
        v = lax.psum_scatter(v.astype(F32), "mp", scatter_dimension=wide, tiled=True)
        return lax.psum_scatter(v, "dp", scatter_dimension=axis, tiled=True)

    small_sum = both(small, 0, 2)[0]
    sums = [both(g, 1, 2) for g in grads]
    ox = 1 - lax.axis_index("mp")
    swap = [(0, 1), (1, 0)]
    peer_out = lax.ppermute(own_out, "mp", swap)
    peer_dx = lax.ppermute(own_dx, "mp", swap)
    peer_small = lax.ppermute(small_sum, "mp", swap)
    squares = sum(squared(g) for g in sums) + squared(small_sum[:-4])
    total = lax.psum(squares, ("dp", "mp"))
    return [small_sum] + sums + [peer_out, peer_dx, peer_small, jnp.full((8, 128), total)]


def forward_plain(lengths, tokens, w_qkv, w_attn, w_inner, w_outer, w_proj, vectors):
    mp = lax.axis_index("mp")
    n_dp = lax.axis_size("dp")
    seqs = lengths.shape[0]
    all_rows, width = tokens.shape
    seq_len = all_rows // seqs
    full = seqs // 2
    n_full, n_half = full * seq_len, seq_len // 2
    n_own = n_full + n_half
    heads = width // HEAD_DIM
    rows, half_ff = w_qkv.shape[1], w_inner.shape[1]
    nvec, vec_lanes = vectors.shape
    half_rows = rows // 2
    score_scale = HEAD_DIM ** (-0.5)

    def two(v):
        return v.reshape(rows, 2, half_ff // 2).transpose(1, 0, 2)

    qk_s = w_qkv[:2].astype(BF)
    va_s = jnp.stack([w_qkv[2], w_attn]).astype(BF)
    vec_pad = jnp.pad(vectors, ((0, 0), (0, 128 - vec_lanes)))
    proj_half = lax.dynamic_slice_in_dim(w_proj, mp * half_rows, half_rows, 0)
    small_s = jnp.concatenate([proj_half, vec_pad], axis=0)
    small_g, qk, va, inner, outer = gather_plain(
        [qk_s, va_s, two(w_inner.astype(BF)), two(w_outer.astype(BF))], small_s, rows
    )
    small_g = small_g.reshape(n_dp, half_rows + nvec, 2, 128)
    proj = small_g[:, :half_rows].transpose(0, 2, 1, 3).reshape(width, 128)
    vec = small_g[:, half_rows:, :, :vec_lanes].transpose(1, 0, 2, 3).reshape(nvec, width)
    ff_rows = nvec - 8
    b_inner = vec[5 : 5 + ff_rows].reshape(2, 2, half_ff // 2).transpose(1, 0, 2).reshape(2, half_ff)

    a0 = mp * (n_full + seq_len)
    h0 = n_full + mp * n_half
    o0 = n_full + (1 - mp) * n_half
    x_all = jnp.concatenate(
        [
            lax.dynamic_slice_in_dim(tokens, a0, n_full, 0),
            lax.dynamic_slice_in_dim(tokens, h0, n_half, 0),
            lax.dynamic_slice_in_dim(tokens, o0, n_half, 0),
        ]
    )
    x_own = x_all[:n_own]
    my_seqs = jnp.concatenate([mp * (full + 1) + jnp.arange(full), jnp.array([full])])
    my_len = lengths[my_seqs]
    pos = jnp.arange(seq_len)
    pos_last = jnp.where(pos < n_half, pos + mp * n_half, pos - n_half + (1 - mp) * n_half)
    valids = (pos[None, :] < my_len[:full, None], pos_last[None, :] < my_len[full:, None])

    q = (jnp.dot(x_own, qk[0], preferred_element_type=F32) + vec[0]).astype(BF)
    k = jnp.dot(x_all, qk[1], preferred_element_type=F32).astype(BF)
    v = (jnp.dot(x_all, va[0], preferred_element_type=F32) + vec[1]).astype(BF)
    probs, outs = [], []
    for qh, kh, vh, valid in zip(*(halves(t, n_full, seq_len) for t in (q, k, v)), valids):
        s = jnp.einsum("gqhe,gkhe->ghqk", qh, kh, preferred_element_type=F32) * score_scale
        s = jnp.where(valid[:, None, None, :], s, -1000000000.0)
        pb = jax.nn.softmax(s, axis=-1).astype(BF)
        o = jnp.einsum("ghqk,gkhe->gqhe", pb, vh, preferred_element_type=F32)
        outs.append(o.reshape(-1, width).astype(BF))
        probs.append(pb.reshape((-1,) + pb.shape[2:]))
    mixed = jnp.concatenate(outs)

    def norm(z):
        centred = z - jnp.mean(z, axis=-1, keepdims=True)
        root = lax.rsqrt(jnp.mean(centred * centred, axis=-1, keepdims=True) + ln_epsilon)
        return centred * root, jnp.broadcast_to(root, (n_own, 128))

    attn = jnp.einsum("te,de->td", mixed, va[1], preferred_element_type=F32)
    xh1, r1 = norm(x_own.astype(F32) + attn + vec[2])
    h1 = xh1 * vec[3] + vec[4]
    u = jnp.einsum("td,hdf->htf", h1.astype(BF), inner, preferred_element_type=F32) + b_inner[:, None, :]
    tail = 0.5 * (1.0 + lax.erf(u * 0.7071067811865476))
    g = (u * tail).astype(BF)
    gp = (tail + u * (0.3989422804014327 * jnp.exp(-0.5 * u * u))).astype(BF)
    f = jnp.einsum("htf,hdf->td", g, outer, preferred_element_type=F32)
    xh2, r2 = norm(h1 + f + vec[5 + ff_rows])
    out_own = (xh2 * vec[6 + ff_rows] + vec[7 + ff_rows]).astype(BF)
    vec = jnp.pad(vec, ((0, 16 - nvec), (0, 0)))
    return [qk, va, inner, outer, x_all, q, k, v, *probs, mixed, xh1, r1, g, gp, xh2, r2, proj, vec, out_own]


def halves(t, n_full, seq_len):
    heads = t.shape[1] // HEAD_DIM
    last = t.shape[0] - n_full
    return (
        t[:n_full].reshape(n_full // seq_len, seq_len, heads, HEAD_DIM),
        t[n_full:].reshape(1, last, heads, HEAD_DIM),
    )


def pass_plain(lengths, tokens, cotangent, doc_ids, doc_rows, w_qkv, w_attn, w_inner, w_outer, w_proj, vectors):
    mp = lax.axis_index("mp")
    n_dp, n_mp = lax.axis_size("dp"), lax.axis_size("mp")
    seqs = lengths.shape[0]
    all_rows, width = tokens.shape
    seq_len = all_rows // seqs
    full = seqs // 2
    n_full, n_half = full * seq_len, seq_len // 2
    n_own = n_full + n_half
    rows, half_ff = w_qkv.shape[1], w_inner.shape[1]
    half_rows = rows // 2
    nvec, vec_lanes = vectors.shape
    ff_rows = nvec - 8
    score_scale = HEAD_DIM ** (-0.5)

    saved = forward_plain(lengths, tokens, w_qkv, w_attn, w_inner, w_outer, w_proj, vectors)
    (qk, va, inner, outer, x_all, q, k, v, p_ab, p_c, mixed, xh1, r1, act_low, slope, xh2, r2, proj, vec, out_own) = saved
    qk = qk.reshape(2, width, width)
    va = va.reshape(2, width, width)
    inner = inner.reshape(2, width, half_ff)
    outer = outer.reshape(2, width, half_ff)
    x_own = x_all[:n_own]
    proj = proj.astype(BF)
    a0 = mp * (n_full + seq_len)
    h0 = n_full + mp * n_half
    cot = jnp.concatenate(
        [lax.dynamic_slice_in_dim(cotangent, a0, n_full, 0), lax.dynamic_slice_in_dim(cotangent, h0, n_half, 0)]
    )
    my_seqs = jnp.concatenate([mp * (full + 1) + jnp.arange(full), jnp.array([full])])

    n_mine = full + 1
    mine = jnp.where((jnp.arange(n_mine) < full) | (mp == 0), 1.0, 0.0).astype(F32)
    cls_low = out_own[:: seq_len][:n_mine]
    docs = doc_rows[my_seqs].astype(F32)
    ids = doc_ids[my_seqs]
    query = jnp.dot(cls_low, proj, preferred_element_type=F32).astype(BF)
    query_float = query.astype(F32)
    doc_scores = jnp.einsum("gp,gkp->gk", query_float, docs, precision=highest_mode) * retrieval_scale
    soft = jax.nn.softmax(doc_scores, axis=-1)
    target = (jnp.arange(doc_scores.shape[1]) == 0).astype(F32)
    score_grad = (soft - target[None, :]) * retrieval_scale * mine[:, None]
    query_grad = jnp.einsum("gk,gkp->gp", score_grad, docs, precision=highest_mode).astype(BF)
    row_grads = score_grad[:, :, None] * query_float[:, None, :]
    cls_grad = jnp.einsum("gp,dp->gd", query_grad, proj, preferred_element_type=F32)
    proj_grad = jnp.einsum("gd,gp->dp", cls_low, query_grad, preferred_element_type=F32)
    table_rows = TAB_DEV * n_dp
    one_hot = (jnp.arange(table_rows)[:, None] == ids.reshape(1, -1)).astype(F32)
    table_local = jnp.dot(one_hot, row_grads.reshape(-1, row_grads.shape[2]), precision=highest_mode)

    def norm_back(dy, hat, root, gain):
        e = dy * gain
        back_ = e - jnp.mean(e, axis=-1, keepdims=True) - hat * jnp.mean(e * hat, axis=-1, keepdims=True)
        return back_ * root[:, :1], jnp.sum(dy * hat, axis=0), jnp.sum(dy, axis=0)

    dy = cot.astype(F32)
    first_rows = jnp.arange(n_mine) * seq_len
    dy = dy.at[first_rows].add(cls_grad)
    dz2, dg2, dc2 = norm_back(dy, xh2, r2, vec[6 + ff_rows])
    df = dz2.astype(BF)
    dg = jnp.einsum("td,hdf->htf", df, outer, preferred_element_type=F32)
    g_outer = jnp.einsum("td,htf->hdf", df, act_low, preferred_element_type=F32).astype(BF)
    du = (dg * slope.astype(F32)).astype(BF)
    normed_low = (xh1 * vec[3] + vec[4]).astype(BF)
    g_inner = jnp.einsum("td,htf->hdf", normed_low, du, preferred_element_type=F32).astype(BF)
    dh1 = jnp.einsum("htf,hdf->td", du, inner, preferred_element_type=F32) + dz2
    dz1, dg1, dc1 = norm_back(dh1, xh1, r1, vec[3])
    da = dz1.astype(BF)
    do = jnp.dot(da, va[1], preferred_element_type=F32).astype(BF)
    g_attn = jnp.einsum("td,te->de", da, mixed, preferred_element_type=F32)
    dqs, dks, dvs = [], [], []
    probs_of = (p_ab.reshape(full, -1, seq_len, seq_len), p_c.reshape(1, -1, n_half, seq_len))
    for qh, kh, vh, doh, pb in zip(*(halves(t, n_full, seq_len) for t in (q, k, v, do)), probs_of):
        probs = pb.astype(F32)
        dp_ = jnp.einsum("gqhe,gkhe->ghqk", doh, vh, preferred_element_type=F32)
        delta = jnp.sum(probs * dp_, axis=-1, keepdims=True)
        ds_ = (probs * (dp_ - delta)).astype(BF)
        dqs.append((jnp.einsum("ghqk,gkhe->gqhe", ds_, kh, preferred_element_type=F32) * score_scale).reshape(-1, width))
        dks.append((jnp.einsum("ghqk,gqhe->gkhe", ds_, qh, preferred_element_type=F32) * score_scale).reshape(-1, width))
        dvs.append(jnp.einsum("ghqk,gqhe->gkhe", pb, doh, preferred_element_type=F32).reshape(-1, width))
    dq = jnp.concatenate(dqs).astype(BF)
    dk = jnp.concatenate(dks).astype(BF)
    dv = jnp.concatenate(dvs).astype(BF)
    g_q = jnp.einsum("td,te->de", x_own, dq, preferred_element_type=F32)
    g_k = jnp.einsum("td,te->de", x_all, dk, preferred_element_type=F32)
    g_v = jnp.einsum("td,te->de", x_all, dv, preferred_element_type=F32)
    g_qk = jnp.stack([g_q, g_k]).astype(BF)
    g_va = jnp.stack([g_v, g_attn]).astype(BF)
    dx_own = jnp.einsum("te,de->td", dq, qk[0], preferred_element_type=F32) + dz1
    dx_all = jnp.einsum("te,de->td", dk, qk[1], preferred_element_type=F32)
    dx_all = dx_all + jnp.einsum("te,de->td", dv, va[0], preferred_element_type=F32)
    dx = jnp.concatenate([dx_all[:n_own] + dx_own, dx_all[n_own:]]).astype(BF)
    db_inner = jnp.sum(du.astype(F32), axis=1)
    db_inner = db_inner.reshape(2, 2, half_ff // 2).transpose(1, 0, 2).reshape(ff_rows, width)
    vec_grad = jnp.concatenate(
        [
            jnp.stack(
                [
                    jnp.sum(dq.astype(F32), axis=0),
                    jnp.sum(dv.astype(F32), axis=0),
                    jnp.sum(dz1, axis=0),
                    dg1,
                    dc1,
                ]
            ),
            db_inner,
            jnp.stack([jnp.sum(dz2, axis=0), dg2, dc2]),
        ]
    )
    vg = vec_grad.reshape(nvec, n_dp, 2, vec_lanes).transpose(1, 0, 2, 3)
    vg = jnp.pad(vg, ((0, 0), (0, 0), (0, 0), (0, 128 - vec_lanes))).reshape(n_dp, nvec, 256)
    pg = proj_grad.reshape(n_dp, 2, half_rows, 128).transpose(0, 2, 1, 3).reshape(n_dp, half_rows, 256)
    tg = table_local.reshape(n_dp, 2, TAB_DEV // 2, 128).transpose(0, 2, 1, 3).reshape(n_dp, TAB_DEV // 2, 256)
    small = jnp.concatenate([pg, vg, tg], axis=1)

    return out_own, dx, *reduce_plain([g_qk, g_va, g_inner, g_outer], small, out_own, dx, rows)


def local(
    tokens, cotangent, lengths, doc_ids, doc_rows,
    w_qkv, m_qkv, v_qkv, w_attn, m_attn, v_attn, w_inner, m_inner, v_inner,
    w_outer, m_outer, v_outer, w_proj, m_proj, v_proj, vectors, m_vectors, v_vectors,
):
    mp = lax.axis_index("mp")
    n_dp, n_mp = lax.axis_size("dp"), lax.axis_size("mp")
    fast = n_dp == NZ * NY * NC and n_mp == NX
    seqs = lengths.shape[0]
    all_rows, width = tokens.shape
    seq_len = all_rows // seqs
    full = seqs // 2
    n_full, n_half = full * seq_len, seq_len // 2
    n_own = n_full + n_half
    rows, half_ff = w_qkv.shape[1], w_inner.shape[1]
    half_rows = rows // 2
    nvec, vec_lanes = vectors.shape
    ff_rows = nvec - 8
    score_scale = HEAD_DIM ** (-0.5)

    if fast:
        saved = forward_fast(lengths, tokens, w_qkv, w_attn, w_inner, w_outer, w_proj, vectors)
        reduced = backward_fast(doc_ids, cotangent, doc_rows, saved, rows)
        params = (w_qkv, m_qkv, v_qkv, w_attn, m_attn, v_attn, w_inner, m_inner, v_inner)
        params += (w_outer, m_outer, v_outer, w_proj, m_proj, v_proj, vectors, m_vectors, v_vectors)
        return finish_fast(reduced, saved[-1], params, all_rows)
    if not fast:
        (out_own, dx, small_r, qk_r, va_r, inner_r, outer_r, peer_out, peer_dx, peer_small, total) = pass_plain(
            lengths, tokens, cotangent, doc_ids, doc_rows, w_qkv, w_attn, w_inner, w_outer, w_proj, vectors
        )
        vector_r = small_r[half_rows : half_rows + nvec, :vec_lanes]
        table_at = half_rows + nvec

    def whole_rows(own, peer):
        lo = jnp.where(mp == 0, own[:n_own], peer[:n_own])
        hi = jnp.where(mp == 0, peer[:n_own], own[:n_own])
        return lo, hi

    lo, hi = whole_rows(out_own, peer_out)
    out_tokens = jnp.concatenate([lo, hi[n_full:], hi[:n_full]])
    lo, hi = whole_rows(dx.astype(F32), peer_dx.astype(F32))
    tail = jnp.where(mp == 0, dx[n_own:], peer_dx[n_own:]).astype(F32)
    tail_hi = jnp.where(mp == 0, peer_dx[n_own:], dx[n_own:]).astype(F32)
    input_grad = jnp.concatenate(
        [lo[:n_full], lo[n_full:] + tail_hi, hi[n_full:] + tail, hi[:n_full]]
    )

    def both_halves(at, count):
        mine_, peer_ = small_r[at : at + count], peer_small[at : at + count]
        return jnp.concatenate(
            [jnp.where(mp == 0, mine_, peer_), jnp.where(mp == 0, peer_, mine_)]
        )

    proj_r = both_halves(0, half_rows)
    table_grad = both_halves(table_at, TAB_DEV // 2)
    qkv_r = jnp.stack([qk_r[0], qk_r[1], va_r[0]])
    attn_r = va_r[1]

    def back(v):
        return v.transpose(1, 0, 2).reshape(rows, half_ff)

    inner_r, outer_r = back(inner_r), back(outer_r)
    grad_norm = jnp.sqrt(total[0, 0])
    clip = clip_norm / jnp.maximum(grad_norm, clip_norm)
    results = [out_tokens, input_grad, grad_norm]
    for w, m, s, g, dec, rate in (
        (w_qkv, m_qkv, v_qkv, qkv_r, decay_rate, learn_rate),
        (w_attn, m_attn, v_attn, attn_r, decay_rate, learn_rate),
        (w_inner, m_inner, v_inner, inner_r, decay_rate, learn_rate),
        (w_outer, m_outer, v_outer, outer_r, decay_rate, learn_rate),
        (w_proj, m_proj, v_proj, proj_r, decay_rate, learn_rate),
        (vectors, m_vectors, v_vectors, vector_r, 0.0, vector_rate),
    ):
        results += list(adamw_update(w, m, s, g * clip, dec, rate))
    return tuple(results) + (table_grad,)


def solution(mesh):
    mat = P("dp", "mp")
    rep = P("dp", None)
    qkv = P(None, "dp", "mp")
    vec = P(None, ("dp", "mp"))
    placed = (rep, rep, P("dp"), rep, P("dp", None, None), qkv, qkv, qkv)
    placed += (mat,) * 9 + (rep,) * 3 + (vec,) * 3
    given = (rep, rep, P(), qkv, qkv, qkv) + (mat,) * 9 + (rep,) * 3 + (vec,) * 3 + (rep,)
    return jax.shard_map(local, mesh=mesh, in_specs=placed, out_specs=given, check_vma=False)
```

```python
import functools

import jax
import jax.numpy as jnp
from jax import lax
from jax.experimental import pallas as pl
from jax.experimental.pallas import tpu as pltpu
from jax.sharding import PartitionSpec as P

HEAD_DIM = 64
STEP = 10
TAB_DEV = 8
MESH = pl.DeviceIdType.MESH
ANY = pl.ANY
BF = jnp.bfloat16
F32 = jnp.float32
NZ, NY, NC, NX = 4, 2, 2, 2

highest_mode = lax.Precision.HIGHEST
retrieval_scale = 0.17677669529663687
ln_epsilon = 1e-12
beta_first = 0.9
beta_second = 0.999
learn_rate = 0.05
vector_rate = 0.5
decay_rate = 0.01
adam_epsilon = 1e-08
clip_norm = 1.0


def layer_norm(values, gain_row, shift_row):
    centre = jnp.mean(values, axis=-1, keepdims=True)
    centred = values - centre
    spread = jnp.mean(centred * centred, axis=-1, keepdims=True)
    return centred * lax.rsqrt(spread + ln_epsilon) * gain_row + shift_row


def gelu_exact(values):
    return jax.nn.gelu(values, approximate=False)


def adamw_update(weight, moment, second, gradient, decay_factor, step_rate):
    moment_new = beta_first * moment + (1.0 - beta_first) * gradient
    second_new = beta_second * second + (1.0 - beta_second) * gradient * gradient
    first_hat = moment_new / (1.0 - beta_first**STEP)
    second_hat = second_new / (1.0 - beta_second**STEP)
    weight_new = weight - step_rate * (
        first_hat / (jnp.sqrt(second_hat) + adam_epsilon) + decay_factor * weight
    )
    return (moment_new, second_new, weight_new)


def squared(values):
    return jnp.sum(values * values)


class Place:
    def __init__(self):
        dp = lax.axis_index("dp")
        self.x = lax.axis_index("mp")
        self.c = lax.rem(dp, NC)
        self.y = lax.rem(dp // NC, NY)
        self.z = dp // (NC * NY)

    def dev(self, z=None, y=None, c=None, x=None):
        z = self.z if z is None else z
        y = self.y if y is None else y
        c = self.c if c is None else c
        x = self.x if x is None else x
        return ((z * NY + y) * NC + c, x)

    def others(self):
        out = [self.dev(z=lax.rem(self.z + k, NZ)) for k in range(1, NZ)]
        out.append(self.dev(x=1 - self.x))
        out.append(self.dev(y=1 - self.y))
        out.append(self.dev(c=1 - self.c))
        return out

    def eights(self):
        out = []
        for k in range(1, 8):
            dx, dy, dc = k & 1, (k >> 1) & 1, k >> 2
            out.append(
                self.dev(
                    x=self.x + dx - 2 * dx * self.x,
                    y=self.y + dy - 2 * dy * self.y,
                    c=self.c + dc - 2 * dc * self.c,
                )
            )
        return out


def greet(devices):
    barrier = pltpu.get_barrier_semaphore()
    for d in devices:
        pl.semaphore_signal(barrier, inc=1, device_id=d, device_id_type=MESH)
    pl.semaphore_wait(barrier, len(devices))


def greet_send(devices):
    barrier = pltpu.get_barrier_semaphore()
    for d in devices:
        pl.semaphore_signal(barrier, inc=1, device_id=d, device_id_type=MESH)


def greet_wait(count):
    pl.semaphore_wait(pltpu.get_barrier_semaphore(), count)


def remote(src, dst, ssem, rsem, dev):
    return pltpu.make_async_remote_copy(
        src_ref=src, dst_ref=dst, send_sem=ssem, recv_sem=rsem, device_id=dev, device_id_type=MESH
    )


def cols(x, half):
    return pl.ds(pl.multiple_of(x * half, 128), half)


def dma(*shape):
    return pltpu.SemaphoreType.DMA(shape)


def mm(a, b):
    return jnp.dot(a, b, preferred_element_type=F32)


def mm_nt(a, b):
    return lax.dot_general(a, b, (((1,), (1,)), ((), ())), preferred_element_type=F32)


def mm_tn(a, b):
    return lax.dot_general(a, b, (((0,), (0,)), ((), ())), preferred_element_type=F32)


def flat(value):
    return value.reshape(-1, value.shape[-1])


def lanes(i, n=128):
    return pl.ds(pl.multiple_of(i * n, 128), n)


def rows_at(i, n, at=0):
    return pl.ds(pl.multiple_of(at + i * n, 16), n)


def each(n, body):
    lax.fori_loop(0, n, lambda i, c: (body(i), c)[1], 0)


gather_orders = ("zxy", "zxy", "yzx", "zxy", "zyx", "zxy", "zyx", "zxy", "zyx", "zxy", "zyx", "zxy", "xyz", "yxz", "zyx")


def with_jobs(n, body, go, jobs):
    def one(i):
        body(i)
        for at, todo in enumerate(jobs):
            if todo:

                @pl.when(i == at)
                def _(todo=todo):
                    for job in todo:
                        go(*job)

    each(n, one)


def stack_heads(pair, wide=None):
    low = jnp.where(lax.broadcasted_iota(jnp.int32, (1, 128), 1) < HEAD_DIM, 1.0, 0.0)
    parts = []
    for mask in (low, 1.0 - low):
        parts.append(pair * mask.astype(BF))
        if wide is not None:
            parts.append(jnp.zeros((wide - pair.shape[0], 128), BF))
    return jnp.concatenate(parts, axis=0)


class Gather:
    def __init__(self, me, pieces, sems):
        self.me, self.pieces = me, pieces
        self.lsem, self.ss, self.rs, self.ds, self.dr = sems
        self.waits = []

    def region(self, p, stage, c, **at):
        dst, me, done = self.pieces[p][1], self.me, gather_orders[p][:stage]
        half = dst.shape[-1] // 2
        z = at.get("z", None if "z" in done else me.z)
        y = at.get("y", None if "y" in done else me.y)
        x = at.get("x", None if "x" in done else me.x)
        zs = slice(None) if z is None else pl.ds(0, NZ - 1) if z == "three" else pl.ds(z, 1)
        ys = slice(None) if y is None else pl.ds(y, 1)
        xs = slice(None) if x is None else cols(x, half)
        return dst.at[zs, ys, c, :, xs]

    def bulk(self, p, stage, c):
        axis = gather_orders[p][stage]
        return self.region(p, stage, c, z="three") if axis == "z" else self.coming(p, stage, c)[0]

    def coming(self, p, stage, c):
        me, axis = self.me, gather_orders[p][stage]
        if axis == "z":
            return [self.region(p, stage, c, z=lax.rem(me.z + NZ - k, NZ)) for k in range(1, NZ)]
        return [self.region(p, stage, c, **{axis: 1 - (me.y if axis == "y" else me.x)})]

    def send(self, p, stage):
        me, axis = self.me, gather_orders[p][stage]
        src, dst = self.pieces[p]
        if stage == 0:
            to = dst.at[me.z, me.y, me.c, :, cols(me.x, dst.shape[-1] // 2)]
        else:
            src = to = self.region(p, stage, me.c)
        if axis == "z":
            devs = [me.dev(z=lax.rem(me.z + k, NZ)) for k in range(1, NZ)]
        else:
            devs = [me.dev(**{axis: 1 - (me.y if axis == "y" else me.x)})]
        for dev in devs:
            remote(src, to, self.ss.at[p, stage], self.rs.at[p, stage], dev).start()
        self.waits.append((p, stage, False))

    def arrived(self, ref, sem):
        remote(ref, ref, sem, sem, self.me.dev(c=1 - self.me.c)).wait_recv()

    def receive(self, p, stage):
        self.arrived(self.bulk(p, stage, self.me.c), self.rs.at[p, stage])

    def crossing(self, p, stage, c):
        if stage == 0:
            ref = self.region(p, 1, c)
            return [ref], ref
        return self.coming(p, stage, c), self.bulk(p, stage, c)

    def cross(self, p, stage):
        refs = self.crossing(p, stage, self.me.c)[0]
        for ref in refs:
            remote(ref, ref, self.ds.at[p, stage], self.dr.at[p, stage], self.me.dev(c=1 - self.me.c)).start()
        self.waits.append((p, stage, True))

    def own_copy(self, p):
        me = self.me
        src, dst = self.pieces[p]
        blk = dst.at[me.z, me.y, me.c, :, cols(me.x, dst.shape[-1] // 2)]
        return pltpu.make_async_copy(src, blk, self.lsem.at[p])

    def step1(self, p):
        self.send(p, 0)
        self.own_copy(p).start()

    def step2(self, p):
        self.own_copy(p).wait()
        self.receive(p, 0)
        self.send(p, 1)
        self.cross(p, 0)

    def step3(self, p):
        self.receive(p, 1)
        self.send(p, 2)
        self.cross(p, 1)

    def step4(self, p):
        self.receive(p, 2)
        self.cross(p, 2)

    def step5(self, p):
        for stage in range(3):
            self.arrived(self.crossing(p, stage, 1 - self.me.c)[1], self.dr.at[p, stage])

    def end(self):
        c = self.me.c
        for p, stage, over in self.waits:
            ref = self.crossing(p, stage, c)[1] if over else self.bulk(p, stage, c)
            sem = (self.ds if over else self.ss).at[p, stage]
            remote(ref, ref, sem, sem, self.me.dev(c=1 - c)).wait_send()


def norm_rows(z_ref, r_ref, n_rows, put, start=0):
    step = 48

    def body(i):
        at = rows_at(i, step, start)
        z = z_ref[at, :]
        centred = z - jnp.mean(z, axis=-1, keepdims=True)
        spread = jnp.mean(centred * centred, axis=-1, keepdims=True)
        root = lax.rsqrt(spread + ln_epsilon)
        hat = centred * root
        z_ref[at, :] = hat
        r_ref[at, :] = jnp.broadcast_to(root, (step, 128))
        put(at, hat)

    each(n_rows // step, body)


def forward_kernel(*refs):
    (lens, tokens, w_qkv, w_attn, w_inner, w_outer, w_proj, vectors) = refs[:8]
    outs = refs[8:27]
    scr = refs[27:]
    (vec_s, proj_s, qk_s, va_s, inner_s, outer_s, vec_g, proj_g, qk, va, inner, outer) = scr[:12]
    (xt, q, k, v, p, o, xh1, r1, g, gp, xh2, r2, out_own, proj, vec, x_all, h1b, vecp, bias_ff) = scr[12:31]
    gsems, tsem, osem = scr[31:36], scr[36], scr[37]
    me = Place()
    mp = me.x
    n_all, width = x_all.shape
    n_own = q.shape[0]
    half_seq = n_all - n_own
    seq = 2 * half_seq
    full = (n_own - half_seq) // seq
    n_full = full * seq
    half_ff = inner.shape[-1]
    rows = qk_s.shape[1]
    half_rows = rows // 2

    starts = (
        (mp * (n_full + seq), 0, n_full),
        (n_full + mp * half_seq, n_full, half_seq),
        (n_full + (1 - mp) * half_seq, n_own, half_seq),
    )
    loads = []
    for i, (at, to, n) in enumerate(starts):
        cp = pltpu.make_async_copy(
            tokens.at[pl.ds(pl.multiple_of(at, 16), n)], x_all.at[pl.ds(to, n)], tsem.at[i]
        )
        cp.start()
        loads.append(cp)

    greet_send(me.others())
    vecp[...] = jnp.zeros_like(vecp)
    nvec, nlane = vectors.shape
    vecp[0:nvec, 0:nlane] = vectors[...]
    proj_s[...] = w_proj[pl.ds(pl.multiple_of(mp * half_rows, 8), half_rows), :]
    vec_s[...] = jnp.transpose(vecp[...])[0:nlane]
    qk_s[...] = w_qkv[0:2].astype(BF)
    va_s[0] = w_qkv[2].astype(BF)
    va_s[1] = w_attn[...].astype(BF)
    hf = half_ff // 2
    for h in range(2):
        inner_s[h] = w_inner[:, h * hf : (h + 1) * hf].astype(BF)
        outer_s[h] = w_outer[:, h * hf : (h + 1) * hf].astype(BF)

    greet_wait(len(me.others()))
    row_cut = 32
    pieces = [
        (vec_s, vec_g),
        (qk_s.at[0], qk.at[0]),
        (qk_s.at[1], qk.at[1]),
        (va_s.at[0, pl.ds(0, row_cut)], va.at[0, :, :, :, pl.ds(0, row_cut)]),
        (va_s.at[0, pl.ds(row_cut, rows - row_cut)], va.at[0, :, :, :, pl.ds(row_cut, rows - row_cut)]),
        (va_s.at[1], va.at[1]),
    ]
    for shard, whole in ((inner_s, inner), (outer_s, outer)):
        for h in range(2):
            for j in range(2):
                src = shard.at[h, :, pl.ds(j * (hf // 2), hf // 2)]
                pieces.append((src, whole.at[h, :, :, :, :, pl.ds(j * hf, hf)]))
    pieces.append((proj_s, proj_g))
    net = Gather(me, pieces, gsems)

    def go(step, *members):
        for piece in members:
            (net.step1, net.step2, net.step3, net.step4, net.step5)[step - 1](piece)

    go(1, 0, 1, 2, 12, 13)
    saves = []

    def save(i, ref):
        cp = pltpu.make_async_copy(ref, outs[i], osem.at[i])
        cp.start()
        saves.append(cp)

    for cp in loads:
        cp.wait()

    def x_turn(i):
        xt[rows_at(i, 256), :] = jnp.transpose(x_all[:, lanes(i, 256)])

    each(width // 256, x_turn)
    save(4, xt)
    go(2, 2, 0)
    go(1, 3, 4)
    go(2, 1, 12, 13)
    go(1, 5)
    go(3, 0, 1, 2)
    go(1, 6)
    go(2, 3, 4)
    go(1, 7)
    go(4, 0)
    go(5, 0)
    big = []
    for z in range(NZ):
        for y in range(NY):
            for c in range(NC):
                for x in range(NX):
                    big.append(vec_g[z, y, c, :, x * 128 : (x + 1) * 128])
    vec[...] = jnp.transpose(jnp.concatenate(big, axis=0))[0 : vec.shape[0]]
    for h in range(2):
        for x in range(NX):
            for j in range(2):
                row = vec[5 + NX * x + h : 6 + NX * x + h, j * (hf // 2) : (j + 1) * (hf // 2)]
                bias_ff[h : h + 1, j * hf + x * (hf // 2) : j * hf + (x + 1) * (hf // 2)] = row
    save(17, vec)

    def project(w_ref, src_rows, dst, bias):
        n_tile = 256

        def body(i):
            w = flat(w_ref[:, :, :, :, lanes(i, n_tile)])
            r = mm(x_all[0:src_rows], w)
            if bias is not None:
                r = r + vec[bias : bias + 1, lanes(i, n_tile)]
            dst[:, lanes(i, n_tile)] = r.astype(BF)

        each(width // n_tile, body)

    go(3, 3)
    go(4, 1)
    go(3, 4)
    go(2, 5)
    go(1, 8)
    go(4, 2)
    go(5, 1)
    project(qk.at[0], n_own, q, 0)
    go(5, 2)
    go(2, 6)
    go(1, 9)
    project(qk.at[1], n_all, k, None)
    save(0, qk)
    go(4, 3, 4)
    go(3, 5)
    go(5, 3, 4)
    project(va.at[0], n_all, v, 1)
    go(2, 7)
    go(3, 6)
    go(1, 10)
    save(5, q)
    save(6, k)
    save(7, v)

    wide = 384
    pos = lax.broadcasted_iota(jnp.int32, (1, wide), 1)
    beyond = jnp.where(pos < seq, 0, 1 << 20)

    def attend(q0, nq, k0, slab, length, place):
        at_q = pl.ds(pl.multiple_of(q0, 16), nq)
        at_k = pl.ds(pl.multiple_of(k0, 16), seq)
        for pair in range(2):
            l = lanes(2 * slab + pair)
            s = mm_nt(q[at_q, l], stack_heads(k[at_k, l], wide)) * (HEAD_DIM**-0.5)
            both = []
            for h in range(2):
                part = jnp.where(place < length, s[:, h * wide : (h + 1) * wide], -1000000000.0)
                e = jnp.exp(part - jnp.max(part, axis=-1, keepdims=True))
                both.append((e * (1.0 / jnp.sum(e, axis=-1, keepdims=True))).astype(BF))
            pb = jnp.concatenate(both, axis=1)
            p[slab, at_q, 2 * wide * pair : 2 * wide * (pair + 1)] = pb
            o[at_q, l] = mm(pb, stack_heads(v[at_k, l], wide)).astype(BF)

    slabs = p.shape[0]
    jobs = [[(2, 8), (1, 11, 14), (3, 12)], [(3, 7)], [(2, 9)], [(4, 5), (3, 13)], [(2, 10), (4, 6)], [(3, 8), (5, 5, 6)]]
    for s in range(full):
        length = lens[mp * (full + 1) + s]
        with_jobs(slabs, lambda i: attend(s * seq, seq, s * seq, i, length, pos + beyond), go, jobs[3 * s : 3 * s + 3])
    length = lens[full]
    pos_c = jnp.where(pos < half_seq, pos + mp * half_seq, pos - half_seq + (1 - mp) * half_seq) + beyond
    with_jobs(slabs, lambda i: attend(n_full, half_seq, n_full, i, length, pos_c), go, [[], [(3, 9)], []])
    go(2, 11, 14)
    save(8, p)
    save(9, o)

    tile = 720
    tiles = n_own // tile

    def attn_out(i):
        a = mm_nt(o[rows_at(i, tile), :], flat(va[1]))
        xh1[rows_at(i, tile), :] = x_all[rows_at(i, tile), :].astype(F32) + a + vec[2:3, :]

    each(tiles, attn_out)
    go(4, 7)
    save(1, va)

    def put_h1(at, hat):
        h1b[at, :] = (hat * vec[3:4, :] + vec[4:5, :]).astype(BF)

    norm_rows(xh1, r1, n_own, put_h1)
    save(10, xh1)
    save(11, r1)
    go(5, 7)
    go(3, 10)
    go(4, 8)

    def feed(h):
        n_tile = 256

        def body(i):
            w = flat(inner[h, :, :, :, :, lanes(i, n_tile)])
            for t in range(tiles):
                at = pl.ds(t * tile, tile)
                u = mm(h1b[at, :], w)
                u = u + bias_ff[h : h + 1, lanes(i, n_tile)]
                tail = 0.5 * (1.0 + lax.erf(u * 0.7071067811865476))
                g[h, at, lanes(i, n_tile)] = (u * tail).astype(BF)
                slope = tail + u * (0.3989422804014327 * jnp.exp(-0.5 * u * u))
                gp[h, at, lanes(i, n_tile)] = slope.astype(BF)

        each(half_ff // n_tile, body)

    feed(0)
    go(3, 11)
    go(5, 8)
    go(4, 9)
    go(5, 9)
    feed(1)
    go(3, 14)
    go(4, 10, 12, 11, 13)
    go(5, 10, 12, 11, 13)
    save(2, inner)
    save(12, g)
    save(13, gp)

    def ff_out(i):
        at = rows_at(i, tile)
        f = mm_nt(g[0, at, :], flat(outer[0])) + mm_nt(g[1, at, :], flat(outer[1]))
        h1 = xh1[at, :] * vec[3:4, :] + vec[4:5, :]
        xh2[at, :] = h1 + f + vec[9:10, :]

    each(tiles, ff_out)
    save(3, outer)
    go(4, 14)

    def put_y(at, hat):
        out_own[at, :] = (hat * vec[10:11, :] + vec[11:12, :]).astype(BF)

    cut = n_own // 96 * 48 + 48
    for at, n, slot in ((0, cut, 0), (cut, n_own - cut, 1)):
        norm_rows(xh2, r2, n, put_y, at)
        for i, ref in ((14, xh2), (15, r2), (18, out_own)):
            part = pl.ds(at, n)
            sem = osem.at[i] if slot == 0 else osem.at[19 + (14, 15, 18).index(i)]
            cp = pltpu.make_async_copy(ref.at[part], outs[i].at[part], sem)
            cp.start()
            saves.append(cp)
    go(5, 14)
    for d in range(NZ * NY * NC * NX):
        block = proj_g[d // 8, d // 4 % 2, d // 2 % 2, :, d % 2 * 128 : (d % 2 + 1) * 128]
        proj[d * half_rows : (d + 1) * half_rows] = block
    save(16, proj)
    net.end()
    for cp in saves:
        cp.wait()


def forward_fast(lengths, tokens, w_qkv, w_attn, w_inner, w_outer, w_proj, vectors):
    seqs = lengths.shape[0]
    all_rows, width = tokens.shape
    seq = all_rows // seqs
    full = seqs // 2
    n_own = full * seq + seq // 2
    n_all = n_own + seq // 2
    rows, half_ff = w_qkv.shape[1], w_inner.shape[1]
    heads = width // HEAD_DIM
    zyc = (NZ, NY, NC)
    hr, nlane = rows // 2, vectors.shape[1]
    weights = [
        ((2,) + zyc + (rows, width), BF),
        ((2,) + zyc + (rows, width), BF),
        ((2,) + zyc + (rows, half_ff), BF),
        ((2,) + zyc + (rows, half_ff), BF),
    ]
    kept = [
        ((width, n_all), BF),
        ((n_own, width), BF),
        ((n_all, width), BF),
        ((n_all, width), BF),
        ((heads // 4, n_own, 4 * 384), BF),
        ((n_own, width), BF),
        ((n_own, width), F32),
        ((n_own, 128), F32),
        ((2, n_own, half_ff), BF),
        ((2, n_own, half_ff), BF),
        ((n_own, width), F32),
        ((n_own, 128), F32),
        ((width, 128), F32),
        ((16, width), F32),
        ((n_own, width), BF),
    ]
    order = kept[:12] + [kept[14], kept[12], kept[13]]
    scratch = [
        ((nlane, 128), F32),
        ((hr, 128), F32),
        ((2, rows, width // 2), BF),
        ((2, rows, width // 2), BF),
        ((2, rows, half_ff // 2), BF),
        ((2, rows, half_ff // 2), BF),
        (zyc + (nlane, 256), F32),
        (zyc + (hr, 256), F32),
    ]
    scratch += weights + order
    scratch += [((n_all, width), BF), ((n_own, width), BF), ((128, 128), F32), ((8, half_ff), F32)]
    n = 15
    vm = pl.BlockSpec(memory_space=pltpu.VMEM)
    hb = pl.BlockSpec(memory_space=ANY)
    sm = pl.BlockSpec(memory_space=pltpu.SMEM)
    return pl.pallas_call(
        forward_kernel,
        out_shape=[jax.ShapeDtypeStruct(s, d) for s, d in weights + kept],
        in_specs=[sm, hb] + [vm] * 6,
        out_specs=[hb] * 19,
        scratch_shapes=[pltpu.VMEM(s, d) for s, d in scratch]
        + [
            dma(n), dma(n, 3), dma(n, 3), dma(n, 3), dma(n, 3),
            dma(3), dma(22),
        ],
        compiler_params=pltpu.CompilerParams(
            collective_id=1, has_side_effects=True, vmem_limit_bytes=60 * 2**20
        ),
        name="forward",
    )(lengths, tokens, w_qkv, w_attn, w_inner, w_outer, w_proj, vectors)


class Reduce:
    def __init__(self, me, pieces, sems):
        self.me, self.pieces = me, pieces
        self.ds, self.dr, self.ss, self.rs = sems
        self.waits, self.sent = [], []
        self.squares = jnp.zeros((1, 1), F32)

    def go(self, copy):
        copy.start()
        self.waits.append(copy)

    def arrived(self, ref, ssem, rsem):
        remote(ref, ref, ssem, rsem, self.me.dev(c=1 - self.me.c)).wait_recv()

    def region(self, p, stage, **at):
        order, src = self.pieces[p][0], self.pieces[p][2]
        me, done = self.me, order[:stage]
        half = src.shape[-1] // 2
        z = at.get("z", me.z if "z" in done else None)
        y = at.get("y", me.y if "y" in done else None)
        x = at.get("x", me.x if "x" in done else None)
        zs = slice(None) if z is None else pl.ds(0, NZ - 1) if z == "three" else pl.ds(z, 1)
        ys = slice(None) if y is None else pl.ds(y, 1)
        xs = slice(None) if x is None else cols(x, half)
        return src.at[zs, ys, me.c, :, xs]

    def send(self, p, stage):
        order, got, me = self.pieces[p][0], self.pieces[p][4 + stage], self.me
        ss, rs = self.ss, self.rs
        if order[stage] == "z":
            for k in range(1, NZ):
                tz = lax.rem(me.z + k, NZ)
                part = self.region(p, stage, z=tz)
                remote(part, got.at[pl.ds(k, 1)], ss.at[p, stage], rs.at[p, stage], me.dev(z=tz)).start()
        else:
            far = 1 - (me.y if order[stage] == "y" else me.x)
            part = self.region(p, stage, **{order[stage]: far})
            dev = me.dev(**{order[stage]: far})
            remote(part, got, ss.at[p, stage], rs.at[p, stage], dev).start()
        self.sent.append((p, stage))

    def receive(self, p, stage):
        order, got = self.pieces[p][0], self.pieces[p][4 + stage]
        if order[stage] == "z":
            got = got.at[pl.ds(1, NZ - 1)]
        self.arrived(got, self.ss.at[p, stage], self.rs.at[p, stage])

    def add(self, p, stage):
        order, _, src, _, *gots = self.pieces[p]
        got, me = gots[stage], self.me
        done = order[: stage + 1]
        half = src.shape[-1] // 2
        xs = cols(me.x, half) if "x" in done else slice(None)
        ys = [(me.y, 0)] if "y" in done else [(y, y) for y in range(NY)]
        if order[stage] == "z":
            for y, i in ys:
                total = src[me.z, y, me.c, :, xs].astype(F32)
                for k in range(1, NZ):
                    total = total + got[k, i].astype(F32)
                src[me.z, y, me.c, :, xs] = total.astype(src.dtype)
            return

        def one(z):
            for y, i in ys:
                src[z, y, me.c, :, xs] = src[z, y, me.c, :, xs] + got[0 if "z" in done else z, i]

        if "z" in done:
            one(me.z)
        else:
            each(NZ, one)

    def step1(self, p):
        src, got = self.pieces[p][2], self.pieces[p][3]
        oc = 1 - self.me.c
        remote(src.at[:, :, oc], got, self.ds.at[p], self.dr.at[p], self.me.dev(c=oc)).start()
        self.sent.append((p, None))

    def step2(self, p):
        src, got, c = self.pieces[p][2], self.pieces[p][3], self.me.c
        self.arrived(got, self.ds.at[p], self.dr.at[p])

        def one(z):
            for y in range(NY):
                src[z, y, c] = src[z, y, c] + got[z, y]

        each(NZ, one)
        self.send(p, 0)

    def step3(self, p):
        self.receive(p, 0)
        self.add(p, 0)
        self.send(p, 1)

    def step4(self, p):
        self.receive(p, 1)
        self.add(p, 1)
        self.send(p, 2)

    def step5(self, p, counted=None):
        order, dst, src, _, *gots = self.pieces[p]
        me = self.me
        self.receive(p, 2)
        total = src[me.z, me.y, me.c, :, cols(me.x, src.shape[-1] // 2)].astype(F32)
        for k in range(1, NZ) if order[2] == "z" else (0,):
            total = total + gots[2][k, 0].astype(F32)
        dst[...] = total
        total = total[:counted]
        self.squares = self.squares + jnp.sum(total * total, keepdims=True)

    def end(self):
        oc = 1 - self.me.c
        for p, stage in self.sent:
            if stage is None:
                part, sem = self.pieces[p][2].at[:, :, oc], self.ds.at[p]
            else:
                axis = self.pieces[p][0][stage]
                far = "three" if axis == "z" else 1 - (self.me.y if axis == "y" else self.me.x)
                part, sem = self.region(p, stage, **{axis: far}), self.ss.at[p, stage]
            remote(part, part, sem, sem, self.me.dev(c=oc)).wait_send()
        for copy in self.waits:
            copy.wait_send()


def got_shapes(order, r, w):
    out, done = [], ""
    for axis in order:
        done += axis
        nz = NZ if axis == "z" or "z" not in done else 1
        out.append((nz, 1 if "y" in done else NY, r, w // 2 if "x" in done else w))
    return out


orders = ("yxz", "yxz", "zyx", "zyx", "yxz", "yxz", "yzx", "yxz", "yxz", "zyx", "yxz", "yxz", "yxz", "yxz")


def all_squares(me, net, total, sq4, sq8, sems):
    qs, qr, es, er = sems
    sq4[0] = jnp.broadcast_to(total, (8, 128))
    copies = []
    for k in range(1, NZ):
        copies.append(remote(sq4.at[0], sq4.at[k], qs.at[k], qr.at[k], me.dev(z=lax.rem(me.z + k, NZ))))
    for copy in copies:
        net.go(copy)
    for copy in copies:
        copy.wait_recv()

    def at_z(z):
        out = jnp.zeros((8, 128), F32)
        for k in range(NZ):
            out = out + jnp.where(lax.rem(me.z + NZ - k, NZ) == z, sq4[k], 0.0)
        return out

    sq8[0] = at_z(0) + at_z(1) + at_z(2) + at_z(3)
    copies = []
    for k, dev in enumerate(me.eights(), 1):
        copies.append(remote(sq8.at[0], sq8.at[k], es.at[k], er.at[k], dev))
    for copy in copies:
        net.go(copy)
    for copy in copies:
        copy.wait_recv()

    def at_code(w):
        out = jnp.zeros((8, 128), F32)
        for k in range(8):
            dx, dy, dc = k & 1, (k >> 1) & 1, k >> 2
            src = (
                (me.x + dx - 2 * dx * me.x)
                + 2 * (me.y + dy - 2 * dy * me.y)
                + 4 * (me.c + dc - 2 * dc * me.c)
            )
            out = out + jnp.where(src == w, sq8[k], 0.0)
        return out

    whole = at_code(0)
    for w in range(1, 8):
        whole = whole + at_code(w)
    return whole


def fold(value):
    return jnp.sum(value.reshape(-1, 8, value.shape[-1]), axis=0)


def norm_back_rows(n_rows, get_dy, hat_ref, root_ref, gain, put, acc):
    step = 48

    def body(i):
        at = rows_at(i, step)
        dy, hat = get_dy(i, at), hat_ref[at, :]
        e = dy * gain
        root = root_ref[at, 0:1]
        m1 = jnp.mean(e, axis=-1, keepdims=True)
        m2 = jnp.mean(e * hat, axis=-1, keepdims=True)
        dz = (e - m1 - hat * m2) * root
        acc[0] = acc[0] + fold(dy * hat)
        acc[1] = acc[1] + fold(dy)
        acc[2] = acc[2] + fold(dz)
        hat_ref[at, :] = dz
        put(at, dz)

    each(n_rows // step, body)


def backward_kernel(*refs):
    doc_ids, cotangent, doc_rows = refs[:3]
    (qk_h, va_h, inner_h, outer_h, xt_h, q_h, k_h, v_h, p_h, o_h, xh1_h, r1_h, g_h, gp_h, xh2_h, r2_h, proj_h, vec_h, out_h) = refs[3:22]
    outs = refs[22:32]
    small_r, qk_r, va_r, inner_r, outer_r, dx, peer_out, peer_dx, peer_small, norm_ref = outs
    scr = list(refs[32:])

    def take(n):
        got = scr[:n]
        del scr[:n]
        return got

    (inner, outer, attn, xt, q, k, v, o, xh1, gg, xh2, r2, proj, vec, cls_in, cot, df, dft) = take(18)
    (cls_grad, acc1, acc2, ffacc, vg, early, late) = take(7)
    grads = take(4)
    bufs = take(14 * 4)
    sq4, sq8 = take(2)
    lsem, rsems, xs, xr, qsems = take(1)[0], take(4), *take(2), take(4)
    do, da, dat, h1t, r1 = cot, df, dft, dft, r2
    me = Place()
    mp = me.x
    n_all, width = dx.shape
    n_own = q.shape[0]
    half_seq = n_all - n_own
    seq = 2 * half_seq
    n_full = n_own - half_seq
    full = n_full // seq
    half_ff = inner.shape[-1]
    other = me.dev(x=1 - mp)

    for i in range(4):
        grads.append(inner.at[i // 2, :, :, :, :, pl.ds(width * (i % 2), width)])
    copies = {}

    def load(name, i, src, dst):
        cp = pltpu.make_async_copy(src, dst, lsem.at[i])
        cp.start()
        copies[name] = cp

    def need(*names):
        for name in names:
            copies[name].wait()

    load("vec", 0, vec_h, vec)
    load("proj", 1, proj_h, proj)
    for s in range(full + 1):
        load("cls%d" % s, 2 + s, out_h.at[pl.ds(s * seq, 16)], cls_in.at[s])
    load("cot0", 5, cotangent.at[pl.ds(pl.multiple_of(mp * (n_full + seq), 16), n_full)], cot.at[pl.ds(0, n_full)])
    load("cot1", 6, cotangent.at[pl.ds(pl.multiple_of(n_full + mp * half_seq, 16), half_seq)], cot.at[pl.ds(n_full, half_seq)])
    load("xh2", 7, xh2_h, xh2)
    load("r2", 8, r2_h, r2)
    load("g", 9, g_h, gg.at[pl.ds(0, 2)])
    load("outer", 10, outer_h, outer)
    load("gp", 11, gp_h, gg.at[pl.ds(2, 2)])
    load("xh1", 12, xh1_h, xh1)
    load("inner", 14, inner_h, inner)
    load("attn", 15, va_h.at[1], attn)
    load("o", 16, o_h, o)
    load("q", 17, q_h, q)
    load("k", 18, k_h, k)
    load("v", 19, v_h, v)
    load("xt", 20, xt_h, xt)

    greet(me.others() + me.eights())
    pieces = []
    hr = width // (NZ * NY * NC * NX)
    n_early = early.shape[3]
    hf = half_ff // 2
    dsts, srcs = [], []
    for i, ref in enumerate((outer_r, inner_r)):
        for h in range(2):
            for j in range(2):
                dsts.append(ref.at[h, :, pl.ds(j * (hf // 2), hf // 2)])
                srcs.append(grads[2 * i + h].at[:, :, :, :, pl.ds(j * hf, hf)])
    dsts += [va_r.at[1], va_r.at[0], qk_r.at[0], qk_r.at[1]]
    dsts += [small_r.at[pl.ds(0, n_early)], small_r.at[pl.ds(n_early, hr)]]
    srcs += grads[4:] + [early, late]
    for i in range(14):
        pieces.append((orders[i], dsts[i], srcs[i]) + tuple(bufs[4 * i : 4 * i + 4]))
    net = Reduce(me, pieces, rsems)

    def go(step, *members):
        for piece in members:
            if step == 5 and piece == 12:
                net.step5(piece, hr)
            else:
                (net.step1, net.step2, net.step3, net.step4, net.step5)[step - 1](piece)

    send_out = remote(out_h, peer_out, xs.at[0], xr.at[0], other)
    net.go(send_out)

    vg[...] = jnp.zeros_like(vg)
    early[...] = jnp.zeros_like(early)
    acc1[...] = jnp.zeros_like(acc1)
    acc2[...] = jnp.zeros_like(acc2)
    ffacc[...] = jnp.zeros_like(ffacc)
    need("vec", "proj", *["cls%d" % s for s in range(full + 1)])
    row16 = lax.broadcasted_iota(jnp.int32, (16, 1), 0)
    cls = jnp.zeros((16, width), F32)
    for s in range(full + 1):
        cls = jnp.where(row16 == s, cls_in[s].astype(F32)[0:1], cls)
    cls = cls.astype(BF)
    proj_low = proj[...].astype(BF)
    query = mm(cls, proj_low).astype(BF).astype(F32)
    row8 = lax.broadcasted_iota(jnp.int32, (8, 1), 0)
    dcq = jnp.zeros((16, 128), F32)
    row_grads = []
    cands = doc_ids.shape[1]
    seq_ids = [mp * (full + 1) + s for s in range(full)] + [full]
    for s in range(full + 1):
        docs = doc_rows[seq_ids[s]].astype(F32)
        mine = 1.0 if s < full else jnp.where(mp == 0, 1.0, 0.0)
        query_s = query[s : s + 1]
        score = jnp.sum(query_s * docs, axis=-1, keepdims=True) * retrieval_scale
        e = jnp.exp(score - jnp.max(score, axis=0, keepdims=True))
        soft = e / jnp.sum(e, axis=0, keepdims=True)
        sg = (soft - jnp.where(row8 == 0, 1.0, 0.0)) * (retrieval_scale * mine)
        dcq = jnp.where(row16 == s, jnp.sum(sg * docs, axis=0, keepdims=True), dcq)
        row_grads.append(sg * query_s)
    dcq = dcq.astype(BF)
    cls_grad[...] = mm_nt(dcq, proj_low)
    proj_grad = mm_tn(cls, dcq)
    n_dev = NZ * NY * NC * NX
    table_row = lax.broadcasted_iota(jnp.int32, (TAB_DEV * n_dev // NX, 1), 0)
    table = jnp.zeros((TAB_DEV * n_dev // NX, 128), F32)
    for s in range(full + 1):
        for i in range(cands):
            table = table + jnp.where(table_row == doc_ids[seq_ids[s], i], row_grads[s][i : i + 1], 0.0)
    tr = TAB_DEV // NX
    for d in range(n_dev):
        z, y, c, x = d // 8, d // 4 % 2, d // 2 % 2, d % 2
        l = slice(x * 128, (x + 1) * 128)
        t0 = (d // 2) * TAB_DEV + x * tr
        early[z, y, c, 0:hr, l] = proj_grad[d * hr : (d + 1) * hr]
        early[z, y, c, hr : hr + tr, l] = table[t0 : t0 + tr]
    go(1, 12)

    per = seq // 48
    row48 = lax.broadcasted_iota(jnp.int32, (48, 1), 0)

    def get_dy(i, at):
        first = (row48 == 0) & (lax.rem(i, per) == 0)
        return cot[at, :].astype(F32) + jnp.where(first, cls_grad[pl.ds(i // per, 1), :], 0.0)

    def put_df(at, dz):
        df[at, :] = dz.astype(BF)

    need("cot0", "cot1", "xh2", "r2")
    norm_back_rows(n_own, get_dy, xh2, r2, vec[10:11, :], put_df, acc2)

    def turn(src, dst, n_rows):
        def body(i):
            dst[rows_at(i, 256), 0:n_rows] = jnp.transpose(src[:, lanes(i, 256)])

        each(width // 256, body)

    load("r1", 13, r1_h, r1)
    turn(df, dft, n_own)
    go(2, 12)
    n_tile = 256
    shape5 = (NZ, NY, NC, width // (NZ * NY * NC))

    def weight_grad(left, right, dst, n, at=0):
        def body(i):
            r = mm(left(), right(lanes(i + at, n_tile)))
            dst[:, :, :, :, lanes(i + at, n_tile)] = r.astype(BF).reshape(shape5 + (n_tile,))

        each(n // n_tile, body)

    need("g")
    for h in range(2):
        for j in range(2):
            weight_grad(lambda: dft[:, 0:n_own], lambda l: gg[h, :, l], grads[h], hf, j * (hf // n_tile))
            i = 2 * h + j
            go(1, i)
            if i > 1:
                go(2, i - 2)

    need("outer", "gp")
    tile = 720
    tiles = n_own // tile

    def hidden(h):
        def body(i):
            w = flat(outer[h, :, :, :, :, lanes(i, n_tile)])
            for t in range(tiles):
                at = pl.ds(t * tile, tile)
                du = (mm(df[at, :], w) * gg[2 + h, at, lanes(i, n_tile)].astype(F32)).astype(BF)
                gg[2 + h, at, lanes(i, n_tile)] = du
                ffacc[h, :, lanes(i, n_tile)] = ffacc[h, :, lanes(i, n_tile)] + fold(du.astype(F32))

        each(half_ff // n_tile, body)

    go(2, 2)
    hidden(0)
    go(2, 3)
    go(3, 12)
    hidden(1)
    load("p0", 21, p_h.at[0], gg.at[0])
    load("p1", 22, p_h.at[1], gg.at[1])
    load("wq", 23, qk_h.at[0], outer.at[0, :, :, :, :, pl.ds(0, width)])
    load("wk", 24, qk_h.at[1], outer.at[0, :, :, :, :, pl.ds(width, width)])
    load("wv", 25, va_h.at[0], outer.at[1, :, :, :, :, pl.ds(0, width)])
    need("xh1", "r1")

    def h1_turn(i):
        l = lanes(i, 256)
        h1 = (xh1[:, l] * vec[3:4, l] + vec[4:5, l]).astype(BF)
        h1t[rows_at(i, 256), 0:n_own] = jnp.transpose(h1)

    each(width // 256, h1_turn)
    for h in range(2):
        for j in range(2):
            weight_grad(lambda: h1t[:, 0:n_own], lambda l: gg[2 + h, :, l], grads[2 + h], hf, j * (hf // n_tile))
            i = 4 + 2 * h + j
            go(1, i)
            if i > 5:
                go(2, i - 2)
            if i == 5:
                go(3, 0)
            if i == 7:
                go(3, 1)
    need("inner")

    def hidden_back(i):
        at = rows_at(i, tile)
        d = mm_nt(gg[2, at, :], flat(inner[0])) + mm_nt(gg[3, at, :], flat(inner[1]))
        xh2[at, :] = d + xh2[at, :]

    each(tiles, hidden_back)
    load("p2", 26, p_h.at[2], gg.at[2])
    go(2, 6, 7)

    norm_back_rows(n_own, lambda i, at: xh2[at, :], xh1, r1, vec[3:4, :], put_df, acc1)
    need("attn", "o")

    def mixed_back(i):
        do[:, lanes(i, n_tile)] = mm(da[...], flat(attn[:, :, :, :, lanes(i, n_tile)])).astype(BF)

    each(width // n_tile, mixed_back)
    turn(da, dat, n_own)
    weight_grad(lambda: dat[:, 0:n_own], lambda l: o[:, l], grads[4], width)
    go(1, 8)
    go(3, 4, 2)

    need("q", "k", "v", "p0", "p1", "p2")
    wide = 384
    scale = HEAD_DIM**-0.5

    def attend(q0, nq, k0, slab):
        at_q = pl.ds(pl.multiple_of(q0, 16), nq)
        at_k = pl.ds(pl.multiple_of(k0, 16), seq)
        for pair in range(2):
            l = lanes(2 * slab + pair)
            qp, kp, dop = q[at_q, l], k[at_k, l], do[at_q, l]
            pb = gg[slab, at_q, 2 * wide * pair : 2 * wide * (pair + 1)]
            p = pb.astype(F32)
            pd = p * mm_nt(dop, stack_heads(v[at_k, l], wide))
            ds, pbs = [], []
            for h in range(2):
                at = slice(h * wide, (h + 1) * wide)
                ds.append((pd[:, at] - p[:, at] * jnp.sum(pd[:, at], axis=-1, keepdims=True)).astype(BF))
                pbs.append(pb[:, h * wide : h * wide + seq])
            q[at_q, l] = (mm(jnp.concatenate(ds, axis=1), stack_heads(kp, wide)) * scale).astype(BF)
            ds = jnp.concatenate([d[:, 0:seq] for d in ds], axis=0)
            k[at_k, l] = (mm_tn(ds, stack_heads(qp)) * scale).astype(BF)
            v[at_k, l] = mm_tn(jnp.concatenate(pbs, axis=0), stack_heads(dop)).astype(BF)

    slabs = p_h.shape[0]
    jobs = (
        ([(2, 8), (4, 0, 1)], [(3, 5)], [(3, 3), (4, 12)]),
        ([(4, 4)], [(3, 6)], []),
        ([(3, 7)], [(4, 5)], [(4, 2)]),
    )

    def tokens_back(at, own):
        d = mm_nt(k[at, :], flat(outer[0, :, :, :, :, width : 2 * width]))
        d = d + mm_nt(v[at, :], flat(outer[1, :, :, :, :, 0:width]))
        if own:
            d = d + mm_nt(q[at, :], flat(outer[0, :, :, :, :, 0:width])) + xh1[at, :]
            o[at, :] = d.astype(BF)
        else:
            df[0:half_seq, :] = d.astype(BF)

    keeps = []

    def send_dx(i, src, at):
        net.go(remote(src, peer_dx.at[at], xs.at[1 + i], xr.at[1 + i], other))
        cp = pltpu.make_async_copy(src, dx.at[at], lsem.at[27 + i])
        cp.start()
        keeps.append(cp)

    need("wq", "wk", "wv")
    for s in range(full):
        with_jobs(slabs, lambda i: attend(s * seq, seq, s * seq, i), go, jobs[s])
        tokens_back(pl.ds(s * seq, seq), True)
        size = seq if s == 0 else half_seq
        send_dx(s, o.at[pl.ds(s * seq, size)], pl.ds(s * seq, size))
    with_jobs(slabs, lambda i: attend(n_full, half_seq, n_full, i), go, jobs[full])
    need("xt")
    weight_grad(lambda: xt[...], lambda l: v[:, l], grads[5], width)
    go(1, 9)
    send_dx(2, o.at[pl.ds(n_full - half_seq, half_seq)], pl.ds(n_full - half_seq, half_seq))
    weight_grad(lambda: xt[:, 0:n_own], lambda l: q[:, l], grads[6], width)
    go(1, 10)
    go(2, 9)
    go(4, 6)
    weight_grad(lambda: xt[...], lambda l: k[:, l], grads[7], width)
    go(1, 11)
    go(2, 10)
    go(3, 8)
    go(4, 3)
    tokens_back(pl.ds(n_full, half_seq), True)
    go(2, 11)
    tokens_back(pl.ds(n_own, half_seq), False)

    vg[0:1, :] = jnp.sum(q[...].astype(F32), axis=0, keepdims=True)
    vg[1:2, :] = jnp.sum(v[...].astype(F32), axis=0, keepdims=True)
    vg[2:3, :] = jnp.sum(acc1[2], axis=0, keepdims=True)
    vg[3:4, :] = jnp.sum(acc1[0], axis=0, keepdims=True)
    vg[4:5, :] = jnp.sum(acc1[1], axis=0, keepdims=True)
    for h in range(2):
        both = jnp.sum(ffacc[h], axis=0, keepdims=True)
        for x in range(NX):
            for j in range(2):
                at = j * hf + x * (hf // 2)
                vg[5 + NX * x + h : 6 + NX * x + h, j * (hf // 2) : (j + 1) * (hf // 2)] = both[:, at : at + hf // 2]
    vg[9:10, :] = jnp.sum(acc2[2], axis=0, keepdims=True)
    vg[10:11, :] = jnp.sum(acc2[0], axis=0, keepdims=True)
    vg[11:12, :] = jnp.sum(acc2[1], axis=0, keepdims=True)
    turned = jnp.transpose(vg[...])
    for d in range(n_dev):
        z, y, c, x = d // 8, d // 4 % 2, d // 2 % 2, d % 2
        late[z, y, c, :, x * 128 : (x + 1) * 128] = turned[d * hr : (d + 1) * hr]
    go(1, 13)
    go(2, 13)
    go(4, 7)
    go(5, 0, 1, 4, 5, 12)
    go(3, 10)
    go(3, 11)
    go(4, 8)
    go(3, 9)
    go(4, 10)
    go(3, 13)
    send_dx(3, o.at[pl.ds(n_full, half_seq)], pl.ds(n_full, half_seq))
    go(4, 9)
    go(4, 11)
    send_dx(4, df.at[pl.ds(0, half_seq)], pl.ds(n_own, half_seq))
    go(4, 13)
    go(5, 2, 3, 6, 7, 8, 10, 9)
    go(5, 11, 13)
    net.go(remote(small_r, peer_small, xs.at[6], xr.at[6], other))
    norm_ref[...] = all_squares(me, net, net.squares, sq4, sq8, qsems)
    parts = [pl.ds(0, seq)] + [pl.ds(seq + i * half_seq, half_seq) for i in range(4)]
    for i, ref in enumerate([peer_out] + [peer_dx.at[at] for at in parts] + [peer_small]):
        net.arrived(ref, xs.at[i], xr.at[i])
    for cp in keeps:
        cp.wait()
    net.end()


def backward_fast(doc_ids, cotangent, doc_rows, saved, rows):
    (qk, va, inner, outer, xt, q, k, v, p, o, xh1, r1, g, gp, xh2, r2, proj, vec, out_own) = saved
    n_own, width = q.shape
    n_all = k.shape[0]
    half_ff = inner.shape[-1]
    zyc = (NZ, NY, NC)
    hr = rows // NX
    n_early = hr + 8
    small_rows = n_early + hr
    ins = [doc_ids, cotangent, doc_rows] + list(saved)
    out_shape = [
        ((small_rows, 128), F32),
        ((2, rows, width // 2), F32),
        ((2, rows, width // 2), F32),
        ((2, rows, half_ff // 2), F32),
        ((2, rows, half_ff // 2), F32),
        ((n_all, width), BF),
        ((n_own, width), BF),
        ((n_all, width), BF),
        ((small_rows, 128), F32),
        ((8, 128), F32),
    ]
    like = lambda a: (a.shape, a.dtype)
    wide = width // 128 * 128
    scratch = [
        like(inner), like(outer), (va.shape[1:], BF), like(xt), like(q), like(k), like(v), like(o),
        like(xh1), ((4,) + g.shape[1:], BF), like(xh2), like(r2), like(proj), like(vec),
        ((3, 16, width), BF), ((n_own, width), BF), ((n_own, width), BF),
        ((width, wide), BF),
        ((16, width), F32), ((3, 8, width), F32), ((3, 8, width), F32), ((2, 8, half_ff), F32),
        ((128, width), F32), (zyc + (n_early, 256), F32), (zyc + (hr, 256), F32),
    ]
    sizes = [half_ff] * 4 + [width] * 4
    scratch += [(zyc + (rows, w), BF) for w in sizes[:4]]
    smalls = [(n_early, 256, F32), (hr, 256, F32)]
    for i, (r, w, dt) in enumerate([(rows, width, BF)] * 12 + smalls):
        scratch += [((NZ, NY, r, w), dt)] + [(shape, dt) for shape in got_shapes(orders[i], r, w)]
    scratch += [((NZ, 8, 128), F32), ((8, 8, 128), F32)]
    vm = pl.BlockSpec(memory_space=pltpu.VMEM)
    hb = pl.BlockSpec(memory_space=ANY)
    sm = pl.BlockSpec(memory_space=pltpu.SMEM)
    n = 14
    return pl.pallas_call(
        backward_kernel,
        out_shape=[jax.ShapeDtypeStruct(s, d) for s, d in out_shape],
        in_specs=[sm, hb, vm] + [hb] * 19,
        out_specs=[vm] * 5 + [hb, hb, hb, vm, vm],
        scratch_shapes=[pltpu.VMEM(s, d) for s, d in scratch]
        + [
            dma(32), dma(n), dma(n), dma(n, 3), dma(n, 3),
            dma(7), dma(7), dma(NZ), dma(NZ), dma(8), dma(8),
        ],
        compiler_params=pltpu.CompilerParams(
            collective_id=2, has_side_effects=True, vmem_limit_bytes=63 * 2**20
        ),
        name="backward",
    )(*ins)


def finish_kernel(*refs):
    small_r, peer_small, qk_r, va_r, inner_r, outer_r, total = refs[:7]
    out_own, peer_out, dx, peer_dx = refs[7:11]
    params = [refs[11 + 3 * i : 14 + 3 * i] for i in range(6)]
    outs = refs[29:51]
    turn, sem, lo, hi, mid = refs[51:]
    out_tokens, input_grad, norm = outs[0:3]
    news = [outs[3 + 3 * i : 6 + 3 * i] for i in range(6)]
    table_grad = outs[21]
    mp = lax.axis_index("mp")
    n_own = out_own.shape[0]
    n_all = dx.shape[0]
    half_seq = n_all - n_own
    n_full = n_own - half_seq
    seq = 2 * half_seq
    copies = []
    for i, (src, first) in enumerate(((out_own, mp), (peer_out, 1 - mp))):
        at = pl.multiple_of(first * (n_full + seq), 16)
        copies.append((src.at[pl.ds(0, n_full)], out_tokens.at[pl.ds(at, n_full)]))
        at = pl.multiple_of(n_full + first * half_seq, 16)
        copies.append((src.at[pl.ds(n_full, half_seq)], out_tokens.at[pl.ds(at, half_seq)]))
    copies = [pltpu.make_async_copy(s, d, sem.at[i]) for i, (s, d) in enumerate(copies)]
    for cp in copies:
        cp.start()
    lo[...] = dx[0:n_full].astype(F32)
    hi[...] = peer_dx[0:n_full].astype(F32)
    own_mid = dx[n_full:n_own].astype(F32) + peer_dx[n_own:n_all].astype(F32)
    peer_mid = peer_dx[n_full:n_own].astype(F32) + dx[n_own:n_all].astype(F32)
    mid[pl.ds(pl.multiple_of(mp * half_seq, 16), half_seq)] = own_mid
    mid[pl.ds(pl.multiple_of((1 - mp) * half_seq, 16), half_seq)] = peer_mid
    grads = (
        (lo, pl.multiple_of(mp * (n_full + seq), 16), n_full),
        (hi, pl.multiple_of((1 - mp) * (n_full + seq), 16), n_full),
        (mid, n_full, seq),
    )
    for i, (src, at, n) in enumerate(grads):
        cp = pltpu.make_async_copy(src, input_grad.at[pl.ds(at, n)], sem.at[4 + i])
        cp.start()
        copies.append(cp)

    root = jnp.sqrt(total[...])
    norm[0, 0] = jnp.max(root)
    clip = clip_norm / jnp.maximum(root[0:1, 0:1], clip_norm)
    hf = inner_r.shape[-1]
    hr = params[4][0].shape[0] // 2
    nvec, nlane = params[5][0].shape
    tr = table_grad.shape[0] // 2

    def adam(which, at, g, dec, rate):
        w, m, s = (ref[at] for ref in params[which])
        for ref, new in zip(news[which], adamw_update(w, m, s, g * clip, dec, rate)):
            ref[at] = new

    for j in range(3):
        g = qk_r[j] if j < 2 else va_r[0]
        adam(0, (j,), g, decay_rate, learn_rate)
    adam(1, (slice(None), slice(None)), va_r[1], decay_rate, learn_rate)
    for which, ref in ((2, inner_r), (3, outer_r)):
        for h in range(2):
            adam(which, (slice(None), slice(h * hf, (h + 1) * hf)), ref[h], decay_rate, learn_rate)
    turn[...] = jnp.zeros_like(turn)
    turn[0:nlane] = small_r[hr + 8 : hr + 8 + nlane]
    adam(5, (slice(None), slice(None)), jnp.transpose(turn[...])[0:nvec, 0:nlane], 0.0, vector_rate)
    for block, first in ((small_r, mp), (peer_small, 1 - mp)):
        at = pl.ds(pl.multiple_of(first * hr, 8), hr)
        adam(4, (at, slice(None)), block[0:hr], decay_rate, learn_rate)
    own_t, peer_t = small_r[hr : hr + tr], peer_small[hr : hr + tr]
    table_grad[0:tr] = jnp.where(mp == 0, own_t, peer_t)
    table_grad[tr : 2 * tr] = jnp.where(mp == 0, peer_t, own_t)
    for cp in copies:
        cp.wait()


def finish_fast(reduced, out_own, params, n_rows):
    (small_r, qk_r, va_r, inner_r, outer_r, dx, peer_out, peer_dx, peer_small, total) = reduced
    n_own, width = out_own.shape
    n_all = dx.shape[0]
    half_seq = n_all - n_own
    like = lambda a: jax.ShapeDtypeStruct(a.shape, a.dtype)
    vm = pl.BlockSpec(memory_space=pltpu.VMEM)
    hb = pl.BlockSpec(memory_space=ANY)
    sm = pl.BlockSpec(memory_space=pltpu.SMEM)
    out_shape = [
        jax.ShapeDtypeStruct((n_rows, width), BF),
        jax.ShapeDtypeStruct((n_rows, width), F32),
        jax.ShapeDtypeStruct((1, 1), F32),
    ]
    out_shape += [like(a) for a in params] + [jax.ShapeDtypeStruct((TAB_DEV, 128), F32)]
    n_full = n_own - half_seq
    outs = pl.pallas_call(
        finish_kernel,
        out_shape=out_shape,
        in_specs=[vm] * 29,
        out_specs=[hb, hb, sm] + [vm] * 19,
        scratch_shapes=[
            pltpu.VMEM((128, 128), F32),
            dma(7),
            pltpu.VMEM((n_full, width), F32),
            pltpu.VMEM((n_full, width), F32),
            pltpu.VMEM((2 * half_seq, width), F32),
        ],
        compiler_params=pltpu.CompilerParams(vmem_limit_bytes=63 * 2**20),
        name="finish",
    )(small_r, peer_small, qk_r, va_r, inner_r, outer_r, total, out_own, peer_out, dx, peer_dx, *params)
    return tuple(outs[:2]) + (outs[2].reshape(()),) + tuple(outs[3:])


def gather_plain(shards, small, rows):
    def both(v, axis):
        v = lax.all_gather(v, "dp", axis=axis, tiled=True)
        return lax.all_gather(v, "mp", axis=2, tiled=True)

    return [both(small[None], 0)] + [both(v, 1) for v in shards]


def reduce_plain(grads, small, own_out, own_dx, rows):
    def both(v, axis, wide):
        v = lax.psum_scatter(v.astype(F32), "mp", scatter_dimension=wide, tiled=True)
        return lax.psum_scatter(v, "dp", scatter_dimension=axis, tiled=True)

    small_sum = both(small, 0, 2)[0]
    sums = [both(g, 1, 2) for g in grads]
    ox = 1 - lax.axis_index("mp")
    swap = [(0, 1), (1, 0)]
    peer_out = lax.ppermute(own_out, "mp", swap)
    peer_dx = lax.ppermute(own_dx, "mp", swap)
    peer_small = lax.ppermute(small_sum, "mp", swap)
    squares = sum(squared(g) for g in sums) + squared(small_sum[:-4])
    total = lax.psum(squares, ("dp", "mp"))
    return [small_sum] + sums + [peer_out, peer_dx, peer_small, jnp.full((8, 128), total)]


def forward_plain(lengths, tokens, w_qkv, w_attn, w_inner, w_outer, w_proj, vectors):
    mp = lax.axis_index("mp")
    n_dp = lax.axis_size("dp")
    seqs = lengths.shape[0]
    all_rows, width = tokens.shape
    seq_len = all_rows // seqs
    full = seqs // 2
    n_full, n_half = full * seq_len, seq_len // 2
    n_own = n_full + n_half
    heads = width // HEAD_DIM
    rows, half_ff = w_qkv.shape[1], w_inner.shape[1]
    nvec, vec_lanes = vectors.shape
    half_rows = rows // 2
    score_scale = HEAD_DIM ** (-0.5)

    def two(v):
        return v.reshape(rows, 2, half_ff // 2).transpose(1, 0, 2)

    qk_s = w_qkv[:2].astype(BF)
    va_s = jnp.stack([w_qkv[2], w_attn]).astype(BF)
    vec_pad = jnp.pad(vectors, ((0, 0), (0, 128 - vec_lanes)))
    proj_half = lax.dynamic_slice_in_dim(w_proj, mp * half_rows, half_rows, 0)
    small_s = jnp.concatenate([proj_half, vec_pad], axis=0)
    small_g, qk, va, inner, outer = gather_plain(
        [qk_s, va_s, two(w_inner.astype(BF)), two(w_outer.astype(BF))], small_s, rows
    )
    small_g = small_g.reshape(n_dp, half_rows + nvec, 2, 128)
    proj = small_g[:, :half_rows].transpose(0, 2, 1, 3).reshape(width, 128)
    vec = small_g[:, half_rows:, :, :vec_lanes].transpose(1, 0, 2, 3).reshape(nvec, width)
    ff_rows = nvec - 8
    b_inner = vec[5 : 5 + ff_rows].reshape(2, 2, half_ff // 2).transpose(1, 0, 2).reshape(2, half_ff)

    a0 = mp * (n_full + seq_len)
    h0 = n_full + mp * n_half
    o0 = n_full + (1 - mp) * n_half
    x_all = jnp.concatenate(
        [
            lax.dynamic_slice_in_dim(tokens, a0, n_full, 0),
            lax.dynamic_slice_in_dim(tokens, h0, n_half, 0),
            lax.dynamic_slice_in_dim(tokens, o0, n_half, 0),
        ]
    )
    x_own = x_all[:n_own]
    my_seqs = jnp.concatenate([mp * (full + 1) + jnp.arange(full), jnp.array([full])])
    my_len = lengths[my_seqs]
    pos = jnp.arange(seq_len)
    pos_last = jnp.where(pos < n_half, pos + mp * n_half, pos - n_half + (1 - mp) * n_half)
    valids = (pos[None, :] < my_len[:full, None], pos_last[None, :] < my_len[full:, None])

    q = (jnp.dot(x_own, qk[0], preferred_element_type=F32) + vec[0]).astype(BF)
    k = jnp.dot(x_all, qk[1], preferred_element_type=F32).astype(BF)
    v = (jnp.dot(x_all, va[0], preferred_element_type=F32) + vec[1]).astype(BF)
    probs, outs = [], []
    for qh, kh, vh, valid in zip(*(halves(t, n_full, seq_len) for t in (q, k, v)), valids):
        s = jnp.einsum("gqhe,gkhe->ghqk", qh, kh, preferred_element_type=F32) * score_scale
        s = jnp.where(valid[:, None, None, :], s, -1000000000.0)
        pb = jax.nn.softmax(s, axis=-1).astype(BF)
        o = jnp.einsum("ghqk,gkhe->gqhe", pb, vh, preferred_element_type=F32)
        outs.append(o.reshape(-1, width).astype(BF))
        probs.append(pb.reshape((-1,) + pb.shape[2:]))
    mixed = jnp.concatenate(outs)

    def norm(z):
        centred = z - jnp.mean(z, axis=-1, keepdims=True)
        root = lax.rsqrt(jnp.mean(centred * centred, axis=-1, keepdims=True) + ln_epsilon)
        return centred * root, jnp.broadcast_to(root, (n_own, 128))

    attn = jnp.einsum("te,de->td", mixed, va[1], preferred_element_type=F32)
    xh1, r1 = norm(x_own.astype(F32) + attn + vec[2])
    h1 = xh1 * vec[3] + vec[4]
    u = jnp.einsum("td,hdf->htf", h1.astype(BF), inner, preferred_element_type=F32) + b_inner[:, None, :]
    tail = 0.5 * (1.0 + lax.erf(u * 0.7071067811865476))
    g = (u * tail).astype(BF)
    gp = (tail + u * (0.3989422804014327 * jnp.exp(-0.5 * u * u))).astype(BF)
    f = jnp.einsum("htf,hdf->td", g, outer, preferred_element_type=F32)
    xh2, r2 = norm(h1 + f + vec[5 + ff_rows])
    out_own = (xh2 * vec[6 + ff_rows] + vec[7 + ff_rows]).astype(BF)
    vec = jnp.pad(vec, ((0, 16 - nvec), (0, 0)))
    return [qk, va, inner, outer, x_all, q, k, v, *probs, mixed, xh1, r1, g, gp, xh2, r2, proj, vec, out_own]


def halves(t, n_full, seq_len):
    heads = t.shape[1] // HEAD_DIM
    last = t.shape[0] - n_full
    return (
        t[:n_full].reshape(n_full // seq_len, seq_len, heads, HEAD_DIM),
        t[n_full:].reshape(1, last, heads, HEAD_DIM),
    )


def pass_plain(lengths, tokens, cotangent, doc_ids, doc_rows, w_qkv, w_attn, w_inner, w_outer, w_proj, vectors):
    mp = lax.axis_index("mp")
    n_dp, n_mp = lax.axis_size("dp"), lax.axis_size("mp")
    seqs = lengths.shape[0]
    all_rows, width = tokens.shape
    seq_len = all_rows // seqs
    full = seqs // 2
    n_full, n_half = full * seq_len, seq_len // 2
    n_own = n_full + n_half
    rows, half_ff = w_qkv.shape[1], w_inner.shape[1]
    half_rows = rows // 2
    nvec, vec_lanes = vectors.shape
    ff_rows = nvec - 8
    score_scale = HEAD_DIM ** (-0.5)

    saved = forward_plain(lengths, tokens, w_qkv, w_attn, w_inner, w_outer, w_proj, vectors)
    (qk, va, inner, outer, x_all, q, k, v, p_ab, p_c, mixed, xh1, r1, act_low, slope, xh2, r2, proj, vec, out_own) = saved
    qk = qk.reshape(2, width, width)
    va = va.reshape(2, width, width)
    inner = inner.reshape(2, width, half_ff)
    outer = outer.reshape(2, width, half_ff)
    x_own = x_all[:n_own]
    proj = proj.astype(BF)
    a0 = mp * (n_full + seq_len)
    h0 = n_full + mp * n_half
    cot = jnp.concatenate(
        [lax.dynamic_slice_in_dim(cotangent, a0, n_full, 0), lax.dynamic_slice_in_dim(cotangent, h0, n_half, 0)]
    )
    my_seqs = jnp.concatenate([mp * (full + 1) + jnp.arange(full), jnp.array([full])])

    n_mine = full + 1
    mine = jnp.where((jnp.arange(n_mine) < full) | (mp == 0), 1.0, 0.0).astype(F32)
    cls_low = out_own[:: seq_len][:n_mine]
    docs = doc_rows[my_seqs].astype(F32)
    ids = doc_ids[my_seqs]
    query = jnp.dot(cls_low, proj, preferred_element_type=F32).astype(BF)
    query_float = query.astype(F32)
    doc_scores = jnp.einsum("gp,gkp->gk", query_float, docs, precision=highest_mode) * retrieval_scale
    soft = jax.nn.softmax(doc_scores, axis=-1)
    target = (jnp.arange(doc_scores.shape[1]) == 0).astype(F32)
    score_grad = (soft - target[None, :]) * retrieval_scale * mine[:, None]
    query_grad = jnp.einsum("gk,gkp->gp", score_grad, docs, precision=highest_mode).astype(BF)
    row_grads = score_grad[:, :, None] * query_float[:, None, :]
    cls_grad = jnp.einsum("gp,dp->gd", query_grad, proj, preferred_element_type=F32)
    proj_grad = jnp.einsum("gd,gp->dp", cls_low, query_grad, preferred_element_type=F32)
    table_rows = TAB_DEV * n_dp
    one_hot = (jnp.arange(table_rows)[:, None] == ids.reshape(1, -1)).astype(F32)
    table_local = jnp.dot(one_hot, row_grads.reshape(-1, row_grads.shape[2]), precision=highest_mode)

    def norm_back(dy, hat, root, gain):
        e = dy * gain
        back_ = e - jnp.mean(e, axis=-1, keepdims=True) - hat * jnp.mean(e * hat, axis=-1, keepdims=True)
        return back_ * root[:, :1], jnp.sum(dy * hat, axis=0), jnp.sum(dy, axis=0)

    dy = cot.astype(F32)
    first_rows = jnp.arange(n_mine) * seq_len
    dy = dy.at[first_rows].add(cls_grad)
    dz2, dg2, dc2 = norm_back(dy, xh2, r2, vec[6 + ff_rows])
    df = dz2.astype(BF)
    dg = jnp.einsum("td,hdf->htf", df, outer, preferred_element_type=F32)
    g_outer = jnp.einsum("td,htf->hdf", df, act_low, preferred_element_type=F32).astype(BF)
    du = (dg * slope.astype(F32)).astype(BF)
    normed_low = (xh1 * vec[3] + vec[4]).astype(BF)
    g_inner = jnp.einsum("td,htf->hdf", normed_low, du, preferred_element_type=F32).astype(BF)
    dh1 = jnp.einsum("htf,hdf->td", du, inner, preferred_element_type=F32) + dz2
    dz1, dg1, dc1 = norm_back(dh1, xh1, r1, vec[3])
    da = dz1.astype(BF)
    do = jnp.dot(da, va[1], preferred_element_type=F32).astype(BF)
    g_attn = jnp.einsum("td,te->de", da, mixed, preferred_element_type=F32)
    dqs, dks, dvs = [], [], []
    probs_of = (p_ab.reshape(full, -1, seq_len, seq_len), p_c.reshape(1, -1, n_half, seq_len))
    for qh, kh, vh, doh, pb in zip(*(halves(t, n_full, seq_len) for t in (q, k, v, do)), probs_of):
        probs = pb.astype(F32)
        dp_ = jnp.einsum("gqhe,gkhe->ghqk", doh, vh, preferred_element_type=F32)
        delta = jnp.sum(probs * dp_, axis=-1, keepdims=True)
        ds_ = (probs * (dp_ - delta)).astype(BF)
        dqs.append((jnp.einsum("ghqk,gkhe->gqhe", ds_, kh, preferred_element_type=F32) * score_scale).reshape(-1, width))
        dks.append((jnp.einsum("ghqk,gqhe->gkhe", ds_, qh, preferred_element_type=F32) * score_scale).reshape(-1, width))
        dvs.append(jnp.einsum("ghqk,gqhe->gkhe", pb, doh, preferred_element_type=F32).reshape(-1, width))
    dq = jnp.concatenate(dqs).astype(BF)
    dk = jnp.concatenate(dks).astype(BF)
    dv = jnp.concatenate(dvs).astype(BF)
    g_q = jnp.einsum("td,te->de", x_own, dq, preferred_element_type=F32)
    g_k = jnp.einsum("td,te->de", x_all, dk, preferred_element_type=F32)
    g_v = jnp.einsum("td,te->de", x_all, dv, preferred_element_type=F32)
    g_qk = jnp.stack([g_q, g_k]).astype(BF)
    g_va = jnp.stack([g_v, g_attn]).astype(BF)
    dx_own = jnp.einsum("te,de->td", dq, qk[0], preferred_element_type=F32) + dz1
    dx_all = jnp.einsum("te,de->td", dk, qk[1], preferred_element_type=F32)
    dx_all = dx_all + jnp.einsum("te,de->td", dv, va[0], preferred_element_type=F32)
    dx = jnp.concatenate([dx_all[:n_own] + dx_own, dx_all[n_own:]]).astype(BF)
    db_inner = jnp.sum(du.astype(F32), axis=1)
    db_inner = db_inner.reshape(2, 2, half_ff // 2).transpose(1, 0, 2).reshape(ff_rows, width)
    vec_grad = jnp.concatenate(
        [
            jnp.stack(
                [
                    jnp.sum(dq.astype(F32), axis=0),
                    jnp.sum(dv.astype(F32), axis=0),
                    jnp.sum(dz1, axis=0),
                    dg1,
                    dc1,
                ]
            ),
            db_inner,
            jnp.stack([jnp.sum(dz2, axis=0), dg2, dc2]),
        ]
    )
    vg = vec_grad.reshape(nvec, n_dp, 2, vec_lanes).transpose(1, 0, 2, 3)
    vg = jnp.pad(vg, ((0, 0), (0, 0), (0, 0), (0, 128 - vec_lanes))).reshape(n_dp, nvec, 256)
    pg = proj_grad.reshape(n_dp, 2, half_rows, 128).transpose(0, 2, 1, 3).reshape(n_dp, half_rows, 256)
    tg = table_local.reshape(n_dp, 2, TAB_DEV // 2, 128).transpose(0, 2, 1, 3).reshape(n_dp, TAB_DEV // 2, 256)
    small = jnp.concatenate([pg, vg, tg], axis=1)

    return out_own, dx, *reduce_plain([g_qk, g_va, g_inner, g_outer], small, out_own, dx, rows)


def local(
    tokens, cotangent, lengths, doc_ids, doc_rows,
    w_qkv, m_qkv, v_qkv, w_attn, m_attn, v_attn, w_inner, m_inner, v_inner,
    w_outer, m_outer, v_outer, w_proj, m_proj, v_proj, vectors, m_vectors, v_vectors,
):
    mp = lax.axis_index("mp")
    n_dp, n_mp = lax.axis_size("dp"), lax.axis_size("mp")
    fast = n_dp == NZ * NY * NC and n_mp == NX
    seqs = lengths.shape[0]
    all_rows, width = tokens.shape
    seq_len = all_rows // seqs
    full = seqs // 2
    n_full, n_half = full * seq_len, seq_len // 2
    n_own = n_full + n_half
    rows, half_ff = w_qkv.shape[1], w_inner.shape[1]
    half_rows = rows // 2
    nvec, vec_lanes = vectors.shape
    ff_rows = nvec - 8
    score_scale = HEAD_DIM ** (-0.5)

    if fast:
        saved = forward_fast(lengths, tokens, w_qkv, w_attn, w_inner, w_outer, w_proj, vectors)
        reduced = backward_fast(doc_ids, cotangent, doc_rows, saved, rows)
        params = (w_qkv, m_qkv, v_qkv, w_attn, m_attn, v_attn, w_inner, m_inner, v_inner)
        params += (w_outer, m_outer, v_outer, w_proj, m_proj, v_proj, vectors, m_vectors, v_vectors)
        return finish_fast(reduced, saved[-1], params, all_rows)
    if not fast:
        (out_own, dx, small_r, qk_r, va_r, inner_r, outer_r, peer_out, peer_dx, peer_small, total) = pass_plain(
            lengths, tokens, cotangent, doc_ids, doc_rows, w_qkv, w_attn, w_inner, w_outer, w_proj, vectors
        )
        vector_r = small_r[half_rows : half_rows + nvec, :vec_lanes]
        table_at = half_rows + nvec

    def whole_rows(own, peer):
        lo = jnp.where(mp == 0, own[:n_own], peer[:n_own])
        hi = jnp.where(mp == 0, peer[:n_own], own[:n_own])
        return lo, hi

    lo, hi = whole_rows(out_own, peer_out)
    out_tokens = jnp.concatenate([lo, hi[n_full:], hi[:n_full]])
    lo, hi = whole_rows(dx.astype(F32), peer_dx.astype(F32))
    tail = jnp.where(mp == 0, dx[n_own:], peer_dx[n_own:]).astype(F32)
    tail_hi = jnp.where(mp == 0, peer_dx[n_own:], dx[n_own:]).astype(F32)
    input_grad = jnp.concatenate(
        [lo[:n_full], lo[n_full:] + tail_hi, hi[n_full:] + tail, hi[:n_full]]
    )

    def both_halves(at, count):
        mine_, peer_ = small_r[at : at + count], peer_small[at : at + count]
        return jnp.concatenate(
            [jnp.where(mp == 0, mine_, peer_), jnp.where(mp == 0, peer_, mine_)]
        )

    proj_r = both_halves(0, half_rows)
    table_grad = both_halves(table_at, TAB_DEV // 2)
    qkv_r = jnp.stack([qk_r[0], qk_r[1], va_r[0]])
    attn_r = va_r[1]

    def back(v):
        return v.transpose(1, 0, 2).reshape(rows, half_ff)

    inner_r, outer_r = back(inner_r), back(outer_r)
    grad_norm = jnp.sqrt(total[0, 0])
    clip = clip_norm / jnp.maximum(grad_norm, clip_norm)
    results = [out_tokens, input_grad, grad_norm]
    for w, m, s, g, dec, rate in (
        (w_qkv, m_qkv, v_qkv, qkv_r, decay_rate, learn_rate),
        (w_attn, m_attn, v_attn, attn_r, decay_rate, learn_rate),
        (w_inner, m_inner, v_inner, inner_r, decay_rate, learn_rate),
        (w_outer, m_outer, v_outer, outer_r, decay_rate, learn_rate),
        (w_proj, m_proj, v_proj, proj_r, decay_rate, learn_rate),
        (vectors, m_vectors, v_vectors, vector_r, 0.0, vector_rate),
    ):
        results += list(adamw_update(w, m, s, g * clip, dec, rate))
    return tuple(results) + (table_grad,)


def solution(mesh):
    mat = P("dp", "mp")
    rep = P("dp", None)
    qkv = P(None, "dp", "mp")
    vec = P(None, ("dp", "mp"))
    placed = (rep, rep, P("dp"), rep, P("dp", None, None), qkv, qkv, qkv)
    placed += (mat,) * 9 + (rep,) * 3 + (vec,) * 3
    given = (rep, rep, P(), qkv, qkv, qkv) + (mat,) * 9 + (rep,) * 3 + (vec,) * 3 + (rep,)
    return jax.shard_map(local, mesh=mesh, in_specs=placed, out_specs=given, check_vma=False)
```
